32 devices in a mesh: dp: 4 (over y, x), seq: 8 (over z, core).
Axes of the slice: x: 2, y: 2, z: 4, core: 2. Of those that a mesh axis runs over, the one named last changes fastest.
Arguments:
- inputs: bfloat16 [4, 1280, 1152], P('dp', 'seq'), may hold values from -6 to 6
- skipped: bfloat16 [4, 1280, 1152], P('dp', 'seq'), may hold values from -6 to 6
- item_lengths: int32 [4, 5], P('dp'), may hold values from 0 to 1026, as said below
- skip_w: bfloat16 [2304, 1152], P(('dp', 'seq')), may hold values from -0.125 to 0.125
- qkv_w: bfloat16 [1152, 3456], P(('dp', 'seq')), may hold values from -0.25 to 0.25
- proj_w: bfloat16 [1152, 1152], P(('dp', 'seq')), may hold values from -1 to 1
- fc1_w: bfloat16 [1152, 4608], P(('dp', 'seq')), may hold values from -0.1875 to 0.1875
- fc2_w: bfloat16 [4608, 1152], P(('dp', 'seq')), may hold values from -0.09375 to 0.09375
- skip_b: bfloat16 [1152], P(('dp', 'seq')), may hold values from -3 to 3
- ln1_g: bfloat16 [1152], P(('dp', 'seq')), may hold values from 0.25 to 1.75
- ln1_b: bfloat16 [1152], P(('dp', 'seq')), may hold values from -3 to 3
- proj_b: bfloat16 [1152], P(('dp', 'seq')), may hold values from -3 to 3
- ln2_g: bfloat16 [1152], P(('dp', 'seq')), may hold values from 0.25 to 1.75
- ln2_b: bfloat16 [1152], P(('dp', 'seq')), may hold values from -3 to 3
- fc1_b: bfloat16 [4608], P(('dp', 'seq')), may hold values from -3 to 3
- fc2_b: bfloat16 [1152], P(('dp', 'seq')), may hold values from -3 to 3
- cotangent: bfloat16 [4, 1280, 1152], P('dp', 'seq'), may hold values from -6 to 6
Outputs:
- output: bfloat16 [4, 1280, 1152], P('dp', 'seq')
- input_grad: float32 [4, 1280, 1152], P('dp', 'seq')
- skip_grad: float32 [4, 1280, 1152], P('dp', 'seq')
- skip_w_grad: float32 [2304, 1152], P(('dp', 'seq'))
- qkv_w_grad: float32 [1152, 3456], P(('dp', 'seq'))
- proj_w_grad: float32 [1152, 1152], P(('dp', 'seq'))
- fc1_w_grad: float32 [1152, 4608], P(('dp', 'seq'))
- fc2_w_grad: float32 [4608, 1152], P(('dp', 'seq'))
- skip_b_grad: float32 [1152], P(('dp', 'seq'))
- ln1_g_grad: float32 [1152], P(('dp', 'seq'))
- ln1_b_grad: float32 [1152], P(('dp', 'seq'))
- proj_b_grad: float32 [1152], P(('dp', 'seq'))
- ln2_g_grad: float32 [1152], P(('dp', 'seq'))
- ln2_b_grad: float32 [1152], P(('dp', 'seq'))
- fc1_b_grad: float32 [4608], P(('dp', 'seq'))
- fc2_b_grad: float32 [1152], P(('dp', 'seq'))
The draws below stay inside these ranges and needn't reach their ends.
Inputs may be any that keep to these rules, and one draw needn't show every extreme that they name: `item_lengths`: in each row the nonzero lengths, each 258 or 1026, stand first and sum to at most 1280; the first is 1026; later slots are 0.
All inputs are finite; a program needn't handle non-finite values.
Results may differ from the reference program's by a relative error of at most 0.024.
Values may be sent and summed in bfloat16 or wider, within the bound.
No kernel may reach another device: no remote copies, remote signals or barrier semaphores. Data moves between devices by JAX's collectives and lax.ppermute only.
A program may use at most 256 MiB of HBM per device.

```python
import math
import jax
import jax.numpy as jnp
from jax import lax

D = 1152
FF = 4608
HEADS = 16
HEAD_DIM = 72
ITEM_S = 258
ITEM_L = 1026
ROWS = 4
ROW_TOK = 1280
SLOTS = 5


def draw_item_lengths(key, part):
    picks = jax.random.randint(key, (ROWS, SLOTS), 0, 2)
    raw = jnp.where(picks == 1, ITEM_L, ITEM_S).astype(jnp.int32)
    raw = raw.at[:, 0].set(ITEM_L)
    ends = jnp.cumsum(raw, axis=1)
    return jnp.where(ends <= ROW_TOK, raw, 0).astype(jnp.int32)


def shard_levels(own_key, shape, split, smallest, largest):
    def one(dim, shards_of):
        draws = jax.random.uniform(jax.random.fold_in(jax.random.fold_in(own_key, 6), dim), (shards_of,), jnp.float32, smallest / len(split), largest / len(split))
        return jnp.repeat(jnp.exp(draws), shape[dim] // shards_of).reshape((-1,) + (1,) * (len(shape) - dim - 1))

    factor_of = one(*split[0])
    for cut in split[1:]:
        factor_of = factor_of * one(*cut)
    return factor_of


def normal_values(key, dims, width, limit, split=(), held_as=jnp.bfloat16):
    values = jax.random.normal(key, dims, jnp.float32) * width
    if len(split) > 0:
        values = shard_levels(key, dims, split, -0.22, 0.18) * values
    return jnp.clip(values, min=-limit, max=limit).astype(held_as)


def setup_inputs(seed: int = 0) -> dict:
    key_list = jax.random.split(jax.random.key(seed), 18)
    inputs = normal_values(key_list[0], (ROWS, ROW_TOK, D), 1.0, 6.0, ((0, 4), (1, 8)))
    skipped = normal_values(key_list[1], (ROWS, ROW_TOK, D), 1.0, 6.0, ((0, 4), (1, 8)))
    item_lengths = draw_item_lengths(jax.random.fold_in(key_list[17], 71), 0)
    skip_w = normal_values(key_list[3], (2 * D, D), (2 * D) ** -0.5, 0.125, ((0, 32),))
    qkv_w = normal_values(key_list[4], (D, 3 * D), (D // 2) ** -0.5, 0.25, ((0, 32),))
    proj_w = normal_values(key_list[5], (D, D), (D // 32) ** -0.5, 1.0, ((0, 32),))
    fc1_w = normal_values(key_list[6], (D, FF), D ** -0.5, 0.1875, ((0, 32),))
    fc2_w = normal_values(key_list[7], (FF, D), FF ** -0.5, 0.09375, ((0, 32),))
    skip_b = normal_values(key_list[8], (D,), 0.5, 3.0, ((0, 32),))
    ln1_g = jnp.clip(1.0 + 0.15 * jax.random.normal(key_list[9], (D,), jnp.float32), 0.25, 1.75).astype(jnp.bfloat16)
    ln1_b = normal_values(key_list[10], (D,), 0.5, 3.0, ((0, 32),))
    proj_b = normal_values(key_list[11], (D,), 0.5, 3.0, ((0, 32),))
    ln2_g = jnp.clip(1.0 + 0.15 * jax.random.normal(key_list[12], (D,), jnp.float32), 0.25, 1.75).astype(jnp.bfloat16)
    ln2_b = normal_values(key_list[13], (D,), 0.5, 3.0, ((0, 32),))
    fc1_b = normal_values(key_list[14], (FF,), 0.5, 3.0, ((0, 32),))
    fc2_b = normal_values(key_list[15], (D,), 0.5, 3.0, ((0, 32),))
    cotangent = normal_values(key_list[16], (ROWS, ROW_TOK, D), 1.0, 6.0, ((0, 4), (1, 8)))
    return dict(inputs=inputs, skipped=skipped, item_lengths=item_lengths, skip_w=skip_w, qkv_w=qkv_w, proj_w=proj_w, fc1_w=fc1_w, fc2_w=fc2_w, skip_b=skip_b, ln1_g=ln1_g, ln1_b=ln1_b, proj_b=proj_b, ln2_g=ln2_g, ln2_b=ln2_b, fc1_b=fc1_b, fc2_b=fc2_b, cotangent=cotangent)


@jax.custom_vjp
def low(v):
    return lax.optimization_barrier(v.astype(jnp.bfloat16)).astype(jnp.float32)

@jax.custom_vjp
def low_back(v):
    return v

def low_keep(v):
    return (low(v), None)

def low_pass(kept, grad):
    return (grad,)

def back_keep(v):
    return (v, None)

def back_low(kept, grad):
    return (low(grad),)
low.defvjp(low_keep, low_pass)
low_back.defvjp(back_keep, back_low)
EPSILON = 1e-05
HIGHEST = lax.Precision.HIGHEST
NEGATIVE = -1e+30

def matmul(left, right):
    return jnp.dot(left, right, precision=HIGHEST, preferred_element_type=jnp.float32)

def layer_norm(hvals, gain_factor, shift_bias):
    centered_rows = hvals - lax.optimization_barrier(jnp.mean(hvals, axis=-1, keepdims=True))
    spread = lax.optimization_barrier(jnp.mean(centered_rows * centered_rows, axis=-1, keepdims=True))
    return centered_rows * lax.rsqrt(spread + EPSILON) * gain_factor + shift_bias

def segment_ids(lengths):
    ends = jnp.cumsum(lengths)
    places = jnp.arange(ROW_TOK, dtype=jnp.int32)
    return lax.optimization_barrier(jnp.sum((ends[None, :] <= places[:, None]).astype(jnp.int32), axis=1))

def forward_over_rows(row_input, row_skip, params, segment_labels):
    skip_w, qkv_w, proj_w, fc1_w, fc2_w, skip_b, ln1_g, ln1_b, proj_b, ln2_g, ln2_b, fc1_b, fc2_b = params
    joined = jnp.concatenate([row_input, row_skip], axis=1)
    first_output = low_back(matmul(joined, skip_w)) + skip_b
    first_normalized = low(layer_norm(first_output, ln1_g, ln1_b))
    triple = low(low_back(matmul(first_normalized, qkv_w)))
    queries = triple[:, :D].reshape(ROW_TOK, HEADS, HEAD_DIM)
    keys = triple[:, D:2 * D].reshape(ROW_TOK, HEADS, HEAD_DIM)
    values = triple[:, 2 * D:].reshape(ROW_TOK, HEADS, HEAD_DIM)
    scale = HEAD_DIM ** (-0.5)

    def one_block(item):
        qblock, sblock = item
        raw = low_back(jnp.einsum('qhd,khd->hqk', qblock, keys, precision=HIGHEST))
        allowed = sblock[:, None] == segment_labels[None, :]
        logits = jnp.where(allowed[None], raw * scale, NEGATIVE)
        probs = low(jax.nn.softmax(logits, axis=-1))
        return jnp.einsum('hqk,khd->qhd', probs, values, precision=HIGHEST)
    block_len = math.gcd(ROW_TOK, 512)
    qblocks = queries.reshape(ROW_TOK // block_len, block_len, HEADS, HEAD_DIM)
    sblocks = segment_labels.reshape(ROW_TOK // block_len, block_len)
    attended = lax.map(jax.checkpoint(one_block), (qblocks, sblocks)).reshape(ROW_TOK, D)
    attended = low(low_back(attended))
    second_output = first_output + low_back(matmul(attended, proj_w)) + proj_b
    second_normalized = low(layer_norm(second_output, ln2_g, ln2_b))
    hidden = low(jax.nn.gelu(low_back(matmul(second_normalized, fc1_w)) + fc1_b, approximate=False))
    return second_output + low_back(matmul(hidden, fc2_w)) + fc2_b

def reference(inputs, skipped, item_lengths, skip_w, qkv_w, proj_w, fc1_w, fc2_w, skip_b, ln1_g, ln1_b, proj_b, ln2_g, ln2_b, fc1_b, fc2_b, cotangent):
    params = tuple((p.astype(jnp.float32) for p in (skip_w, qkv_w, proj_w, fc1_w, fc2_w, skip_b, ln1_g, ln1_b, proj_b, ln2_g, ln2_b, fc1_b, fc2_b)))

    def one_row(totals, row):
        row_input, row_skip, lengths, row_cot = row
        segment_labels = segment_ids(lengths)

        def execute_block(input_values, skip_values, parameter_values):
            return forward_over_rows(input_values, skip_values, parameter_values, segment_labels)
        result, pull = jax.vjp(execute_block, row_input.astype(jnp.float32), row_skip.astype(jnp.float32), params)
        grad_input, grad_skip, grad_params = pull(row_cot.astype(jnp.float32))
        totals = jax.tree.map(jnp.add, totals, grad_params)
        return (totals, (result.astype(jnp.bfloat16), grad_input, grad_skip))
    zeros = tuple((jnp.zeros_like(p) for p in params))
    totals, (outputs, input_grads, skip_grads) = lax.scan(one_row, zeros, (inputs, skipped, item_lengths, cotangent))
    return (outputs, input_grads, skip_grads) + tuple(totals)
```

```python
from functools import partial
import math

import jax
import jax.numpy as jnp
from jax import lax
from jax.sharding import PartitionSpec as P

HEADS = 16
HEAD_DIM = 72


EPSILON = 1e-05
NEGATIVE = -1e30


def norm_forward_pieces(hvals, gain_factor, shift_bias):
    centered_rows = hvals - jnp.mean(hvals, axis=-1, keepdims=True)
    inverse_deviation = lax.rsqrt(
        jnp.mean(centered_rows * centered_rows, axis=-1, keepdims=True) + EPSILON
    )
    standardized_input = centered_rows * inverse_deviation
    return (standardized_input * gain_factor + shift_bias, standardized_input, inverse_deviation)


def norm_backward_rows(incoming_gradient, standardized_input, inverse_deviation, gain_factor):
    scaled_rows = incoming_gradient * gain_factor
    passed_through = inverse_deviation * (
        scaled_rows
        - jnp.mean(scaled_rows, axis=-1, keepdims=True)
        - standardized_input * jnp.mean(scaled_rows * standardized_input, axis=-1, keepdims=True)
    )
    return (
        passed_through,
        jnp.sum(incoming_gradient * standardized_input, axis=0),
        jnp.sum(incoming_gradient, axis=0),
    )


def segment_of(lengths, places):
    running = jnp.zeros_like(lengths[:, :1])
    passed = jnp.zeros((lengths.shape[0], places.shape[0]), jnp.int32)
    for slot in range(lengths.shape[1]):
        running = running + lengths[:, slot : slot + 1]
        passed = passed + (running <= places[None, :]).astype(jnp.int32)
    return passed


def inner(left, right):
    return lax.dot_general(
        left, right, (((0,), (0,)), ((), ())), preferred_element_type=jnp.float32
    )


def times_transposed(left, right):
    return lax.dot_general(
        left, right, (((1,), (1,)), ((), ())), preferred_element_type=jnp.float32
    )


def key_blocks(step_fn, carry, piece):
    count = jax.tree.leaves(piece)[0].shape[1]
    block_len = math.gcd(count, 512)

    def advance(index, state):
        block = jax.tree.map(
            lambda part_array: lax.dynamic_slice_in_dim(
                part_array, index * block_len, block_len, 1
            ),
            piece,
        )
        return step_fn(state, block, index * block_len)

    return lax.fori_loop(0, count // block_len, advance, carry)


def on_device(
    inputs,
    skipped,
    item_lengths,
    skip_w,
    qkv_w,
    proj_w,
    fc1_w,
    fc2_w,
    skip_b,
    ln1_g,
    ln1_b,
    proj_b,
    ln2_g,
    ln2_b,
    fc1_b,
    fc2_b,
    cotangent,
):
    row_count, local_len, features = inputs.shape
    head_count = HEADS
    head_size = HEAD_DIM
    token_count = row_count * local_len
    scale = head_size ** (-0.5)
    single_precision = jnp.float32
    bf16 = jnp.bfloat16
    full = (
        lax.all_gather(skip_w, ("dp", "seq"), axis=0, tiled=True),
        lax.all_gather(qkv_w, ("dp", "seq"), axis=0, tiled=True),
        lax.all_gather(proj_w, ("dp", "seq"), axis=0, tiled=True),
        lax.all_gather(fc1_w, ("dp", "seq"), axis=0, tiled=True),
        lax.all_gather(fc2_w, ("dp", "seq"), axis=0, tiled=True),
        lax.all_gather(skip_b, ("dp", "seq"), axis=0, tiled=True),
        lax.all_gather(ln1_g, ("dp", "seq"), axis=0, tiled=True),
        lax.all_gather(ln1_b, ("dp", "seq"), axis=0, tiled=True),
        lax.all_gather(proj_b, ("dp", "seq"), axis=0, tiled=True),
        lax.all_gather(ln2_g, ("dp", "seq"), axis=0, tiled=True),
        lax.all_gather(ln2_b, ("dp", "seq"), axis=0, tiled=True),
        lax.all_gather(fc1_b, ("dp", "seq"), axis=0, tiled=True),
        lax.all_gather(fc2_b, ("dp", "seq"), axis=0, tiled=True),
    )
    (
        w_skip,
        w_qkv,
        w_proj,
        w_up,
        w_down,
        b_skip,
        first_norm_gain,
        first_norm_bias,
        b_proj,
        second_norm_gain,
        second_norm_bias,
        b_up,
        b_down,
    ) = full
    joined = jnp.concatenate([inputs, skipped], axis=2).reshape(token_count, 2 * features)
    first_output = jnp.dot(joined, w_skip, preferred_element_type=single_precision) + b_skip.astype(
        single_precision
    )
    first_normalized, first_standardized, first_inverse_deviation = norm_forward_pieces(
        first_output,
        first_norm_gain.astype(single_precision),
        first_norm_bias.astype(single_precision),
    )
    first_normalized = first_normalized.astype(bf16)
    triple = jnp.dot(first_normalized, w_qkv, preferred_element_type=single_precision).astype(bf16)
    queries = triple[:, :features].reshape(row_count, local_len, head_count, head_size)
    pairs = triple[:, features:].reshape(row_count, local_len, 2 * features)
    own_keys = pairs[:, :, :features].reshape(row_count, local_len, head_count, head_size)
    own_values = pairs[:, :, features:].reshape(row_count, local_len, head_count, head_size)
    offset = lax.axis_index("seq") * local_len
    query_segs = segment_of(item_lengths, offset + jnp.arange(local_len, dtype=jnp.int32))

    def scores_for(block, start):
        count = block.shape[1]
        keys = block[:, :, :features].reshape(row_count, count, head_count, head_size)
        values = block[:, :, features:].reshape(row_count, count, head_count, head_size)
        key_segs = segment_of(item_lengths, start + jnp.arange(count, dtype=jnp.int32))
        allowed = query_segs[:, None, :, None] == key_segs[:, None, None, :]
        raw = jnp.einsum("rqhd,rkhd->rhqk", queries, keys, preferred_element_type=single_precision)
        return (raw * scale, allowed, keys, values)

    def forward_block(carry, block, start):
        top, total, accum = carry
        logits, allowed, keys, values = scores_for(block, start)
        logits = jnp.where(allowed, logits, NEGATIVE)
        new_top = jnp.maximum(top, jnp.max(logits, axis=3))
        weights = jnp.where(allowed, jnp.exp(logits - new_top[..., None]), 0.0)
        decay = jnp.exp(top - new_top)
        total = total * decay + jnp.sum(weights, axis=3)
        update = jnp.einsum(
            "rhqk,rkhd->rqhd", weights.astype(bf16), values, preferred_element_type=single_precision
        )
        accum = accum * jnp.swapaxes(decay, 1, 2)[..., None] + update
        return (new_top, total, accum)

    start_state = (
        jnp.full((row_count, head_count, local_len), NEGATIVE, single_precision),
        jnp.zeros((row_count, head_count, local_len), single_precision),
        jnp.zeros((row_count, local_len, head_count, head_size), single_precision),
    )
    top, total, accum = key_blocks(
        forward_block, start_state, lax.all_gather(pairs, "seq", axis=1, tiled=True)
    )
    attended = accum / jnp.swapaxes(total, 1, 2)[..., None]
    log_total = top + jnp.log(total)
    attended_low = attended.reshape(token_count, features).astype(bf16)
    second_output = (
        first_output
        + jnp.dot(attended_low, w_proj, preferred_element_type=single_precision)
        + b_proj.astype(single_precision)
    )
    second_normalized, second_standardized, second_inverse_deviation = norm_forward_pieces(
        second_output,
        second_norm_gain.astype(single_precision),
        second_norm_bias.astype(single_precision),
    )
    second_normalized = second_normalized.astype(bf16)
    pre = jnp.dot(second_normalized, w_up, preferred_element_type=single_precision) + b_up.astype(
        single_precision
    )
    hidden = jax.nn.gelu(pre, approximate=False).astype(bf16)
    final = (
        second_output
        + jnp.dot(hidden, w_down, preferred_element_type=single_precision)
        + b_down.astype(single_precision)
    )
    output = final.astype(bf16).reshape(row_count, local_len, features)
    back = (
        lax.all_gather(skip_w, ("dp", "seq"), axis=0, tiled=True),
        lax.all_gather(qkv_w, ("dp", "seq"), axis=0, tiled=True),
        lax.all_gather(proj_w, ("dp", "seq"), axis=0, tiled=True),
        lax.all_gather(fc1_w, ("dp", "seq"), axis=0, tiled=True),
        lax.all_gather(fc2_w, ("dp", "seq"), axis=0, tiled=True),
        lax.all_gather(ln1_g, ("dp", "seq"), axis=0, tiled=True),
        lax.all_gather(ln2_g, ("dp", "seq"), axis=0, tiled=True),
    )
    k_skip, k_qkv, k_proj, k_up, k_down, first_gain_again, second_gain_again = back
    grad_out = cotangent.reshape(token_count, features)
    fc2_w_grad = inner(hidden, grad_out)
    fc2_b_grad = jnp.sum(grad_out.astype(single_precision), axis=0)
    hidden_grad = times_transposed(grad_out, k_down)
    gelu_value, gelu_pull = jax.vjp(partial(jax.nn.gelu, approximate=False), pre)
    pre_grad = gelu_pull(hidden_grad)[0]
    fc1_b_grad = jnp.sum(pre_grad, axis=0)
    pre_low = pre_grad.astype(bf16)
    fc1_w_grad = inner(second_normalized, pre_low)
    second_normalized_gradient = times_transposed(pre_low, k_up)
    through_two, ln2_g_grad, ln2_b_grad = norm_backward_rows(
        second_normalized_gradient,
        second_standardized,
        second_inverse_deviation,
        second_gain_again.astype(single_precision),
    )
    second_grad = grad_out.astype(single_precision) + through_two
    proj_b_grad = jnp.sum(second_grad, axis=0)
    second_low = second_grad.astype(bf16)
    proj_w_grad = inner(attended_low, second_low)
    attended_grad = (
        times_transposed(second_low, k_proj)
        .astype(bf16)
        .reshape(row_count, local_len, head_count, head_size)
    )
    delta = jnp.swapaxes(jnp.sum(attended_grad.astype(single_precision) * attended, axis=3), 1, 2)

    def query_terms(block, start):
        logits, allowed, keys, values = scores_for(block, start)
        probs = jnp.where(allowed, jnp.exp(logits - log_total[..., None]), 0.0)
        prob_grad = jnp.einsum(
            "rqhd,rkhd->rhqk", attended_grad, values, preferred_element_type=single_precision
        )
        logit_grad = (probs * (prob_grad - delta[..., None]) * scale).astype(bf16)
        return (probs, logit_grad, keys)

    def query_block(carry, block, start):
        probs, logit_grad, keys = query_terms(block, start)
        return carry + jnp.einsum(
            "rhqk,rkhd->rqhd", logit_grad, keys, preferred_element_type=single_precision
        )

    query_grad = key_blocks(
        query_block,
        jnp.zeros((row_count, local_len, head_count, head_size), single_precision),
        lax.all_gather(pairs, "seq", axis=1, tiled=True),
    )
    row_lse, row_delta = (
        lax.all_gather(jnp.swapaxes(log_total, 1, 2), "seq", axis=1, tiled=True),
        lax.all_gather(jnp.swapaxes(delta, 1, 2), "seq", axis=1, tiled=True),
    )

    def key_block(carry, piece, start):
        key_total, value_total = carry
        far_queries, far_grads = piece
        count = far_queries.shape[1]
        far_segs = segment_of(item_lengths, start + jnp.arange(count, dtype=jnp.int32))
        allowed = far_segs[:, None, :, None] == query_segs[:, None, None, :]
        lse_piece = jnp.swapaxes(lax.dynamic_slice_in_dim(row_lse, start, count, 1), 1, 2)
        delta_piece = jnp.swapaxes(lax.dynamic_slice_in_dim(row_delta, start, count, 1), 1, 2)
        logits = (
            jnp.einsum(
                "rqhd,rkhd->rhqk", far_queries, own_keys, preferred_element_type=single_precision
            )
            * scale
        )
        probs = jnp.where(allowed, jnp.exp(logits - lse_piece[..., None]), 0.0)
        value_total = value_total + jnp.einsum(
            "rhqk,rqhd->rkhd",
            probs.astype(bf16),
            far_grads,
            preferred_element_type=single_precision,
        )
        prob_grad = jnp.einsum(
            "rqhd,rkhd->rhqk", far_grads, own_values, preferred_element_type=single_precision
        )
        logit_grad = (probs * (prob_grad - delta_piece[..., None]) * scale).astype(bf16)
        key_total = key_total + jnp.einsum(
            "rhqk,rqhd->rkhd", logit_grad, far_queries, preferred_element_type=single_precision
        )
        return (key_total, value_total)

    zero_side = jnp.zeros((row_count, local_len, head_count, head_size), single_precision)
    key_total, value_total = key_blocks(
        key_block,
        (zero_side, zero_side),
        (
            lax.all_gather(queries, "seq", axis=1, tiled=True),
            lax.all_gather(attended_grad, "seq", axis=1, tiled=True),
        ),
    )
    own_pair_grad = jnp.concatenate(
        [
            key_total.reshape(row_count, local_len, features),
            value_total.reshape(row_count, local_len, features),
        ],
        axis=2,
    )
    triple_grad = jnp.concatenate(
        [
            query_grad.reshape(token_count, features),
            own_pair_grad.reshape(token_count, 2 * features),
        ],
        axis=1,
    ).astype(bf16)
    qkv_w_grad = inner(first_normalized, triple_grad)
    first_normalized_gradient = times_transposed(triple_grad, k_qkv)
    through_one, ln1_g_grad, ln1_b_grad = norm_backward_rows(
        first_normalized_gradient,
        first_standardized,
        first_inverse_deviation,
        first_gain_again.astype(single_precision),
    )
    first_grad = second_grad + through_one
    skip_b_grad = jnp.sum(first_grad, axis=0)
    first_low = first_grad.astype(bf16)
    skip_w_grad = inner(joined, first_low)
    joined_grad = times_transposed(first_low, k_skip)
    input_grad = joined_grad[:, :features].reshape(row_count, local_len, features)
    skip_grad = joined_grad[:, features:].reshape(row_count, local_len, features)
    owned_grads = (
        lax.psum_scatter(skip_w_grad, ("dp", "seq"), scatter_dimension=0, tiled=True),
        lax.psum_scatter(qkv_w_grad, ("dp", "seq"), scatter_dimension=0, tiled=True),
        lax.psum_scatter(proj_w_grad, ("dp", "seq"), scatter_dimension=0, tiled=True),
        lax.psum_scatter(fc1_w_grad, ("dp", "seq"), scatter_dimension=0, tiled=True),
        lax.psum_scatter(fc2_w_grad, ("dp", "seq"), scatter_dimension=0, tiled=True),
        lax.psum_scatter(skip_b_grad, ("dp", "seq"), scatter_dimension=0, tiled=True),
        lax.psum_scatter(ln1_g_grad, ("dp", "seq"), scatter_dimension=0, tiled=True),
        lax.psum_scatter(ln1_b_grad, ("dp", "seq"), scatter_dimension=0, tiled=True),
        lax.psum_scatter(proj_b_grad, ("dp", "seq"), scatter_dimension=0, tiled=True),
        lax.psum_scatter(ln2_g_grad, ("dp", "seq"), scatter_dimension=0, tiled=True),
        lax.psum_scatter(ln2_b_grad, ("dp", "seq"), scatter_dimension=0, tiled=True),
        lax.psum_scatter(fc1_b_grad, ("dp", "seq"), scatter_dimension=0, tiled=True),
        lax.psum_scatter(fc2_b_grad, ("dp", "seq"), scatter_dimension=0, tiled=True),
    )
    return (output, input_grad, skip_grad) + tuple(owned_grads)


def solution(mesh):
    in_specs = (
        P("dp", "seq", None),
        P("dp", "seq", None),
        P("dp", None),
        P(("dp", "seq"), None),
        P(("dp", "seq"), None),
        P(("dp", "seq"), None),
        P(("dp", "seq"), None),
        P(("dp", "seq"), None),
        P(("dp", "seq")),
        P(("dp", "seq")),
        P(("dp", "seq")),
        P(("dp", "seq")),
        P(("dp", "seq")),
        P(("dp", "seq")),
        P(("dp", "seq")),
        P(("dp", "seq")),
        P("dp", "seq", None),
    )
    out_specs = (
        P("dp", "seq", None),
        P("dp", "seq", None),
        P("dp", "seq", None),
        P(("dp", "seq"), None),
        P(("dp", "seq"), None),
        P(("dp", "seq"), None),
        P(("dp", "seq"), None),
        P(("dp", "seq"), None),
        P(("dp", "seq")),
        P(("dp", "seq")),
        P(("dp", "seq")),
        P(("dp", "seq")),
        P(("dp", "seq")),
        P(("dp", "seq")),
        P(("dp", "seq")),
        P(("dp", "seq")),
    )
    return jax.shard_map(
        on_device, mesh=mesh, in_specs=in_specs, out_specs=out_specs, check_vma=False
    )
```

```python
from functools import partial

import jax
import jax.numpy as jnp
from jax import lax
from jax.sharding import PartitionSpec as P

HEADS = 16
HEAD_DIM = 72
EPSILON = 1e-05
NEGATIVE = -1e30
F32 = jnp.float32
BF16 = jnp.bfloat16


def norm_pieces(hvals):
    centered = hvals - jnp.mean(hvals, axis=-1, keepdims=True)
    inverse = lax.rsqrt(jnp.mean(centered * centered, axis=-1, keepdims=True) + EPSILON)
    return centered * inverse, inverse


def norm_back(incoming, standardized, inverse, gain):
    scaled = incoming * gain
    passed = inverse * (
        scaled
        - jnp.mean(scaled, axis=-1, keepdims=True)
        - standardized * jnp.mean(scaled * standardized, axis=-1, keepdims=True)
    )
    return passed, jnp.sum(incoming * standardized, axis=0), jnp.sum(incoming, axis=0)


def segment_of(lengths, places):
    running = jnp.zeros((), jnp.int32)
    passed = jnp.zeros(places.shape, jnp.int32)
    for slot in range(lengths.shape[1]):
        running = running + lengths[0, slot]
        passed = passed + (running <= places).astype(jnp.int32)
    return passed


def dot(left, right):
    return jnp.dot(left, right, preferred_element_type=F32)


def inner(left, right):
    return lax.dot_general(left, right, (((0,), (0,)), ((), ())), preferred_element_type=F32)


def times_transposed(left, right):
    return lax.dot_general(left, right, (((1,), (1,)), ((), ())), preferred_element_type=F32)


def on_device(
    nd, ns,
    inputs, skipped, item_lengths,
    skip_w, qkv_w, proj_w, fc1_w, fc2_w,
    skip_b, ln1_g, ln1_b, proj_b, ln2_g, ln2_b, fc1_b, fc2_b,
    cotangent,
):
    _, local, features = inputs.shape
    hidden_units = fc1_w.shape[1]
    n = nd * ns
    row_len = local * ns
    heads = HEADS // ns
    head_cols = heads * HEAD_DIM
    scale = HEAD_DIM ** (-0.5)
    dp_at = lax.axis_index("dp")
    hidden_part = hidden_units // nd
    joined_part = 2 * features // nd

    def swap(v, k):
        return lax.ppermute(v, "dp", [(i, i ^ k) for i in range(nd)])

    def gather_rows(v):
        return jnp.concatenate([v] + [swap(v, k) for k in range(1, nd)], axis=0)

    def add_rows(partial_sums):
        own = partial_sums[:local]
        low = partial_sums.astype(BF16)
        for k in range(1, nd):
            own = own + swap(low[k * local : (k + 1) * local], k).astype(F32)
        return own

    def seq_exchange(v):
        return lax.all_to_all(v, "seq", 0, 0, tiled=True)

    skip_part = lax.all_gather(skip_w, "seq", axis=0, tiled=True)

    own_vectors = (skip_b, ln1_g, ln1_b, proj_b, ln2_g, ln2_b, fc2_b, fc1_b)
    packed = jnp.concatenate(own_vectors)
    own_size = packed.shape[0]
    padded = -(-own_size // 1024) * 1024
    packed = jnp.pad(packed, (0, padded - own_size)).reshape(padded // 128, 128)
    vectors = lax.all_gather(packed, ("dp", "seq"), axis=0, tiled=True).reshape(n, padded)
    vectors = vectors.astype(F32)
    small = features // n

    def vector(index):
        return vectors[:, index * small : (index + 1) * small].reshape(features)

    b_skip, g_one, b_one, b_proj, g_two, b_two, b_down = (vector(i) for i in range(7))
    up_bias = lax.dynamic_slice_in_dim(vectors[:, 7 * small : own_size], dp_at * ns, ns, 0)
    up_bias = up_bias.reshape(hidden_part)

    joined = jnp.concatenate([inputs[0], skipped[0]], axis=1)
    joined_slices = jnp.swapaxes(joined.reshape(local, nd, joined_part), 0, 1)
    joined_blocks = []
    for k in range(nd):
        away = lax.dynamic_index_in_dim(joined_slices, dp_at ^ k, 0, keepdims=False)
        joined_blocks.append(away if k == 0 else swap(away, k))
    joined_here = jnp.concatenate(joined_blocks, axis=0)
    first = add_rows(dot(joined_here, skip_part)) + b_skip
    xhat_one, inverse_one = norm_pieces(first)
    normed_one = (xhat_one * g_one + b_one).astype(BF16)

    qkv_mine = seq_exchange(
        qkv_w.reshape(features // n, 3, ns, head_cols).transpose(2, 0, 1, 3)
        .reshape(ns, features // n, 3 * head_cols)
    )
    qkv_mine = lax.all_gather(
        qkv_mine.reshape(features // nd, 3 * head_cols), "dp", axis=0, tiled=True
    )
    normed_one_row = lax.all_gather(normed_one, "seq", axis=0, tiled=True)
    triple = dot(normed_one_row, qkv_mine).astype(BF16)
    queries, keys, values = (
        jnp.swapaxes(
            triple[:, i * head_cols : (i + 1) * head_cols].reshape(row_len, heads, HEAD_DIM), 0, 1
        )
        for i in range(3)
    )
    segments = segment_of(item_lengths, jnp.arange(row_len, dtype=jnp.int32))
    allowed = (segments[:, None] == segments[None, :])[None]

    def head_dot(spec, left, right):
        return jnp.einsum(spec, left, right, preferred_element_type=F32)

    logits = jnp.where(allowed, head_dot("hqd,hkd->hqk", queries, keys) * scale, NEGATIVE)
    top = jnp.max(logits, axis=2, keepdims=True)
    total = jnp.sum(jnp.exp(logits - top), axis=2, keepdims=True)
    lse = top + jnp.log(total)
    probs_low = jnp.exp(logits - lse).astype(BF16)
    attended_heads = head_dot("hqk,hkd->hqd", probs_low, values)

    def heads_to_tokens(v):
        v = jnp.swapaxes(v.astype(BF16), 0, 1).reshape(ns, local, head_cols)
        return jnp.swapaxes(seq_exchange(v), 0, 1).reshape(local, features)

    def tokens_to_heads(v):
        v = seq_exchange(jnp.swapaxes(v.reshape(local, ns, head_cols), 0, 1))
        return jnp.swapaxes(v.reshape(row_len, heads, HEAD_DIM), 0, 1)

    attended_low = heads_to_tokens(attended_heads)
    w_proj = lax.all_gather(proj_w, ("dp", "seq"), axis=0, tiled=True)
    second = first + dot(attended_low, w_proj) + b_proj
    xhat_two, inverse_two = norm_pieces(second)
    normed_two = (xhat_two * g_two + b_two).astype(BF16)

    up_slices = jnp.swapaxes(fc1_w.reshape(features // n, nd, hidden_part), 0, 1)
    up_part = lax.all_gather(
        lax.all_to_all(up_slices, "dp", 0, 0, tiled=True), "seq", axis=0, tiled=False
    )
    up_part = jnp.swapaxes(up_part, 0, 1).reshape(features, hidden_part)
    down_part = lax.all_gather(fc2_w, "seq", axis=0, tiled=True)
    grad_out = cotangent[0]
    grad_out_rows = gather_rows(grad_out)
    normed_two_rows = gather_rows(normed_two)
    pre = dot(normed_two_rows, up_part) + up_bias
    gelu_value, gelu_pull = jax.vjp(partial(jax.nn.gelu, approximate=False), pre)
    hidden = gelu_value.astype(BF16)
    output = second + add_rows(dot(hidden, down_part)) + b_down
    output = output.astype(BF16)[None]

    pre_grad = gelu_pull(times_transposed(grad_out_rows, down_part))[0]
    pre_low = pre_grad.astype(BF16)
    normed_two_grad = add_rows(times_transposed(pre_low, up_part))
    fc2_w_grad = lax.psum_scatter(
        inner(hidden, grad_out_rows).astype(BF16), "seq", scatter_dimension=0, tiled=True
    ).astype(F32)

    def by_seq(grad):
        grad = grad.reshape(nd, ns, features // n, grad.shape[1]).astype(BF16)
        grad = jnp.swapaxes(grad, 0, 1).reshape(features, grad.shape[3])
        grad = lax.psum_scatter(grad, "seq", scatter_dimension=0, tiled=True)
        return lax.all_to_all(
            grad.reshape(nd, features // n, grad.shape[1]), "dp", 0, 0, tiled=True
        )

    fc1_w_grad = jnp.swapaxes(by_seq(inner(normed_two_rows, pre_low)), 0, 1)
    fc1_w_grad = fc1_w_grad.reshape(features // n, hidden_units).astype(F32)
    through_two, ln2_g_grad, ln2_b_grad = norm_back(normed_two_grad, xhat_two, inverse_two, g_two)
    second_grad = grad_out.astype(F32) + through_two
    second_low = second_grad.astype(BF16)
    proj_w_grad = jnp.sum(by_seq(inner(attended_low, second_low)).astype(F32), axis=0)
    attended_grad = tokens_to_heads(times_transposed(second_low, w_proj).astype(BF16))
    delta = jnp.sum(attended_grad.astype(F32) * attended_heads, axis=2, keepdims=True)
    probs = jnp.exp(logits - lse)
    prob_grad = head_dot("hqd,hkd->hqk", attended_grad, values)
    logit_grad = (probs * (prob_grad - delta) * scale).astype(BF16)
    triple_grad = jnp.concatenate(
        [
            jnp.swapaxes(v, 0, 1).reshape(row_len, head_cols).astype(BF16)
            for v in (
                head_dot("hqk,hkd->hqd", logit_grad, keys),
                head_dot("hqk,hqd->hkd", logit_grad, queries),
                head_dot("hqk,hqd->hkd", probs.astype(BF16), attended_grad),
            )
        ],
        axis=1,
    )
    normed_one_grad = lax.psum_scatter(
        times_transposed(triple_grad, qkv_mine).astype(BF16), "seq", scatter_dimension=0, tiled=True
    ).astype(F32)
    qkv_terms = inner(normed_one_row, triple_grad).astype(BF16)
    qkv_terms = lax.all_to_all(
        qkv_terms.reshape(nd, features // nd, 3 * head_cols), "dp", 0, 0, tiled=True
    )
    qkv_terms = jnp.sum(qkv_terms.astype(F32), axis=0).astype(BF16)
    qkv_w_grad = seq_exchange(qkv_terms.reshape(ns, features // n, 3 * head_cols))
    qkv_w_grad = (
        qkv_w_grad.reshape(ns, features // n, 3, head_cols)
        .transpose(1, 2, 0, 3).reshape(features // n, 3 * features).astype(F32)
    )
    through_one, ln1_g_grad, ln1_b_grad = norm_back(normed_one_grad, xhat_one, inverse_one, g_one)
    first_grad = second_grad + through_one
    first_low_rows = gather_rows(first_grad.astype(BF16))
    skip_w_grad = lax.psum_scatter(
        inner(joined_here, first_low_rows).astype(BF16), "seq", scatter_dimension=0, tiled=True
    ).astype(F32)
    joined_grad_part = times_transposed(first_low_rows, skip_part).astype(BF16)
    away = []
    for k in range(nd):
        block = joined_grad_part[k * local : (k + 1) * local]
        away.append(block if k == 0 else swap(block, k))
    away = jnp.stack(away, axis=0)
    joined_grad = jnp.concatenate(
        [lax.dynamic_index_in_dim(away, dp_at ^ k, 0, keepdims=False) for k in range(nd)], axis=1
    ).astype(F32)
    input_grad = joined_grad[None, :, :features]
    skip_grad = joined_grad[None, :, features:]

    vector_grads = jnp.stack(
        [
            jnp.sum(first_grad, axis=0),
            ln1_g_grad,
            ln1_b_grad,
            jnp.sum(second_grad, axis=0),
            ln2_g_grad,
            ln2_b_grad,
            jnp.sum(grad_out.astype(F32), axis=0),
        ]
    )
    vector_grads = jnp.swapaxes(vector_grads.reshape(7, n, small), 0, 1).reshape(n, 7 * small)
    up_grads = jnp.sum(pre_grad, axis=0).reshape(ns, hidden_units // n)
    up_grads = lax.dynamic_update_slice_in_dim(
        jnp.zeros((n, hidden_units // n), F32), up_grads, dp_at * ns, 0
    )
    vector_grads = jnp.concatenate([vector_grads, up_grads], axis=1)
    vector_grads = jnp.pad(vector_grads, ((0, 0), (0, padded - own_size)))
    vector_grads = lax.all_to_all(
        vector_grads.reshape(n, padded // 128, 128), ("dp", "seq"), 0, 0, tiled=True
    )
    vector_grads = jnp.sum(vector_grads, axis=0).reshape(padded)
    skip_b_grad, ln1_g_grad, ln1_b_grad, proj_b_grad, ln2_g_grad, ln2_b_grad, fc2_b_grad = (
        vector_grads[i * small : (i + 1) * small] for i in range(7)
    )
    fc1_b_grad = vector_grads[7 * small : own_size]
    return (
        output, input_grad, skip_grad,
        skip_w_grad, qkv_w_grad, proj_w_grad, fc1_w_grad, fc2_w_grad,
        skip_b_grad, ln1_g_grad, ln1_b_grad, proj_b_grad, ln2_g_grad, ln2_b_grad,
        fc1_b_grad, fc2_b_grad,
    )


def solution(mesh):
    tokens = P("dp", "seq", None)
    matrix = P(("dp", "seq"), None)
    flat = P(("dp", "seq"))
    in_specs = (tokens, tokens, P("dp", None)) + (matrix,) * 5 + (flat,) * 8 + (tokens,)
    out_specs = (tokens,) * 3 + (matrix,) * 5 + (flat,) * 8
    return jax.shard_map(
        partial(on_device, mesh.shape["dp"], mesh.shape["seq"]),
        mesh=mesh, in_specs=in_specs, out_specs=out_specs, check_vma=False,
    )
```

```python
from functools import partial

import jax
import jax.numpy as jnp
from jax import lax
from jax.sharding import PartitionSpec as P

HEADS = 16
HEAD_DIM = 72
EPSILON = 1e-05
NEGATIVE = -1e30
F32 = jnp.float32
BF16 = jnp.bfloat16


def norm_pieces(hvals):
    centered = hvals - jnp.mean(hvals, axis=-1, keepdims=True)
    inverse = lax.rsqrt(jnp.mean(centered * centered, axis=-1, keepdims=True) + EPSILON)
    return centered * inverse, inverse


def norm_back(incoming, standardized, inverse, gain):
    scaled = incoming * gain
    passed = inverse * (
        scaled
        - jnp.mean(scaled, axis=-1, keepdims=True)
        - standardized * jnp.mean(scaled * standardized, axis=-1, keepdims=True)
    )
    return passed, jnp.sum(incoming * standardized, axis=0), jnp.sum(incoming, axis=0)


def segment_of(lengths, places):
    running = jnp.zeros((), jnp.int32)
    passed = jnp.zeros(places.shape, jnp.int32)
    for slot in range(lengths.shape[1]):
        running = running + lengths[0, slot]
        passed = passed + (running <= places).astype(jnp.int32)
    return passed


def dot(left, right):
    return jnp.dot(left, right, preferred_element_type=F32)


def inner(left, right):
    return lax.dot_general(left, right, (((0,), (0,)), ((), ())), preferred_element_type=F32)


def times_transposed(left, right):
    return lax.dot_general(left, right, (((1,), (1,)), ((), ())), preferred_element_type=F32)


def on_device(
    nd, ns,
    inputs, skipped, item_lengths,
    skip_w, qkv_w, proj_w, fc1_w, fc2_w,
    skip_b, ln1_g, ln1_b, proj_b, ln2_g, ln2_b, fc1_b, fc2_b,
    cotangent,
):
    _, local, features = inputs.shape
    hidden_units = fc1_w.shape[1]
    n = nd * ns
    row_len = local * ns
    heads = HEADS // ns
    head_cols = heads * HEAD_DIM
    scale = HEAD_DIM ** (-0.5)
    dp_at = lax.axis_index("dp")
    hidden_part = hidden_units // nd
    joined_part = 2 * features // nd

    def swap(v, k):
        return lax.ppermute(v, "dp", [(i, i ^ k) for i in range(nd)])

    def gather_rows(v):
        return jnp.concatenate([v] + [swap(v, k) for k in range(1, nd)], axis=0)

    def add_rows(partial_sums):
        own = partial_sums[:local]
        low = partial_sums.astype(BF16)
        for k in range(1, nd):
            own = own + swap(low[k * local : (k + 1) * local], k).astype(F32)
        return own

    def seq_exchange(v):
        return lax.all_to_all(v, "seq", 0, 0, tiled=True)

    def spread(v, axes, count):
        copies = jnp.broadcast_to(v[None], (count,) + v.shape)
        return lax.all_to_all(copies, axes, 0, 0, tiled=True)

    after = lax.optimization_barrier

    skip_part = lax.all_gather(skip_w, "seq", axis=0, tiled=True)

    own_vectors = (skip_b, ln1_g, ln1_b, proj_b, ln2_g, ln2_b, fc2_b, fc1_b)
    packed = jnp.concatenate(own_vectors)
    own_size = packed.shape[0]
    padded = -(-own_size // 1024) * 1024
    packed = jnp.pad(packed, (0, padded - own_size)).reshape(padded // 128, 128)
    vectors = spread(packed, ("dp", "seq"), n).reshape(n, padded).astype(F32)
    small = features // n

    def vector(index):
        return vectors[:, index * small : (index + 1) * small].reshape(features)

    b_skip, g_one, b_one, b_proj, g_two, b_two, b_down = (vector(i) for i in range(7))
    up_bias = lax.dynamic_slice_in_dim(vectors[:, 7 * small : own_size], dp_at * ns, ns, 0)
    up_bias = up_bias.reshape(hidden_part)

    joined_slices = jnp.stack(
        [
            half[:, at * joined_part : (at + 1) * joined_part]
            for half in (inputs[0], skipped[0])
            for at in range(nd // 2)
        ]
    )
    joined_blocks = []
    for k in range(nd):
        away = lax.dynamic_index_in_dim(joined_slices, dp_at ^ k, 0, keepdims=False)
        joined_blocks.append(away if k == 0 else swap(away, k))
    joined_here = jnp.concatenate(joined_blocks, axis=0)
    first = add_rows(dot(joined_here, skip_part)) + b_skip
    xhat_one, inverse_one = norm_pieces(first)
    normed_one = (xhat_one * g_one + b_one).astype(BF16)

    qkv_mine = seq_exchange(
        qkv_w.reshape(features // n, 3, ns, head_cols).transpose(2, 0, 1, 3)
        .reshape(ns, features // n, 3 * head_cols)
    )
    qkv_mine = spread(qkv_mine.reshape(features // nd, 3 * head_cols), "dp", nd)
    qkv_mine = qkv_mine.reshape(features, 3 * head_cols)
    own_proj, skip_part = after((proj_w, skip_part))
    w_proj = lax.all_gather(own_proj, "seq", axis=0, tiled=True)
    normed_one, w_proj = after((normed_one, w_proj))
    normed_one_row = lax.all_gather(normed_one, "seq", axis=0, tiled=True)
    w_proj = spread(w_proj, "dp", nd).reshape(features, features)
    triple = dot(normed_one_row, qkv_mine).astype(BF16)
    queries, keys, values = (
        jnp.swapaxes(
            triple[:, i * head_cols : (i + 1) * head_cols].reshape(row_len, heads, HEAD_DIM), 0, 1
        )
        for i in range(3)
    )
    segments = segment_of(item_lengths, jnp.arange(row_len, dtype=jnp.int32))
    allowed = (segments[:, None] == segments[None, :])[None]

    def head_dot(spec, left, right):
        return jnp.einsum(spec, left, right, preferred_element_type=F32)

    logits = jnp.where(allowed, head_dot("hqd,hkd->hqk", queries, keys) * scale, NEGATIVE)
    top = jnp.max(logits, axis=2, keepdims=True)
    total = jnp.sum(jnp.exp(logits - top), axis=2, keepdims=True)
    lse = top + jnp.log(total)
    probs_low = jnp.exp(logits - lse).astype(BF16)
    attended_heads = head_dot("hqk,hkd->hqd", probs_low, values)

    def heads_to_tokens(v):
        v = jnp.swapaxes(v.astype(BF16), 0, 1).reshape(ns, local, head_cols)
        return jnp.swapaxes(seq_exchange(v), 0, 1).reshape(local, features)

    def tokens_to_heads(v):
        v = seq_exchange(jnp.swapaxes(v.reshape(local, ns, head_cols), 0, 1))
        return jnp.swapaxes(v.reshape(row_len, heads, HEAD_DIM), 0, 1)

    attended_low = heads_to_tokens(attended_heads)
    second = first + dot(attended_low, w_proj) + b_proj
    xhat_two, inverse_two = norm_pieces(second)
    normed_two = (xhat_two * g_two + b_two).astype(BF16)

    up_slices = jnp.swapaxes(fc1_w.reshape(features // n, nd, hidden_part), 0, 1)
    up_slices = lax.all_to_all(up_slices, "dp", 0, 0, tiled=True)
    up_slices, normed_one_row = after((up_slices, normed_one_row))
    up_part = lax.all_gather(
        up_slices.reshape(features // ns, hidden_part), "seq", axis=0, tiled=True
    )
    own_down, up_part = after((fc2_w, up_part))
    down_part = lax.all_gather(own_down, "seq", axis=0, tiled=True)
    up_part = jnp.swapaxes(up_part.reshape(ns, nd, features // n, hidden_part), 0, 1)
    up_part = up_part.reshape(features, hidden_part)
    grad_out = cotangent[0]
    grad_out_rows = gather_rows(grad_out)
    normed_two_rows = gather_rows(normed_two)
    pre = dot(normed_two_rows, up_part) + up_bias
    gelu_value, gelu_pull = jax.vjp(partial(jax.nn.gelu, approximate=False), pre)
    hidden = gelu_value.astype(BF16)

    pre_grad = gelu_pull(times_transposed(grad_out_rows, down_part))[0]
    pre_low = pre_grad.astype(BF16)
    normed_two_grad = add_rows(times_transposed(pre_low, up_part))
    fc2_w_grad = lax.psum_scatter(
        inner(hidden, grad_out_rows).astype(BF16), "seq", scatter_dimension=0, tiled=True
    )
    normed_two_grad, hidden = after((normed_two_grad, hidden))
    output = second + add_rows(dot(hidden, down_part)) + b_down
    output = output.astype(BF16)[None]

    def by_seq(grad):
        grad = grad.reshape(nd, ns, features // n, grad.shape[1]).astype(BF16)
        return jnp.swapaxes(grad, 0, 1).reshape(features, grad.shape[3])

    def from_dp(grad):
        grad = grad.reshape(nd, features // n, grad.shape[1])
        return lax.all_to_all(grad, "dp", 0, 0, tiled=True)

    fc1_terms, fc2_w_grad = after((by_seq(inner(normed_two_rows, pre_low)), fc2_w_grad))
    fc1_terms = lax.psum_scatter(fc1_terms, "seq", scatter_dimension=0, tiled=True)
    fc2_w_grad = fc2_w_grad.astype(F32)
    through_two, ln2_g_grad, ln2_b_grad = norm_back(normed_two_grad, xhat_two, inverse_two, g_two)
    second_grad = grad_out.astype(F32) + through_two
    second_low = second_grad.astype(BF16)
    proj_terms = by_seq(inner(attended_low, second_low))
    attended_grad = tokens_to_heads(times_transposed(second_low, w_proj).astype(BF16))
    delta = jnp.sum(attended_grad.astype(F32) * attended_heads, axis=2, keepdims=True)
    probs = jnp.exp(logits - lse)
    prob_grad = head_dot("hqd,hkd->hqk", attended_grad, values)
    logit_grad = (probs * (prob_grad - delta) * scale).astype(BF16)
    triple_grad = jnp.concatenate(
        [
            jnp.swapaxes(v, 0, 1).reshape(row_len, head_cols).astype(BF16)
            for v in (
                head_dot("hqk,hkd->hqd", logit_grad, keys),
                head_dot("hqk,hqd->hkd", logit_grad, queries),
                head_dot("hqk,hqd->hkd", probs.astype(BF16), attended_grad),
            )
        ],
        axis=1,
    )
    triple_grad, fc1_terms = after((triple_grad, fc1_terms))
    fc1_w_grad = jnp.swapaxes(from_dp(fc1_terms), 0, 1)
    fc1_w_grad = fc1_w_grad.reshape(features // n, hidden_units).astype(F32)
    normed_one_grad = lax.psum_scatter(
        times_transposed(triple_grad, qkv_mine).astype(BF16), "seq", scatter_dimension=0, tiled=True
    )
    normed_one_grad, proj_terms = after((normed_one_grad, proj_terms))
    normed_one_grad = normed_one_grad.astype(F32)
    proj_terms = lax.psum_scatter(proj_terms, "seq", scatter_dimension=0, tiled=True)
    qkv_terms = inner(normed_one_row, triple_grad).astype(BF16)
    qkv_terms = lax.all_to_all(
        qkv_terms.reshape(nd, features // nd, 3 * head_cols), "dp", 0, 0, tiled=True
    )
    qkv_terms = jnp.sum(qkv_terms.astype(F32), axis=0).astype(BF16)
    qkv_w_grad = seq_exchange(qkv_terms.reshape(ns, features // n, 3 * head_cols))
    qkv_w_grad = (
        qkv_w_grad.reshape(ns, features // n, 3, head_cols)
        .transpose(1, 2, 0, 3).reshape(features // n, 3 * features).astype(F32)
    )
    through_one, ln1_g_grad, ln1_b_grad = norm_back(normed_one_grad, xhat_one, inverse_one, g_one)
    first_grad = second_grad + through_one
    first_low_rows = gather_rows(first_grad.astype(BF16))
    skip_terms, proj_terms = after((inner(joined_here, first_low_rows).astype(BF16), proj_terms))
    proj_w_grad = jnp.sum(from_dp(proj_terms).astype(F32), axis=0)
    skip_w_grad = lax.psum_scatter(
        skip_terms, "seq", scatter_dimension=0, tiled=True
    ).astype(F32)
    joined_grad_part = times_transposed(first_low_rows, skip_part).astype(BF16)
    away = []
    for k in range(nd):
        block = joined_grad_part[k * local : (k + 1) * local]
        away.append(block if k == 0 else swap(block, k))
    away = jnp.stack(away, axis=0)
    joined_grad = jnp.concatenate(
        [lax.dynamic_index_in_dim(away, dp_at ^ k, 0, keepdims=False) for k in range(nd)], axis=1
    ).astype(F32)
    input_grad = joined_grad[None, :, :features]
    skip_grad = joined_grad[None, :, features:]

    vector_grads = jnp.stack(
        [
            jnp.sum(first_grad, axis=0),
            ln1_g_grad,
            ln1_b_grad,
            jnp.sum(second_grad, axis=0),
            ln2_g_grad,
            ln2_b_grad,
            jnp.sum(grad_out.astype(F32), axis=0),
        ]
    )
    vector_grads = jnp.swapaxes(vector_grads.reshape(7, n, small), 0, 1).reshape(n, 7 * small)
    up_grads = jnp.sum(pre_grad, axis=0).reshape(ns, hidden_units // n)
    up_grads = lax.dynamic_update_slice_in_dim(
        jnp.zeros((n, hidden_units // n), F32), up_grads, dp_at * ns, 0
    )
    vector_grads = jnp.concatenate([vector_grads, up_grads], axis=1)
    vector_grads = jnp.pad(vector_grads, ((0, 0), (0, padded - own_size)))
    vector_grads = lax.all_to_all(
        vector_grads.reshape(n, padded // 128, 128), ("dp", "seq"), 0, 0, tiled=True
    )
    vector_grads = jnp.sum(vector_grads, axis=0).reshape(padded)
    skip_b_grad, ln1_g_grad, ln1_b_grad, proj_b_grad, ln2_g_grad, ln2_b_grad, fc2_b_grad = (
        vector_grads[i * small : (i + 1) * small] for i in range(7)
    )
    fc1_b_grad = vector_grads[7 * small : own_size]
    return (
        output, input_grad, skip_grad,
        skip_w_grad, qkv_w_grad, proj_w_grad, fc1_w_grad, fc2_w_grad,
        skip_b_grad, ln1_g_grad, ln1_b_grad, proj_b_grad, ln2_g_grad, ln2_b_grad,
        fc1_b_grad, fc2_b_grad,
    )


def solution(mesh):
    tokens = P("dp", "seq", None)
    matrix = P(("dp", "seq"), None)
    flat = P(("dp", "seq"))
    in_specs = (tokens, tokens, P("dp", None)) + (matrix,) * 5 + (flat,) * 8 + (tokens,)
    out_specs = (tokens,) * 3 + (matrix,) * 5 + (flat,) * 8
    return jax.shard_map(
        partial(on_device, mesh.shape["dp"], mesh.shape["seq"]),
        mesh=mesh, in_specs=in_specs, out_specs=out_specs, check_vma=False,
    )
```

```python
import math
from functools import partial

import jax
import jax.numpy as jnp
from jax import lax
from jax.experimental import pallas as pl
from jax.experimental.pallas import tpu as pltpu
from jax.sharding import PartitionSpec as P

HEADS = 16
HEAD_DIM = 72
EPSILON = 1e-05
NEGATIVE = -1e30
F32 = jnp.float32
BF16 = jnp.bfloat16


def norm_pieces(hvals):
    centered = hvals - jnp.mean(hvals, axis=-1, keepdims=True)
    inverse = lax.rsqrt(jnp.mean(centered * centered, axis=-1, keepdims=True) + EPSILON)
    return centered * inverse, inverse


def norm_back(incoming, standardized, inverse, gain):
    scaled = incoming * gain
    passed = inverse * (
        scaled
        - jnp.mean(scaled, axis=-1, keepdims=True)
        - standardized * jnp.mean(scaled * standardized, axis=-1, keepdims=True)
    )
    return passed, jnp.sum(incoming * standardized, axis=0), jnp.sum(incoming, axis=0)


def segment_of(lengths, places):
    running = jnp.zeros((), jnp.int32)
    passed = jnp.zeros(places.shape, jnp.int32)
    for slot in range(lengths.shape[1]):
        running = running + lengths[0, slot]
        passed = passed + (running <= places).astype(jnp.int32)
    return passed


def dot(left, right):
    return jnp.dot(left, right, preferred_element_type=F32)


def inner(left, right):
    return lax.dot_general(left, right, (((0,), (0,)), ((), ())), preferred_element_type=F32)


def times_transposed(left, right):
    return lax.dot_general(left, right, (((1,), (1,)), ((), ())), preferred_element_type=F32)


def gelu_kernel(rows_at_once, x_ref, w_ref, bias_ref, value_ref, slope_ref):
    for start in range(0, x_ref.shape[0], rows_at_once):
        at = pl.ds(start, rows_at_once)
        pre = dot(x_ref[at, :], w_ref[...]) + bias_ref[...]
        bell = jnp.exp(-0.5 * pre * pre)
        t = 1.0 / (1.0 + (0.3275911 * 0.5**0.5) * jnp.abs(pre))
        tail = 0.5 * 1.061405429
        for c in (-1.453152027, 1.421413741, -0.284496736, 0.254829592):
            tail = tail * t + 0.5 * c
        tail = tail * t * bell
        below = jnp.where(pre < 0.0, tail, 1.0 - tail)
        value_ref[at, :] = (pre * below).astype(BF16)
        slope_ref[at, :] = below + pre * bell * (0.5 / math.pi) ** 0.5


def gelu_of_matmul(x, w, bias):
    rows, depth = x.shape
    columns = w.shape[1]
    step = 384 if columns % 384 == 0 else columns
    rows_at_once = 160 if rows % 160 == 0 else rows
    block = pl.BlockSpec((rows, step), lambda j: (0, j))
    return pl.pallas_call(
        partial(gelu_kernel, rows_at_once),
        grid=(columns // step,),
        in_specs=[
            pl.BlockSpec((rows, depth), lambda j: (0, 0)),
            pl.BlockSpec((depth, step), lambda j: (0, j)),
            pl.BlockSpec((1, step), lambda j: (0, j)),
        ],
        out_specs=[block, block],
        out_shape=[
            jax.ShapeDtypeStruct((rows, columns), BF16),
            jax.ShapeDtypeStruct((rows, columns), F32),
        ],
        compiler_params=pltpu.CompilerParams(vmem_limit_bytes=40 * 2**20),
        cost_estimate=pl.CostEstimate(
            flops=2 * rows * depth * columns,
            bytes_accessed=2 * depth * (rows + columns) + 6 * rows * columns,
            transcendentals=rows * columns,
        ),
    )(x, w, bias.reshape(1, columns))


def on_device(
    nd, ns,
    inputs, skipped, item_lengths,
    skip_w, qkv_w, proj_w, fc1_w, fc2_w,
    skip_b, ln1_g, ln1_b, proj_b, ln2_g, ln2_b, fc1_b, fc2_b,
    cotangent,
):
    _, local, features = inputs.shape
    hidden_units = fc1_w.shape[1]
    n = nd * ns
    row_len = local * ns
    heads = HEADS // ns
    head_cols = heads * HEAD_DIM
    scale = HEAD_DIM ** (-0.5)
    dp_at = lax.axis_index("dp")
    hidden_part = hidden_units // nd
    joined_part = 2 * features // nd

    def swap(v, k):
        return lax.ppermute(v, "dp", [(i, i ^ k) for i in range(nd)])

    def gather_rows(v):
        return jnp.concatenate([v] + [swap(v, k) for k in range(1, nd)], axis=0)

    def add_rows(partial_sums):
        own = partial_sums[:local]
        low = partial_sums.astype(BF16)
        for k in range(1, nd):
            own = own + swap(low[k * local : (k + 1) * local], k).astype(F32)
        return own

    def seq_exchange(v):
        return lax.all_to_all(v, "seq", 0, 0, tiled=True)

    def spread(v, axes, count):
        copies = jnp.broadcast_to(v[None], (count,) + v.shape)
        return lax.all_to_all(copies, axes, 0, 0, tiled=True)

    after = lax.optimization_barrier

    skip_part = lax.all_gather(skip_w, "seq", axis=0, tiled=True)

    rows = features // n
    wide = 3 * head_cols
    own_vectors = (skip_b, ln1_g, ln1_b, proj_b, ln2_g, ln2_b, fc2_b, fc1_b)
    packed = jnp.concatenate(own_vectors)
    own_size = packed.shape[0]
    extra = -(-own_size // wide)
    extra += -(rows + extra) % 8
    packed = jnp.pad(packed, (0, extra * wide - own_size)).reshape(1, extra, wide)
    qkv_out = qkv_w.reshape(rows, 3, ns, head_cols).transpose(2, 0, 1, 3).reshape(ns, rows, wide)
    qkv_out = jnp.concatenate([qkv_out, jnp.broadcast_to(packed, (ns, extra, wide))], axis=1)
    qkv_mine = spread(seq_exchange(qkv_out).reshape(ns * (rows + extra), wide), "dp", nd)
    qkv_mine = qkv_mine.reshape(n, rows + extra, wide)
    vectors = qkv_mine[:, rows:].reshape(n, extra * wide).astype(F32)
    qkv_mine = qkv_mine[:, :rows].reshape(features, wide)
    small = rows

    def vector(index):
        return vectors[:, index * small : (index + 1) * small].reshape(features)

    b_skip, g_one, b_one, b_proj, g_two, b_two, b_down = (vector(i) for i in range(7))
    up_bias = lax.dynamic_slice_in_dim(vectors[:, 7 * small : own_size], dp_at * ns, ns, 0)
    up_bias = up_bias.reshape(hidden_part)

    joined_slices = jnp.stack(
        [
            half[:, at * joined_part : (at + 1) * joined_part]
            for half in (inputs[0], skipped[0])
            for at in range(nd // 2)
        ]
    )
    joined_blocks = []
    for k in range(nd):
        away = lax.dynamic_index_in_dim(joined_slices, dp_at ^ k, 0, keepdims=False)
        joined_blocks.append(away if k == 0 else swap(away, k))
    joined_here = jnp.concatenate(joined_blocks, axis=0)
    first = add_rows(dot(joined_here, skip_part)) + b_skip
    xhat_one, inverse_one = norm_pieces(first)
    normed_one = (xhat_one * g_one + b_one).astype(BF16)

    own_proj, skip_part = after((proj_w, skip_part))
    w_proj = lax.all_gather(own_proj, "seq", axis=0, tiled=True)
    normed_one, w_proj = after((normed_one, w_proj))
    normed_one_row = lax.all_gather(normed_one, "seq", axis=0, tiled=True)
    up_slices = jnp.swapaxes(fc1_w.reshape(features // n, nd, hidden_part), 0, 1)
    up_slices = lax.all_to_all(up_slices, "dp", 0, 0, tiled=True)
    w_proj = spread(w_proj, "dp", nd).reshape(features, features)
    normed_one_row, w_proj, up_slices, qkv_mine = after(
        (normed_one_row, w_proj, up_slices, qkv_mine)
    )
    up_part = lax.all_gather(
        up_slices.reshape(features // ns, hidden_part), "seq", axis=0, tiled=True
    )
    triple = dot(normed_one_row, qkv_mine).astype(BF16)
    queries, keys, values = (
        jnp.swapaxes(
            triple[:, i * head_cols : (i + 1) * head_cols].reshape(row_len, heads, HEAD_DIM), 0, 1
        )
        for i in range(3)
    )
    segments = segment_of(item_lengths, jnp.arange(row_len, dtype=jnp.int32))
    allowed = (segments[:, None] == segments[None, :])[None]

    def head_dot(spec, left, right):
        return jnp.einsum(spec, left, right, preferred_element_type=F32)

    logits = jnp.where(allowed, head_dot("hqd,hkd->hqk", queries, keys) * scale, NEGATIVE)
    top = jnp.max(logits, axis=2, keepdims=True)
    total = jnp.sum(jnp.exp(logits - top), axis=2, keepdims=True)
    lse = top + jnp.log(total)
    probs_low = jnp.exp(logits - lse).astype(BF16)
    attended_heads = head_dot("hqk,hkd->hqd", probs_low, values)

    def heads_to_tokens(v):
        v = jnp.swapaxes(v.astype(BF16), 0, 1).reshape(ns, local, head_cols)
        return jnp.swapaxes(seq_exchange(v), 0, 1).reshape(local, features)

    def tokens_to_heads(v):
        v = seq_exchange(jnp.swapaxes(v.reshape(local, ns, head_cols), 0, 1))
        return jnp.swapaxes(v.reshape(row_len, heads, HEAD_DIM), 0, 1)

    attended_low = heads_to_tokens(attended_heads)
    own_down, up_part = after((fc2_w, up_part))
    down_part = lax.all_gather(own_down, "seq", axis=0, tiled=True)
    up_part = jnp.swapaxes(up_part.reshape(ns, nd, features // n, hidden_part), 0, 1)
    up_part = up_part.reshape(features, hidden_part)
    grad_out = cotangent[0]
    grad_out_rows = gather_rows(grad_out)
    attended_low, up_part, grad_out_rows = after((attended_low, up_part, grad_out_rows))
    second = first + dot(attended_low, w_proj) + b_proj
    xhat_two, inverse_two = norm_pieces(second)
    normed_two = (xhat_two * g_two + b_two).astype(BF16)

    normed_two_rows = gather_rows(normed_two)
    hidden, slope = gelu_of_matmul(normed_two_rows, up_part, up_bias)

    pre_grad = times_transposed(grad_out_rows, down_part) * slope
    pre_low = pre_grad.astype(BF16)
    normed_two_grad = add_rows(times_transposed(pre_low, up_part))
    hidden_again, pre_low = after((hidden, pre_low))
    fc2_w_grad = lax.psum_scatter(
        inner(hidden_again, grad_out_rows).astype(BF16), "seq", scatter_dimension=0, tiled=True
    )

    def by_seq(grad):
        grad = grad.reshape(nd, ns, features // n, grad.shape[1]).astype(BF16)
        return jnp.swapaxes(grad, 0, 1).reshape(features, grad.shape[3])

    def from_dp(grad):
        grad = grad.reshape(nd, features // n, grad.shape[1])
        return lax.all_to_all(grad, "dp", 0, 0, tiled=True)

    fc1_terms = by_seq(inner(normed_two_rows, pre_low))
    normed_two_grad, fc1_terms = after((normed_two_grad, fc1_terms))
    fc1_terms, fc2_w_grad = after((fc1_terms, fc2_w_grad))
    fc1_terms = lax.psum_scatter(fc1_terms, "seq", scatter_dimension=0, tiled=True)
    fc2_w_grad = fc2_w_grad.astype(F32)
    through_two, ln2_g_grad, ln2_b_grad = norm_back(normed_two_grad, xhat_two, inverse_two, g_two)
    second_grad = grad_out.astype(F32) + through_two
    second_low = second_grad.astype(BF16)
    attended_grad = tokens_to_heads(times_transposed(second_low, w_proj).astype(BF16))
    proj_terms = inner(attended_low, second_low).reshape(nd, features // nd, features)
    proj_sum = lax.dynamic_index_in_dim(proj_terms, dp_at, 0, keepdims=False)
    proj_low = proj_terms.astype(BF16)
    for k in range(1, nd):
        away = lax.dynamic_index_in_dim(proj_low, dp_at ^ k, 0, keepdims=False)
        proj_sum = proj_sum + swap(away, k).astype(F32)
    proj_sum = proj_sum.astype(BF16).reshape(ns, features // n, features)
    delta = jnp.sum(attended_grad.astype(F32) * attended_heads, axis=2, keepdims=True)
    probs = jnp.exp(logits - lse)
    prob_grad = head_dot("hqd,hkd->hqk", attended_grad, values)
    logit_grad = (probs * (prob_grad - delta) * scale).astype(BF16)
    triple_grad = jnp.concatenate(
        [
            jnp.swapaxes(v, 0, 1).reshape(row_len, head_cols).astype(BF16)
            for v in (
                head_dot("hqk,hkd->hqd", logit_grad, keys),
                head_dot("hqk,hqd->hkd", logit_grad, queries),
                head_dot("hqk,hqd->hkd", probs.astype(BF16), attended_grad),
            )
        ],
        axis=1,
    )
    triple_grad, fc1_terms, proj_sum, hidden_late = after(
        (triple_grad, fc1_terms, proj_sum, hidden)
    )
    normed_one_grad = lax.psum_scatter(
        times_transposed(triple_grad, qkv_mine).astype(BF16), "seq", scatter_dimension=0, tiled=True
    )
    qkv_terms = inner(normed_one_row, triple_grad).astype(BF16)
    qkv_terms = lax.all_to_all(
        qkv_terms.reshape(nd, features // nd, wide), "dp", 0, 0, tiled=True
    )
    qkv_terms = jnp.sum(qkv_terms.astype(F32), axis=0).astype(BF16)
    output = (second + add_rows(dot(hidden_late, down_part)) + b_down).astype(BF16)
    fc1_w_grad = jnp.swapaxes(from_dp(fc1_terms), 0, 1)
    fc1_w_grad = fc1_w_grad.reshape(features // n, hidden_units).astype(F32)
    normed_one_grad, qkv_terms, output, fc1_w_grad, proj_sum = after(
        (normed_one_grad, qkv_terms, output, fc1_w_grad, proj_sum)
    )
    output = output[None]
    normed_one_grad = normed_one_grad.astype(F32)
    proj_w_grad = jnp.sum(seq_exchange(proj_sum).astype(F32), axis=0)
    qkv_w_grad = seq_exchange(qkv_terms.reshape(ns, features // n, wide))
    qkv_w_grad = (
        qkv_w_grad.reshape(ns, features // n, 3, head_cols)
        .transpose(1, 2, 0, 3).reshape(features // n, 3 * features).astype(F32)
    )
    through_one, ln1_g_grad, ln1_b_grad = norm_back(normed_one_grad, xhat_one, inverse_one, g_one)
    first_grad = second_grad + through_one
    first_low_rows = gather_rows(first_grad.astype(BF16))
    skip_w_grad = lax.psum_scatter(
        inner(joined_here, first_low_rows).astype(BF16), "seq", scatter_dimension=0, tiled=True
    ).astype(F32)
    joined_grad_part = times_transposed(first_low_rows, skip_part).astype(BF16)
    away = []
    for k in range(nd):
        block = joined_grad_part[k * local : (k + 1) * local]
        away.append(block if k == 0 else swap(block, k))
    away = jnp.stack(away, axis=0)
    joined_grad = jnp.concatenate(
        [lax.dynamic_index_in_dim(away, dp_at ^ k, 0, keepdims=False) for k in range(nd)], axis=1
    ).astype(F32)
    input_grad = joined_grad[None, :, :features]
    skip_grad = joined_grad[None, :, features:]

    vector_grads = jnp.stack(
        [
            jnp.sum(first_grad, axis=0),
            ln1_g_grad,
            ln1_b_grad,
            jnp.sum(second_grad, axis=0),
            ln2_g_grad,
            ln2_b_grad,
            jnp.sum(grad_out.astype(F32), axis=0),
        ]
    )
    vector_grads = jnp.swapaxes(vector_grads.reshape(7, n, small), 0, 1).reshape(n, 7 * small)
    up_grads = jnp.sum(pre_grad, axis=0).reshape(ns, hidden_units // n)
    up_grads = lax.dynamic_update_slice_in_dim(
        jnp.zeros((n, hidden_units // n), F32), up_grads, dp_at * ns, 0
    )
    vector_grads = jnp.concatenate([vector_grads, up_grads], axis=1)
    padded = -(-own_size // 1024) * 1024
    vector_grads = jnp.pad(vector_grads, ((0, 0), (0, padded - own_size)))
    vector_grads = lax.all_to_all(
        vector_grads.reshape(n, padded // 128, 128), ("dp", "seq"), 0, 0, tiled=True
    )
    vector_grads = jnp.sum(vector_grads, axis=0).reshape(padded)
    skip_b_grad, ln1_g_grad, ln1_b_grad, proj_b_grad, ln2_g_grad, ln2_b_grad, fc2_b_grad = (
        vector_grads[i * small : (i + 1) * small] for i in range(7)
    )
    fc1_b_grad = vector_grads[7 * small : own_size]
    return (
        output, input_grad, skip_grad,
        skip_w_grad, qkv_w_grad, proj_w_grad, fc1_w_grad, fc2_w_grad,
        skip_b_grad, ln1_g_grad, ln1_b_grad, proj_b_grad, ln2_g_grad, ln2_b_grad,
        fc1_b_grad, fc2_b_grad,
    )


def solution(mesh):
    tokens = P("dp", "seq", None)
    matrix = P(("dp", "seq"), None)
    flat = P(("dp", "seq"))
    in_specs = (tokens, tokens, P("dp", None)) + (matrix,) * 5 + (flat,) * 8 + (tokens,)
    out_specs = (tokens,) * 3 + (matrix,) * 5 + (flat,) * 8
    return jax.shard_map(
        partial(on_device, mesh.shape["dp"], mesh.shape["seq"]),
        mesh=mesh, in_specs=in_specs, out_specs=out_specs, check_vma=False,
    )
```

```python
import math
from functools import partial

import jax
import jax.numpy as jnp
from jax import lax
from jax.experimental import pallas as pl
from jax.experimental.pallas import tpu as pltpu
from jax.sharding import PartitionSpec as P

HEADS = 16
HEAD_DIM = 72
EPSILON = 1e-05
NEGATIVE = -1e30
F32 = jnp.float32
BF16 = jnp.bfloat16


def norm_pieces(hvals):
    centered = hvals - jnp.mean(hvals, axis=-1, keepdims=True)
    inverse = lax.rsqrt(jnp.mean(centered * centered, axis=-1, keepdims=True) + EPSILON)
    return centered * inverse, inverse


def norm_back(incoming, standardized, inverse, gain):
    scaled = incoming * gain
    passed = inverse * (
        scaled
        - jnp.mean(scaled, axis=-1, keepdims=True)
        - standardized * jnp.mean(scaled * standardized, axis=-1, keepdims=True)
    )
    return passed, jnp.sum(incoming * standardized, axis=0), jnp.sum(incoming, axis=0)


def segment_of(lengths, places):
    running = jnp.zeros((), jnp.int32)
    passed = jnp.zeros(places.shape, jnp.int32)
    for slot in range(lengths.shape[1]):
        running = running + lengths[0, slot]
        passed = passed + (running <= places).astype(jnp.int32)
    return passed


def dot(left, right):
    return jnp.dot(left, right, preferred_element_type=F32)


def inner(left, right):
    return lax.dot_general(left, right, (((0,), (0,)), ((), ())), preferred_element_type=F32)


def times_transposed(left, right):
    return lax.dot_general(left, right, (((1,), (1,)), ((), ())), preferred_element_type=F32)


def gelu_kernel(rows_at_once, x_ref, w_ref, bias_ref, value_ref, slope_ref):
    for start in range(0, x_ref.shape[0], rows_at_once):
        at = pl.ds(start, rows_at_once)
        pre = dot(x_ref[at, :], w_ref[...]) + bias_ref[...]
        bell = jnp.exp(-0.5 * pre * pre)
        t = 1.0 / (1.0 + (0.3275911 * 0.5**0.5) * jnp.abs(pre))
        tail = 0.5 * 1.061405429
        for c in (-1.453152027, 1.421413741, -0.284496736, 0.254829592):
            tail = tail * t + 0.5 * c
        tail = tail * t * bell
        below = jnp.where(pre < 0.0, tail, 1.0 - tail)
        value_ref[at, :] = (pre * below).astype(BF16)
        slope_ref[at, :] = below + pre * bell * (0.5 / math.pi) ** 0.5


def gelu_of_matmul(x, w, bias):
    rows, depth = x.shape
    columns = w.shape[1]
    step = 384 if columns % 384 == 0 else columns
    rows_at_once = 160 if rows % 160 == 0 else rows
    block = pl.BlockSpec((rows, step), lambda j: (0, j))
    return pl.pallas_call(
        partial(gelu_kernel, rows_at_once),
        grid=(columns // step,),
        in_specs=[
            pl.BlockSpec((rows, depth), lambda j: (0, 0)),
            pl.BlockSpec((depth, step), lambda j: (0, j)),
            pl.BlockSpec((1, step), lambda j: (0, j)),
        ],
        out_specs=[block, block],
        out_shape=[
            jax.ShapeDtypeStruct((rows, columns), BF16),
            jax.ShapeDtypeStruct((rows, columns), F32),
        ],
        compiler_params=pltpu.CompilerParams(vmem_limit_bytes=40 * 2**20),
        cost_estimate=pl.CostEstimate(
            flops=2 * rows * depth * columns,
            bytes_accessed=2 * depth * (rows + columns) + 6 * rows * columns,
            transcendentals=rows * columns,
        ),
    )(x, w, bias.reshape(1, columns))


def on_device(
    nd, ns,
    inputs, skipped, item_lengths,
    skip_w, qkv_w, proj_w, fc1_w, fc2_w,
    skip_b, ln1_g, ln1_b, proj_b, ln2_g, ln2_b, fc1_b, fc2_b,
    cotangent,
):
    _, local, features = inputs.shape
    hidden_units = fc1_w.shape[1]
    n = nd * ns
    row_len = local * ns
    heads = HEADS // ns
    head_cols = heads * HEAD_DIM
    scale = HEAD_DIM ** (-0.5)
    dp_at = lax.axis_index("dp")
    hidden_part = hidden_units // nd
    joined_part = 2 * features // nd

    def swap(v, k):
        return lax.ppermute(v, "dp", [(i, i ^ k) for i in range(nd)])

    def gather_rows(v):
        return jnp.concatenate([v] + [swap(v, k) for k in range(1, nd)], axis=0)

    def add_rows(partial_sums):
        own = partial_sums[:local]
        low = partial_sums.astype(BF16)
        for k in range(1, nd):
            own = own + swap(low[k * local : (k + 1) * local], k).astype(F32)
        return own

    def seq_exchange(v):
        return lax.all_to_all(v, "seq", 0, 0, tiled=True)

    def spread(v, axes, count):
        copies = jnp.broadcast_to(v[None], (count,) + v.shape)
        return lax.all_to_all(copies, axes, 0, 0, tiled=True)

    after = lax.optimization_barrier
    core = lax.axis_index("seq") % 2
    places = ns // 2

    def other_core(v):
        return lax.ppermute(v, "seq", [(i, i ^ 1) for i in range(ns)])

    def add_over_seq(terms):
        terms = terms.reshape((places, 2) + terms.shape[1:])
        given = lax.dynamic_index_in_dim(terms, 1 - core, 1, keepdims=False).astype(BF16)
        kept = lax.dynamic_index_in_dim(terms, core, 1, keepdims=False).astype(F32)
        sums = (kept + other_core(given).astype(F32)).astype(BF16)
        groups = [[i * 2 + c for i in range(places)] for c in range(2)]
        return lax.all_to_all(sums, "seq", 0, 0, axis_index_groups=groups, tiled=True)

    skip_part = lax.all_gather(skip_w, "seq", axis=0, tiled=True)

    own_vectors = (skip_b, ln1_g, ln1_b, proj_b, ln2_g, ln2_b, fc2_b, fc1_b)
    packed = jnp.concatenate(own_vectors)
    own_size = packed.shape[0]
    padded = -(-own_size // 1024) * 1024
    packed = jnp.pad(packed, (0, padded - own_size)).reshape(padded // 128, 128)
    vectors = spread(packed, ("dp", "seq"), n).reshape(n, padded).astype(F32)
    small = features // n
    wide = 3 * head_cols

    def vector(index):
        return vectors[:, index * small : (index + 1) * small].reshape(features)

    b_skip, g_one, b_one, b_proj, g_two, b_two, b_down = (vector(i) for i in range(7))
    up_bias = lax.dynamic_slice_in_dim(vectors[:, 7 * small : own_size], dp_at * ns, ns, 0)
    up_bias = up_bias.reshape(hidden_part)

    joined_slices = jnp.stack(
        [
            half[:, at * joined_part : (at + 1) * joined_part]
            for half in (inputs[0], skipped[0])
            for at in range(nd // 2)
        ]
    )
    joined_blocks = []
    for k in range(nd):
        away = lax.dynamic_index_in_dim(joined_slices, dp_at ^ k, 0, keepdims=False)
        joined_blocks.append(away if k == 0 else swap(away, k))
    joined_here = jnp.concatenate(joined_blocks, axis=0)
    first = add_rows(dot(joined_here, skip_part)) + b_skip
    xhat_one, inverse_one = norm_pieces(first)
    normed_one = (xhat_one * g_one + b_one).astype(BF16)

    own_proj, skip_part = after((proj_w, skip_part))
    w_proj = lax.all_gather(own_proj, "seq", axis=0, tiled=True)
    normed_one, w_proj = after((normed_one, w_proj))
    normed_one_row = lax.all_gather(normed_one, "seq", axis=0, tiled=True)
    own_qkv, normed_one = after((qkv_w, normed_one))
    qkv_mine = seq_exchange(
        own_qkv.reshape(features // n, 3, ns, head_cols).transpose(2, 0, 1, 3)
        .reshape(ns, features // n, wide)
    )
    qkv_mine = spread(qkv_mine.reshape(features // nd, wide), "dp", nd).reshape(features, wide)
    own_up, qkv_mine = after((fc1_w, qkv_mine))
    up_slices = jnp.swapaxes(own_up.reshape(features // n, nd, hidden_part), 0, 1)
    up_slices = lax.all_to_all(up_slices, "dp", 0, 0, tiled=True)
    half = features // nd // 2
    own_half = lax.dynamic_slice_in_dim(w_proj, core * half, half, 0)
    all_rows = lax.dynamic_update_slice_in_dim(
        jnp.zeros((features, features), BF16), w_proj, dp_at * 2 * half, 0
    )
    for k in range(1, nd):
        place = (dp_at ^ k) * 2
        here = swap(own_half, k)
        there = other_core(here)
        all_rows = lax.dynamic_update_slice_in_dim(all_rows, here, (place + core) * half, 0)
        all_rows = lax.dynamic_update_slice_in_dim(all_rows, there, (place + 1 - core) * half, 0)
    w_proj = all_rows
    normed_one_row, up_slices, qkv_mine, w_proj = after(
        (normed_one_row, up_slices, qkv_mine, w_proj)
    )
    up_part = lax.all_gather(
        up_slices.reshape(features // ns, hidden_part), "seq", axis=0, tiled=True
    )
    triple = dot(normed_one_row, qkv_mine).astype(BF16)
    queries, keys, values = (
        jnp.swapaxes(
            triple[:, i * head_cols : (i + 1) * head_cols].reshape(row_len, heads, HEAD_DIM), 0, 1
        )
        for i in range(3)
    )
    segments = segment_of(item_lengths, jnp.arange(row_len, dtype=jnp.int32))
    allowed = (segments[:, None] == segments[None, :])[None]

    def head_dot(spec, left, right):
        return jnp.einsum(spec, left, right, preferred_element_type=F32)

    logits = jnp.where(allowed, head_dot("hqd,hkd->hqk", queries, keys) * scale, NEGATIVE)
    top = jnp.max(logits, axis=2, keepdims=True)
    total = jnp.sum(jnp.exp(logits - top), axis=2, keepdims=True)
    lse = top + jnp.log(total)
    probs_low = jnp.exp(logits - lse).astype(BF16)
    attended_heads = head_dot("hqk,hkd->hqd", probs_low, values)

    def heads_to_tokens(v):
        v = jnp.swapaxes(v.astype(BF16), 0, 1).reshape(ns, local, head_cols)
        return jnp.swapaxes(seq_exchange(v), 0, 1).reshape(local, features)

    def tokens_to_heads(v):
        v = seq_exchange(jnp.swapaxes(v.reshape(local, ns, head_cols), 0, 1))
        return jnp.swapaxes(v.reshape(row_len, heads, HEAD_DIM), 0, 1)

    own_down, attended_heads = after((fc2_w, attended_heads))
    attended_low = heads_to_tokens(attended_heads)
    down_part = lax.all_gather(own_down, "seq", axis=0, tiled=True)
    up_part = jnp.swapaxes(up_part.reshape(ns, nd, features // n, hidden_part), 0, 1)
    up_part = up_part.reshape(features, hidden_part)
    grad_out = cotangent[0]
    grad_out_rows = gather_rows(grad_out)
    attended_low, up_part, grad_out_rows = after((attended_low, up_part, grad_out_rows))
    second = first + dot(attended_low, w_proj) + b_proj
    xhat_two, inverse_two = norm_pieces(second)
    normed_two = (xhat_two * g_two + b_two).astype(BF16)

    normed_two_rows = gather_rows(normed_two)
    hidden, slope = gelu_of_matmul(normed_two_rows, up_part, up_bias)

    pre_grad = times_transposed(grad_out_rows, down_part) * slope
    pre_low = pre_grad.astype(BF16)
    up_back = times_transposed(pre_low, up_part)
    up_back, pre_low = after((up_back, pre_low))
    normed_two_grad = add_rows(up_back)

    fc1_terms = inner(normed_two_rows, pre_low).astype(BF16)
    fc1_terms = jnp.swapaxes(fc1_terms.reshape(nd, ns, features // n, hidden_part), 0, 1)
    fc1_terms = fc1_terms.reshape(ns, nd * features // n * hidden_part // features, features)
    fc2_terms = inner(hidden, grad_out_rows).astype(BF16)
    fc2_terms = fc2_terms.reshape(ns, hidden_part // ns, features)
    split_at = fc1_terms.shape[1]
    ff_terms = jnp.concatenate([fc1_terms, fc2_terms], axis=1)
    normed_two_grad, ff_terms = after((normed_two_grad, ff_terms))
    ff_terms = lax.psum_scatter(
        ff_terms.reshape(-1, features), "seq", scatter_dimension=0, tiled=True
    )
    through_two, ln2_g_grad, ln2_b_grad = norm_back(normed_two_grad, xhat_two, inverse_two, g_two)
    second_grad = grad_out.astype(F32) + through_two
    second_low = second_grad.astype(BF16)
    attended_grad = tokens_to_heads(times_transposed(second_low, w_proj).astype(BF16))
    proj_terms = inner(attended_low, second_low).reshape(nd, features // nd, features)
    proj_sum = lax.dynamic_index_in_dim(proj_terms, dp_at, 0, keepdims=False)
    proj_low = proj_terms.astype(BF16)
    for k in range(1, nd):
        away = lax.dynamic_index_in_dim(proj_low, dp_at ^ k, 0, keepdims=False)
        proj_sum = proj_sum + swap(away, k).astype(F32)
    proj_sum = proj_sum.astype(BF16).reshape(ns, features // n, features)
    hidden_late, second_low = after((hidden, second_low))
    down_sums = dot(hidden_late, down_part)
    attended_grad, down_sums, proj_low = after((attended_grad, down_sums, proj_low))
    output = (second + add_rows(down_sums) + b_down).astype(BF16)
    delta = jnp.sum(attended_grad.astype(F32) * attended_heads, axis=2, keepdims=True)
    probs = jnp.exp(logits - lse)
    prob_grad = head_dot("hqd,hkd->hqk", attended_grad, values)
    logit_grad = (probs * (prob_grad - delta) * scale).astype(BF16)
    triple_grad = jnp.concatenate(
        [
            jnp.swapaxes(v, 0, 1).reshape(row_len, head_cols).astype(BF16)
            for v in (
                head_dot("hqk,hkd->hqd", logit_grad, keys),
                head_dot("hqk,hqd->hkd", logit_grad, queries),
                head_dot("hqk,hqd->hkd", probs.astype(BF16), attended_grad),
            )
        ],
        axis=1,
    )
    triple_grad, ff_terms, proj_sum, output = after((triple_grad, ff_terms, proj_sum, output))
    output = output[None]
    normed_one_grad = lax.psum_scatter(
        times_transposed(triple_grad, qkv_mine).astype(BF16), "seq", scatter_dimension=0, tiled=True
    )
    fc1_w_grad = ff_terms[:split_at].reshape(nd, features // n, hidden_part)
    fc1_w_grad = lax.all_to_all(fc1_w_grad, "dp", 0, 0, tiled=True)
    fc2_w_grad = ff_terms[split_at:].astype(F32)
    qkv_terms = inner(normed_one_row, triple_grad).astype(BF16)
    proj_sum = add_over_seq(proj_sum)
    proj_sum, qkv_terms = after((proj_sum, qkv_terms))
    qkv_terms = lax.all_to_all(
        qkv_terms.reshape(nd, features // nd, wide), "dp", 0, 0, tiled=True
    )
    qkv_terms = jnp.sum(qkv_terms.astype(F32), axis=0).astype(BF16)
    normed_one_grad, qkv_terms, fc1_w_grad, fc2_w_grad, proj_sum = after(
        (normed_one_grad, qkv_terms, fc1_w_grad, fc2_w_grad, proj_sum)
    )
    proj_w_grad = jnp.sum(
        proj_sum.reshape(places, features // n, features).astype(F32), axis=0
    )
    normed_one_grad = normed_one_grad.astype(F32)
    through_one, ln1_g_grad, ln1_b_grad = norm_back(normed_one_grad, xhat_one, inverse_one, g_one)
    first_grad = second_grad + through_one
    first_low = first_grad.astype(BF16)
    first_low_rows = gather_rows(first_low)
    qkv_w_grad = seq_exchange(qkv_terms.reshape(ns, features // n, wide))
    vector_grads = jnp.stack(
        [
            jnp.sum(first_grad, axis=0),
            ln1_g_grad,
            ln1_b_grad,
            jnp.sum(second_grad, axis=0),
            ln2_g_grad,
            ln2_b_grad,
            jnp.sum(grad_out.astype(F32), axis=0),
        ]
    )
    vector_grads = jnp.swapaxes(vector_grads.reshape(7, n, small), 0, 1).reshape(n, 7 * small)
    up_grads = jnp.sum(pre_grad, axis=0).reshape(ns, hidden_units // n)
    up_grads = lax.dynamic_update_slice_in_dim(
        jnp.zeros((n, hidden_units // n), F32), up_grads, dp_at * ns, 0
    )
    vector_grads = jnp.concatenate([vector_grads, up_grads], axis=1)
    vector_grads = jnp.pad(vector_grads, ((0, 0), (0, padded - own_size)))
    vector_grads = lax.all_to_all(
        vector_grads.reshape(n, padded // 128, 128), ("dp", "seq"), 0, 0, tiled=True
    )
    first_low_rows, qkv_w_grad, vector_grads = after((first_low_rows, qkv_w_grad, vector_grads))
    fc1_w_grad = jnp.swapaxes(fc1_w_grad, 0, 1).reshape(features // n, hidden_units).astype(F32)
    qkv_w_grad = (
        qkv_w_grad.reshape(ns, features // n, 3, head_cols)
        .transpose(1, 2, 0, 3).reshape(features // n, 3 * features).astype(F32)
    )
    skip_terms = inner(joined_here, first_low_rows).reshape(ns, 2 * features // n, features)
    skip_w_grad = add_over_seq(skip_terms)
    skip_w_grad = jnp.sum(
        skip_w_grad.reshape(places, 2 * features // n, features).astype(F32), axis=0
    )
    joined_grad_part = times_transposed(first_low_rows, skip_part).astype(BF16)
    away = []
    for k in range(nd):
        block = joined_grad_part[k * local : (k + 1) * local]
        away.append(block if k == 0 else swap(block, k))
    away = jnp.stack(away, axis=0)
    joined_grad = jnp.concatenate(
        [lax.dynamic_index_in_dim(away, dp_at ^ k, 0, keepdims=False) for k in range(nd)], axis=1
    ).astype(F32)
    input_grad = joined_grad[None, :, :features]
    skip_grad = joined_grad[None, :, features:]

    vector_grads = jnp.sum(vector_grads, axis=0).reshape(padded)
    skip_b_grad, ln1_g_grad, ln1_b_grad, proj_b_grad, ln2_g_grad, ln2_b_grad, fc2_b_grad = (
        vector_grads[i * small : (i + 1) * small] for i in range(7)
    )
    fc1_b_grad = vector_grads[7 * small : own_size]
    return (
        output, input_grad, skip_grad,
        skip_w_grad, qkv_w_grad, proj_w_grad, fc1_w_grad, fc2_w_grad,
        skip_b_grad, ln1_g_grad, ln1_b_grad, proj_b_grad, ln2_g_grad, ln2_b_grad,
        fc1_b_grad, fc2_b_grad,
    )


def solution(mesh):
    tokens = P("dp", "seq", None)
    matrix = P(("dp", "seq"), None)
    flat = P(("dp", "seq"))
    in_specs = (tokens, tokens, P("dp", None)) + (matrix,) * 5 + (flat,) * 8 + (tokens,)
    out_specs = (tokens,) * 3 + (matrix,) * 5 + (flat,) * 8
    return jax.shard_map(
        partial(on_device, mesh.shape["dp"], mesh.shape["seq"]),
        mesh=mesh, in_specs=in_specs, out_specs=out_specs, check_vma=False,
    )
```

```python
import math
from functools import partial

import jax
import jax.numpy as jnp
from jax import lax
from jax.experimental import pallas as pl
from jax.experimental.pallas import tpu as pltpu
from jax.sharding import PartitionSpec as P

HEADS = 16
HEAD_DIM = 72
EPSILON = 1e-05
NEGATIVE = -1e30
F32 = jnp.float32
BF16 = jnp.bfloat16


def norm_pieces(hvals):
    centered = hvals - jnp.mean(hvals, axis=-1, keepdims=True)
    inverse = lax.rsqrt(jnp.mean(centered * centered, axis=-1, keepdims=True) + EPSILON)
    return centered * inverse, inverse


def norm_back(incoming, standardized, inverse, gain):
    scaled = incoming * gain
    passed = inverse * (
        scaled
        - jnp.mean(scaled, axis=-1, keepdims=True)
        - standardized * jnp.mean(scaled * standardized, axis=-1, keepdims=True)
    )
    return passed, jnp.sum(incoming * standardized, axis=0), jnp.sum(incoming, axis=0)


def segment_of(lengths, places):
    running = jnp.zeros((), jnp.int32)
    passed = jnp.zeros(places.shape, jnp.int32)
    for slot in range(lengths.shape[1]):
        running = running + lengths[0, slot]
        passed = passed + (running <= places).astype(jnp.int32)
    return passed


def dot(left, right):
    return jnp.dot(left, right, preferred_element_type=F32)


def inner(left, right):
    return lax.dot_general(left, right, (((0,), (0,)), ((), ())), preferred_element_type=F32)


def times_transposed(left, right):
    return lax.dot_general(left, right, (((1,), (1,)), ((), ())), preferred_element_type=F32)


def gelu_kernel(rows_at_once, x_ref, w_ref, bias_ref, value_ref, slope_ref):
    for start in range(0, x_ref.shape[0], rows_at_once):
        at = pl.ds(start, rows_at_once)
        pre = dot(x_ref[at, :], w_ref[...]) + bias_ref[...]
        bell = jnp.exp(-0.5 * pre * pre)
        t = 1.0 / (1.0 + (0.3275911 * 0.5**0.5) * jnp.abs(pre))
        tail = 0.5 * 1.061405429
        for c in (-1.453152027, 1.421413741, -0.284496736, 0.254829592):
            tail = tail * t + 0.5 * c
        tail = tail * t * bell
        below = jnp.where(pre < 0.0, tail, 1.0 - tail)
        value_ref[at, :] = (pre * below).astype(BF16)
        slope_ref[at, :] = below + pre * bell * (0.5 / math.pi) ** 0.5


def gelu_of_matmul(x, w, bias):
    rows, depth = x.shape
    columns = w.shape[1]
    step = 384 if columns % 384 == 0 else columns
    rows_at_once = 160 if rows % 160 == 0 else rows
    block = pl.BlockSpec((rows, step), lambda j: (0, j))
    return pl.pallas_call(
        partial(gelu_kernel, rows_at_once),
        grid=(columns // step,),
        in_specs=[
            pl.BlockSpec((rows, depth), lambda j: (0, 0)),
            pl.BlockSpec((depth, step), lambda j: (0, j)),
            pl.BlockSpec((1, step), lambda j: (0, j)),
        ],
        out_specs=[block, block],
        out_shape=[
            jax.ShapeDtypeStruct((rows, columns), BF16),
            jax.ShapeDtypeStruct((rows, columns), F32),
        ],
        compiler_params=pltpu.CompilerParams(vmem_limit_bytes=40 * 2**20),
        cost_estimate=pl.CostEstimate(
            flops=2 * rows * depth * columns,
            bytes_accessed=2 * depth * (rows + columns) + 6 * rows * columns,
            transcendentals=rows * columns,
        ),
    )(x, w, bias.reshape(1, columns))


def on_device(
    nd, ns,
    inputs, skipped, item_lengths,
    skip_w, qkv_w, proj_w, fc1_w, fc2_w,
    skip_b, ln1_g, ln1_b, proj_b, ln2_g, ln2_b, fc1_b, fc2_b,
    cotangent,
):
    _, local, features = inputs.shape
    hidden_units = fc1_w.shape[1]
    n = nd * ns
    row_len = local * ns
    heads = HEADS // ns
    head_cols = heads * HEAD_DIM
    wide = 3 * head_cols
    small = features // n
    scale = HEAD_DIM ** (-0.5)
    hidden_part = hidden_units // nd
    joined_part = 2 * features // nd
    part = features // nd
    places = ns // 2
    dp_at = lax.axis_index("dp")
    seq_at = lax.axis_index("seq")
    core = seq_at % 2
    after = lax.optimization_barrier

    def swap(v, k):
        return lax.ppermute(v, "dp", [(i, i ^ k) for i in range(nd)])

    def other_core(v):
        return lax.ppermute(v, "seq", [(i, i ^ 1) for i in range(ns)])

    def index(v, at, axis=0):
        return lax.dynamic_index_in_dim(v, at, axis, keepdims=False)

    def gather_rows(v):
        return jnp.concatenate([v] + [swap(v, k) for k in range(1, nd)], axis=0)

    def add_blocks(own, low):
        for k in range(1, nd):
            own = own + swap(low[k], k).astype(F32)
        return own

    def low_rows(partial_sums):
        return partial_sums.astype(BF16).reshape(nd, local, features)

    def seq_exchange(v):
        return lax.all_to_all(v, "seq", 0, 0, tiled=True)

    def core_sums(terms):
        terms = terms.reshape((places, 2) + terms.shape[1:])
        given = index(terms, 1 - core, 1).astype(BF16)
        kept = index(terms, core, 1).astype(F32)
        return (kept + other_core(given).astype(F32)).astype(BF16)

    def chip_sums(sums):
        groups = [[i * 2 + c for i in range(places)] for c in range(2)]
        terms = lax.all_to_all(sums, "seq", 0, 0, axis_index_groups=groups, tiled=True)
        return jnp.sum(terms.reshape(sums.shape).astype(F32), axis=0)

    skip_part = lax.all_gather(skip_w, "seq", axis=0, tiled=True)

    own_vectors = (skip_b, ln1_g, ln1_b, proj_b, ln2_g, ln2_b, fc2_b, fc1_b)
    packed = jnp.concatenate(own_vectors)
    own_size = packed.shape[0]
    padded = -(-own_size // 1024) * 1024
    packed = jnp.pad(packed, (0, padded - own_size)).reshape(padded // 128, 128)
    packed = jnp.broadcast_to(packed[None], (n,) + packed.shape)
    vectors = lax.all_to_all(packed, ("dp", "seq"), 0, 0, tiled=True)
    vectors = vectors.reshape(n, padded).astype(F32)

    joined_slices = jnp.stack(
        [
            half[:, at * joined_part : (at + 1) * joined_part]
            for half in (inputs[0], skipped[0])
            for at in range(nd // 2)
        ]
    )
    joined_here = jnp.concatenate(
        [index(joined_slices, dp_at)]
        + [swap(index(joined_slices, dp_at ^ k), k) for k in range(1, nd)],
        axis=0,
    )
    own_qkv, own_proj, skip_part, joined_here, vectors = after(
        (qkv_w, proj_w, skip_part, joined_here, vectors)
    )
    def vector(at):
        return vectors[:, at * small : (at + 1) * small].reshape(features)

    b_skip, g_one, b_one, b_proj, g_two, b_two, b_down = (vector(i) for i in range(7))
    up_bias = lax.dynamic_slice_in_dim(vectors[:, 7 * small : own_size], dp_at * ns, ns, 0)
    up_bias = up_bias.reshape(hidden_part)

    qkv_rows = lax.all_gather(own_qkv, "seq", axis=0, tiled=False)
    first_terms = dot(joined_here, skip_part)
    first = add_blocks(first_terms[:local], low_rows(first_terms)) + b_skip
    proj_rows = lax.all_gather(own_proj, "seq", axis=0, tiled=True)
    xhat_one, inverse_one = norm_pieces(first)
    normed_one = (xhat_one * g_one + b_one).astype(BF16)
    normed_one, proj_rows, qkv_rows = after((normed_one, proj_rows, qkv_rows))
    normed_one_row = lax.all_gather(normed_one, "seq", axis=0, tiled=True)

    qkv_mine = qkv_rows.reshape(part, 3, ns, head_cols)
    qkv_mine = index(qkv_mine, seq_at, 2).reshape(part, wide)
    qkv_blocks = jnp.zeros((features, wide), BF16)
    for k in range(nd):
        block = qkv_mine if k == 0 else swap(qkv_mine, k)
        qkv_blocks = lax.dynamic_update_slice_in_dim(qkv_blocks, block, (dp_at ^ k) * part, 0)
    qkv_mine = qkv_blocks
    up_slices = jnp.swapaxes(fc1_w.reshape(small, nd, hidden_part), 0, 1)
    up_slices = jnp.concatenate(
        [index(up_slices, dp_at)] + [swap(index(up_slices, dp_at ^ k), k) for k in range(1, nd)],
        axis=0,
    )
    half = part // 2
    own_half = lax.dynamic_slice_in_dim(proj_rows, core * half, half, 0)
    w_proj = lax.dynamic_update_slice_in_dim(
        jnp.zeros((features, features), BF16), proj_rows, dp_at * part, 0
    )
    for k in range(1, nd):
        place = (dp_at ^ k) * 2
        here = swap(own_half, k)
        there = other_core(here)
        w_proj = lax.dynamic_update_slice_in_dim(w_proj, here, (place + core) * half, 0)
        w_proj = lax.dynamic_update_slice_in_dim(w_proj, there, (place + 1 - core) * half, 0)
    normed_one_row, up_slices, qkv_mine, grad_out = after(
        (normed_one_row, up_slices, qkv_mine, cotangent[0])
    )
    up_part = lax.all_gather(up_slices, "seq", axis=0, tiled=True)
    at = lax.broadcasted_iota(jnp.int32, (features, features), 0)
    block, row = at // small, at % small
    row = ((block % nd) ^ dp_at) * part + (block // nd) * small + row
    order = (row == lax.broadcasted_iota(jnp.int32, (features, features), 1)).astype(BF16)

    triple = dot(normed_one_row, qkv_mine).astype(BF16)
    queries, keys, values = (
        jnp.swapaxes(
            triple[:, i * head_cols : (i + 1) * head_cols].reshape(row_len, heads, HEAD_DIM), 0, 1
        )
        for i in range(3)
    )
    segments = segment_of(item_lengths, jnp.arange(row_len, dtype=jnp.int32))
    allowed = (segments[:, None] == segments[None, :])[None]

    def head_dot(spec, left, right):
        return jnp.einsum(spec, left, right, preferred_element_type=F32)

    logits = jnp.where(allowed, head_dot("hqd,hkd->hqk", queries, keys) * scale, NEGATIVE)
    top = jnp.max(logits, axis=2, keepdims=True)
    total = jnp.sum(jnp.exp(logits - top), axis=2, keepdims=True)
    lse = top + jnp.log(total)
    probs_low = jnp.exp(logits - lse).astype(BF16)
    attended_heads = head_dot("hqk,hkd->hqd", probs_low, values)

    def heads_to_tokens(v):
        v = jnp.swapaxes(v.astype(BF16), 0, 1).reshape(ns, local, head_cols)
        return jnp.swapaxes(seq_exchange(v), 0, 1).reshape(local, features)

    def tokens_to_heads(v):
        v = seq_exchange(jnp.swapaxes(v.reshape(local, ns, head_cols), 0, 1))
        return jnp.swapaxes(v.reshape(row_len, heads, HEAD_DIM), 0, 1)

    grad_out_rows = gather_rows(grad_out)
    attended_low = heads_to_tokens(attended_heads)
    attended_low, w_proj, grad_out_rows = after((attended_low, w_proj, grad_out_rows))
    own_down, attended_low, up_part = after((fc2_w, attended_low, up_part))
    down_part = lax.all_gather(own_down, "seq", axis=0, tiled=True)
    second = first + dot(attended_low, w_proj) + b_proj
    xhat_two, inverse_two = norm_pieces(second)
    normed_two = (xhat_two * g_two + b_two).astype(BF16)

    normed_two_rows = gather_rows(normed_two)
    up_part = inner(order, up_part).astype(BF16)
    normed_two_rows, up_part, order = after((normed_two_rows, up_part, order))
    hidden, slope = gelu_of_matmul(normed_two_rows, up_part, up_bias)

    fc2_terms = inner(hidden, grad_out_rows).astype(BF16)
    slope, fc2_terms = after((slope, fc2_terms))
    fc2_w_grad = lax.psum_scatter(fc2_terms, "seq", scatter_dimension=0, tiled=True)
    pre_grad = times_transposed(grad_out_rows, down_part) * slope
    pre_low = pre_grad.astype(BF16)
    up_back = times_transposed(pre_low, up_part)
    up_low = low_rows(up_back)
    up_low, pre_late, normed_two_rows = after((up_low, pre_low, normed_two_rows))
    normed_two_grad = add_blocks(up_back[:local], up_low)
    fc1_terms = inner(times_transposed(normed_two_rows, order).astype(BF16), pre_late).astype(BF16)
    normed_two_grad, fc1_terms = after((normed_two_grad, fc1_terms))
    through_two, ln2_g_grad, ln2_b_grad = norm_back(normed_two_grad, xhat_two, inverse_two, g_two)
    second_grad = grad_out.astype(F32) + through_two
    second_low = second_grad.astype(BF16)
    attended_grad = times_transposed(second_low, w_proj).astype(BF16)
    attended_grad, second_late, hidden_late = after((attended_grad, second_low, hidden))
    attended_grad = tokens_to_heads(attended_grad)
    proj_terms = inner(attended_low, second_late).reshape(nd, part, features)
    down_sums = dot(hidden_late, down_part)
    proj_low = proj_terms.astype(BF16)
    proj_blocks = [swap(index(proj_low, dp_at ^ k), k) for k in range(1, nd)]
    attended_grad, down_sums, fc1_terms, fc2_w_grad, proj_blocks[0] = after(
        (attended_grad, down_sums, fc1_terms, fc2_w_grad, proj_blocks[0])
    )
    fc1_terms = lax.psum_scatter(fc1_terms, "seq", scatter_dimension=0, tiled=True)
    proj_sum = index(proj_terms, dp_at)
    for block in proj_blocks:
        proj_sum = proj_sum + block.astype(F32)
    proj_sum = proj_sum.astype(BF16).reshape(ns, small, features)
    down_low, attended_heads = after((low_rows(down_sums), attended_heads))
    output = second + add_blocks(down_sums[:local], down_low) + b_down
    output = output.astype(BF16)
    delta = jnp.sum(attended_grad.astype(F32) * attended_heads, axis=2, keepdims=True)
    probs = jnp.exp(logits - lse)
    prob_grad = head_dot("hqd,hkd->hqk", attended_grad, values)
    logit_grad = (probs * (prob_grad - delta) * scale).astype(BF16)
    triple_grad = jnp.concatenate(
        [
            jnp.swapaxes(v, 0, 1).reshape(row_len, head_cols).astype(BF16)
            for v in (
                head_dot("hqk,hkd->hqd", logit_grad, keys),
                head_dot("hqk,hqd->hkd", logit_grad, queries),
                head_dot("hqk,hqd->hkd", probs.astype(BF16), attended_grad),
            )
        ],
        axis=1,
    )
    one_back = times_transposed(triple_grad, qkv_mine).astype(BF16)
    one_back, triple_late, fc1_terms, output, proj_sum = after(
        (one_back, triple_grad, fc1_terms, output, proj_sum)
    )
    normed_one_grad = lax.psum_scatter(one_back, "seq", scatter_dimension=0, tiled=True)
    qkv_terms = inner(normed_one_row, triple_late).reshape(nd, part, wide)
    qkv_low = qkv_terms.astype(BF16)
    qkv_sum = index(qkv_terms, dp_at)
    for k in range(1, nd):
        qkv_sum = qkv_sum + swap(index(qkv_low, dp_at ^ k), k).astype(F32)
    qkv_sum = qkv_sum.astype(BF16).reshape(ns, small, wide)
    fc1_terms = fc1_terms.reshape(nd, small, hidden_part)
    fc1_blocks = jnp.stack([fc1_terms[0]] + [swap(fc1_terms[k], k) for k in range(1, nd)])
    proj_w_grad = chip_sums(core_sums(proj_sum))
    normed_one_grad, qkv_sum, fc1_blocks, proj_w_grad = after(
        (normed_one_grad, qkv_sum, fc1_blocks, proj_w_grad)
    )
    normed_one_grad = normed_one_grad.astype(F32)
    through_one, ln1_g_grad, ln1_b_grad = norm_back(normed_one_grad, xhat_one, inverse_one, g_one)
    first_grad = second_grad + through_one
    first_low = first_grad.astype(BF16)
    first_low_rows = gather_rows(first_low)
    qkv_w_grad = seq_exchange(qkv_sum)
    vector_grads = jnp.stack(
        [
            jnp.sum(first_grad, axis=0),
            ln1_g_grad,
            ln1_b_grad,
            jnp.sum(second_grad, axis=0),
            ln2_g_grad,
            ln2_b_grad,
            jnp.sum(grad_out.astype(F32), axis=0),
        ]
    )
    vector_grads = jnp.swapaxes(vector_grads.reshape(7, n, small), 0, 1).reshape(n, 7 * small)
    up_grads = jnp.sum(pre_grad, axis=0).reshape(ns, hidden_units // n)
    up_grads = lax.dynamic_update_slice_in_dim(
        jnp.zeros((n, hidden_units // n), F32), up_grads, dp_at * ns, 0
    )
    vector_grads = jnp.concatenate([vector_grads, up_grads], axis=1)
    vector_grads = jnp.pad(vector_grads, ((0, 0), (0, padded - own_size)))
    vector_grads = lax.all_to_all(
        vector_grads.reshape(n, padded // 128, 128), ("dp", "seq"), 0, 0, tiled=True
    )
    first_low_rows, qkv_w_grad, vector_grads = after((first_low_rows, qkv_w_grad, vector_grads))
    skip_terms = inner(joined_here, first_low_rows).reshape(ns, 2 * small, features)
    skip_sums = core_sums(skip_terms)
    joined_grad_part = times_transposed(first_low_rows, skip_part).astype(BF16)
    skip_sums, joined_grad_part = after((skip_sums, joined_grad_part))
    skip_w_grad = chip_sums(skip_sums)
    joined_grad_part = joined_grad_part.reshape(nd, local, joined_part)
    away = jnp.stack(
        [joined_grad_part[0]] + [swap(joined_grad_part[k], k) for k in range(1, nd)]
    )
    joined_grad = jnp.concatenate(
        [index(away, dp_at ^ k) for k in range(nd)], axis=1
    ).astype(F32)
    fc1_w_grad = jnp.concatenate([index(fc1_blocks, dp_at ^ k) for k in range(nd)], axis=1)
    qkv_w_grad = (
        qkv_w_grad.reshape(ns, small, 3, head_cols).transpose(1, 2, 0, 3)
        .reshape(small, 3 * features)
    )
    vector_grads = jnp.sum(vector_grads, axis=0).reshape(padded)
    skip_b_grad, ln1_g_grad, ln1_b_grad, proj_b_grad, ln2_g_grad, ln2_b_grad, fc2_b_grad = (
        vector_grads[i * small : (i + 1) * small] for i in range(7)
    )
    fc1_b_grad = vector_grads[7 * small : own_size]
    return (
        output[None], joined_grad[None, :, :features], joined_grad[None, :, features:],
        skip_w_grad, qkv_w_grad.astype(F32), proj_w_grad,
        fc1_w_grad.astype(F32), fc2_w_grad.astype(F32),
        skip_b_grad, ln1_g_grad, ln1_b_grad, proj_b_grad, ln2_g_grad, ln2_b_grad,
        fc1_b_grad, fc2_b_grad,
    )


def solution(mesh):
    tokens = P("dp", "seq", None)
    matrix = P(("dp", "seq"), None)
    flat = P(("dp", "seq"))
    in_specs = (tokens, tokens, P("dp", None)) + (matrix,) * 5 + (flat,) * 8 + (tokens,)
    out_specs = (tokens,) * 3 + (matrix,) * 5 + (flat,) * 8
    return jax.shard_map(
        partial(on_device, mesh.shape["dp"], mesh.shape["seq"]),
        mesh=mesh, in_specs=in_specs, out_specs=out_specs, check_vma=False,
    )
```

```python
import math
from functools import partial

import jax
import jax.numpy as jnp
from jax import lax
from jax.experimental import pallas as pl
from jax.experimental.pallas import tpu as pltpu
from jax.sharding import PartitionSpec as P

HEADS = 16
HEAD_DIM = 72
EPSILON = 1e-05
NEGATIVE = -1e30
WIDE = 128
F32 = jnp.float32
BF16 = jnp.bfloat16


def norm_pieces(hvals):
    centered = hvals - jnp.mean(hvals, axis=-1, keepdims=True)
    inverse = lax.rsqrt(jnp.mean(centered * centered, axis=-1, keepdims=True) + EPSILON)
    return centered * inverse, inverse


def norm_back(incoming, standardized, inverse, gain):
    scaled = incoming * gain
    passed = inverse * (
        scaled
        - jnp.mean(scaled, axis=-1, keepdims=True)
        - standardized * jnp.mean(scaled * standardized, axis=-1, keepdims=True)
    )
    return passed, jnp.sum(incoming * standardized, axis=0), jnp.sum(incoming, axis=0)


def segment_of(lengths, places):
    running = jnp.zeros((), jnp.int32)
    passed = jnp.zeros(places.shape, jnp.int32)
    for slot in range(lengths.shape[1]):
        running = running + lengths[0, slot]
        passed = passed + (running <= places).astype(jnp.int32)
    return passed


def dot(left, right):
    return jnp.dot(left, right, preferred_element_type=F32)


def inner(left, right):
    return lax.dot_general(left, right, (((0,), (0,)), ((), ())), preferred_element_type=F32)


def times_transposed(left, right):
    return lax.dot_general(left, right, (((1,), (1,)), ((), ())), preferred_element_type=F32)


def attend_kernel(heads, scale, q_ref, k_ref, v_ref, seg_q_ref, seg_k_ref, out_ref, low_ref, lse_ref):
    allowed = seg_q_ref[...] == seg_k_ref[...]
    lane = lax.broadcasted_iota(jnp.int32, (q_ref.shape[0], WIDE), 1)
    logs = jnp.zeros((q_ref.shape[0], WIDE), F32)
    outs = []
    for h in range(heads):
        at = slice(h * WIDE, (h + 1) * WIDE)
        logits = times_transposed(q_ref[:, at], k_ref[:, at]) * scale
        logits = jnp.where(allowed, logits, NEGATIVE)
        top = jnp.max(logits, axis=1, keepdims=True)
        weights = jnp.exp(logits - top)
        total = jnp.sum(weights, axis=1, keepdims=True)
        outs.append(dot(weights.astype(BF16), v_ref[:, at]) / total)
        out_ref[:, at] = outs[h]
        logs = jnp.where(lane == h, top + jnp.log(total), logs)
    lse_ref[...] = jnp.transpose(logs)[:8]
    if heads == 1:
        low_ref[...] = outs[0][:, :HEAD_DIM].astype(BF16)
    else:
        second = pltpu.roll(outs[1], HEAD_DIM, 1)
        rest = heads * HEAD_DIM - WIDE
        low_ref[:, :WIDE] = jnp.where(lane < HEAD_DIM, outs[0], second).astype(BF16)
        low_ref[:, WIDE:] = second[:, :rest].astype(BF16)


def attend(triple, segments, heads, scale):
    rows = triple.shape[0]
    wide = heads * WIDE
    step = 256 if rows % 256 == 0 else rows
    return pl.pallas_call(
        partial(attend_kernel, heads, scale),
        grid=(rows // step,),
        in_specs=[
            pl.BlockSpec((step, wide), lambda i: (i, 0)),
            pl.BlockSpec((rows, wide), lambda i: (0, 1)),
            pl.BlockSpec((rows, wide), lambda i: (0, 2)),
            pl.BlockSpec((step, 1), lambda i: (i, 0)),
            pl.BlockSpec((1, rows), lambda i: (0, 0)),
        ],
        out_specs=[
            pl.BlockSpec((step, wide), lambda i: (i, 0)),
            pl.BlockSpec((step, heads * HEAD_DIM), lambda i: (i, 0)),
            pl.BlockSpec((8, step), lambda i: (0, i)),
        ],
        out_shape=[
            jax.ShapeDtypeStruct((rows, wide), F32),
            jax.ShapeDtypeStruct((rows, heads * HEAD_DIM), BF16),
            jax.ShapeDtypeStruct((8, rows), F32),
        ],
        compiler_params=pltpu.CompilerParams(vmem_limit_bytes=48 * 2**20),
        cost_estimate=pl.CostEstimate(
            flops=8 * rows * rows * wide,
            bytes_accessed=10 * rows * wide,
            transcendentals=heads * rows * rows,
        ),
    )(triple, triple, triple, segments.reshape(rows, 1), segments.reshape(1, rows))


def attend_back_kernel(
    heads, scale, q_ref, k_ref, v_ref, out_grad_ref, out_ref, lse_ref, seg_q_ref, seg_k_ref,
    dq_ref, dk_ref, dv_ref, sum_ref, grad_ref, delta_ref,
):
    step = pl.program_id(0)

    @pl.when(step == 0)
    def _():
        sum_ref[...] = jnp.zeros_like(sum_ref)
        ones = jnp.ones((8, WIDE), F32)
        for h in range(heads):
            grad = out_grad_ref[...]
            if h > 0:
                grad = pltpu.roll(grad.astype(F32), 2 * WIDE - HEAD_DIM, 1).astype(BF16)
            grad = grad[:, :WIDE]
            at = slice(h * WIDE, (h + 1) * WIDE)
            grad_ref[:, at] = grad
            delta = lax.dot_general(
                ones, grad.astype(F32) * out_ref[:, at], (((1,), (1,)), ((), ())),
                precision=lax.Precision.HIGHEST, preferred_element_type=F32,
            )
            delta_ref[h : h + 1, :] = delta[:1]

    allowed = seg_k_ref[...] == seg_q_ref[...]
    for h in range(heads):
        at = slice(h * WIDE, (h + 1) * WIDE)
        queries, keys, out_grad = q_ref[:, at], k_ref[:, at], grad_ref[:, at]
        logits = times_transposed(keys, queries) * scale - lse_ref[h : h + 1, :]
        probs = jnp.where(allowed, jnp.exp(logits), 0.0)
        prob_grad = times_transposed(v_ref[:, at], out_grad)
        logit_grad = (probs * (prob_grad - delta_ref[h : h + 1, :]) * scale).astype(BF16)
        dv_ref[:, at] = dot(probs.astype(BF16), out_grad).astype(BF16)
        dk_ref[:, at] = dot(logit_grad, queries).astype(BF16)
        sum_ref[:, at] += inner(logit_grad, keys)

    @pl.when(step == pl.num_programs(0) - 1)
    def _():
        dq_ref[...] = sum_ref[...].astype(BF16)


def attend_back(triple, out_grad, out, lse, segments, heads, scale):
    rows = triple.shape[0]
    wide = heads * WIDE
    step = 256 if rows % 256 == 0 else rows
    whole = pl.BlockSpec((rows, wide), lambda i: (0, 0))
    out_grad = jnp.pad(out_grad, ((0, 0), (0, wide - out_grad.shape[1])))
    block = pl.BlockSpec((step, wide), lambda i: (i, 0))
    row = pl.BlockSpec((8, rows), lambda i: (0, 0))
    return pl.pallas_call(
        partial(attend_back_kernel, heads, scale),
        grid=(rows // step,),
        in_specs=[
            whole,
            pl.BlockSpec((step, wide), lambda i: (i, 1)),
            pl.BlockSpec((step, wide), lambda i: (i, 2)),
            whole,
            whole,
            row,
            pl.BlockSpec((1, rows), lambda i: (0, 0)),
            pl.BlockSpec((step, 1), lambda i: (i, 0)),
        ],
        out_specs=[whole, block, block],
        out_shape=[jax.ShapeDtypeStruct((rows, wide), BF16)] * 3,
        scratch_shapes=[
            pltpu.VMEM((rows, wide), F32),
            pltpu.VMEM((rows, wide), BF16),
            pltpu.VMEM((8, rows), F32),
        ],
        compiler_params=pltpu.CompilerParams(vmem_limit_bytes=48 * 2**20),
        cost_estimate=pl.CostEstimate(
            flops=20 * rows * rows * wide,
            bytes_accessed=14 * rows * wide,
            transcendentals=heads * rows * rows,
        ),
    )(
        triple, triple, triple, out_grad, out, lse,
        segments.reshape(1, rows), segments.reshape(rows, 1),
    )


def gelu_kernel(rows_at_once, x_ref, w_ref, bias_ref, value_ref, slope_ref):
    for start in range(0, x_ref.shape[0], rows_at_once):
        at = pl.ds(start, rows_at_once)
        pre = dot(x_ref[at, :], w_ref[...]) + bias_ref[...]
        bell = jnp.exp(-0.5 * pre * pre)
        t = 1.0 / (1.0 + (0.3275911 * 0.5**0.5) * jnp.abs(pre))
        tail = 0.5 * 1.061405429
        for c in (-1.453152027, 1.421413741, -0.284496736, 0.254829592):
            tail = tail * t + 0.5 * c
        tail = tail * t * bell
        below = jnp.where(pre < 0.0, tail, 1.0 - tail)
        value_ref[at, :] = (pre * below).astype(BF16)
        slope_ref[at, :] = below + pre * bell * (0.5 / math.pi) ** 0.5


def gelu_of_matmul(x, w, bias):
    rows, depth = x.shape
    columns = w.shape[1]
    step = 384 if columns % 384 == 0 else columns
    rows_at_once = 160 if rows % 160 == 0 else rows
    block = pl.BlockSpec((rows, step), lambda j: (0, j))
    return pl.pallas_call(
        partial(gelu_kernel, rows_at_once),
        grid=(columns // step,),
        in_specs=[
            pl.BlockSpec((rows, depth), lambda j: (0, 0)),
            pl.BlockSpec((depth, step), lambda j: (0, j)),
            pl.BlockSpec((1, step), lambda j: (0, j)),
        ],
        out_specs=[block, block],
        out_shape=[
            jax.ShapeDtypeStruct((rows, columns), BF16),
            jax.ShapeDtypeStruct((rows, columns), F32),
        ],
        compiler_params=pltpu.CompilerParams(vmem_limit_bytes=40 * 2**20),
        cost_estimate=pl.CostEstimate(
            flops=2 * rows * depth * columns,
            bytes_accessed=2 * depth * (rows + columns) + 6 * rows * columns,
            transcendentals=rows * columns,
        ),
    )(x, w, bias.reshape(1, columns))


def on_device(
    nd, ns,
    inputs, skipped, item_lengths,
    skip_w, qkv_w, proj_w, fc1_w, fc2_w,
    skip_b, ln1_g, ln1_b, proj_b, ln2_g, ln2_b, fc1_b, fc2_b,
    cotangent,
):
    _, local, features = inputs.shape
    hidden_units = fc1_w.shape[1]
    n = nd * ns
    row_len = local * ns
    heads = HEADS // ns
    head_cols = heads * HEAD_DIM
    wide = 3 * head_cols
    small = features // n
    scale = HEAD_DIM ** (-0.5)
    hidden_part = hidden_units // nd
    joined_part = 2 * features // nd
    part = features // nd
    places = ns // 2
    dp_at = lax.axis_index("dp")
    seq_at = lax.axis_index("seq")
    core = seq_at % 2
    after = lax.optimization_barrier

    def swap(v, k):
        return lax.ppermute(v, "dp", [(i, i ^ k) for i in range(nd)])

    def other_core(v):
        return lax.ppermute(v, "seq", [(i, i ^ 1) for i in range(ns)])

    def index(v, at, axis=0):
        return lax.dynamic_index_in_dim(v, at, axis, keepdims=False)

    def gather_rows(v):
        return jnp.concatenate([v] + [swap(v, k) for k in range(1, nd)], axis=0)

    def add_blocks(own, low):
        for k in range(1, nd):
            own = own + swap(low[k], k).astype(F32)
        return own

    def low_rows(partial_sums):
        return partial_sums.astype(BF16).reshape(nd, local, features)

    def widen(v):
        v = v.reshape(v.shape[0], v.shape[1] // HEAD_DIM, HEAD_DIM)
        return jnp.pad(v, ((0, 0), (0, 0), (0, WIDE - HEAD_DIM))).reshape(v.shape[0], -1)

    def narrow(v):
        v = v.reshape(v.shape[0], v.shape[1] // WIDE, WIDE)
        return v[:, :, :HEAD_DIM].reshape(v.shape[0], -1)

    def seq_exchange(v):
        return lax.all_to_all(v, "seq", 0, 0, tiled=True)

    def core_sums(terms):
        terms = terms.reshape((places, 2) + terms.shape[1:])
        given = index(terms, 1 - core, 1).astype(BF16)
        kept = index(terms, core, 1).astype(F32)
        return (kept + other_core(given).astype(F32)).astype(BF16)

    def chip_sums(sums):
        groups = [[i * 2 + c for i in range(places)] for c in range(2)]
        terms = lax.all_to_all(sums, "seq", 0, 0, axis_index_groups=groups, tiled=True)
        return jnp.sum(terms.reshape(sums.shape).astype(F32), axis=0)

    skip_part = lax.all_gather(skip_w, "seq", axis=0, tiled=True)

    own_vectors = (skip_b, ln1_g, ln1_b, proj_b, ln2_g, ln2_b, fc2_b, fc1_b)
    packed = jnp.concatenate(own_vectors)
    own_size = packed.shape[0]
    padded = -(-own_size // 1024) * 1024
    packed = jnp.pad(packed, (0, padded - own_size)).reshape(padded // 128, 128)
    packed = jnp.broadcast_to(packed[None], (n,) + packed.shape)
    vectors = lax.all_to_all(packed, ("dp", "seq"), 0, 0, tiled=True)
    vectors = vectors.reshape(n, padded).astype(F32)

    joined_slices = jnp.stack(
        [
            half[:, at * joined_part : (at + 1) * joined_part]
            for half in (inputs[0], skipped[0])
            for at in range(nd // 2)
        ]
    )
    joined_here = jnp.concatenate(
        [index(joined_slices, dp_at)]
        + [swap(index(joined_slices, dp_at ^ k), k) for k in range(1, nd)],
        axis=0,
    )
    at = lax.broadcasted_iota(jnp.int32, (features, features), 0)
    block, row = at // small, at % small
    row = ((block % nd) ^ dp_at) * part + (block // nd) * small + row
    order = (row == lax.broadcasted_iota(jnp.int32, (features, features), 1)).astype(BF16)
    qkv_out = qkv_w.reshape(small, 3, ns, head_cols).transpose(2, 0, 1, 3).reshape(ns, small, wide)
    qkv_out, skip_part, joined_here, vectors, order = after(
        (qkv_out, skip_part, joined_here, vectors, order)
    )
    def vector(at):
        return vectors[:, at * small : (at + 1) * small].reshape(features)

    b_skip, g_one, b_one, b_proj, g_two, b_two, b_down = (vector(i) for i in range(7))
    up_bias = lax.dynamic_slice_in_dim(vectors[:, 7 * small : own_size], dp_at * ns, ns, 0)
    up_bias = up_bias.reshape(hidden_part)

    first_terms = dot(joined_here, skip_part)
    first = add_blocks(first_terms[:local], low_rows(first_terms)) + b_skip
    qkv_mine = seq_exchange(qkv_out).reshape(part, wide)
    xhat_one, inverse_one = norm_pieces(first)
    normed_one = (xhat_one * g_one + b_one).astype(BF16)
    normed_one, qkv_mine, own_proj = after((normed_one, qkv_mine, proj_w))
    normed_one_row = lax.all_gather(normed_one, "seq", axis=0, tiled=True)

    qkv_blocks = jnp.stack([qkv_mine] + [swap(qkv_mine, k) for k in range(1, nd)])
    qkv_mine = jnp.concatenate([index(qkv_blocks, dp_at ^ k) for k in range(nd)], axis=0)
    qkv_mine = widen(qkv_mine)
    proj_rows = lax.all_gather(own_proj, "seq", axis=0, tiled=True)
    up_slices = jnp.swapaxes(fc1_w.reshape(small, nd, hidden_part), 0, 1)
    up_slices = jnp.concatenate(
        [index(up_slices, dp_at)] + [swap(index(up_slices, dp_at ^ k), k) for k in range(1, nd)],
        axis=0,
    )
    half = part // 2
    own_half = lax.dynamic_slice_in_dim(proj_rows, core * half, half, 0)
    w_proj = lax.dynamic_update_slice_in_dim(
        jnp.zeros((features, features), BF16), proj_rows, dp_at * part, 0
    )
    for k in range(1, nd):
        place = (dp_at ^ k) * 2
        here = swap(own_half, k)
        there = other_core(here)
        w_proj = lax.dynamic_update_slice_in_dim(w_proj, here, (place + core) * half, 0)
        w_proj = lax.dynamic_update_slice_in_dim(w_proj, there, (place + 1 - core) * half, 0)
    normed_one_row, up_slices, qkv_mine, w_proj = after(
        (normed_one_row, up_slices, qkv_mine, w_proj)
    )
    up_part = lax.all_gather(up_slices, "seq", axis=0, tiled=True)
    triple = dot(normed_one_row, qkv_mine).astype(BF16)
    segments = segment_of(item_lengths, jnp.arange(row_len, dtype=jnp.int32))
    attended, attended_low, lse = attend(triple, segments, heads, scale)

    def heads_to_tokens(v):
        v = seq_exchange(v.reshape(ns, local, head_cols))
        return jnp.swapaxes(v, 0, 1).reshape(local, features)

    def tokens_to_heads(v):
        v = seq_exchange(jnp.swapaxes(v.reshape(local, ns, head_cols), 0, 1))
        return v.reshape(row_len, head_cols)

    attended_low, grad_out = after((attended_low, cotangent[0]))
    grad_out_rows = gather_rows(grad_out)
    attended_low = heads_to_tokens(attended_low)
    attended_low, grad_out_rows = after((attended_low, grad_out_rows))
    own_down, attended_low, up_part = after((fc2_w, attended_low, up_part))
    down_part = lax.all_gather(own_down, "seq", axis=0, tiled=True)
    second = first + dot(attended_low, w_proj) + b_proj
    xhat_two, inverse_two = norm_pieces(second)
    normed_two = (xhat_two * g_two + b_two).astype(BF16)

    normed_two_rows = gather_rows(normed_two)
    up_part = inner(order, up_part).astype(BF16)
    normed_two_rows, up_part, order = after((normed_two_rows, up_part, order))
    hidden, slope = gelu_of_matmul(normed_two_rows, up_part, up_bias)

    fc2_terms = inner(hidden, grad_out_rows).astype(BF16)
    slope, fc2_terms, attended_low = after((slope, fc2_terms, attended_low))
    attended_slices = jnp.swapaxes(attended_low.reshape(local, nd, part), 0, 1)
    attended_rows = jnp.concatenate(
        [index(attended_slices, dp_at)]
        + [swap(index(attended_slices, dp_at ^ k), k) for k in range(1, nd)],
        axis=0,
    )
    fc2_w_grad = lax.psum_scatter(fc2_terms, "seq", scatter_dimension=0, tiled=True)
    pre_grad = times_transposed(grad_out_rows, down_part) * slope
    pre_low = pre_grad.astype(BF16)
    up_back = times_transposed(pre_low, up_part)
    up_low = low_rows(up_back)
    up_low, pre_late, normed_two_rows, attended_rows = after(
        (up_low, pre_low, normed_two_rows, attended_rows)
    )
    normed_two_grad = add_blocks(up_back[:local], up_low)
    fc1_terms = inner(times_transposed(normed_two_rows, order).astype(BF16), pre_late).astype(BF16)
    normed_two_grad, fc1_terms = after((normed_two_grad, fc1_terms))
    through_two, ln2_g_grad, ln2_b_grad = norm_back(normed_two_grad, xhat_two, inverse_two, g_two)
    second_grad = grad_out.astype(F32) + through_two
    second_low = second_grad.astype(BF16)
    attended_grad = times_transposed(second_low, w_proj).astype(BF16)
    attended_grad, second_late, hidden_late, fc1_terms, fc2_w_grad = after(
        (attended_grad, second_low, hidden, fc1_terms, fc2_w_grad)
    )
    fc1_terms = lax.psum_scatter(fc1_terms, "seq", scatter_dimension=0, tiled=True)
    attended_grad = tokens_to_heads(attended_grad)
    second_rows = gather_rows(second_late)
    down_sums = dot(hidden_late, down_part)
    attended_grad, down_sums, second_rows = after((attended_grad, down_sums, second_rows))
    triple_grad = jnp.concatenate(
        attend_back(triple, attended_grad, attended, lse, segments, heads, scale), axis=1
    )
    one_back = times_transposed(triple_grad, qkv_mine).astype(BF16)
    one_back, triple_late, fc1_terms, down_sums = after(
        (one_back, triple_grad, fc1_terms, down_sums)
    )
    normed_one_grad = lax.psum_scatter(one_back, "seq", scatter_dimension=0, tiled=True)
    qkv_terms = narrow(inner(normed_one_row, triple_late)).reshape(nd, part, wide)
    qkv_low, down_low = qkv_terms.astype(BF16), low_rows(down_sums)
    qkv_low, down_low, second_rows = after((qkv_low, down_low, second_rows))
    proj_terms = inner(attended_rows, second_rows).reshape(ns, small, features)
    proj_w_grad = chip_sums(core_sums(proj_terms))
    output = (second + add_blocks(down_sums[:local], down_low) + b_down).astype(BF16)
    qkv_sum = index(qkv_terms, dp_at)
    for k in range(1, nd):
        qkv_sum = qkv_sum + swap(index(qkv_low, dp_at ^ k), k).astype(F32)
    qkv_sum = qkv_sum.astype(BF16).reshape(ns, small, wide)
    fc1_terms = fc1_terms.reshape(nd, small, hidden_part)
    fc1_blocks = jnp.stack([fc1_terms[0]] + [swap(fc1_terms[k], k) for k in range(1, nd)])
    normed_one_grad, qkv_sum, fc1_blocks, proj_w_grad, output = after(
        (normed_one_grad, qkv_sum, fc1_blocks, proj_w_grad, output)
    )
    normed_one_grad = normed_one_grad.astype(F32)
    through_one, ln1_g_grad, ln1_b_grad = norm_back(normed_one_grad, xhat_one, inverse_one, g_one)
    first_grad = second_grad + through_one
    first_low = first_grad.astype(BF16)
    first_low_rows = gather_rows(first_low)
    qkv_w_grad = seq_exchange(qkv_sum)
    vector_grads = jnp.stack(
        [
            jnp.sum(first_grad, axis=0),
            ln1_g_grad,
            ln1_b_grad,
            jnp.sum(second_grad, axis=0),
            ln2_g_grad,
            ln2_b_grad,
            jnp.sum(grad_out.astype(F32), axis=0),
        ]
    )
    vector_grads = jnp.swapaxes(vector_grads.reshape(7, n, small), 0, 1).reshape(n, 7 * small)
    up_grads = jnp.sum(pre_grad, axis=0).reshape(ns, hidden_units // n)
    up_grads = lax.dynamic_update_slice_in_dim(
        jnp.zeros((n, hidden_units // n), F32), up_grads, dp_at * ns, 0
    )
    vector_grads = jnp.concatenate([vector_grads, up_grads], axis=1)
    vector_grads = jnp.pad(vector_grads, ((0, 0), (0, padded - own_size)))
    vector_grads = lax.all_to_all(
        vector_grads.reshape(n, padded // 128, 128), ("dp", "seq"), 0, 0, tiled=True
    )
    first_low_rows, qkv_w_grad, vector_grads = after((first_low_rows, qkv_w_grad, vector_grads))
    skip_terms = inner(joined_here, first_low_rows).astype(BF16)
    skip_w_grad = lax.psum_scatter(skip_terms, "seq", scatter_dimension=0, tiled=True).astype(F32)
    skip_terms, first_low_rows = after((skip_terms, first_low_rows))
    joined_grad_part = times_transposed(first_low_rows, skip_part).astype(BF16)
    joined_grad_part = joined_grad_part.reshape(nd, local, joined_part)
    away = jnp.stack(
        [joined_grad_part[0]] + [swap(joined_grad_part[k], k) for k in range(1, nd)]
    )
    joined_grad = jnp.concatenate(
        [index(away, dp_at ^ k) for k in range(nd)], axis=1
    ).astype(F32)
    fc1_w_grad = jnp.concatenate([index(fc1_blocks, dp_at ^ k) for k in range(nd)], axis=1)
    qkv_w_grad = (
        qkv_w_grad.reshape(ns, small, 3, head_cols).transpose(1, 2, 0, 3)
        .reshape(small, 3 * features)
    )
    vector_grads = jnp.sum(vector_grads, axis=0).reshape(padded)
    skip_b_grad, ln1_g_grad, ln1_b_grad, proj_b_grad, ln2_g_grad, ln2_b_grad, fc2_b_grad = (
        vector_grads[i * small : (i + 1) * small] for i in range(7)
    )
    fc1_b_grad = vector_grads[7 * small : own_size]
    return (
        output[None], joined_grad[None, :, :features], joined_grad[None, :, features:],
        skip_w_grad, qkv_w_grad.astype(F32), proj_w_grad,
        fc1_w_grad.astype(F32), fc2_w_grad.astype(F32),
        skip_b_grad, ln1_g_grad, ln1_b_grad, proj_b_grad, ln2_g_grad, ln2_b_grad,
        fc1_b_grad, fc2_b_grad,
    )


def solution(mesh):
    tokens = P("dp", "seq", None)
    matrix = P(("dp", "seq"), None)
    flat = P(("dp", "seq"))
    in_specs = (tokens, tokens, P("dp", None)) + (matrix,) * 5 + (flat,) * 8 + (tokens,)
    out_specs = (tokens,) * 3 + (matrix,) * 5 + (flat,) * 8
    return jax.shard_map(
        partial(on_device, mesh.shape["dp"], mesh.shape["seq"]),
        mesh=mesh, in_specs=in_specs, out_specs=out_specs, check_vma=False,
    )
```

```python
import math
from functools import partial

import jax
import jax.numpy as jnp
from jax import lax
from jax.experimental import pallas as pl
from jax.experimental.pallas import tpu as pltpu
from jax.sharding import PartitionSpec as P

HEADS = 16
HEAD_DIM = 72
EPSILON = 1e-05
NEGATIVE = -1e30
WIDE = 128
F32 = jnp.float32
BF16 = jnp.bfloat16


def norm_pieces(hvals):
    centered = hvals - jnp.mean(hvals, axis=-1, keepdims=True)
    inverse = lax.rsqrt(jnp.mean(centered * centered, axis=-1, keepdims=True) + EPSILON)
    return centered * inverse, inverse


def norm_back(incoming, standardized, inverse, gain):
    scaled = incoming * gain
    passed = inverse * (
        scaled
        - jnp.mean(scaled, axis=-1, keepdims=True)
        - standardized * jnp.mean(scaled * standardized, axis=-1, keepdims=True)
    )
    return passed, jnp.sum(incoming * standardized, axis=0), jnp.sum(incoming, axis=0)


def segment_of(lengths, places):
    running = jnp.zeros((), jnp.int32)
    passed = jnp.zeros(places.shape, jnp.int32)
    for slot in range(lengths.shape[1]):
        running = running + lengths[0, slot]
        passed = passed + (running <= places).astype(jnp.int32)
    return passed


def dot(left, right):
    return jnp.dot(left, right, preferred_element_type=F32)


def inner(left, right):
    return lax.dot_general(left, right, (((0,), (0,)), ((), ())), preferred_element_type=F32)


def times_transposed(left, right):
    return lax.dot_general(left, right, (((1,), (1,)), ((), ())), preferred_element_type=F32)


def side_by_side(parts):
    return jnp.concatenate([part[:, :HEAD_DIM] for part in parts], axis=1)


def attend_kernel(heads, scale, q_ref, k_ref, v_ref, seg_q_ref, seg_k_ref, out_ref, low_ref, lse_ref):
    allowed = seg_q_ref[...] == seg_k_ref[...]
    lane = lax.broadcasted_iota(jnp.int32, (q_ref.shape[0], WIDE), 1)
    logs = jnp.zeros((q_ref.shape[0], WIDE), F32)
    outs = []
    for h in range(heads):
        at = slice(h * WIDE, (h + 1) * WIDE)
        logits = times_transposed(q_ref[:, at], k_ref[:, at]) * scale
        logits = jnp.where(allowed, logits, NEGATIVE)
        top = jnp.max(logits, axis=1, keepdims=True)
        weights = jnp.exp(logits - top)
        total = jnp.sum(weights, axis=1, keepdims=True)
        outs.append(dot(weights.astype(BF16), v_ref[:, at]) / total)
        out_ref[:, at] = outs[h]
        logs = jnp.where(lane == h, top + jnp.log(total), logs)
    lse_ref[...] = jnp.transpose(logs)[:8]
    low_ref[...] = side_by_side(outs).astype(BF16)


def attend(triple, segments, heads, scale):
    rows = triple.shape[0]
    wide = heads * WIDE
    step = 256 if rows % 256 == 0 else rows
    return pl.pallas_call(
        partial(attend_kernel, heads, scale),
        grid=(rows // step,),
        in_specs=[
            pl.BlockSpec((step, wide), lambda i: (i, 0)),
            pl.BlockSpec((rows, wide), lambda i: (0, 1)),
            pl.BlockSpec((rows, wide), lambda i: (0, 2)),
            pl.BlockSpec((step, 1), lambda i: (i, 0)),
            pl.BlockSpec((1, rows), lambda i: (0, 0)),
        ],
        out_specs=[
            pl.BlockSpec((step, wide), lambda i: (i, 0)),
            pl.BlockSpec((step, heads * HEAD_DIM), lambda i: (i, 0)),
            pl.BlockSpec((8, step), lambda i: (0, i)),
        ],
        out_shape=[
            jax.ShapeDtypeStruct((rows, wide), F32),
            jax.ShapeDtypeStruct((rows, heads * HEAD_DIM), BF16),
            jax.ShapeDtypeStruct((8, rows), F32),
        ],
        compiler_params=pltpu.CompilerParams(vmem_limit_bytes=48 * 2**20),
        cost_estimate=pl.CostEstimate(
            flops=8 * rows * rows * wide,
            bytes_accessed=10 * rows * wide,
            transcendentals=heads * rows * rows,
        ),
    )(triple, triple, triple, segments.reshape(rows, 1), segments.reshape(1, rows))


def attend_back_kernel(
    heads, scale, q_ref, k_ref, v_ref, out_grad_ref, out_ref, lse_ref, seg_q_ref, seg_k_ref,
    dq_ref, dkv_ref, sum_ref, grad_ref, delta_ref,
):
    step = pl.program_id(0)

    @pl.when(step == 0)
    def _():
        sum_ref[...] = jnp.zeros_like(sum_ref)
        ones = jnp.ones((8, WIDE), F32)
        for h in range(heads):
            grad = out_grad_ref[...]
            if h > 0:
                grad = pltpu.roll(grad.astype(F32), 2 * WIDE - HEAD_DIM, 1).astype(BF16)
            grad = grad[:, :WIDE]
            at = slice(h * WIDE, (h + 1) * WIDE)
            grad_ref[:, at] = grad
            delta = lax.dot_general(
                ones, grad.astype(F32) * out_ref[:, at], (((1,), (1,)), ((), ())),
                precision=lax.Precision.HIGHEST, preferred_element_type=F32,
            )
            delta_ref[h : h + 1, :] = delta[:1]

    allowed = seg_k_ref[...] == seg_q_ref[...]
    key_grads, value_grads = [], []
    for h in range(heads):
        at = slice(h * WIDE, (h + 1) * WIDE)
        queries, keys, out_grad = q_ref[:, at], k_ref[:, at], grad_ref[:, at]
        logits = times_transposed(keys, queries) * scale - lse_ref[h : h + 1, :]
        probs = jnp.where(allowed, jnp.exp(logits), 0.0)
        prob_grad = times_transposed(v_ref[:, at], out_grad)
        logit_grad = (probs * (prob_grad - delta_ref[h : h + 1, :]) * scale).astype(BF16)
        value_grads.append(dot(probs.astype(BF16), out_grad))
        key_grads.append(dot(logit_grad, queries))
        sum_ref[:, at] += inner(logit_grad, keys)
    dkv_ref[...] = side_by_side(key_grads + value_grads).astype(BF16)

    @pl.when(step == pl.num_programs(0) - 1)
    def _():
        dq_ref[...] = side_by_side(
            [sum_ref[:, h * WIDE : (h + 1) * WIDE] for h in range(heads)]
        ).astype(BF16)


def attend_back(triple, out_grad, out, lse, segments, heads, scale):
    rows = triple.shape[0]
    wide = heads * WIDE
    step = 256 if rows % 256 == 0 else rows
    whole = pl.BlockSpec((rows, wide), lambda i: (0, 0))
    out_grad = jnp.pad(out_grad, ((0, 0), (0, wide - out_grad.shape[1])))
    row = pl.BlockSpec((8, rows), lambda i: (0, 0))
    return pl.pallas_call(
        partial(attend_back_kernel, heads, scale),
        grid=(rows // step,),
        in_specs=[
            whole,
            pl.BlockSpec((step, wide), lambda i: (i, 1)),
            pl.BlockSpec((step, wide), lambda i: (i, 2)),
            whole,
            whole,
            row,
            pl.BlockSpec((1, rows), lambda i: (0, 0)),
            pl.BlockSpec((step, 1), lambda i: (i, 0)),
        ],
        out_specs=[
            pl.BlockSpec((rows, heads * HEAD_DIM), lambda i: (0, 0)),
            pl.BlockSpec((step, 2 * heads * HEAD_DIM), lambda i: (i, 0)),
        ],
        out_shape=[
            jax.ShapeDtypeStruct((rows, heads * HEAD_DIM), BF16),
            jax.ShapeDtypeStruct((rows, 2 * heads * HEAD_DIM), BF16),
        ],
        scratch_shapes=[
            pltpu.VMEM((rows, wide), F32),
            pltpu.VMEM((rows, wide), BF16),
            pltpu.VMEM((8, rows), F32),
        ],
        compiler_params=pltpu.CompilerParams(vmem_limit_bytes=48 * 2**20),
        cost_estimate=pl.CostEstimate(
            flops=20 * rows * rows * wide,
            bytes_accessed=14 * rows * wide,
            transcendentals=heads * rows * rows,
        ),
    )(
        triple, triple, triple, out_grad, out, lse,
        segments.reshape(1, rows), segments.reshape(rows, 1),
    )


def by_group_kernel(x_ref, w_ref, out_ref):
    groups, rows, columns = out_ref.shape
    product = times_transposed(x_ref[...], w_ref[...]).astype(BF16)
    for g in range(groups):
        out_ref[g] = product[:, g * columns : (g + 1) * columns]


def product_by_group(x, w, groups):
    rows, depth = x.shape
    columns = w.shape[0] // groups
    steps = 2
    return pl.pallas_call(
        by_group_kernel,
        grid=(steps,),
        in_specs=[
            pl.BlockSpec((rows, depth), lambda j: (0, 0)),
            pl.BlockSpec((w.shape[0] // steps, depth), lambda j: (j, 0)),
        ],
        out_specs=pl.BlockSpec((groups // steps, rows, columns), lambda j: (j, 0, 0)),
        out_shape=jax.ShapeDtypeStruct((groups, rows, columns), BF16),
        cost_estimate=pl.CostEstimate(
            flops=2 * rows * depth * w.shape[0],
            bytes_accessed=2 * depth * (rows + w.shape[0]) + 2 * rows * w.shape[0],
            transcendentals=0,
        ),
    )(x, w)


def gelu_kernel(rows_at_once, x_ref, w_ref, bias_ref, value_ref, slope_ref):
    for start in range(0, x_ref.shape[0], rows_at_once):
        at = pl.ds(start, rows_at_once)
        pre = dot(x_ref[at, :], w_ref[...]) + bias_ref[...]
        bell = jnp.exp(-0.5 * pre * pre)
        t = 1.0 / (1.0 + (0.3275911 * 0.5**0.5) * jnp.abs(pre))
        tail = 0.5 * 1.061405429
        for c in (-1.453152027, 1.421413741, -0.284496736, 0.254829592):
            tail = tail * t + 0.5 * c
        tail = tail * t * bell
        below = jnp.where(pre < 0.0, tail, 1.0 - tail)
        value_ref[at, :] = (pre * below).astype(BF16)
        slope_ref[at, :] = below + pre * bell * (0.5 / math.pi) ** 0.5


def gelu_of_matmul(x, w, bias):
    rows, depth = x.shape
    columns = w.shape[1]
    step = 384 if columns % 384 == 0 else columns
    rows_at_once = 160 if rows % 160 == 0 else rows
    block = pl.BlockSpec((rows, step), lambda j: (0, j))
    return pl.pallas_call(
        partial(gelu_kernel, rows_at_once),
        grid=(columns // step,),
        in_specs=[
            pl.BlockSpec((rows, depth), lambda j: (0, 0)),
            pl.BlockSpec((depth, step), lambda j: (0, j)),
            pl.BlockSpec((1, step), lambda j: (0, j)),
        ],
        out_specs=[block, block],
        out_shape=[
            jax.ShapeDtypeStruct((rows, columns), BF16),
            jax.ShapeDtypeStruct((rows, columns), F32),
        ],
        compiler_params=pltpu.CompilerParams(vmem_limit_bytes=40 * 2**20),
        cost_estimate=pl.CostEstimate(
            flops=2 * rows * depth * columns,
            bytes_accessed=2 * depth * (rows + columns) + 6 * rows * columns,
            transcendentals=rows * columns,
        ),
    )(x, w, bias.reshape(1, columns))


def on_device(
    nd, ns,
    inputs, skipped, item_lengths,
    skip_w, qkv_w, proj_w, fc1_w, fc2_w,
    skip_b, ln1_g, ln1_b, proj_b, ln2_g, ln2_b, fc1_b, fc2_b,
    cotangent,
):
    _, local, features = inputs.shape
    hidden_units = fc1_w.shape[1]
    n = nd * ns
    row_len = local * ns
    heads = HEADS // ns
    head_cols = heads * HEAD_DIM
    wide = 3 * head_cols
    small = features // n
    scale = HEAD_DIM ** (-0.5)
    hidden_part = hidden_units // nd
    joined_part = 2 * features // nd
    part = features // nd
    places = ns // 2
    dp_at = lax.axis_index("dp")
    seq_at = lax.axis_index("seq")
    core = seq_at % 2
    after = lax.optimization_barrier

    def swap(v, k):
        return lax.ppermute(v, "dp", [(i, i ^ k) for i in range(nd)])

    def other_core(v):
        return lax.ppermute(v, "seq", [(i, i ^ 1) for i in range(ns)])

    def index(v, at, axis=0):
        return lax.dynamic_index_in_dim(v, at, axis, keepdims=False)

    def gather_rows(v):
        return jnp.concatenate([v] + [swap(v, k) for k in range(1, nd)], axis=0)

    def add_blocks(own, low):
        for k in range(1, nd):
            own = own + swap(low[k], k).astype(F32)
        return own

    def low_rows(partial_sums):
        return partial_sums.astype(BF16).reshape(nd, local, features)

    def widen(v):
        v = v.reshape(v.shape[0], v.shape[1] // HEAD_DIM, HEAD_DIM)
        return jnp.pad(v, ((0, 0), (0, 0), (0, WIDE - HEAD_DIM))).reshape(v.shape[0], -1)

    def seq_exchange(v):
        return lax.all_to_all(v, "seq", 0, 0, tiled=True)

    def core_sums(terms):
        terms = terms.reshape((places, 2) + terms.shape[1:])
        given = index(terms, 1 - core, 1).astype(BF16)
        kept = index(terms, core, 1).astype(F32)
        return (kept + other_core(given).astype(F32)).astype(BF16)

    def chip_sums(sums):
        groups = [[i * 2 + c for i in range(places)] for c in range(2)]
        terms = lax.all_to_all(sums, "seq", 0, 0, axis_index_groups=groups, tiled=True)
        return jnp.sum(terms.reshape(sums.shape).astype(F32), axis=0)

    skip_part = lax.all_gather(skip_w, "seq", axis=0, tiled=True)

    own_vectors = (skip_b, ln1_g, ln1_b, proj_b, ln2_g, ln2_b, fc2_b, fc1_b)
    packed = jnp.concatenate(own_vectors)
    own_size = packed.shape[0]
    padded = -(-own_size // 1024) * 1024
    packed = jnp.pad(packed, (0, padded - own_size)).reshape(padded // 128, 128)
    packed = jnp.broadcast_to(packed[None], (n,) + packed.shape)
    vectors = lax.all_to_all(packed, ("dp", "seq"), 0, 0, tiled=True)
    vectors = vectors.reshape(n, padded).astype(F32)

    joined_slices = jnp.stack(
        [
            half[:, at * joined_part : (at + 1) * joined_part]
            for half in (inputs[0], skipped[0])
            for at in range(nd // 2)
        ]
    )
    joined_here = jnp.concatenate(
        [index(joined_slices, dp_at)]
        + [swap(index(joined_slices, dp_at ^ k), k) for k in range(1, nd)],
        axis=0,
    )
    at = lax.broadcasted_iota(jnp.int32, (features, features), 0)
    block, row = at // small, at % small
    row = ((block % nd) ^ dp_at) * part + (block // nd) * small + row
    order = (row == lax.broadcasted_iota(jnp.int32, (features, features), 1)).astype(BF16)
    qkv_out = qkv_w.reshape(small, 3, ns, head_cols).transpose(2, 0, 1, 3).reshape(ns, small, wide)
    segments = segment_of(item_lengths, jnp.arange(row_len, dtype=jnp.int32))
    own_proj, skip_part, joined_here, vectors = after((proj_w, skip_part, joined_here, vectors))
    def vector(at):
        return vectors[:, at * small : (at + 1) * small].reshape(features)

    b_skip, g_one, b_one, b_proj, g_two, b_two, b_down = (vector(i) for i in range(7))
    up_bias = lax.dynamic_slice_in_dim(vectors[:, 7 * small : own_size], dp_at * ns, ns, 0)
    up_bias = up_bias.reshape(hidden_part)

    first_terms = dot(joined_here, skip_part)
    first = add_blocks(first_terms[:local], low_rows(first_terms)) + b_skip
    proj_rows = lax.all_gather(own_proj, "seq", axis=0, tiled=True)
    xhat_one, inverse_one = norm_pieces(first)
    normed_one = (xhat_one * g_one + b_one).astype(BF16)
    normed_one, qkv_out, proj_rows = after((normed_one, qkv_out, proj_rows))
    normed_one_row = lax.all_gather(normed_one, "seq", axis=0, tiled=True)

    qkv_mine = seq_exchange(qkv_out).reshape(part, wide)
    qkv_blocks = jnp.stack([qkv_mine] + [swap(qkv_mine, k) for k in range(1, nd)])
    qkv_mine = jnp.concatenate([index(qkv_blocks, dp_at ^ k) for k in range(nd)], axis=0)
    up_slices = jnp.swapaxes(fc1_w.reshape(small, nd, hidden_part), 0, 1)
    up_slices = jnp.concatenate(
        [index(up_slices, dp_at)] + [swap(index(up_slices, dp_at ^ k), k) for k in range(1, nd)],
        axis=0,
    )
    half = part // 2
    own_half = lax.dynamic_slice_in_dim(proj_rows, core * half, half, 0)
    proj_halves = [swap(own_half, k) for k in range(1, nd)]
    normed_one_row, up_slices, qkv_mine, qkv_wide, segments, proj_halves = after(
        (normed_one_row, up_slices, qkv_mine, widen(qkv_mine), segments, proj_halves)
    )
    up_part = lax.all_gather(up_slices, "seq", axis=0, tiled=True)
    triple = dot(normed_one_row, qkv_wide).astype(BF16)
    attended, attended_low, lse = attend(triple, segments, heads, scale)

    def heads_to_tokens(v):
        v = seq_exchange(v.reshape(ns, local, head_cols))
        return jnp.swapaxes(v, 0, 1).reshape(local, features)

    w_proj = lax.dynamic_update_slice_in_dim(
        jnp.zeros((features, features), BF16), proj_rows, dp_at * part, 0
    )
    for k in range(1, nd):
        place = (dp_at ^ k) * 2
        here = proj_halves[k - 1]
        there = other_core(here)
        w_proj = lax.dynamic_update_slice_in_dim(w_proj, here, (place + core) * half, 0)
        w_proj = lax.dynamic_update_slice_in_dim(w_proj, there, (place + 1 - core) * half, 0)
    attended_low, grad_out = after((attended_low, cotangent[0]))
    grad_out_rows = gather_rows(grad_out)
    attended_low = heads_to_tokens(attended_low)
    attended_low, grad_out_rows, w_proj = after((attended_low, grad_out_rows, w_proj))
    own_down, attended_low, up_part = after((fc2_w, attended_low, up_part))
    down_part = lax.all_gather(own_down, "seq", axis=0, tiled=True)
    second = first + dot(attended_low, w_proj) + b_proj
    xhat_two, inverse_two = norm_pieces(second)
    normed_two = (xhat_two * g_two + b_two).astype(BF16)

    normed_two_rows = gather_rows(normed_two)
    up_part = inner(order, up_part).astype(BF16)
    normed_two_rows, up_part, order = after((normed_two_rows, up_part, order))
    hidden, slope = gelu_of_matmul(normed_two_rows, up_part, up_bias)

    fc2_terms = inner(hidden, grad_out_rows).astype(BF16)
    slope, fc2_terms = after((slope, fc2_terms))
    fc2_w_grad = lax.psum_scatter(fc2_terms, "seq", scatter_dimension=0, tiled=True)
    pre_grad = times_transposed(grad_out_rows, down_part) * slope
    pre_low = pre_grad.astype(BF16)
    up_back = times_transposed(pre_low, up_part)
    up_low = low_rows(up_back)
    up_low, pre_late, normed_two_rows = after((up_low, pre_low, normed_two_rows))
    normed_two_grad = add_blocks(up_back[:local], up_low)
    fc1_terms = inner(times_transposed(normed_two_rows, order).astype(BF16), pre_late).astype(BF16)
    normed_two_grad, fc1_terms, fc2_w_grad = after((normed_two_grad, fc1_terms, fc2_w_grad))
    fc1_terms = lax.psum_scatter(fc1_terms, "seq", scatter_dimension=0, tiled=True)
    through_two, ln2_g_grad, ln2_b_grad = norm_back(normed_two_grad, xhat_two, inverse_two, g_two)
    second_grad = grad_out.astype(F32) + through_two
    second_low = second_grad.astype(BF16)
    attended_grad = product_by_group(second_low, w_proj, ns)
    attended_grad, second_late, hidden_late, attended_low = after(
        (attended_grad, second_low, hidden, attended_low)
    )
    attended_grad = seq_exchange(attended_grad).reshape(row_len, head_cols)
    down_sums = dot(hidden_late, down_part)
    attended_slices = jnp.swapaxes(attended_low.reshape(local, nd, part), 0, 1)
    attended_grad, down_sums, second_late, attended_slices = after(
        (attended_grad, down_sums, second_late, attended_slices)
    )
    second_blocks = [second_late] + [swap(second_late, k) for k in range(1, nd)]
    triple_grad = jnp.concatenate(
        attend_back(triple, attended_grad, attended, lse, segments, heads, scale), axis=1
    )
    one_back = times_transposed(triple_grad, qkv_mine).astype(BF16)
    one_back, triple_late, fc1_terms, down_sums, second_rows = after(
        (one_back, triple_grad, fc1_terms, down_sums, jnp.concatenate(second_blocks, axis=0))
    )
    normed_one_grad = lax.psum_scatter(one_back, "seq", scatter_dimension=0, tiled=True)
    qkv_terms = inner(normed_one_row, triple_late).reshape(nd, part, wide)
    qkv_low, down_low = qkv_terms.astype(BF16), low_rows(down_sums)
    qkv_low, down_low, second_rows, attended_slices = after(
        (qkv_low, down_low, second_rows, attended_slices)
    )
    qkv_blocks = [swap(index(qkv_low, dp_at ^ k), k) for k in range(1, nd)]
    attended_rows = jnp.concatenate(
        [index(attended_slices, dp_at)]
        + [swap(index(attended_slices, dp_at ^ k), k) for k in range(1, nd)],
        axis=0,
    )
    proj_terms = inner(attended_rows, second_rows).reshape(ns, small, features)
    proj_w_grad = chip_sums(core_sums(proj_terms))
    output = (second + add_blocks(down_sums[:local], down_low) + b_down).astype(BF16)
    qkv_sum = index(qkv_terms, dp_at)
    for block in qkv_blocks:
        qkv_sum = qkv_sum + block.astype(F32)
    qkv_sum = qkv_sum.astype(BF16).reshape(ns, small, wide)
    fc1_terms = fc1_terms.reshape(nd, small, hidden_part)
    fc1_blocks = jnp.stack([fc1_terms[0]] + [swap(fc1_terms[k], k) for k in range(1, nd)])
    normed_one_grad, qkv_sum, fc1_blocks, proj_w_grad, output = after(
        (normed_one_grad, qkv_sum, fc1_blocks, proj_w_grad, output)
    )
    normed_one_grad = normed_one_grad.astype(F32)
    through_one, ln1_g_grad, ln1_b_grad = norm_back(normed_one_grad, xhat_one, inverse_one, g_one)
    first_grad = second_grad + through_one
    first_low = first_grad.astype(BF16)
    first_low_rows = gather_rows(first_low)
    qkv_w_grad = seq_exchange(qkv_sum)
    vector_grads = jnp.stack(
        [
            jnp.sum(first_grad, axis=0),
            ln1_g_grad,
            ln1_b_grad,
            jnp.sum(second_grad, axis=0),
            ln2_g_grad,
            ln2_b_grad,
            jnp.sum(grad_out.astype(F32), axis=0),
        ]
    )
    vector_grads = jnp.swapaxes(vector_grads.reshape(7, n, small), 0, 1).reshape(n, 7 * small)
    up_grads = jnp.sum(pre_grad, axis=0).reshape(ns, hidden_units // n)
    up_grads = lax.dynamic_update_slice_in_dim(
        jnp.zeros((n, hidden_units // n), F32), up_grads, dp_at * ns, 0
    )
    vector_grads = jnp.concatenate([vector_grads, up_grads], axis=1)
    vector_grads = jnp.pad(vector_grads, ((0, 0), (0, padded - own_size)))
    vector_grads = lax.all_to_all(
        vector_grads.reshape(n, padded // 128, 128), ("dp", "seq"), 0, 0, tiled=True
    )
    first_low_rows, qkv_w_grad, vector_grads = after((first_low_rows, qkv_w_grad, vector_grads))
    skip_terms = inner(joined_here, first_low_rows).astype(BF16)
    skip_w_grad = lax.psum_scatter(skip_terms, "seq", scatter_dimension=0, tiled=True).astype(F32)
    skip_terms, first_low_rows = after((skip_terms, first_low_rows))
    joined_grad_part = times_transposed(first_low_rows, skip_part).astype(BF16)
    joined_grad_part = joined_grad_part.reshape(nd, local, joined_part)
    away = jnp.stack(
        [joined_grad_part[0]] + [swap(joined_grad_part[k], k) for k in range(1, nd)]
    )
    joined_grad = jnp.concatenate(
        [index(away, dp_at ^ k) for k in range(nd)], axis=1
    ).astype(F32)
    fc1_w_grad = jnp.concatenate([index(fc1_blocks, dp_at ^ k) for k in range(nd)], axis=1)
    qkv_w_grad = (
        qkv_w_grad.reshape(ns, small, 3, head_cols).transpose(1, 2, 0, 3)
        .reshape(small, 3 * features)
    )
    vector_grads = jnp.sum(vector_grads, axis=0).reshape(padded)
    skip_b_grad, ln1_g_grad, ln1_b_grad, proj_b_grad, ln2_g_grad, ln2_b_grad, fc2_b_grad = (
        vector_grads[i * small : (i + 1) * small] for i in range(7)
    )
    fc1_b_grad = vector_grads[7 * small : own_size]
    return (
        output[None], joined_grad[None, :, :features], joined_grad[None, :, features:],
        skip_w_grad, qkv_w_grad.astype(F32), proj_w_grad,
        fc1_w_grad.astype(F32), fc2_w_grad.astype(F32),
        skip_b_grad, ln1_g_grad, ln1_b_grad, proj_b_grad, ln2_g_grad, ln2_b_grad,
        fc1_b_grad, fc2_b_grad,
    )


def solution(mesh):
    tokens = P("dp", "seq", None)
    matrix = P(("dp", "seq"), None)
    flat = P(("dp", "seq"))
    in_specs = (tokens, tokens, P("dp", None)) + (matrix,) * 5 + (flat,) * 8 + (tokens,)
    out_specs = (tokens,) * 3 + (matrix,) * 5 + (flat,) * 8
    return jax.shard_map(
        partial(on_device, mesh.shape["dp"], mesh.shape["seq"]),
        mesh=mesh, in_specs=in_specs, out_specs=out_specs, check_vma=False,
    )
```

```python
import math
from functools import partial

import jax
import jax.numpy as jnp
from jax import lax
from jax.experimental import pallas as pl
from jax.experimental.pallas import tpu as pltpu
from jax.sharding import PartitionSpec as P

HEADS = 16
HEAD_DIM = 72
EPSILON = 1e-05
NEGATIVE = -1e30
WIDE = 128
F32 = jnp.float32
BF16 = jnp.bfloat16


def norm_pieces(hvals):
    centered = hvals - jnp.mean(hvals, axis=-1, keepdims=True)
    inverse = lax.rsqrt(jnp.mean(centered * centered, axis=-1, keepdims=True) + EPSILON)
    return centered * inverse, inverse


def norm_back(incoming, standardized, inverse, gain):
    scaled = incoming * gain
    passed = inverse * (
        scaled
        - jnp.mean(scaled, axis=-1, keepdims=True)
        - standardized * jnp.mean(scaled * standardized, axis=-1, keepdims=True)
    )
    return passed, jnp.sum(incoming * standardized, axis=0), jnp.sum(incoming, axis=0)


def segment_of(lengths, places):
    running = jnp.zeros((), jnp.int32)
    passed = jnp.zeros(places.shape, jnp.int32)
    for slot in range(lengths.shape[1]):
        running = running + lengths[0, slot]
        passed = passed + (running <= places).astype(jnp.int32)
    return passed


def dot(left, right):
    return jnp.dot(left, right, preferred_element_type=F32)


def inner(left, right):
    return lax.dot_general(left, right, (((0,), (0,)), ((), ())), preferred_element_type=F32)


def times_transposed(left, right):
    return lax.dot_general(left, right, (((1,), (1,)), ((), ())), preferred_element_type=F32)


def side_by_side(parts):
    return jnp.concatenate([part[:, :HEAD_DIM] for part in parts], axis=1)


def attend_kernel(heads, scale, q_ref, k_ref, v_ref, seg_q_ref, seg_k_ref, out_ref, low_ref, lse_ref):
    allowed = seg_q_ref[...] == seg_k_ref[...]
    lane = lax.broadcasted_iota(jnp.int32, (q_ref.shape[0], WIDE), 1)
    logs = jnp.zeros((q_ref.shape[0], WIDE), F32)
    outs = []
    for h in range(heads):
        at = slice(h * WIDE, (h + 1) * WIDE)
        logits = times_transposed(q_ref[:, at], k_ref[:, at]) * scale
        logits = jnp.where(allowed, logits, NEGATIVE)
        top = jnp.max(logits, axis=1, keepdims=True)
        weights = jnp.exp(logits - top)
        total = jnp.sum(weights, axis=1, keepdims=True)
        outs.append(dot(weights.astype(BF16), v_ref[:, at]) / total)
        out_ref[:, at] = outs[h]
        logs = jnp.where(lane == h, top + jnp.log(total), logs)
    lse_ref[...] = jnp.transpose(logs)[:8]
    low_ref[...] = side_by_side(outs).astype(BF16)


def attend(triple, segments, heads, scale):
    rows = triple.shape[0]
    wide = heads * WIDE
    step = 256 if rows % 256 == 0 else rows
    return pl.pallas_call(
        partial(attend_kernel, heads, scale),
        grid=(rows // step,),
        in_specs=[
            pl.BlockSpec((step, wide), lambda i: (i, 0)),
            pl.BlockSpec((rows, wide), lambda i: (0, 1)),
            pl.BlockSpec((rows, wide), lambda i: (0, 2)),
            pl.BlockSpec((step, 1), lambda i: (i, 0)),
            pl.BlockSpec((1, rows), lambda i: (0, 0)),
        ],
        out_specs=[
            pl.BlockSpec((step, wide), lambda i: (i, 0)),
            pl.BlockSpec((step, heads * HEAD_DIM), lambda i: (i, 0)),
            pl.BlockSpec((8, step), lambda i: (0, i)),
        ],
        out_shape=[
            jax.ShapeDtypeStruct((rows, wide), F32),
            jax.ShapeDtypeStruct((rows, heads * HEAD_DIM), BF16),
            jax.ShapeDtypeStruct((8, rows), F32),
        ],
        compiler_params=pltpu.CompilerParams(vmem_limit_bytes=48 * 2**20),
        cost_estimate=pl.CostEstimate(
            flops=8 * rows * rows * wide,
            bytes_accessed=10 * rows * wide,
            transcendentals=heads * rows * rows,
        ),
    )(triple, triple, triple, segments.reshape(rows, 1), segments.reshape(1, rows))


def attend_back_kernel(
    heads, scale, q_ref, k_ref, v_ref, out_grad_ref, out_ref, lse_ref, seg_q_ref, seg_k_ref,
    dq_ref, dkv_ref, sum_ref, grad_ref, delta_ref,
):
    step = pl.program_id(0)

    @pl.when(step == 0)
    def _():
        sum_ref[...] = jnp.zeros_like(sum_ref)
        ones = jnp.ones((8, WIDE), F32)
        for h in range(heads):
            grad = out_grad_ref[...]
            if h > 0:
                grad = pltpu.roll(grad.astype(F32), 2 * WIDE - HEAD_DIM, 1).astype(BF16)
            grad = grad[:, :WIDE]
            at = slice(h * WIDE, (h + 1) * WIDE)
            grad_ref[:, at] = grad
            delta = lax.dot_general(
                ones, grad.astype(F32) * out_ref[:, at], (((1,), (1,)), ((), ())),
                precision=lax.Precision.HIGHEST, preferred_element_type=F32,
            )
            delta_ref[h : h + 1, :] = delta[:1]

    allowed = seg_k_ref[...] == seg_q_ref[...]
    key_grads, value_grads = [], []
    for h in range(heads):
        at = slice(h * WIDE, (h + 1) * WIDE)
        queries, keys, out_grad = q_ref[:, at], k_ref[:, at], grad_ref[:, at]
        logits = times_transposed(keys, queries) * scale - lse_ref[h : h + 1, :]
        probs = jnp.where(allowed, jnp.exp(logits), 0.0)
        prob_grad = times_transposed(v_ref[:, at], out_grad)
        logit_grad = (probs * (prob_grad - delta_ref[h : h + 1, :]) * scale).astype(BF16)
        value_grads.append(dot(probs.astype(BF16), out_grad))
        key_grads.append(dot(logit_grad, queries))
        sum_ref[:, at] += inner(logit_grad, keys)
    dkv_ref[...] = side_by_side(key_grads + value_grads).astype(BF16)

    @pl.when(step == pl.num_programs(0) - 1)
    def _():
        dq_ref[...] = side_by_side(
            [sum_ref[:, h * WIDE : (h + 1) * WIDE] for h in range(heads)]
        ).astype(BF16)


def attend_back(triple, out_grad, out, lse, segments, heads, scale):
    rows = triple.shape[0]
    wide = heads * WIDE
    step = 256 if rows % 256 == 0 else rows
    whole = pl.BlockSpec((rows, wide), lambda i: (0, 0))
    out_grad = jnp.pad(out_grad, ((0, 0), (0, wide - out_grad.shape[1])))
    row = pl.BlockSpec((8, rows), lambda i: (0, 0))
    return pl.pallas_call(
        partial(attend_back_kernel, heads, scale),
        grid=(rows // step,),
        in_specs=[
            whole,
            pl.BlockSpec((step, wide), lambda i: (i, 1)),
            pl.BlockSpec((step, wide), lambda i: (i, 2)),
            whole,
            whole,
            row,
            pl.BlockSpec((1, rows), lambda i: (0, 0)),
            pl.BlockSpec((step, 1), lambda i: (i, 0)),
        ],
        out_specs=[
            pl.BlockSpec((rows, heads * HEAD_DIM), lambda i: (0, 0)),
            pl.BlockSpec((step, 2 * heads * HEAD_DIM), lambda i: (i, 0)),
        ],
        out_shape=[
            jax.ShapeDtypeStruct((rows, heads * HEAD_DIM), BF16),
            jax.ShapeDtypeStruct((rows, 2 * heads * HEAD_DIM), BF16),
        ],
        scratch_shapes=[
            pltpu.VMEM((rows, wide), F32),
            pltpu.VMEM((rows, wide), BF16),
            pltpu.VMEM((8, rows), F32),
        ],
        compiler_params=pltpu.CompilerParams(vmem_limit_bytes=48 * 2**20),
        cost_estimate=pl.CostEstimate(
            flops=20 * rows * rows * wide,
            bytes_accessed=14 * rows * wide,
            transcendentals=heads * rows * rows,
        ),
    )(
        triple, triple, triple, out_grad, out, lse,
        segments.reshape(1, rows), segments.reshape(rows, 1),
    )


def by_group_kernel(x_ref, w_ref, out_ref):
    groups, rows, columns = out_ref.shape
    product = times_transposed(x_ref[...], w_ref[...]).astype(BF16)
    for g in range(groups):
        out_ref[g] = product[:, g * columns : (g + 1) * columns]


def product_by_group(x, w, groups):
    rows, depth = x.shape
    columns = w.shape[0] // groups
    steps = 2
    return pl.pallas_call(
        by_group_kernel,
        grid=(steps,),
        in_specs=[
            pl.BlockSpec((rows, depth), lambda j: (0, 0)),
            pl.BlockSpec((w.shape[0] // steps, depth), lambda j: (j, 0)),
        ],
        out_specs=pl.BlockSpec((groups // steps, rows, columns), lambda j: (j, 0, 0)),
        out_shape=jax.ShapeDtypeStruct((groups, rows, columns), BF16),
        cost_estimate=pl.CostEstimate(
            flops=2 * rows * depth * w.shape[0],
            bytes_accessed=2 * depth * (rows + w.shape[0]) + 2 * rows * w.shape[0],
            transcendentals=0,
        ),
    )(x, w)


def feed_forward_kernel(
    local, rows_at_once, x_ref, grad_ref, up_ref, down_ref, bias_ref,
    hidden_ref, low_ref, sums_ref, back_ref, own_ref,
):
    sums = jnp.zeros(sums_ref.shape, F32)
    for start in range(0, x_ref.shape[0], rows_at_once):
        at = pl.ds(start, rows_at_once)
        pre = dot(x_ref[at, :], up_ref[...]) + bias_ref[...]
        bell = jnp.exp(-0.5 * pre * pre)
        t = 1.0 / (1.0 + (0.3275911 * 0.5**0.5) * jnp.abs(pre))
        tail = 0.5 * 1.061405429
        for c in (-1.453152027, 1.421413741, -0.284496736, 0.254829592):
            tail = tail * t + 0.5 * c
        tail = tail * t * bell
        below = jnp.where(pre < 0.0, tail, 1.0 - tail)
        hidden_ref[at, :] = (pre * below).astype(BF16)
        slope = below + pre * bell * (0.5 / math.pi) ** 0.5
        pre_grad = times_transposed(grad_ref[at, :], down_ref[...]) * slope
        sums = sums + jnp.sum(pre_grad, axis=0, keepdims=True)
        low = pre_grad.astype(BF16)
        low_ref[at, :] = low
        back = times_transposed(low, up_ref[...])
        if start == 0:
            own_ref[...] = back[:local]
        back_ref[at, :] = back.astype(BF16)
    sums_ref[...] = sums


def feed_forward(x, grad, up, down, bias, local):
    rows, depth = x.shape
    columns = up.shape[1]
    rows_at_once = 640 if rows % 640 == 0 else rows
    return pl.pallas_call(
        partial(feed_forward_kernel, local, rows_at_once),
        out_shape=[
            jax.ShapeDtypeStruct((rows, columns), BF16),
            jax.ShapeDtypeStruct((rows, columns), BF16),
            jax.ShapeDtypeStruct((1, columns), F32),
            jax.ShapeDtypeStruct((rows, depth), BF16),
            jax.ShapeDtypeStruct((local, depth), F32),
        ],
        compiler_params=pltpu.CompilerParams(vmem_limit_bytes=52 * 2**20),
        cost_estimate=pl.CostEstimate(
            flops=6 * rows * depth * columns,
            bytes_accessed=4 * depth * (rows + columns) + 4 * rows * columns + 2 * rows * depth,
            transcendentals=rows * columns,
        ),
    )(x, grad, up, down, bias.reshape(1, columns))


def on_device(
    nd, ns,
    inputs, skipped, item_lengths,
    skip_w, qkv_w, proj_w, fc1_w, fc2_w,
    skip_b, ln1_g, ln1_b, proj_b, ln2_g, ln2_b, fc1_b, fc2_b,
    cotangent,
):
    _, local, features = inputs.shape
    hidden_units = fc1_w.shape[1]
    n = nd * ns
    row_len = local * ns
    heads = HEADS // ns
    head_cols = heads * HEAD_DIM
    wide = 3 * head_cols
    small = features // n
    scale = HEAD_DIM ** (-0.5)
    hidden_part = hidden_units // nd
    joined_part = 2 * features // nd
    part = features // nd
    places = ns // 2
    dp_at = lax.axis_index("dp")
    seq_at = lax.axis_index("seq")
    core = seq_at % 2
    after = lax.optimization_barrier

    def swap(v, k):
        return lax.ppermute(v, "dp", [(i, i ^ k) for i in range(nd)])

    def other_core(v):
        return lax.ppermute(v, "seq", [(i, i ^ 1) for i in range(ns)])

    def index(v, at, axis=0):
        return lax.dynamic_index_in_dim(v, at, axis, keepdims=False)

    def gather_rows(v):
        return jnp.concatenate([v] + [swap(v, k) for k in range(1, nd)], axis=0)

    def add_blocks(own, low):
        for k in range(1, nd):
            own = own + swap(low[k], k).astype(F32)
        return own

    def low_rows(partial_sums):
        return partial_sums.astype(BF16).reshape(nd, local, features)

    def widen(v):
        v = v.reshape(v.shape[0], v.shape[1] // HEAD_DIM, HEAD_DIM)
        return jnp.pad(v, ((0, 0), (0, 0), (0, WIDE - HEAD_DIM))).reshape(v.shape[0], -1)

    def seq_exchange(v):
        return lax.all_to_all(v, "seq", 0, 0, tiled=True)

    def core_sums(terms):
        terms = terms.reshape((places, 2) + terms.shape[1:])
        given = index(terms, 1 - core, 1).astype(BF16)
        kept = index(terms, core, 1).astype(F32)
        return (kept + other_core(given).astype(F32)).astype(BF16)

    def chip_sums(sums):
        groups = [[i * 2 + c for i in range(places)] for c in range(2)]
        terms = lax.all_to_all(sums, "seq", 0, 0, axis_index_groups=groups, tiled=True)
        return jnp.sum(terms.reshape(sums.shape).astype(F32), axis=0)

    skip_part = lax.all_gather(skip_w, "seq", axis=0, tiled=True)

    own_vectors = (skip_b, ln1_g, ln1_b, proj_b, ln2_g, ln2_b, fc2_b, fc1_b)
    packed = jnp.concatenate(own_vectors)
    own_size = packed.shape[0]
    padded = -(-own_size // 1024) * 1024
    packed = jnp.pad(packed, (0, padded - own_size)).reshape(padded // 128, 128)
    packed = jnp.broadcast_to(packed[None], (n,) + packed.shape)
    vectors = lax.all_to_all(packed, ("dp", "seq"), 0, 0, tiled=True)
    vectors = vectors.reshape(n, padded).astype(F32)

    joined_slices = jnp.stack(
        [
            half[:, at * joined_part : (at + 1) * joined_part]
            for half in (inputs[0], skipped[0])
            for at in range(nd // 2)
        ]
    )
    joined_here = jnp.concatenate(
        [index(joined_slices, dp_at)]
        + [swap(index(joined_slices, dp_at ^ k), k) for k in range(1, nd)],
        axis=0,
    )
    at = lax.broadcasted_iota(jnp.int32, (features, features), 0)
    block, row = at // small, at % small
    row = ((block % nd) ^ dp_at) * part + (block // nd) * small + row
    order = (row == lax.broadcasted_iota(jnp.int32, (features, features), 1)).astype(BF16)
    qkv_out = qkv_w.reshape(small, 3, ns, head_cols).transpose(2, 0, 1, 3).reshape(ns, small, wide)
    segments = segment_of(item_lengths, jnp.arange(row_len, dtype=jnp.int32))
    own_proj, skip_part, joined_here, vectors = after((proj_w, skip_part, joined_here, vectors))
    def vector(at):
        return vectors[:, at * small : (at + 1) * small].reshape(features)

    b_skip, g_one, b_one, b_proj, g_two, b_two, b_down = (vector(i) for i in range(7))
    up_bias = lax.dynamic_slice_in_dim(vectors[:, 7 * small : own_size], dp_at * ns, ns, 0)
    up_bias = up_bias.reshape(hidden_part)

    first_terms = dot(joined_here, skip_part)
    first = add_blocks(first_terms[:local], low_rows(first_terms)) + b_skip
    proj_rows = lax.all_gather(own_proj, "seq", axis=0, tiled=True)
    xhat_one, inverse_one = norm_pieces(first)
    normed_one = (xhat_one * g_one + b_one).astype(BF16)
    normed_one, qkv_out, proj_rows = after((normed_one, qkv_out, proj_rows))
    normed_one_row = lax.all_gather(normed_one, "seq", axis=0, tiled=True)

    qkv_mine = seq_exchange(qkv_out).reshape(part, wide)
    up_slices = jnp.swapaxes(fc1_w.reshape(small, nd, hidden_part), 0, 1)
    up_slices = jnp.concatenate(
        [index(up_slices, dp_at)] + [swap(index(up_slices, dp_at ^ k), k) for k in range(1, nd)],
        axis=0,
    )
    half = part // 2
    own_half = lax.dynamic_slice_in_dim(proj_rows, core * half, half, 0)
    proj_halves = [swap(own_half, k) for k in range(1, nd)]
    qkv_mine, up_slices, proj_halves = after((qkv_mine, up_slices, proj_halves))
    qkv_mine = lax.all_gather(qkv_mine, "dp", axis=0, tiled=True)
    normed_one_row, up_slices, qkv_mine, qkv_wide, segments, order = after(
        (normed_one_row, up_slices, qkv_mine, widen(qkv_mine), segments, order)
    )
    up_part = lax.all_gather(up_slices, "seq", axis=0, tiled=True)
    triple = dot(normed_one_row, qkv_wide).astype(BF16)
    attended, attended_low, lse = attend(triple, segments, heads, scale)

    def heads_to_tokens(v):
        v = seq_exchange(v.reshape(ns, local, head_cols))
        return jnp.swapaxes(v, 0, 1).reshape(local, features)

    w_proj = lax.dynamic_update_slice_in_dim(
        jnp.zeros((features, features), BF16), proj_rows, dp_at * part, 0
    )
    for k in range(1, nd):
        place = (dp_at ^ k) * 2
        here = proj_halves[k - 1]
        there = other_core(here)
        w_proj = lax.dynamic_update_slice_in_dim(w_proj, here, (place + core) * half, 0)
        w_proj = lax.dynamic_update_slice_in_dim(w_proj, there, (place + 1 - core) * half, 0)
    attended_low, grad_out = after((attended_low, cotangent[0]))
    grad_out_rows = gather_rows(grad_out)
    attended_low = heads_to_tokens(attended_low)
    attended_low, grad_out_rows, w_proj = after((attended_low, grad_out_rows, w_proj))
    own_down, attended_low, up_part = after((fc2_w, attended_low, up_part))
    down_part = lax.all_gather(own_down, "seq", axis=0, tiled=True)
    second = first + dot(attended_low, w_proj) + b_proj
    xhat_two, inverse_two = norm_pieces(second)
    normed_two = (xhat_two * g_two + b_two).astype(BF16)

    normed_two_rows = gather_rows(normed_two)
    up_part = inner(order, up_part).astype(BF16)
    normed_two_rows, up_part, order = after((normed_two_rows, up_part, order))
    hidden, pre_low, up_sums, up_low, own_back = feed_forward(
        normed_two_rows, grad_out_rows, up_part, down_part, up_bias, local
    )

    normed_two_grad = add_blocks(own_back, up_low.reshape(nd, local, features))
    fc2_terms = inner(hidden, grad_out_rows).astype(BF16)
    fc2_w_grad = lax.psum_scatter(fc2_terms, "seq", scatter_dimension=0, tiled=True)
    fc1_terms = inner(times_transposed(normed_two_rows, order).astype(BF16), pre_low).astype(BF16)
    normed_two_grad, fc2_terms, fc1_terms = after((normed_two_grad, fc2_terms, fc1_terms))
    through_two, ln2_g_grad, ln2_b_grad = norm_back(normed_two_grad, xhat_two, inverse_two, g_two)
    second_grad = grad_out.astype(F32) + through_two
    second_low = second_grad.astype(BF16)
    attended_grad = product_by_group(second_low, w_proj, ns)
    attended_grad, second_late, hidden_late, attended_low, fc1_terms = after(
        (attended_grad, second_low, hidden, attended_low, fc1_terms)
    )
    fc1_terms = lax.psum_scatter(fc1_terms, "seq", scatter_dimension=0, tiled=True)
    attended_grad = seq_exchange(attended_grad).reshape(row_len, head_cols)
    down_sums = dot(hidden_late, down_part)
    attended_slices = jnp.swapaxes(attended_low.reshape(local, nd, part), 0, 1)
    attended_grad, down_sums, second_late, attended_slices = after(
        (attended_grad, down_sums, second_late, attended_slices)
    )
    triple_grad = jnp.concatenate(
        attend_back(triple, attended_grad, attended, lse, segments, heads, scale), axis=1
    )
    one_back = times_transposed(triple_grad, qkv_mine).astype(BF16)
    one_back, triple_late, down_sums, second_late, fc1_terms, fc2_w_grad = after(
        (one_back, triple_grad, down_sums, second_late, fc1_terms, fc2_w_grad)
    )
    normed_one_grad = lax.psum_scatter(one_back, "seq", scatter_dimension=0, tiled=True)
    second_rows = gather_rows(second_late)
    qkv_terms = inner(normed_one_row, triple_late).reshape(nd, part, wide)
    qkv_low, second_rows = after((qkv_terms.astype(BF16), second_rows))
    qkv_blocks = [swap(index(qkv_low, dp_at ^ k), k) for k in range(1, nd)]
    attended_rows = jnp.concatenate(
        [index(attended_slices, dp_at)]
        + [swap(index(attended_slices, dp_at ^ k), k) for k in range(1, nd)],
        axis=0,
    )
    proj_terms = inner(attended_rows, second_rows).reshape(ns, small, features)
    proj_w_grad = chip_sums(core_sums(proj_terms))
    qkv_sum = index(qkv_terms, dp_at)
    for block in qkv_blocks:
        qkv_sum = qkv_sum + block.astype(F32)
    qkv_sum = qkv_sum.astype(BF16).reshape(ns, small, wide)
    normed_one_grad, qkv_sum, proj_w_grad = after((normed_one_grad, qkv_sum, proj_w_grad))
    normed_one_grad = normed_one_grad.astype(F32)
    through_one, ln1_g_grad, ln1_b_grad = norm_back(normed_one_grad, xhat_one, inverse_one, g_one)
    first_grad = second_grad + through_one
    first_low = first_grad.astype(BF16)
    first_low_rows = gather_rows(first_low)
    first_low_rows, qkv_sum, first_grad, fc1_terms, down_sums = after(
        (first_low_rows, qkv_sum, first_grad, fc1_terms, down_sums)
    )
    skip_terms = inner(joined_here, first_low_rows).astype(BF16)
    skip_w_grad = lax.psum_scatter(skip_terms, "seq", scatter_dimension=0, tiled=True).astype(F32)
    skip_terms, first_low_rows, first_grad, qkv_sum, fc1_terms, down_sums = after(
        (skip_terms, first_low_rows, first_grad, qkv_sum, fc1_terms, down_sums)
    )
    qkv_w_grad = seq_exchange(qkv_sum)
    fc1_terms = fc1_terms.reshape(nd, small, hidden_part)
    fc1_blocks = jnp.stack([fc1_terms[0]] + [swap(fc1_terms[k], k) for k in range(1, nd)])
    output = second + add_blocks(down_sums[:local], low_rows(down_sums)) + b_down
    output = output.astype(BF16)
    vector_grads = jnp.stack(
        [
            jnp.sum(first_grad, axis=0),
            ln1_g_grad,
            ln1_b_grad,
            jnp.sum(second_grad, axis=0),
            ln2_g_grad,
            ln2_b_grad,
            jnp.sum(grad_out.astype(F32), axis=0),
        ]
    )
    vector_grads = jnp.swapaxes(vector_grads.reshape(7, n, small), 0, 1).reshape(n, 7 * small)
    up_grads = up_sums.reshape(ns, hidden_units // n)
    up_grads = lax.dynamic_update_slice_in_dim(
        jnp.zeros((n, hidden_units // n), F32), up_grads, dp_at * ns, 0
    )
    vector_grads = jnp.concatenate([vector_grads, up_grads], axis=1)
    vector_grads = jnp.pad(vector_grads, ((0, 0), (0, padded - own_size)))
    vector_grads = lax.all_to_all(
        vector_grads.reshape(n, padded // 128, 128), ("dp", "seq"), 0, 0, tiled=True
    )
    joined_grad_part = times_transposed(first_low_rows, skip_part).astype(BF16)
    joined_grad_part = joined_grad_part.reshape(nd, local, joined_part)
    away = jnp.stack(
        [joined_grad_part[0]] + [swap(joined_grad_part[k], k) for k in range(1, nd)]
    )
    joined_grad = jnp.concatenate(
        [index(away, dp_at ^ k) for k in range(nd)], axis=1
    ).astype(F32)
    fc1_w_grad = jnp.concatenate([index(fc1_blocks, dp_at ^ k) for k in range(nd)], axis=1)
    qkv_w_grad = (
        qkv_w_grad.reshape(ns, small, 3, head_cols).transpose(1, 2, 0, 3)
        .reshape(small, 3 * features)
    )
    vector_grads = jnp.sum(vector_grads, axis=0).reshape(padded)
    skip_b_grad, ln1_g_grad, ln1_b_grad, proj_b_grad, ln2_g_grad, ln2_b_grad, fc2_b_grad = (
        vector_grads[i * small : (i + 1) * small] for i in range(7)
    )
    fc1_b_grad = vector_grads[7 * small : own_size]
    return (
        output[None], joined_grad[None, :, :features], joined_grad[None, :, features:],
        skip_w_grad, qkv_w_grad.astype(F32), proj_w_grad,
        fc1_w_grad.astype(F32), fc2_w_grad.astype(F32),
        skip_b_grad, ln1_g_grad, ln1_b_grad, proj_b_grad, ln2_g_grad, ln2_b_grad,
        fc1_b_grad, fc2_b_grad,
    )


def solution(mesh):
    tokens = P("dp", "seq", None)
    matrix = P(("dp", "seq"), None)
    flat = P(("dp", "seq"))
    in_specs = (tokens, tokens, P("dp", None)) + (matrix,) * 5 + (flat,) * 8 + (tokens,)
    out_specs = (tokens,) * 3 + (matrix,) * 5 + (flat,) * 8
    return jax.shard_map(
        partial(on_device, mesh.shape["dp"], mesh.shape["seq"]),
        mesh=mesh, in_specs=in_specs, out_specs=out_specs, check_vma=False,
    )
```

```python
import math
from functools import partial

import jax
import jax.numpy as jnp
from jax import lax
from jax.experimental import pallas as pl
from jax.experimental.pallas import tpu as pltpu
from jax.sharding import PartitionSpec as P

HEADS = 16
HEAD_DIM = 72
EPSILON = 1e-05
NEGATIVE = -1e30
WIDE = 128
F32 = jnp.float32
BF16 = jnp.bfloat16


def norm_pieces(hvals):
    centered = hvals - jnp.mean(hvals, axis=-1, keepdims=True)
    inverse = lax.rsqrt(jnp.mean(centered * centered, axis=-1, keepdims=True) + EPSILON)
    return centered * inverse, inverse


def norm_back(incoming, standardized, inverse, gain):
    scaled = incoming * gain
    passed = inverse * (
        scaled
        - jnp.mean(scaled, axis=-1, keepdims=True)
        - standardized * jnp.mean(scaled * standardized, axis=-1, keepdims=True)
    )
    return passed, jnp.sum(incoming * standardized, axis=0), jnp.sum(incoming, axis=0)


def segment_of(lengths, places):
    running = jnp.zeros((), jnp.int32)
    passed = jnp.zeros(places.shape, jnp.int32)
    for slot in range(lengths.shape[1]):
        running = running + lengths[0, slot]
        passed = passed + (running <= places).astype(jnp.int32)
    return passed


def dot(left, right):
    return jnp.dot(left, right, preferred_element_type=F32)


def inner(left, right):
    return lax.dot_general(left, right, (((0,), (0,)), ((), ())), preferred_element_type=F32)


def times_transposed(left, right):
    return lax.dot_general(left, right, (((1,), (1,)), ((), ())), preferred_element_type=F32)


def side_by_side(parts):
    return jnp.concatenate([part[:, :HEAD_DIM] for part in parts], axis=1)


def attend_kernel(heads, scale, q_ref, k_ref, v_ref, seg_q_ref, seg_k_ref, out_ref, low_ref, lse_ref):
    allowed = seg_q_ref[...] == seg_k_ref[...]
    lane = lax.broadcasted_iota(jnp.int32, (q_ref.shape[0], WIDE), 1)
    logs = jnp.zeros((q_ref.shape[0], WIDE), F32)
    outs = []
    for h in range(heads):
        at = slice(h * WIDE, (h + 1) * WIDE)
        logits = times_transposed(q_ref[:, at], k_ref[:, at]) * scale
        logits = jnp.where(allowed, logits, NEGATIVE)
        top = jnp.max(logits, axis=1, keepdims=True)
        weights = jnp.exp(logits - top)
        total = jnp.sum(weights, axis=1, keepdims=True)
        outs.append(dot(weights.astype(BF16), v_ref[:, at]) / total)
        out_ref[:, at] = outs[h]
        logs = jnp.where(lane == h, top + jnp.log(total), logs)
    lse_ref[...] = jnp.transpose(logs)[:8]
    low_ref[...] = side_by_side(outs).astype(BF16)


def attend(triple, segments, heads, scale):
    rows = triple.shape[0]
    wide = heads * WIDE
    step = 256 if rows % 256 == 0 else rows
    return pl.pallas_call(
        partial(attend_kernel, heads, scale),
        grid=(rows // step,),
        in_specs=[
            pl.BlockSpec((step, wide), lambda i: (i, 0)),
            pl.BlockSpec((rows, wide), lambda i: (0, 1)),
            pl.BlockSpec((rows, wide), lambda i: (0, 2)),
            pl.BlockSpec((step, 1), lambda i: (i, 0)),
            pl.BlockSpec((1, rows), lambda i: (0, 0)),
        ],
        out_specs=[
            pl.BlockSpec((step, wide), lambda i: (i, 0)),
            pl.BlockSpec((step, heads * HEAD_DIM), lambda i: (i, 0)),
            pl.BlockSpec((8, step), lambda i: (0, i)),
        ],
        out_shape=[
            jax.ShapeDtypeStruct((rows, wide), F32),
            jax.ShapeDtypeStruct((rows, heads * HEAD_DIM), BF16),
            jax.ShapeDtypeStruct((8, rows), F32),
        ],
        compiler_params=pltpu.CompilerParams(vmem_limit_bytes=48 * 2**20),
        cost_estimate=pl.CostEstimate(
            flops=8 * rows * rows * wide,
            bytes_accessed=10 * rows * wide,
            transcendentals=heads * rows * rows,
        ),
    )(triple, triple, triple, segments.reshape(rows, 1), segments.reshape(1, rows))


def attend_back_kernel(
    heads, scale, q_ref, k_ref, v_ref, out_grad_ref, out_ref, lse_ref, seg_q_ref, seg_k_ref,
    dq_ref, dkv_ref, sum_ref, grad_ref, delta_ref,
):
    step = pl.program_id(0)

    @pl.when(step == 0)
    def _():
        sum_ref[...] = jnp.zeros_like(sum_ref)
        ones = jnp.ones((8, WIDE), F32)
        for h in range(heads):
            grad = out_grad_ref[...]
            if h > 0:
                grad = pltpu.roll(grad.astype(F32), 2 * WIDE - HEAD_DIM, 1).astype(BF16)
            grad = grad[:, :WIDE]
            at = slice(h * WIDE, (h + 1) * WIDE)
            grad_ref[:, at] = grad
            delta = lax.dot_general(
                ones, grad.astype(F32) * out_ref[:, at], (((1,), (1,)), ((), ())),
                precision=lax.Precision.HIGHEST, preferred_element_type=F32,
            )
            delta_ref[h : h + 1, :] = delta[:1]

    allowed = seg_k_ref[...] == seg_q_ref[...]
    key_grads, value_grads = [], []
    for h in range(heads):
        at = slice(h * WIDE, (h + 1) * WIDE)
        queries, keys, out_grad = q_ref[:, at], k_ref[:, at], grad_ref[:, at]
        logits = times_transposed(keys, queries) * scale - lse_ref[h : h + 1, :]
        probs = jnp.where(allowed, jnp.exp(logits), 0.0)
        prob_grad = times_transposed(v_ref[:, at], out_grad)
        logit_grad = (probs * (prob_grad - delta_ref[h : h + 1, :]) * scale).astype(BF16)
        value_grads.append(dot(probs.astype(BF16), out_grad))
        key_grads.append(dot(logit_grad, queries))
        sum_ref[:, at] += inner(logit_grad, keys)
    dkv_ref[...] = side_by_side(key_grads + value_grads).astype(BF16)

    @pl.when(step == pl.num_programs(0) - 1)
    def _():
        dq_ref[...] = side_by_side(
            [sum_ref[:, h * WIDE : (h + 1) * WIDE] for h in range(heads)]
        ).astype(BF16)


def attend_back(triple, out_grad, out, lse, segments, heads, scale):
    rows = triple.shape[0]
    wide = heads * WIDE
    step = 256 if rows % 256 == 0 else rows
    whole = pl.BlockSpec((rows, wide), lambda i: (0, 0))
    out_grad = jnp.pad(out_grad, ((0, 0), (0, wide - out_grad.shape[1])))
    row = pl.BlockSpec((8, rows), lambda i: (0, 0))
    return pl.pallas_call(
        partial(attend_back_kernel, heads, scale),
        grid=(rows // step,),
        in_specs=[
            whole,
            pl.BlockSpec((step, wide), lambda i: (i, 1)),
            pl.BlockSpec((step, wide), lambda i: (i, 2)),
            whole,
            whole,
            row,
            pl.BlockSpec((1, rows), lambda i: (0, 0)),
            pl.BlockSpec((step, 1), lambda i: (i, 0)),
        ],
        out_specs=[
            pl.BlockSpec((rows, heads * HEAD_DIM), lambda i: (0, 0)),
            pl.BlockSpec((step, 2 * heads * HEAD_DIM), lambda i: (i, 0)),
        ],
        out_shape=[
            jax.ShapeDtypeStruct((rows, heads * HEAD_DIM), BF16),
            jax.ShapeDtypeStruct((rows, 2 * heads * HEAD_DIM), BF16),
        ],
        scratch_shapes=[
            pltpu.VMEM((rows, wide), F32),
            pltpu.VMEM((rows, wide), BF16),
            pltpu.VMEM((8, rows), F32),
        ],
        compiler_params=pltpu.CompilerParams(vmem_limit_bytes=48 * 2**20),
        cost_estimate=pl.CostEstimate(
            flops=20 * rows * rows * wide,
            bytes_accessed=14 * rows * wide,
            transcendentals=heads * rows * rows,
        ),
    )(
        triple, triple, triple, out_grad, out, lse,
        segments.reshape(1, rows), segments.reshape(rows, 1),
    )


def by_group_kernel(x_ref, w_ref, out_ref):
    groups, rows, columns = out_ref.shape
    product = times_transposed(x_ref[...], w_ref[...]).astype(BF16)
    for g in range(groups):
        out_ref[g] = product[:, g * columns : (g + 1) * columns]


def product_by_group(x, w, groups):
    rows, depth = x.shape
    columns = w.shape[0] // groups
    steps = 2
    return pl.pallas_call(
        by_group_kernel,
        grid=(steps,),
        in_specs=[
            pl.BlockSpec((rows, depth), lambda j: (0, 0)),
            pl.BlockSpec((w.shape[0] // steps, depth), lambda j: (j, 0)),
        ],
        out_specs=pl.BlockSpec((groups // steps, rows, columns), lambda j: (j, 0, 0)),
        out_shape=jax.ShapeDtypeStruct((groups, rows, columns), BF16),
        cost_estimate=pl.CostEstimate(
            flops=2 * rows * depth * w.shape[0],
            bytes_accessed=2 * depth * (rows + w.shape[0]) + 2 * rows * w.shape[0],
            transcendentals=0,
        ),
    )(x, w)


def feed_forward_kernel(
    local, rows_at_once, x_ref, grad_ref, up_ref, down_ref, bias_ref,
    hidden_ref, low_ref, sums_ref, own_ref, *back_refs,
):
    sums = jnp.zeros(sums_ref.shape, F32)
    for start in range(0, x_ref.shape[0], rows_at_once):
        at = pl.ds(start, rows_at_once)
        pre = dot(x_ref[at, :], up_ref[...]) + bias_ref[...]
        bell = jnp.exp(-0.5 * pre * pre)
        t = 1.0 / (1.0 + (0.3275911 * 0.5**0.5) * jnp.abs(pre))
        tail = 0.5 * 1.061405429
        for c in (-1.453152027, 1.421413741, -0.284496736, 0.254829592):
            tail = tail * t + 0.5 * c
        tail = tail * t * bell
        below = jnp.where(pre < 0.0, tail, 1.0 - tail)
        hidden_ref[at, :] = (pre * below).astype(BF16)
        slope = below + pre * bell * (0.5 / math.pi) ** 0.5
        pre_grad = times_transposed(grad_ref[at, :], down_ref[...]) * slope
        sums = sums + jnp.sum(pre_grad, axis=0, keepdims=True)
        low = pre_grad.astype(BF16)
        low_ref[at, :] = low
        back = times_transposed(low, up_ref[...])
        for k in range(start // local, (start + rows_at_once) // local):
            block = back[k * local - start : (k + 1) * local - start]
            if k == 0:
                own_ref[...] = block
            else:
                back_refs[k - 1][...] = block.astype(BF16)
    sums_ref[...] = sums


def feed_forward(x, grad, up, down, bias, local):
    rows, depth = x.shape
    columns = up.shape[1]
    rows_at_once = 640 if rows % 640 == 0 else rows
    return pl.pallas_call(
        partial(feed_forward_kernel, local, rows_at_once),
        out_shape=[
            jax.ShapeDtypeStruct((rows, columns), BF16),
            jax.ShapeDtypeStruct((rows, columns), BF16),
            jax.ShapeDtypeStruct((1, columns), F32),
            jax.ShapeDtypeStruct((local, depth), F32),
        ]
        + [jax.ShapeDtypeStruct((local, depth), BF16)] * (rows // local - 1),
        compiler_params=pltpu.CompilerParams(vmem_limit_bytes=52 * 2**20),
        cost_estimate=pl.CostEstimate(
            flops=6 * rows * depth * columns,
            bytes_accessed=4 * depth * (rows + columns) + 4 * rows * columns + 2 * rows * depth,
            transcendentals=rows * columns,
        ),
    )(x, grad, up, down, bias.reshape(1, columns))


def on_device(
    nd, ns,
    inputs, skipped, item_lengths,
    skip_w, qkv_w, proj_w, fc1_w, fc2_w,
    skip_b, ln1_g, ln1_b, proj_b, ln2_g, ln2_b, fc1_b, fc2_b,
    cotangent,
):
    _, local, features = inputs.shape
    hidden_units = fc1_w.shape[1]
    n = nd * ns
    row_len = local * ns
    heads = HEADS // ns
    head_cols = heads * HEAD_DIM
    wide = 3 * head_cols
    small = features // n
    scale = HEAD_DIM ** (-0.5)
    hidden_part = hidden_units // nd
    joined_part = 2 * features // nd
    part = features // nd
    places = ns // 2
    dp_at = lax.axis_index("dp")
    seq_at = lax.axis_index("seq")
    core = seq_at % 2
    after = lax.optimization_barrier

    def swap(v, k):
        return lax.ppermute(v, "dp", [(i, i ^ k) for i in range(nd)])

    def other_core(v):
        return lax.ppermute(v, "seq", [(i, i ^ 1) for i in range(ns)])

    def index(v, at, axis=0):
        return lax.dynamic_index_in_dim(v, at, axis, keepdims=False)

    def gather_rows(v):
        return jnp.concatenate([v] + [swap(v, k) for k in range(1, nd)], axis=0)

    def add_blocks(own, low):
        for k in range(1, nd):
            own = own + swap(low[k], k).astype(F32)
        return own

    def low_rows(partial_sums):
        return partial_sums.astype(BF16).reshape(nd, local, features)

    def widen(v):
        v = v.reshape(v.shape[0], v.shape[1] // HEAD_DIM, HEAD_DIM)
        return jnp.pad(v, ((0, 0), (0, 0), (0, WIDE - HEAD_DIM))).reshape(v.shape[0], -1)

    def seq_exchange(v):
        return lax.all_to_all(v, "seq", 0, 0, tiled=True)

    def core_sums(terms):
        terms = terms.reshape((places, 2) + terms.shape[1:])
        given = index(terms, 1 - core, 1).astype(BF16)
        kept = index(terms, core, 1).astype(F32)
        return (kept + other_core(given).astype(F32)).astype(BF16)

    def chip_sums(sums):
        groups = [[i * 2 + c for i in range(places)] for c in range(2)]
        terms = lax.all_to_all(sums, "seq", 0, 0, axis_index_groups=groups, tiled=True)
        return jnp.sum(terms.reshape(sums.shape).astype(F32), axis=0)

    skip_rows = skip_w.shape[0]
    skip_proj = jnp.concatenate([skip_w, jnp.pad(proj_w, ((0, -(skip_rows + small) % 8), (0, 0)))])
    skip_proj = lax.all_gather(skip_proj, "seq", axis=0, tiled=False)
    skip_part = skip_proj[:, :skip_rows].reshape(joined_part, features)

    own_vectors = (skip_b, ln1_g, ln1_b, proj_b, ln2_g, ln2_b, fc2_b, fc1_b)
    packed = jnp.concatenate(own_vectors)
    own_size = packed.shape[0]
    padded = -(-own_size // 1024) * 1024
    packed = jnp.pad(packed, (0, padded - own_size)).reshape(padded // 128, 128)
    packed = jnp.broadcast_to(packed[None], (n,) + packed.shape)
    vectors = lax.all_to_all(packed, ("dp", "seq"), 0, 0, tiled=True)
    vectors = vectors.reshape(n, padded).astype(F32)

    joined_slices = jnp.stack(
        [
            half[:, at * joined_part : (at + 1) * joined_part]
            for half in (inputs[0], skipped[0])
            for at in range(nd // 2)
        ]
    )
    joined_here = jnp.concatenate(
        [index(joined_slices, dp_at)]
        + [swap(index(joined_slices, dp_at ^ k), k) for k in range(1, nd)],
        axis=0,
    )
    at = lax.broadcasted_iota(jnp.int32, (features, features), 0)
    block, row = at // small, at % small
    row = ((block % nd) ^ dp_at) * part + (block // nd) * small + row
    order = (row == lax.broadcasted_iota(jnp.int32, (features, features), 1)).astype(BF16)
    qkv_out = qkv_w.reshape(small, 3, ns, head_cols).transpose(2, 0, 1, 3).reshape(ns, small, wide)
    segments = segment_of(item_lengths, jnp.arange(row_len, dtype=jnp.int32))
    qkv_out = qkv_w.reshape(small, 3, ns, head_cols).transpose(2, 0, 1, 3).reshape(ns, small, wide)
    qkv_out, skip_proj, skip_part, joined_here, vectors = after(
        (qkv_out, skip_proj, skip_part, joined_here, vectors)
    )
    def vector(at):
        return vectors[:, at * small : (at + 1) * small].reshape(features)

    b_skip, g_one, b_one, b_proj, g_two, b_two, b_down = (vector(i) for i in range(7))
    up_bias = lax.dynamic_slice_in_dim(vectors[:, 7 * small : own_size], dp_at * ns, ns, 0)
    up_bias = up_bias.reshape(hidden_part)

    first_terms = dot(joined_here, skip_part)
    first = add_blocks(first_terms[:local], low_rows(first_terms)) + b_skip
    qkv_mine = seq_exchange(qkv_out).reshape(part, wide)
    proj_rows = skip_proj[:, skip_rows : skip_rows + small].reshape(part, features)
    xhat_one, inverse_one = norm_pieces(first)
    normed_one = (xhat_one * g_one + b_one).astype(BF16)
    normed_one, qkv_mine, proj_rows = after((normed_one, qkv_mine, proj_rows))
    normed_one_row = lax.all_gather(normed_one, "seq", axis=0, tiled=True)

    qkv_mine = lax.all_gather(qkv_mine, "dp", axis=0, tiled=True)
    up_slices = jnp.swapaxes(fc1_w.reshape(small, nd, hidden_part), 0, 1)
    up_slices = jnp.concatenate(
        [index(up_slices, dp_at)] + [swap(index(up_slices, dp_at ^ k), k) for k in range(1, nd)],
        axis=0,
    )
    half = part // 2
    own_half = lax.dynamic_slice_in_dim(proj_rows, core * half, half, 0)
    proj_halves = [swap(own_half, k) for k in range(1, nd)]
    normed_one_row, up_slices, qkv_mine, qkv_wide, segments, order, proj_halves = after(
        (normed_one_row, up_slices, qkv_mine, widen(qkv_mine), segments, order, proj_halves)
    )
    up_rows = up_slices.size // features
    up_down = jnp.concatenate([up_slices.reshape(up_rows, features), fc2_w], axis=0)
    up_down = lax.all_gather(up_down, "seq", axis=0, tiled=False)

    triple = dot(normed_one_row, qkv_wide).astype(BF16)
    attended, attended_low, lse = attend(triple, segments, heads, scale)

    def heads_to_tokens(v):
        v = seq_exchange(v.reshape(ns, local, head_cols))
        return jnp.swapaxes(v, 0, 1).reshape(local, features)

    w_proj = lax.dynamic_update_slice_in_dim(
        jnp.zeros((features, features), BF16), proj_rows, dp_at * part, 0
    )
    for k in range(1, nd):
        place = (dp_at ^ k) * 2
        here = proj_halves[k - 1]
        there = other_core(here)
        w_proj = lax.dynamic_update_slice_in_dim(w_proj, here, (place + core) * half, 0)
        w_proj = lax.dynamic_update_slice_in_dim(w_proj, there, (place + 1 - core) * half, 0)
    attended_low, grad_out = after((attended_low, cotangent[0]))
    grad_out_rows = gather_rows(grad_out)
    attended_low = heads_to_tokens(attended_low)
    attended_low, grad_out_rows, w_proj = after((attended_low, grad_out_rows, w_proj))
    second = first + dot(attended_low, w_proj) + b_proj
    xhat_two, inverse_two = norm_pieces(second)
    normed_two = (xhat_two * g_two + b_two).astype(BF16)

    normed_two_rows = gather_rows(normed_two)
    up_part = inner(order, up_down[:, :up_rows].reshape(features, hidden_part)).astype(BF16)
    down_part = up_down[:, up_rows:].reshape(hidden_part, features)
    normed_two_rows, up_part, down_part, order = after(
        (normed_two_rows, up_part, down_part, order)
    )
    hidden, pre_low, up_sums, normed_two_grad, *up_blocks = feed_forward(
        normed_two_rows, grad_out_rows, up_part, down_part, up_bias, local
    )

    up_blocks = [swap(block, k + 1) for k, block in enumerate(up_blocks)]
    fc1_terms = inner(times_transposed(normed_two_rows, order).astype(BF16), pre_low).astype(BF16)
    up_blocks[0], hidden = after((up_blocks[0], hidden))
    fc2_terms = inner(hidden, grad_out_rows).astype(BF16)
    fc2_w_grad = lax.psum_scatter(fc2_terms, "seq", scatter_dimension=0, tiled=True)
    for block in up_blocks:
        normed_two_grad = normed_two_grad + block.astype(F32)
    normed_two_grad, fc2_terms, fc1_terms = after((normed_two_grad, fc2_terms, fc1_terms))
    through_two, ln2_g_grad, ln2_b_grad = norm_back(normed_two_grad, xhat_two, inverse_two, g_two)
    second_grad = grad_out.astype(F32) + through_two
    second_low = second_grad.astype(BF16)
    attended_grad = product_by_group(second_low, w_proj, ns)
    attended_grad, second_late, hidden_late, attended_low = after(
        (attended_grad, second_low, hidden, attended_low)
    )
    attended_grad = seq_exchange(attended_grad).reshape(row_len, head_cols)
    down_sums = dot(hidden_late, down_part)
    attended_slices = jnp.swapaxes(attended_low.reshape(local, nd, part), 0, 1)
    down_blocks = low_rows(down_sums)
    down_blocks = [swap(down_blocks[k], k) for k in range(1, nd)]
    attended_grad, down_blocks[0], second_late, attended_slices = after(
        (attended_grad, down_blocks[0], second_late, attended_slices)
    )
    triple_grad = jnp.concatenate(
        attend_back(triple, attended_grad, attended, lse, segments, heads, scale), axis=1
    )
    one_back = times_transposed(triple_grad, qkv_mine).astype(BF16)
    output = second + down_sums[:local] + b_down
    for block in down_blocks:
        output = output + block.astype(F32)
    output = output.astype(BF16)
    one_back, triple_late, output, second_late, fc2_w_grad = after(
        (one_back, triple_grad, output, second_late, fc2_w_grad)
    )
    normed_one_grad = lax.psum_scatter(one_back, "seq", scatter_dimension=0, tiled=True)
    second_rows = gather_rows(second_late)
    qkv_terms = inner(normed_one_row, triple_late).reshape(nd, part, wide)
    qkv_low, second_rows = after((qkv_terms.astype(BF16), second_rows))
    qkv_blocks = [swap(index(qkv_low, dp_at ^ k), k) for k in range(1, nd)]
    attended_rows = jnp.concatenate(
        [index(attended_slices, dp_at)]
        + [swap(index(attended_slices, dp_at ^ k), k) for k in range(1, nd)],
        axis=0,
    )
    proj_terms = inner(attended_rows, second_rows).reshape(ns, small, features)
    proj_sums = core_sums(proj_terms)
    qkv_sum = index(qkv_terms, dp_at)
    for block in qkv_blocks:
        qkv_sum = qkv_sum + block.astype(F32)
    qkv_sum = qkv_sum.astype(BF16).reshape(ns, small, wide)
    normed_one_grad, qkv_sum, proj_sums, fc1_terms = after(
        (normed_one_grad, qkv_sum, proj_sums, fc1_terms)
    )
    fc1_terms = lax.psum_scatter(fc1_terms, "seq", scatter_dimension=0, tiled=True)
    normed_one_grad = normed_one_grad.astype(F32)
    through_one, ln1_g_grad, ln1_b_grad = norm_back(normed_one_grad, xhat_one, inverse_one, g_one)
    first_grad = second_grad + through_one
    first_low = first_grad.astype(BF16)
    first_low_rows = gather_rows(first_low)
    qkv_w_grad = seq_exchange(qkv_sum)
    first_low_rows, first_grad, qkv_w_grad = after((first_low_rows, first_grad, qkv_w_grad))
    skip_terms = inner(joined_here, first_low_rows).astype(BF16)
    skip_terms, fc1_terms = after((skip_terms, fc1_terms))
    skip_w_grad = lax.psum_scatter(skip_terms, "seq", scatter_dimension=0, tiled=True).astype(F32)
    skip_terms, first_low_rows, first_grad, fc1_terms, proj_sums = after(
        (skip_terms, first_low_rows, first_grad, fc1_terms, proj_sums)
    )
    proj_w_grad = chip_sums(proj_sums)
    fc1_terms = fc1_terms.reshape(nd, small, hidden_part)
    fc1_blocks = jnp.stack([fc1_terms[0]] + [swap(fc1_terms[k], k) for k in range(1, nd)])
    vector_grads = jnp.stack(
        [
            jnp.sum(first_grad, axis=0),
            ln1_g_grad,
            ln1_b_grad,
            jnp.sum(second_grad, axis=0),
            ln2_g_grad,
            ln2_b_grad,
            jnp.sum(grad_out.astype(F32), axis=0),
        ]
    )
    vector_grads = jnp.swapaxes(vector_grads.reshape(7, n, small), 0, 1).reshape(n, 7 * small)
    up_grads = up_sums.reshape(ns, hidden_units // n)
    up_grads = lax.dynamic_update_slice_in_dim(
        jnp.zeros((n, hidden_units // n), F32), up_grads, dp_at * ns, 0
    )
    vector_grads = jnp.concatenate([vector_grads, up_grads], axis=1)
    vector_grads = jnp.pad(vector_grads, ((0, 0), (0, padded - own_size)))
    vector_grads = lax.all_to_all(
        vector_grads.reshape(n, padded // 128, 128), ("dp", "seq"), 0, 0, tiled=True
    )
    joined_grad_part = times_transposed(first_low_rows, skip_part).astype(BF16)
    joined_grad_part = joined_grad_part.reshape(nd, local, joined_part)
    away = jnp.stack(
        [joined_grad_part[0]] + [swap(joined_grad_part[k], k) for k in range(1, nd)]
    )
    joined_grad = jnp.concatenate(
        [index(away, dp_at ^ k) for k in range(nd)], axis=1
    ).astype(F32)
    fc1_w_grad = jnp.concatenate([index(fc1_blocks, dp_at ^ k) for k in range(nd)], axis=1)
    qkv_w_grad = (
        qkv_w_grad.reshape(ns, small, 3, head_cols).transpose(1, 2, 0, 3)
        .reshape(small, 3 * features)
    )
    vector_grads = jnp.sum(vector_grads, axis=0).reshape(padded)
    skip_b_grad, ln1_g_grad, ln1_b_grad, proj_b_grad, ln2_g_grad, ln2_b_grad, fc2_b_grad = (
        vector_grads[i * small : (i + 1) * small] for i in range(7)
    )
    fc1_b_grad = vector_grads[7 * small : own_size]
    return (
        output[None], joined_grad[None, :, :features], joined_grad[None, :, features:],
        skip_w_grad, qkv_w_grad.astype(F32), proj_w_grad,
        fc1_w_grad.astype(F32), fc2_w_grad.astype(F32),
        skip_b_grad, ln1_g_grad, ln1_b_grad, proj_b_grad, ln2_g_grad, ln2_b_grad,
        fc1_b_grad, fc2_b_grad,
    )


def solution(mesh):
    tokens = P("dp", "seq", None)
    matrix = P(("dp", "seq"), None)
    flat = P(("dp", "seq"))
    in_specs = (tokens, tokens, P("dp", None)) + (matrix,) * 5 + (flat,) * 8 + (tokens,)
    out_specs = (tokens,) * 3 + (matrix,) * 5 + (flat,) * 8
    return jax.shard_map(
        partial(on_device, mesh.shape["dp"], mesh.shape["seq"]),
        mesh=mesh, in_specs=in_specs, out_specs=out_specs, check_vma=False,
    )
```

```python
import math
from functools import partial

import jax
import jax.numpy as jnp
from jax import lax
from jax.experimental import pallas as pl
from jax.experimental.pallas import tpu as pltpu
from jax.sharding import PartitionSpec as P

HEADS = 16
HEAD_DIM = 72
EPSILON = 1e-05
NEGATIVE = -1e30
WIDE = 128
F32 = jnp.float32
BF16 = jnp.bfloat16


def norm_pieces(hvals):
    centered = hvals - jnp.mean(hvals, axis=-1, keepdims=True)
    inverse = lax.rsqrt(jnp.mean(centered * centered, axis=-1, keepdims=True) + EPSILON)
    return centered * inverse, inverse


def norm_back(incoming, standardized, inverse, gain):
    scaled = incoming * gain
    passed = inverse * (
        scaled
        - jnp.mean(scaled, axis=-1, keepdims=True)
        - standardized * jnp.mean(scaled * standardized, axis=-1, keepdims=True)
    )
    return passed, jnp.sum(incoming * standardized, axis=0), jnp.sum(incoming, axis=0)


def segment_of(lengths, places):
    running = jnp.zeros((), jnp.int32)
    passed = jnp.zeros(places.shape, jnp.int32)
    for slot in range(lengths.shape[1]):
        running = running + lengths[0, slot]
        passed = passed + (running <= places).astype(jnp.int32)
    return passed


def dot(left, right):
    return jnp.dot(left, right, preferred_element_type=F32)


def inner(left, right):
    return lax.dot_general(left, right, (((0,), (0,)), ((), ())), preferred_element_type=F32)


def times_transposed(left, right):
    return lax.dot_general(left, right, (((1,), (1,)), ((), ())), preferred_element_type=F32)


def side_by_side(parts):
    return jnp.concatenate([part[:, :HEAD_DIM] for part in parts], axis=1)


def attend_kernel(heads, scale, q_ref, k_ref, v_ref, seg_q_ref, seg_k_ref, out_ref, low_ref, lse_ref):
    allowed = seg_q_ref[...] == seg_k_ref[...]
    lane = lax.broadcasted_iota(jnp.int32, (q_ref.shape[0], WIDE), 1)
    logs = jnp.zeros((q_ref.shape[0], WIDE), F32)
    outs = []
    for h in range(heads):
        at = slice(h * WIDE, (h + 1) * WIDE)
        logits = times_transposed(q_ref[:, at], k_ref[:, at]) * scale
        logits = jnp.where(allowed, logits, NEGATIVE)
        top = jnp.max(logits, axis=1, keepdims=True)
        weights = jnp.exp(logits - top)
        total = jnp.sum(weights, axis=1, keepdims=True)
        outs.append(dot(weights.astype(BF16), v_ref[:, at]) / total)
        out_ref[:, at] = outs[h]
        logs = jnp.where(lane == h, top + jnp.log(total), logs)
    lse_ref[...] = jnp.transpose(logs)[:8]
    low_ref[...] = side_by_side(outs).astype(BF16)


def attend(triple, segments, heads, scale):
    rows = triple.shape[0]
    wide = heads * WIDE
    step = 256 if rows % 256 == 0 else rows
    return pl.pallas_call(
        partial(attend_kernel, heads, scale),
        grid=(rows // step,),
        in_specs=[
            pl.BlockSpec((step, wide), lambda i: (i, 0)),
            pl.BlockSpec((rows, wide), lambda i: (0, 1)),
            pl.BlockSpec((rows, wide), lambda i: (0, 2)),
            pl.BlockSpec((step, 1), lambda i: (i, 0)),
            pl.BlockSpec((1, rows), lambda i: (0, 0)),
        ],
        out_specs=[
            pl.BlockSpec((step, wide), lambda i: (i, 0)),
            pl.BlockSpec((step, heads * HEAD_DIM), lambda i: (i, 0)),
            pl.BlockSpec((8, step), lambda i: (0, i)),
        ],
        out_shape=[
            jax.ShapeDtypeStruct((rows, wide), F32),
            jax.ShapeDtypeStruct((rows, heads * HEAD_DIM), BF16),
            jax.ShapeDtypeStruct((8, rows), F32),
        ],
        compiler_params=pltpu.CompilerParams(vmem_limit_bytes=48 * 2**20),
        cost_estimate=pl.CostEstimate(
            flops=8 * rows * rows * wide,
            bytes_accessed=10 * rows * wide,
            transcendentals=heads * rows * rows,
        ),
    )(triple, triple, triple, segments.reshape(rows, 1), segments.reshape(1, rows))


def attend_back_kernel(
    heads, scale, q_ref, k_ref, v_ref, out_grad_ref, out_ref, lse_ref, seg_q_ref, seg_k_ref,
    dq_ref, dkv_ref, sum_ref, grad_ref, delta_ref,
):
    step = pl.program_id(0)

    @pl.when(step == 0)
    def _():
        sum_ref[...] = jnp.zeros_like(sum_ref)
        ones = jnp.ones((8, WIDE), F32)
        for h in range(heads):
            grad = out_grad_ref[...]
            if h > 0:
                grad = pltpu.roll(grad.astype(F32), 2 * WIDE - HEAD_DIM, 1).astype(BF16)
            grad = grad[:, :WIDE]
            at = slice(h * WIDE, (h + 1) * WIDE)
            grad_ref[:, at] = grad
            delta = lax.dot_general(
                ones, grad.astype(F32) * out_ref[:, at], (((1,), (1,)), ((), ())),
                precision=lax.Precision.HIGHEST, preferred_element_type=F32,
            )
            delta_ref[h : h + 1, :] = delta[:1]

    allowed = seg_k_ref[...] == seg_q_ref[...]
    key_grads, value_grads = [], []
    for h in range(heads):
        at = slice(h * WIDE, (h + 1) * WIDE)
        queries, keys, out_grad = q_ref[:, at], k_ref[:, at], grad_ref[:, at]
        logits = times_transposed(keys, queries) * scale - lse_ref[h : h + 1, :]
        probs = jnp.where(allowed, jnp.exp(logits), 0.0)
        prob_grad = times_transposed(v_ref[:, at], out_grad)
        logit_grad = (probs * (prob_grad - delta_ref[h : h + 1, :]) * scale).astype(BF16)
        value_grads.append(dot(probs.astype(BF16), out_grad))
        key_grads.append(dot(logit_grad, queries))
        sum_ref[:, at] += inner(logit_grad, keys)
    dkv_ref[...] = side_by_side(key_grads + value_grads).astype(BF16)

    @pl.when(step == pl.num_programs(0) - 1)
    def _():
        dq_ref[...] = side_by_side(
            [sum_ref[:, h * WIDE : (h + 1) * WIDE] for h in range(heads)]
        ).astype(BF16)


def attend_back(triple, out_grad, out, lse, segments, heads, scale):
    rows = triple.shape[0]
    wide = heads * WIDE
    step = 256 if rows % 256 == 0 else rows
    whole = pl.BlockSpec((rows, wide), lambda i: (0, 0))
    out_grad = jnp.pad(out_grad, ((0, 0), (0, wide - out_grad.shape[1])))
    row = pl.BlockSpec((8, rows), lambda i: (0, 0))
    return pl.pallas_call(
        partial(attend_back_kernel, heads, scale),
        grid=(rows // step,),
        in_specs=[
            whole,
            pl.BlockSpec((step, wide), lambda i: (i, 1)),
            pl.BlockSpec((step, wide), lambda i: (i, 2)),
            whole,
            whole,
            row,
            pl.BlockSpec((1, rows), lambda i: (0, 0)),
            pl.BlockSpec((step, 1), lambda i: (i, 0)),
        ],
        out_specs=[
            pl.BlockSpec((rows, heads * HEAD_DIM), lambda i: (0, 0)),
            pl.BlockSpec((step, 2 * heads * HEAD_DIM), lambda i: (i, 0)),
        ],
        out_shape=[
            jax.ShapeDtypeStruct((rows, heads * HEAD_DIM), BF16),
            jax.ShapeDtypeStruct((rows, 2 * heads * HEAD_DIM), BF16),
        ],
        scratch_shapes=[
            pltpu.VMEM((rows, wide), F32),
            pltpu.VMEM((rows, wide), BF16),
            pltpu.VMEM((8, rows), F32),
        ],
        compiler_params=pltpu.CompilerParams(vmem_limit_bytes=48 * 2**20),
        cost_estimate=pl.CostEstimate(
            flops=20 * rows * rows * wide,
            bytes_accessed=14 * rows * wide,
            transcendentals=heads * rows * rows,
        ),
    )(
        triple, triple, triple, out_grad, out, lse,
        segments.reshape(1, rows), segments.reshape(rows, 1),
    )


def by_group_kernel(x_ref, w_ref, out_ref):
    groups, rows, columns = out_ref.shape
    product = times_transposed(x_ref[...], w_ref[...]).astype(BF16)
    for g in range(groups):
        out_ref[g] = product[:, g * columns : (g + 1) * columns]


def product_by_group(x, w, groups):
    rows, depth = x.shape
    columns = w.shape[0] // groups
    steps = 2
    return pl.pallas_call(
        by_group_kernel,
        grid=(steps,),
        in_specs=[
            pl.BlockSpec((rows, depth), lambda j: (0, 0)),
            pl.BlockSpec((w.shape[0] // steps, depth), lambda j: (j, 0)),
        ],
        out_specs=pl.BlockSpec((groups // steps, rows, columns), lambda j: (j, 0, 0)),
        out_shape=jax.ShapeDtypeStruct((groups, rows, columns), BF16),
        cost_estimate=pl.CostEstimate(
            flops=2 * rows * depth * w.shape[0],
            bytes_accessed=2 * depth * (rows + w.shape[0]) + 2 * rows * w.shape[0],
            transcendentals=0,
        ),
    )(x, w)


def gelu_kernel(rows_at_once, x_ref, up_ref, bias_ref, value_ref, slope_ref):
    for start in range(0, x_ref.shape[0], rows_at_once):
        at = pl.ds(start, rows_at_once)
        pre = dot(x_ref[at, :], up_ref[...]) + bias_ref[...]
        bell = jnp.exp(-0.5 * pre * pre)
        t = 1.0 / (1.0 + (0.3275911 * 0.5**0.5) * jnp.abs(pre))
        tail = 0.5 * 1.061405429
        for c in (-1.453152027, 1.421413741, -0.284496736, 0.254829592):
            tail = tail * t + 0.5 * c
        tail = tail * t * bell
        below = jnp.where(pre < 0.0, tail, 1.0 - tail)
        value_ref[at, :] = (pre * below).astype(BF16)
        slope_ref[at, :] = below + pre * bell * (0.5 / math.pi) ** 0.5


def gelu_of_matmul(x, up, bias):
    rows, depth = x.shape
    columns = up.shape[1]
    step = 384 if columns % 384 == 0 else columns
    block = pl.BlockSpec((rows, step), lambda j: (0, j))
    return pl.pallas_call(
        partial(gelu_kernel, 640 if rows % 640 == 0 else rows),
        grid=(columns // step,),
        in_specs=[
            pl.BlockSpec((rows, depth), lambda j: (0, 0)),
            pl.BlockSpec((depth, step), lambda j: (0, j)),
            pl.BlockSpec((1, step), lambda j: (0, j)),
        ],
        out_specs=[block, block],
        out_shape=[
            jax.ShapeDtypeStruct((rows, columns), BF16),
            jax.ShapeDtypeStruct((rows, columns), F32),
        ],
        compiler_params=pltpu.CompilerParams(vmem_limit_bytes=40 * 2**20),
        cost_estimate=pl.CostEstimate(
            flops=2 * rows * depth * columns,
            bytes_accessed=2 * depth * (rows + columns) + 6 * rows * columns,
            transcendentals=rows * columns,
        ),
    )(x, up, bias.reshape(1, columns))


def feed_back_kernel(
    local, grad_ref, up_ref, down_ref, slope_ref, low_ref, sums_ref, own_ref, *back_refs
):
    pre_grad = times_transposed(grad_ref[...], down_ref[...]) * slope_ref[...]
    sums_ref[...] = jnp.sum(pre_grad, axis=0, keepdims=True)
    low = pre_grad.astype(BF16)
    low_ref[...] = low
    back = times_transposed(low, up_ref[...])
    own_ref[...] = back[:local]
    for k, back_ref in enumerate(back_refs):
        back_ref[...] = back[(k + 1) * local : (k + 2) * local].astype(BF16)


def feed_back(grad, up, down, slope, local):
    rows, depth = grad.shape
    columns = up.shape[1]
    return pl.pallas_call(
        partial(feed_back_kernel, local),
        out_shape=[
            jax.ShapeDtypeStruct((rows, columns), BF16),
            jax.ShapeDtypeStruct((1, columns), F32),
            jax.ShapeDtypeStruct((local, depth), F32),
        ]
        + [jax.ShapeDtypeStruct((local, depth), BF16)] * (rows // local - 1),
        compiler_params=pltpu.CompilerParams(vmem_limit_bytes=52 * 2**20),
        cost_estimate=pl.CostEstimate(
            flops=4 * rows * depth * columns,
            bytes_accessed=4 * depth * columns + 6 * rows * columns + 4 * rows * depth,
            transcendentals=0,
        ),
    )(grad, up, down, slope)


def on_device(
    nd, ns,
    inputs, skipped, item_lengths,
    skip_w, qkv_w, proj_w, fc1_w, fc2_w,
    skip_b, ln1_g, ln1_b, proj_b, ln2_g, ln2_b, fc1_b, fc2_b,
    cotangent,
):
    _, local, features = inputs.shape
    hidden_units = fc1_w.shape[1]
    n = nd * ns
    row_len = local * ns
    heads = HEADS // ns
    head_cols = heads * HEAD_DIM
    wide = 3 * head_cols
    small = features // n
    scale = HEAD_DIM ** (-0.5)
    hidden_part = hidden_units // nd
    joined_part = 2 * features // nd
    part = features // nd
    places = ns // 2
    dp_at = lax.axis_index("dp")
    seq_at = lax.axis_index("seq")
    core = seq_at % 2
    after = lax.optimization_barrier

    def swap(v, k):
        return lax.ppermute(v, "dp", [(i, i ^ k) for i in range(nd)])

    def other_core(v):
        return lax.ppermute(v, "seq", [(i, i ^ 1) for i in range(ns)])

    def index(v, at, axis=0):
        return lax.dynamic_index_in_dim(v, at, axis, keepdims=False)

    def gather_rows(v):
        return jnp.concatenate([v] + [swap(v, k) for k in range(1, nd)], axis=0)

    def add_blocks(own, low):
        for k in range(1, nd):
            own = own + swap(low[k], k).astype(F32)
        return own

    def low_rows(partial_sums):
        return partial_sums.astype(BF16).reshape(nd, local, features)

    def widen(v):
        v = v.reshape(v.shape[0], v.shape[1] // HEAD_DIM, HEAD_DIM)
        return jnp.pad(v, ((0, 0), (0, 0), (0, WIDE - HEAD_DIM))).reshape(v.shape[0], -1)

    def seq_exchange(v):
        return lax.all_to_all(v, "seq", 0, 0, tiled=True)

    def core_sums(terms):
        terms = terms.reshape((places, 2) + terms.shape[1:])
        given = index(terms, 1 - core, 1).astype(BF16)
        kept = index(terms, core, 1).astype(F32)
        return (kept + other_core(given).astype(F32)).astype(BF16)

    def chip_sums(sums):
        groups = [[i * 2 + c for i in range(places)] for c in range(2)]
        terms = lax.all_to_all(sums, "seq", 0, 0, axis_index_groups=groups, tiled=True)
        return jnp.sum(terms.reshape(sums.shape).astype(F32), axis=0)

    skip_part = lax.all_gather(skip_w, "seq", axis=0, tiled=True)

    own_vectors = (skip_b, ln1_g, ln1_b, proj_b, ln2_g, ln2_b, fc2_b, fc1_b)
    packed = jnp.concatenate(own_vectors)
    own_size = packed.shape[0]
    padded = -(-own_size // 1024) * 1024
    packed = jnp.pad(packed, (0, padded - own_size)).reshape(padded // 128, 128)
    packed = jnp.broadcast_to(packed[None], (n,) + packed.shape)
    vectors = lax.all_to_all(packed, ("dp", "seq"), 0, 0, tiled=True)
    vectors = vectors.reshape(n, padded).astype(F32)

    joined_slices = jnp.stack(
        [
            half[:, at * joined_part : (at + 1) * joined_part]
            for half in (inputs[0], skipped[0])
            for at in range(nd // 2)
        ]
    )
    joined_here = jnp.concatenate(
        [index(joined_slices, dp_at)]
        + [swap(index(joined_slices, dp_at ^ k), k) for k in range(1, nd)],
        axis=0,
    )
    at = lax.broadcasted_iota(jnp.int32, (features, features), 0)
    block, row = at // small, at % small
    row = ((block % nd) ^ dp_at) * part + (block // nd) * small + row
    order = (row == lax.broadcasted_iota(jnp.int32, (features, features), 1)).astype(BF16)
    qkv_out = qkv_w.reshape(small, 3, ns, head_cols).transpose(2, 0, 1, 3).reshape(ns, small, wide)
    segments = segment_of(item_lengths, jnp.arange(row_len, dtype=jnp.int32))
    own_proj, skip_part, joined_here, vectors = after((proj_w, skip_part, joined_here, vectors))
    def vector(at):
        return vectors[:, at * small : (at + 1) * small].reshape(features)

    b_skip, g_one, b_one, b_proj, g_two, b_two, b_down = (vector(i) for i in range(7))
    up_bias = lax.dynamic_slice_in_dim(vectors[:, 7 * small : own_size], dp_at * ns, ns, 0)
    up_bias = up_bias.reshape(hidden_part)

    first_terms = dot(joined_here, skip_part)
    first = add_blocks(first_terms[:local], low_rows(first_terms)) + b_skip
    proj_rows = lax.all_gather(own_proj, "seq", axis=0, tiled=True)
    xhat_one, inverse_one = norm_pieces(first)
    normed_one = (xhat_one * g_one + b_one).astype(BF16)
    normed_one, qkv_out, proj_rows = after((normed_one, qkv_out, proj_rows))
    normed_one_row = lax.all_gather(normed_one, "seq", axis=0, tiled=True)

    qkv_mine = seq_exchange(qkv_out).reshape(part, wide)
    half = part // 2
    own_half = lax.dynamic_slice_in_dim(proj_rows, core * half, half, 0)
    proj_halves = [swap(own_half, k) for k in range(1, nd)]
    qkv_mine, own_up, proj_halves = after((qkv_mine, fc1_w, proj_halves))
    qkv_mine = lax.all_gather(qkv_mine, "dp", axis=0, tiled=True)
    up_slices = jnp.swapaxes(own_up.reshape(small, nd, hidden_part), 0, 1)
    up_slices = jnp.concatenate(
        [index(up_slices, dp_at)] + [swap(index(up_slices, dp_at ^ k), k) for k in range(1, nd)],
        axis=0,
    )
    normed_one_row, up_slices, qkv_mine, qkv_wide, segments = after(
        (normed_one_row, up_slices, qkv_mine, widen(qkv_mine), segments)
    )
    up_part = lax.all_gather(up_slices, "seq", axis=0, tiled=True)
    triple = dot(normed_one_row, qkv_wide).astype(BF16)
    attended, attended_low, lse = attend(triple, segments, heads, scale)

    def heads_to_tokens(v):
        v = seq_exchange(v.reshape(ns, local, head_cols))
        return jnp.swapaxes(v, 0, 1).reshape(local, features)

    attended_low, grad_out, proj_halves, proj_rows = after(
        (attended_low, cotangent[0], proj_halves, proj_rows)
    )
    w_proj = lax.dynamic_update_slice_in_dim(
        jnp.zeros((features, features), BF16), proj_rows, dp_at * part, 0
    )
    for k in range(1, nd):
        place = (dp_at ^ k) * 2
        here = proj_halves[k - 1]
        there = other_core(here)
        w_proj = lax.dynamic_update_slice_in_dim(w_proj, here, (place + core) * half, 0)
        w_proj = lax.dynamic_update_slice_in_dim(w_proj, there, (place + 1 - core) * half, 0)
    grad_out_rows = gather_rows(grad_out)
    attended_low = heads_to_tokens(attended_low)
    attended_low, grad_out_rows, w_proj, order = after(
        (attended_low, grad_out_rows, w_proj, order)
    )
    own_down, attended_low, up_part = after((fc2_w, attended_low, up_part))
    down_part = lax.all_gather(own_down, "seq", axis=0, tiled=True)
    second = first + dot(attended_low, w_proj) + b_proj
    xhat_two, inverse_two = norm_pieces(second)
    normed_two = (xhat_two * g_two + b_two).astype(BF16)

    normed_two_rows = gather_rows(normed_two)
    up_part = inner(order, up_part).astype(BF16)
    normed_two_rows, up_part, order = after((normed_two_rows, up_part, order))
    hidden, slope = gelu_of_matmul(normed_two_rows, up_part, up_bias)

    fc2_terms = inner(hidden, grad_out_rows).astype(BF16)
    fc2_w_grad = lax.psum_scatter(fc2_terms, "seq", scatter_dimension=0, tiled=True)
    slope, fc2_terms = after((slope, fc2_terms))
    pre_low, up_sums, normed_two_grad, *up_blocks = feed_back(
        grad_out_rows, up_part, down_part, slope, local
    )
    up_blocks = [swap(block, k + 1) for k, block in enumerate(up_blocks)]
    fc1_terms = inner(times_transposed(normed_two_rows, order).astype(BF16), pre_low).astype(BF16)
    for block in up_blocks:
        normed_two_grad = normed_two_grad + block.astype(F32)
    normed_two_grad, fc1_terms = after((normed_two_grad, fc1_terms))
    through_two, ln2_g_grad, ln2_b_grad = norm_back(normed_two_grad, xhat_two, inverse_two, g_two)
    second_grad = grad_out.astype(F32) + through_two
    second_low = second_grad.astype(BF16)
    attended_grad = product_by_group(second_low, w_proj, ns)
    attended_grad, second_late, hidden_late, attended_low, fc1_terms = after(
        (attended_grad, second_low, hidden, attended_low, fc1_terms)
    )
    fc1_terms = lax.psum_scatter(fc1_terms, "seq", scatter_dimension=0, tiled=True)
    attended_grad = seq_exchange(attended_grad).reshape(row_len, head_cols)
    down_sums = dot(hidden_late, down_part)
    attended_slices = jnp.swapaxes(attended_low.reshape(local, nd, part), 0, 1)
    down_blocks = low_rows(down_sums)
    down_blocks = [swap(down_blocks[k], k) for k in range(1, nd)]
    attended_grad, down_blocks[0], second_late, attended_slices = after(
        (attended_grad, down_blocks[0], second_late, attended_slices)
    )
    triple_grad = jnp.concatenate(
        attend_back(triple, attended_grad, attended, lse, segments, heads, scale), axis=1
    )
    one_back = times_transposed(triple_grad, qkv_mine).astype(BF16)
    output = second + down_sums[:local] + b_down
    for block in down_blocks:
        output = output + block.astype(F32)
    output = output.astype(BF16)
    one_back, triple_late, output, second_late, fc1_terms, fc2_w_grad = after(
        (one_back, triple_grad, output, second_late, fc1_terms, fc2_w_grad)
    )
    normed_one_grad = lax.psum_scatter(one_back, "seq", scatter_dimension=0, tiled=True)
    second_rows = gather_rows(second_late)
    qkv_terms = inner(normed_one_row, triple_late).reshape(nd, part, wide)
    qkv_low, second_rows = after((qkv_terms.astype(BF16), second_rows))
    qkv_blocks = [swap(index(qkv_low, dp_at ^ k), k) for k in range(1, nd)]
    attended_rows = jnp.concatenate(
        [index(attended_slices, dp_at)]
        + [swap(index(attended_slices, dp_at ^ k), k) for k in range(1, nd)],
        axis=0,
    )
    proj_terms = inner(attended_rows, second_rows).reshape(ns, small, features)
    proj_sums = core_sums(proj_terms)
    qkv_sum = index(qkv_terms, dp_at)
    for block in qkv_blocks:
        qkv_sum = qkv_sum + block.astype(F32)
    qkv_sum = qkv_sum.astype(BF16).reshape(ns, small, wide)
    normed_one_grad, qkv_sum, proj_sums = after((normed_one_grad, qkv_sum, proj_sums))
    normed_one_grad = normed_one_grad.astype(F32)
    through_one, ln1_g_grad, ln1_b_grad = norm_back(normed_one_grad, xhat_one, inverse_one, g_one)
    first_grad = second_grad + through_one
    first_low = first_grad.astype(BF16)
    first_low_rows = gather_rows(first_low)
    qkv_w_grad = seq_exchange(qkv_sum)
    first_low_rows, first_grad, qkv_w_grad = after((first_low_rows, first_grad, qkv_w_grad))
    skip_terms = inner(joined_here, first_low_rows).astype(BF16)
    skip_w_grad = lax.psum_scatter(skip_terms, "seq", scatter_dimension=0, tiled=True).astype(F32)
    skip_terms, first_low_rows, first_grad, fc1_terms, proj_sums, qkv_w_grad = after(
        (skip_terms, first_low_rows, first_grad, fc1_terms, proj_sums, qkv_w_grad)
    )
    proj_w_grad = chip_sums(proj_sums)
    fc1_terms = fc1_terms.reshape(nd, small, hidden_part)
    fc1_blocks = jnp.stack([fc1_terms[0]] + [swap(fc1_terms[k], k) for k in range(1, nd)])
    vector_grads = jnp.stack(
        [
            jnp.sum(first_grad, axis=0),
            ln1_g_grad,
            ln1_b_grad,
            jnp.sum(second_grad, axis=0),
            ln2_g_grad,
            ln2_b_grad,
            jnp.sum(grad_out.astype(F32), axis=0),
        ]
    )
    vector_grads = jnp.swapaxes(vector_grads.reshape(7, n, small), 0, 1).reshape(n, 7 * small)
    up_grads = up_sums.reshape(ns, hidden_units // n)
    up_grads = lax.dynamic_update_slice_in_dim(
        jnp.zeros((n, hidden_units // n), F32), up_grads, dp_at * ns, 0
    )
    vector_grads = jnp.concatenate([vector_grads, up_grads], axis=1)
    vector_grads = jnp.pad(vector_grads, ((0, 0), (0, padded - own_size)))
    vector_grads = lax.all_to_all(
        vector_grads.reshape(n, padded // 128, 128), ("dp", "seq"), 0, 0, tiled=True
    )
    joined_grad_part = times_transposed(first_low_rows, skip_part).astype(BF16)
    joined_grad_part = joined_grad_part.reshape(nd, local, joined_part)
    away = [joined_grad_part[0]] + [swap(joined_grad_part[k], k) for k in range(1, nd)]
    away, proj_w_grad = after((away, proj_w_grad))
    away = jnp.stack(away)
    joined_grad = jnp.concatenate(
        [index(away, dp_at ^ k) for k in range(nd)], axis=1
    ).astype(F32)
    fc1_w_grad = jnp.concatenate([index(fc1_blocks, dp_at ^ k) for k in range(nd)], axis=1)
    qkv_w_grad = (
        qkv_w_grad.reshape(ns, small, 3, head_cols).transpose(1, 2, 0, 3)
        .reshape(small, 3 * features)
    )
    vector_grads = jnp.sum(vector_grads, axis=0).reshape(padded)
    skip_b_grad, ln1_g_grad, ln1_b_grad, proj_b_grad, ln2_g_grad, ln2_b_grad, fc2_b_grad = (
        vector_grads[i * small : (i + 1) * small] for i in range(7)
    )
    fc1_b_grad = vector_grads[7 * small : own_size]
    return (
        output[None], joined_grad[None, :, :features], joined_grad[None, :, features:],
        skip_w_grad, qkv_w_grad.astype(F32), proj_w_grad,
        fc1_w_grad.astype(F32), fc2_w_grad.astype(F32),
        skip_b_grad, ln1_g_grad, ln1_b_grad, proj_b_grad, ln2_g_grad, ln2_b_grad,
        fc1_b_grad, fc2_b_grad,
    )


def solution(mesh):
    tokens = P("dp", "seq", None)
    matrix = P(("dp", "seq"), None)
    flat = P(("dp", "seq"))
    in_specs = (tokens, tokens, P("dp", None)) + (matrix,) * 5 + (flat,) * 8 + (tokens,)
    out_specs = (tokens,) * 3 + (matrix,) * 5 + (flat,) * 8
    return jax.shard_map(
        partial(on_device, mesh.shape["dp"], mesh.shape["seq"]),
        mesh=mesh, in_specs=in_specs, out_specs=out_specs, check_vma=False,
    )
```

```python
import math
from functools import partial

import jax
import jax.numpy as jnp
from jax import lax
from jax.experimental import pallas as pl
from jax.experimental.pallas import tpu as pltpu
from jax.sharding import PartitionSpec as P

HEADS = 16
HEAD_DIM = 72
EPSILON = 1e-05
NEGATIVE = -1e30
WIDE = 128
F32 = jnp.float32
BF16 = jnp.bfloat16


def norm_pieces(hvals):
    centered = hvals - jnp.mean(hvals, axis=-1, keepdims=True)
    inverse = lax.rsqrt(jnp.mean(centered * centered, axis=-1, keepdims=True) + EPSILON)
    return centered * inverse, inverse


def norm_back(incoming, standardized, inverse, gain):
    scaled = incoming * gain
    passed = inverse * (
        scaled
        - jnp.mean(scaled, axis=-1, keepdims=True)
        - standardized * jnp.mean(scaled * standardized, axis=-1, keepdims=True)
    )
    return passed, jnp.sum(incoming * standardized, axis=0), jnp.sum(incoming, axis=0)


def segment_of(lengths, places):
    running = jnp.zeros((), jnp.int32)
    passed = jnp.zeros(places.shape, jnp.int32)
    for slot in range(lengths.shape[1]):
        running = running + lengths[0, slot]
        passed = passed + (running <= places).astype(jnp.int32)
    return passed


def dot(left, right):
    return jnp.dot(left, right, preferred_element_type=F32)


def inner(left, right):
    return lax.dot_general(left, right, (((0,), (0,)), ((), ())), preferred_element_type=F32)


def times_transposed(left, right):
    return lax.dot_general(left, right, (((1,), (1,)), ((), ())), preferred_element_type=F32)


def side_by_side(parts):
    return jnp.concatenate([part[:, :HEAD_DIM] for part in parts], axis=1)


def attend_kernel(heads, scale, q_ref, k_ref, v_ref, seg_q_ref, seg_k_ref, out_ref, low_ref, lse_ref):
    allowed = seg_q_ref[...] == seg_k_ref[...]
    lane = lax.broadcasted_iota(jnp.int32, (q_ref.shape[0], WIDE), 1)
    logs = jnp.zeros((q_ref.shape[0], WIDE), F32)
    outs = []
    for h in range(heads):
        at = slice(h * WIDE, (h + 1) * WIDE)
        logits = times_transposed(q_ref[:, at], k_ref[:, at]) * scale
        logits = jnp.where(allowed, logits, NEGATIVE)
        top = jnp.max(logits, axis=1, keepdims=True)
        weights = jnp.exp(logits - top)
        total = jnp.sum(weights, axis=1, keepdims=True)
        outs.append(dot(weights.astype(BF16), v_ref[:, at]) / total)
        out_ref[:, at] = outs[h]
        logs = jnp.where(lane == h, top + jnp.log(total), logs)
    lse_ref[...] = jnp.transpose(logs)[:8]
    low_ref[...] = side_by_side(outs).astype(BF16)


def attend(triple, segments, heads, scale):
    rows = triple.shape[0]
    wide = heads * WIDE
    step = 256 if rows % 256 == 0 else rows
    return pl.pallas_call(
        partial(attend_kernel, heads, scale),
        grid=(rows // step,),
        in_specs=[
            pl.BlockSpec((step, wide), lambda i: (i, 0)),
            pl.BlockSpec((rows, wide), lambda i: (0, 1)),
            pl.BlockSpec((rows, wide), lambda i: (0, 2)),
            pl.BlockSpec((step, 1), lambda i: (i, 0)),
            pl.BlockSpec((1, rows), lambda i: (0, 0)),
        ],
        out_specs=[
            pl.BlockSpec((step, wide), lambda i: (i, 0)),
            pl.BlockSpec((step, heads * HEAD_DIM), lambda i: (i, 0)),
            pl.BlockSpec((8, step), lambda i: (0, i)),
        ],
        out_shape=[
            jax.ShapeDtypeStruct((rows, wide), F32),
            jax.ShapeDtypeStruct((rows, heads * HEAD_DIM), BF16),
            jax.ShapeDtypeStruct((8, rows), F32),
        ],
        compiler_params=pltpu.CompilerParams(vmem_limit_bytes=48 * 2**20),
        cost_estimate=pl.CostEstimate(
            flops=8 * rows * rows * wide,
            bytes_accessed=10 * rows * wide,
            transcendentals=heads * rows * rows,
        ),
    )(triple, triple, triple, segments.reshape(rows, 1), segments.reshape(1, rows))


def attend_back_kernel(
    heads, scale, q_ref, k_ref, v_ref, out_grad_ref, out_ref, lse_ref, seg_q_ref, seg_k_ref,
    dq_ref, dkv_ref, sum_ref, grad_ref, delta_ref,
):
    step = pl.program_id(0)

    @pl.when(step == 0)
    def _():
        sum_ref[...] = jnp.zeros_like(sum_ref)
        ones = jnp.ones((8, WIDE), F32)
        for h in range(heads):
            grad = out_grad_ref[...]
            if h > 0:
                grad = pltpu.roll(grad.astype(F32), 2 * WIDE - HEAD_DIM, 1).astype(BF16)
            grad = grad[:, :WIDE]
            at = slice(h * WIDE, (h + 1) * WIDE)
            grad_ref[:, at] = grad
            delta = lax.dot_general(
                ones, grad.astype(F32) * out_ref[:, at], (((1,), (1,)), ((), ())),
                precision=lax.Precision.HIGHEST, preferred_element_type=F32,
            )
            delta_ref[h : h + 1, :] = delta[:1]

    allowed = seg_k_ref[...] == seg_q_ref[...]
    key_grads, value_grads = [], []
    for h in range(heads):
        at = slice(h * WIDE, (h + 1) * WIDE)
        queries, keys, out_grad = q_ref[:, at], k_ref[:, at], grad_ref[:, at]
        logits = times_transposed(keys, queries) * scale - lse_ref[h : h + 1, :]
        probs = jnp.where(allowed, jnp.exp(logits), 0.0)
        prob_grad = times_transposed(v_ref[:, at], out_grad)
        logit_grad = (probs * (prob_grad - delta_ref[h : h + 1, :]) * scale).astype(BF16)
        value_grads.append(dot(probs.astype(BF16), out_grad))
        key_grads.append(dot(logit_grad, queries))
        sum_ref[:, at] += inner(logit_grad, keys)
    dkv_ref[...] = side_by_side(key_grads + value_grads).astype(BF16)

    @pl.when(step == pl.num_programs(0) - 1)
    def _():
        dq_ref[...] = side_by_side(
            [sum_ref[:, h * WIDE : (h + 1) * WIDE] for h in range(heads)]
        ).astype(BF16)


def attend_back(triple, out_grad, out, lse, segments, heads, scale):
    rows = triple.shape[0]
    wide = heads * WIDE
    step = 256 if rows % 256 == 0 else rows
    whole = pl.BlockSpec((rows, wide), lambda i: (0, 0))
    out_grad = jnp.pad(out_grad, ((0, 0), (0, wide - out_grad.shape[1])))
    row = pl.BlockSpec((8, rows), lambda i: (0, 0))
    return pl.pallas_call(
        partial(attend_back_kernel, heads, scale),
        grid=(rows // step,),
        in_specs=[
            whole,
            pl.BlockSpec((step, wide), lambda i: (i, 1)),
            pl.BlockSpec((step, wide), lambda i: (i, 2)),
            whole,
            whole,
            row,
            pl.BlockSpec((1, rows), lambda i: (0, 0)),
            pl.BlockSpec((step, 1), lambda i: (i, 0)),
        ],
        out_specs=[
            pl.BlockSpec((rows, heads * HEAD_DIM), lambda i: (0, 0)),
            pl.BlockSpec((step, 2 * heads * HEAD_DIM), lambda i: (i, 0)),
        ],
        out_shape=[
            jax.ShapeDtypeStruct((rows, heads * HEAD_DIM), BF16),
            jax.ShapeDtypeStruct((rows, 2 * heads * HEAD_DIM), BF16),
        ],
        scratch_shapes=[
            pltpu.VMEM((rows, wide), F32),
            pltpu.VMEM((rows, wide), BF16),
            pltpu.VMEM((8, rows), F32),
        ],
        compiler_params=pltpu.CompilerParams(vmem_limit_bytes=48 * 2**20),
        cost_estimate=pl.CostEstimate(
            flops=20 * rows * rows * wide,
            bytes_accessed=14 * rows * wide,
            transcendentals=heads * rows * rows,
        ),
    )(
        triple, triple, triple, out_grad, out, lse,
        segments.reshape(1, rows), segments.reshape(rows, 1),
    )


def by_group_kernel(x_ref, w_ref, out_ref):
    groups, rows, columns = out_ref.shape
    product = times_transposed(x_ref[...], w_ref[...]).astype(BF16)
    for g in range(groups):
        out_ref[g] = product[:, g * columns : (g + 1) * columns]


def product_by_group(x, w, groups):
    rows, depth = x.shape
    columns = w.shape[0] // groups
    steps = 2
    return pl.pallas_call(
        by_group_kernel,
        grid=(steps,),
        in_specs=[
            pl.BlockSpec((rows, depth), lambda j: (0, 0)),
            pl.BlockSpec((w.shape[0] // steps, depth), lambda j: (j, 0)),
        ],
        out_specs=pl.BlockSpec((groups // steps, rows, columns), lambda j: (j, 0, 0)),
        out_shape=jax.ShapeDtypeStruct((groups, rows, columns), BF16),
        cost_estimate=pl.CostEstimate(
            flops=2 * rows * depth * w.shape[0],
            bytes_accessed=2 * depth * (rows + w.shape[0]) + 2 * rows * w.shape[0],
            transcendentals=0,
        ),
    )(x, w)


def gelu_kernel(rows_at_once, x_ref, up_ref, bias_ref, value_ref, slope_ref):
    for start in range(0, x_ref.shape[0], rows_at_once):
        at = pl.ds(start, rows_at_once)
        pre = dot(x_ref[at, :], up_ref[...]) + bias_ref[...]
        bell = jnp.exp(-0.5 * pre * pre)
        t = 1.0 / (1.0 + (0.3275911 * 0.5**0.5) * jnp.abs(pre))
        tail = 0.5 * 1.061405429
        for c in (-1.453152027, 1.421413741, -0.284496736, 0.254829592):
            tail = tail * t + 0.5 * c
        tail = tail * t * bell
        below = jnp.where(pre < 0.0, tail, 1.0 - tail)
        value_ref[at, :] = (pre * below).astype(BF16)
        slope_ref[at, :] = below + pre * bell * (0.5 / math.pi) ** 0.5


def gelu_of_matmul(x, up, bias):
    rows, depth = x.shape
    columns = up.shape[1]
    step = 384 if columns % 384 == 0 else columns
    block = pl.BlockSpec((rows, step), lambda j: (0, j))
    return pl.pallas_call(
        partial(gelu_kernel, 640 if rows % 640 == 0 else rows),
        grid=(columns // step,),
        in_specs=[
            pl.BlockSpec((rows, depth), lambda j: (0, 0)),
            pl.BlockSpec((depth, step), lambda j: (0, j)),
            pl.BlockSpec((1, step), lambda j: (0, j)),
        ],
        out_specs=[block, block],
        out_shape=[
            jax.ShapeDtypeStruct((rows, columns), BF16),
            jax.ShapeDtypeStruct((rows, columns), F32),
        ],
        compiler_params=pltpu.CompilerParams(vmem_limit_bytes=40 * 2**20),
        cost_estimate=pl.CostEstimate(
            flops=2 * rows * depth * columns,
            bytes_accessed=2 * depth * (rows + columns) + 6 * rows * columns,
            transcendentals=rows * columns,
        ),
    )(x, up, bias.reshape(1, columns))


def feed_back_kernel(
    local, grad_ref, up_ref, down_ref, slope_ref, low_ref, sums_ref, own_ref, *back_refs
):
    pre_grad = times_transposed(grad_ref[...], down_ref[...]) * slope_ref[...]
    sums_ref[...] = jnp.sum(pre_grad, axis=0, keepdims=True)
    low = pre_grad.astype(BF16)
    low_ref[...] = low
    back = times_transposed(low, up_ref[...])
    own_ref[...] = back[:local]
    for k, back_ref in enumerate(back_refs):
        back_ref[...] = back[(k + 1) * local : (k + 2) * local].astype(BF16)


def feed_back(grad, up, down, slope, local):
    rows, depth = grad.shape
    columns = up.shape[1]
    return pl.pallas_call(
        partial(feed_back_kernel, local),
        out_shape=[
            jax.ShapeDtypeStruct((rows, columns), BF16),
            jax.ShapeDtypeStruct((1, columns), F32),
            jax.ShapeDtypeStruct((local, depth), F32),
        ]
        + [jax.ShapeDtypeStruct((local, depth), BF16)] * (rows // local - 1),
        compiler_params=pltpu.CompilerParams(vmem_limit_bytes=52 * 2**20),
        cost_estimate=pl.CostEstimate(
            flops=4 * rows * depth * columns,
            bytes_accessed=4 * depth * columns + 6 * rows * columns + 4 * rows * depth,
            transcendentals=0,
        ),
    )(grad, up, down, slope)


def on_device(
    nd, ns,
    inputs, skipped, item_lengths,
    skip_w, qkv_w, proj_w, fc1_w, fc2_w,
    skip_b, ln1_g, ln1_b, proj_b, ln2_g, ln2_b, fc1_b, fc2_b,
    cotangent,
):
    _, local, features = inputs.shape
    hidden_units = fc1_w.shape[1]
    n = nd * ns
    row_len = local * ns
    heads = HEADS // ns
    head_cols = heads * HEAD_DIM
    wide = 3 * head_cols
    small = features // n
    scale = HEAD_DIM ** (-0.5)
    hidden_part = hidden_units // nd
    joined_part = 2 * features // nd
    part = features // nd
    places = ns // 2
    dp_at = lax.axis_index("dp")
    seq_at = lax.axis_index("seq")
    core = seq_at % 2
    after = lax.optimization_barrier

    def swap(v, k):
        return lax.ppermute(v, "dp", [(i, i ^ k) for i in range(nd)])

    def other_core(v):
        return lax.ppermute(v, "seq", [(i, i ^ 1) for i in range(ns)])

    def index(v, at, axis=0):
        return lax.dynamic_index_in_dim(v, at, axis, keepdims=False)

    def gather_rows(v):
        return jnp.concatenate([v] + [swap(v, k) for k in range(1, nd)], axis=0)

    def add_blocks(own, low):
        for k in range(1, nd):
            own = own + swap(low[k], k).astype(F32)
        return own

    def low_rows(partial_sums):
        return partial_sums.astype(BF16).reshape(nd, local, features)

    def widen(v):
        v = v.reshape(v.shape[0], v.shape[1] // HEAD_DIM, HEAD_DIM)
        return jnp.pad(v, ((0, 0), (0, 0), (0, WIDE - HEAD_DIM))).reshape(v.shape[0], -1)

    def seq_exchange(v):
        return lax.all_to_all(v, "seq", 0, 0, tiled=True)

    def core_sums(terms):
        terms = terms.reshape((places, 2) + terms.shape[1:])
        given = index(terms, 1 - core, 1).astype(BF16)
        kept = index(terms, core, 1).astype(F32)
        return (kept + other_core(given).astype(F32)).astype(BF16)

    def chip_sums(sums):
        groups = [[i * 2 + c for i in range(places)] for c in range(2)]
        terms = lax.all_to_all(sums, "seq", 0, 0, axis_index_groups=groups, tiled=True)
        return jnp.sum(terms.reshape(sums.shape).astype(F32), axis=0)

    skip_part = lax.all_gather(skip_w, "seq", axis=0, tiled=True)

    own_vectors = (skip_b, ln1_g, ln1_b, proj_b, ln2_g, ln2_b, fc2_b, fc1_b)
    packed = jnp.concatenate(own_vectors)
    own_size = packed.shape[0]
    padded = -(-own_size // 1024) * 1024
    packed = jnp.pad(packed, (0, padded - own_size)).reshape(padded // 128, 128)
    packed = jnp.broadcast_to(packed[None], (n,) + packed.shape)
    vectors = lax.all_to_all(packed, ("dp", "seq"), 0, 0, tiled=True)
    vectors = vectors.reshape(n, padded).astype(F32)

    joined_slices = jnp.stack(
        [
            half[:, at * joined_part : (at + 1) * joined_part]
            for half in (inputs[0], skipped[0])
            for at in range(nd // 2)
        ]
    )
    joined_here = jnp.concatenate(
        [index(joined_slices, dp_at)]
        + [swap(index(joined_slices, dp_at ^ k), k) for k in range(1, nd)],
        axis=0,
    )
    at = lax.broadcasted_iota(jnp.int32, (features, features), 0)
    block, row = at // small, at % small
    row = ((block % nd) ^ dp_at) * part + (block // nd) * small + row
    order = (row == lax.broadcasted_iota(jnp.int32, (features, features), 1)).astype(BF16)
    qkv_out = qkv_w.reshape(small, 3, ns, head_cols).transpose(2, 0, 1, 3).reshape(ns, small, wide)
    segments = segment_of(item_lengths, jnp.arange(row_len, dtype=jnp.int32))
    qkv_out, skip_part, joined_here, vectors = after((qkv_out, skip_part, joined_here, vectors))
    def vector(at):
        return vectors[:, at * small : (at + 1) * small].reshape(features)

    b_skip, g_one, b_one, b_proj, g_two, b_two, b_down = (vector(i) for i in range(7))
    up_bias = lax.dynamic_slice_in_dim(vectors[:, 7 * small : own_size], dp_at * ns, ns, 0)
    up_bias = up_bias.reshape(hidden_part)

    first_terms = dot(joined_here, skip_part)
    first = add_blocks(first_terms[:local], low_rows(first_terms)) + b_skip
    qkv_mine = seq_exchange(qkv_out).reshape(part, wide)
    xhat_one, inverse_one = norm_pieces(first)
    normed_one = (xhat_one * g_one + b_one).astype(BF16)
    normed_one, qkv_mine, own_proj, own_up = after((normed_one, qkv_mine, proj_w, fc1_w))
    normed_one_row = lax.all_gather(normed_one, "seq", axis=0, tiled=True)

    qkv_mine = lax.all_gather(qkv_mine, "dp", axis=0, tiled=True)
    qkv_mine, own_proj = after((qkv_mine, own_proj))
    proj_rows = lax.all_gather(own_proj, "seq", axis=0, tiled=True)
    half = part // 2
    own_half = lax.dynamic_slice_in_dim(proj_rows, core * half, half, 0)
    proj_halves = [swap(own_half, k) for k in range(1, nd)]
    up_slices = jnp.swapaxes(own_up.reshape(small, nd, hidden_part), 0, 1)
    up_slices = jnp.concatenate(
        [index(up_slices, dp_at)] + [swap(index(up_slices, dp_at ^ k), k) for k in range(1, nd)],
        axis=0,
    )
    normed_one_row, up_slices, qkv_mine, qkv_wide, segments, proj_halves[0], order = after(
        (normed_one_row, up_slices, qkv_mine, widen(qkv_mine), segments, proj_halves[0], order)
    )
    up_part = lax.all_gather(up_slices, "seq", axis=0, tiled=True)
    triple = dot(normed_one_row, qkv_wide).astype(BF16)
    attended, attended_low, lse = attend(triple, segments, heads, scale)

    def heads_to_tokens(v):
        v = seq_exchange(v.reshape(ns, local, head_cols))
        return jnp.swapaxes(v, 0, 1).reshape(local, features)

    attended_low, grad_out, proj_halves, proj_rows = after(
        (attended_low, cotangent[0], proj_halves, proj_rows)
    )
    w_proj = lax.dynamic_update_slice_in_dim(
        jnp.zeros((features, features), BF16), proj_rows, dp_at * part, 0
    )
    for k in range(1, nd):
        place = (dp_at ^ k) * 2
        here = proj_halves[k - 1]
        there = other_core(here)
        w_proj = lax.dynamic_update_slice_in_dim(w_proj, here, (place + core) * half, 0)
        w_proj = lax.dynamic_update_slice_in_dim(w_proj, there, (place + 1 - core) * half, 0)
    grad_out_rows = gather_rows(grad_out)
    attended_low = heads_to_tokens(attended_low)
    attended_low, grad_out_rows, w_proj, order = after(
        (attended_low, grad_out_rows, w_proj, order)
    )
    own_down, attended_low, up_part = after((fc2_w, attended_low, up_part))
    down_part = lax.all_gather(own_down, "seq", axis=0, tiled=True)
    second = first + dot(attended_low, w_proj) + b_proj
    xhat_two, inverse_two = norm_pieces(second)
    normed_two = (xhat_two * g_two + b_two).astype(BF16)

    normed_two_rows = gather_rows(normed_two)
    up_part = inner(order, up_part).astype(BF16)
    normed_two_rows, up_part, order = after((normed_two_rows, up_part, order))
    hidden, slope = gelu_of_matmul(normed_two_rows, up_part, up_bias)

    fc2_terms = inner(hidden, grad_out_rows).astype(BF16)
    fc2_w_grad = lax.psum_scatter(fc2_terms, "seq", scatter_dimension=0, tiled=True)
    slope, fc2_terms = after((slope, fc2_terms))
    pre_low, up_sums, normed_two_grad, *up_blocks = feed_back(
        grad_out_rows, up_part, down_part, slope, local
    )
    up_blocks = [swap(block, k + 1) for k, block in enumerate(up_blocks)]
    fc1_terms = inner(times_transposed(normed_two_rows, order).astype(BF16), pre_low).astype(BF16)
    for block in up_blocks:
        normed_two_grad = normed_two_grad + block.astype(F32)
    normed_two_grad, fc1_terms = after((normed_two_grad, fc1_terms))
    through_two, ln2_g_grad, ln2_b_grad = norm_back(normed_two_grad, xhat_two, inverse_two, g_two)
    second_grad = grad_out.astype(F32) + through_two
    second_low = second_grad.astype(BF16)
    attended_grad = product_by_group(second_low, w_proj, ns)
    attended_grad, second_late, hidden_late, attended_low, fc1_terms = after(
        (attended_grad, second_low, hidden, attended_low, fc1_terms)
    )
    attended_grad = seq_exchange(attended_grad).reshape(row_len, head_cols)
    down_sums = dot(hidden_late, down_part)
    attended_slices = jnp.swapaxes(attended_low.reshape(local, nd, part), 0, 1)
    down_blocks, fc1_terms = after((low_rows(down_sums), fc1_terms))
    fc1_terms = lax.psum_scatter(fc1_terms, "seq", scatter_dimension=0, tiled=True)
    down_blocks = [swap(down_blocks[k], k) for k in range(1, nd)]
    attended_grad, down_blocks[0], second_late, attended_slices = after(
        (attended_grad, down_blocks[0], second_late, attended_slices)
    )
    triple_grad = jnp.concatenate(
        attend_back(triple, attended_grad, attended, lse, segments, heads, scale), axis=1
    )
    one_back = times_transposed(triple_grad, qkv_mine).astype(BF16)
    output = second + down_sums[:local] + b_down
    for block in down_blocks:
        output = output + block.astype(F32)
    output = output.astype(BF16)
    one_back, triple_late, output, second_late, fc1_terms, fc2_w_grad = after(
        (one_back, triple_grad, output, second_late, fc1_terms, fc2_w_grad)
    )
    normed_one_grad = lax.psum_scatter(one_back, "seq", scatter_dimension=0, tiled=True)
    second_rows = gather_rows(second_late)
    qkv_terms = inner(normed_one_row, triple_late).reshape(nd, part, wide)
    qkv_low, second_rows = after((qkv_terms.astype(BF16), second_rows))
    qkv_blocks = [swap(index(qkv_low, dp_at ^ k), k) for k in range(1, nd)]
    attended_rows = jnp.concatenate(
        [index(attended_slices, dp_at)]
        + [swap(index(attended_slices, dp_at ^ k), k) for k in range(1, nd)],
        axis=0,
    )
    proj_terms = inner(attended_rows, second_rows).reshape(ns, small, features)
    proj_sums = core_sums(proj_terms)
    qkv_sum = index(qkv_terms, dp_at)
    for block in qkv_blocks:
        qkv_sum = qkv_sum + block.astype(F32)
    qkv_sum = qkv_sum.astype(BF16).reshape(ns, small, wide)
    normed_one_grad = normed_one_grad.astype(F32)
    through_one, ln1_g_grad, ln1_b_grad = norm_back(normed_one_grad, xhat_one, inverse_one, g_one)
    first_grad = second_grad + through_one
    first_low = first_grad.astype(BF16)
    first_low_rows = gather_rows(first_low)
    proj_w_grad = chip_sums(proj_sums)
    qkv_w_grad = seq_exchange(qkv_sum)
    first_low_rows, first_grad, qkv_w_grad, proj_w_grad = after(
        (first_low_rows, first_grad, qkv_w_grad, proj_w_grad)
    )
    skip_terms = inner(joined_here, first_low_rows).astype(BF16)
    skip_w_grad = lax.psum_scatter(skip_terms, "seq", scatter_dimension=0, tiled=True).astype(F32)
    skip_terms, first_low_rows, first_grad, fc1_terms, qkv_w_grad = after(
        (skip_terms, first_low_rows, first_grad, fc1_terms, qkv_w_grad)
    )
    fc1_terms = fc1_terms.reshape(nd, small, hidden_part)
    fc1_blocks = jnp.stack([fc1_terms[0]] + [swap(fc1_terms[k], k) for k in range(1, nd)])
    vector_grads = jnp.stack(
        [
            jnp.sum(first_grad, axis=0),
            ln1_g_grad,
            ln1_b_grad,
            jnp.sum(second_grad, axis=0),
            ln2_g_grad,
            ln2_b_grad,
            jnp.sum(grad_out.astype(F32), axis=0),
        ]
    )
    vector_grads = jnp.swapaxes(vector_grads.reshape(7, n, small), 0, 1).reshape(n, 7 * small)
    up_grads = up_sums.reshape(ns, hidden_units // n)
    up_grads = lax.dynamic_update_slice_in_dim(
        jnp.zeros((n, hidden_units // n), F32), up_grads, dp_at * ns, 0
    )
    vector_grads = jnp.concatenate([vector_grads, up_grads], axis=1)
    vector_grads = jnp.pad(vector_grads, ((0, 0), (0, padded - own_size)))
    vector_grads = lax.all_to_all(
        vector_grads.reshape(n, padded // 128, 128), ("dp", "seq"), 0, 0, tiled=True
    )
    joined_grad_part = times_transposed(first_low_rows, skip_part).astype(BF16)
    joined_grad_part = joined_grad_part.reshape(nd, local, joined_part)
    away = [joined_grad_part[0]] + [swap(joined_grad_part[k], k) for k in range(1, nd)]
    away = jnp.stack(away)
    joined_grad = jnp.concatenate(
        [index(away, dp_at ^ k) for k in range(nd)], axis=1
    ).astype(F32)
    fc1_w_grad = jnp.concatenate([index(fc1_blocks, dp_at ^ k) for k in range(nd)], axis=1)
    qkv_w_grad = (
        qkv_w_grad.reshape(ns, small, 3, head_cols).transpose(1, 2, 0, 3)
        .reshape(small, 3 * features)
    )
    vector_grads = jnp.sum(vector_grads, axis=0).reshape(padded)
    skip_b_grad, ln1_g_grad, ln1_b_grad, proj_b_grad, ln2_g_grad, ln2_b_grad, fc2_b_grad = (
        vector_grads[i * small : (i + 1) * small] for i in range(7)
    )
    fc1_b_grad = vector_grads[7 * small : own_size]
    return (
        output[None], joined_grad[None, :, :features], joined_grad[None, :, features:],
        skip_w_grad, qkv_w_grad.astype(F32), proj_w_grad,
        fc1_w_grad.astype(F32), fc2_w_grad.astype(F32),
        skip_b_grad, ln1_g_grad, ln1_b_grad, proj_b_grad, ln2_g_grad, ln2_b_grad,
        fc1_b_grad, fc2_b_grad,
    )


def solution(mesh):
    tokens = P("dp", "seq", None)
    matrix = P(("dp", "seq"), None)
    flat = P(("dp", "seq"))
    in_specs = (tokens, tokens, P("dp", None)) + (matrix,) * 5 + (flat,) * 8 + (tokens,)
    out_specs = (tokens,) * 3 + (matrix,) * 5 + (flat,) * 8
    return jax.shard_map(
        partial(on_device, mesh.shape["dp"], mesh.shape["seq"]),
        mesh=mesh, in_specs=in_specs, out_specs=out_specs, check_vma=False,
    )
```

```python
import math
from functools import partial

import jax
import jax.numpy as jnp
from jax import lax
from jax.experimental import pallas as pl
from jax.experimental.pallas import tpu as pltpu
from jax.sharding import PartitionSpec as P

HEADS = 16
HEAD_DIM = 72
EPSILON = 1e-05
NEGATIVE = -1e30
WIDE = 128
F32 = jnp.float32
BF16 = jnp.bfloat16


def norm_pieces(hvals):
    centered = hvals - jnp.mean(hvals, axis=-1, keepdims=True)
    inverse = lax.rsqrt(jnp.mean(centered * centered, axis=-1, keepdims=True) + EPSILON)
    return centered * inverse, inverse


def norm_back(incoming, standardized, inverse, gain):
    scaled = incoming * gain
    passed = inverse * (
        scaled
        - jnp.mean(scaled, axis=-1, keepdims=True)
        - standardized * jnp.mean(scaled * standardized, axis=-1, keepdims=True)
    )
    return passed, jnp.sum(incoming * standardized, axis=0), jnp.sum(incoming, axis=0)


def segment_of(lengths, places):
    running = jnp.zeros((), jnp.int32)
    passed = jnp.zeros(places.shape, jnp.int32)
    for slot in range(lengths.shape[1]):
        running = running + lengths[0, slot]
        passed = passed + (running <= places).astype(jnp.int32)
    return passed


def dot(left, right):
    return jnp.dot(left, right, preferred_element_type=F32)


def inner(left, right):
    return lax.dot_general(left, right, (((0,), (0,)), ((), ())), preferred_element_type=F32)


def times_transposed(left, right):
    return lax.dot_general(left, right, (((1,), (1,)), ((), ())), preferred_element_type=F32)


def side_by_side(parts):
    return jnp.concatenate([part[:, :HEAD_DIM] for part in parts], axis=1)


def attend_kernel(heads, scale, q_ref, k_ref, v_ref, seg_q_ref, seg_k_ref, out_ref, low_ref, lse_ref):
    allowed = seg_q_ref[...] == seg_k_ref[...]
    lane = lax.broadcasted_iota(jnp.int32, (q_ref.shape[0], WIDE), 1)
    logs = jnp.zeros((q_ref.shape[0], WIDE), F32)
    outs = []
    for h in range(heads):
        at = slice(h * WIDE, (h + 1) * WIDE)
        logits = times_transposed(q_ref[:, at], k_ref[:, at]) * scale
        logits = jnp.where(allowed, logits, NEGATIVE)
        top = jnp.max(logits, axis=1, keepdims=True)
        weights = jnp.exp(logits - top)
        total = jnp.sum(weights, axis=1, keepdims=True)
        outs.append(dot(weights.astype(BF16), v_ref[:, at]) / total)
        out_ref[:, at] = outs[h]
        logs = jnp.where(lane == h, top + jnp.log(total), logs)
    lse_ref[...] = jnp.transpose(logs)[:8]
    low_ref[...] = side_by_side(outs).astype(BF16)


def attend(triple, segments, heads, scale):
    rows = triple.shape[0]
    wide = heads * WIDE
    step = 256 if rows % 256 == 0 else rows
    return pl.pallas_call(
        partial(attend_kernel, heads, scale),
        grid=(rows // step,),
        in_specs=[
            pl.BlockSpec((step, wide), lambda i: (i, 0)),
            pl.BlockSpec((rows, wide), lambda i: (0, 1)),
            pl.BlockSpec((rows, wide), lambda i: (0, 2)),
            pl.BlockSpec((step, 1), lambda i: (i, 0)),
            pl.BlockSpec((1, rows), lambda i: (0, 0)),
        ],
        out_specs=[
            pl.BlockSpec((step, wide), lambda i: (i, 0)),
            pl.BlockSpec((step, heads * HEAD_DIM), lambda i: (i, 0)),
            pl.BlockSpec((8, step), lambda i: (0, i)),
        ],
        out_shape=[
            jax.ShapeDtypeStruct((rows, wide), F32),
            jax.ShapeDtypeStruct((rows, heads * HEAD_DIM), BF16),
            jax.ShapeDtypeStruct((8, rows), F32),
        ],
        compiler_params=pltpu.CompilerParams(vmem_limit_bytes=48 * 2**20),
        cost_estimate=pl.CostEstimate(
            flops=8 * rows * rows * wide,
            bytes_accessed=10 * rows * wide,
            transcendentals=heads * rows * rows,
        ),
    )(triple, triple, triple, segments.reshape(rows, 1), segments.reshape(1, rows))


def attend_back_kernel(
    heads, scale, q_ref, k_ref, v_ref, out_grad_ref, out_ref, lse_ref, seg_q_ref, seg_k_ref,
    dq_ref, dkv_ref, sum_ref, grad_ref, delta_ref,
):
    step = pl.program_id(0)

    @pl.when(step == 0)
    def _():
        sum_ref[...] = jnp.zeros_like(sum_ref)
        ones = jnp.ones((8, WIDE), F32)
        for h in range(heads):
            grad = out_grad_ref[...]
            if h > 0:
                grad = pltpu.roll(grad.astype(F32), 2 * WIDE - HEAD_DIM, 1).astype(BF16)
            grad = grad[:, :WIDE]
            at = slice(h * WIDE, (h + 1) * WIDE)
            grad_ref[:, at] = grad
            delta = lax.dot_general(
                ones, grad.astype(F32) * out_ref[:, at], (((1,), (1,)), ((), ())),
                precision=lax.Precision.HIGHEST, preferred_element_type=F32,
            )
            delta_ref[h : h + 1, :] = delta[:1]

    allowed = seg_k_ref[...] == seg_q_ref[...]
    key_grads, value_grads = [], []
    for h in range(heads):
        at = slice(h * WIDE, (h + 1) * WIDE)
        queries, keys, out_grad = q_ref[:, at], k_ref[:, at], grad_ref[:, at]
        logits = times_transposed(keys, queries) * scale - lse_ref[h : h + 1, :]
        probs = jnp.where(allowed, jnp.exp(logits), 0.0)
        prob_grad = times_transposed(v_ref[:, at], out_grad)
        logit_grad = (probs * (prob_grad - delta_ref[h : h + 1, :]) * scale).astype(BF16)
        value_grads.append(dot(probs.astype(BF16), out_grad))
        key_grads.append(dot(logit_grad, queries))
        sum_ref[:, at] += inner(logit_grad, keys)
    dkv_ref[...] = side_by_side(key_grads + value_grads).astype(BF16)

    @pl.when(step == pl.num_programs(0) - 1)
    def _():
        dq_ref[...] = side_by_side(
            [sum_ref[:, h * WIDE : (h + 1) * WIDE] for h in range(heads)]
        ).astype(BF16)


def attend_back(triple, out_grad, out, lse, segments, heads, scale):
    rows = triple.shape[0]
    wide = heads * WIDE
    step = 256 if rows % 256 == 0 else rows
    whole = pl.BlockSpec((rows, wide), lambda i: (0, 0))
    out_grad = jnp.pad(out_grad, ((0, 0), (0, wide - out_grad.shape[1])))
    row = pl.BlockSpec((8, rows), lambda i: (0, 0))
    return pl.pallas_call(
        partial(attend_back_kernel, heads, scale),
        grid=(rows // step,),
        in_specs=[
            whole,
            pl.BlockSpec((step, wide), lambda i: (i, 1)),
            pl.BlockSpec((step, wide), lambda i: (i, 2)),
            whole,
            whole,
            row,
            pl.BlockSpec((1, rows), lambda i: (0, 0)),
            pl.BlockSpec((step, 1), lambda i: (i, 0)),
        ],
        out_specs=[
            pl.BlockSpec((rows, heads * HEAD_DIM), lambda i: (0, 0)),
            pl.BlockSpec((step, 2 * heads * HEAD_DIM), lambda i: (i, 0)),
        ],
        out_shape=[
            jax.ShapeDtypeStruct((rows, heads * HEAD_DIM), BF16),
            jax.ShapeDtypeStruct((rows, 2 * heads * HEAD_DIM), BF16),
        ],
        scratch_shapes=[
            pltpu.VMEM((rows, wide), F32),
            pltpu.VMEM((rows, wide), BF16),
            pltpu.VMEM((8, rows), F32),
        ],
        compiler_params=pltpu.CompilerParams(vmem_limit_bytes=48 * 2**20),
        cost_estimate=pl.CostEstimate(
            flops=20 * rows * rows * wide,
            bytes_accessed=14 * rows * wide,
            transcendentals=heads * rows * rows,
        ),
    )(
        triple, triple, triple, out_grad, out, lse,
        segments.reshape(1, rows), segments.reshape(rows, 1),
    )


def by_group_kernel(x_ref, w_ref, out_ref):
    groups, rows, columns = out_ref.shape
    product = times_transposed(x_ref[...], w_ref[...]).astype(BF16)
    for g in range(groups):
        out_ref[g] = product[:, g * columns : (g + 1) * columns]


def product_by_group(x, w, groups):
    rows, depth = x.shape
    columns = w.shape[0] // groups
    steps = 2
    return pl.pallas_call(
        by_group_kernel,
        grid=(steps,),
        in_specs=[
            pl.BlockSpec((rows, depth), lambda j: (0, 0)),
            pl.BlockSpec((w.shape[0] // steps, depth), lambda j: (j, 0)),
        ],
        out_specs=pl.BlockSpec((groups // steps, rows, columns), lambda j: (j, 0, 0)),
        out_shape=jax.ShapeDtypeStruct((groups, rows, columns), BF16),
        cost_estimate=pl.CostEstimate(
            flops=2 * rows * depth * w.shape[0],
            bytes_accessed=2 * depth * (rows + w.shape[0]) + 2 * rows * w.shape[0],
            transcendentals=0,
        ),
    )(x, w)


def gelu_kernel(rows_at_once, x_ref, up_ref, bias_ref, value_ref, slope_ref):
    for start in range(0, x_ref.shape[0], rows_at_once):
        at = pl.ds(start, rows_at_once)
        pre = dot(x_ref[at, :], up_ref[...]) + bias_ref[...]
        bell = jnp.exp(-0.5 * pre * pre)
        t = 1.0 / (1.0 + (0.3275911 * 0.5**0.5) * jnp.abs(pre))
        tail = 0.5 * 1.061405429
        for c in (-1.453152027, 1.421413741, -0.284496736, 0.254829592):
            tail = tail * t + 0.5 * c
        tail = tail * t * bell
        below = jnp.where(pre < 0.0, tail, 1.0 - tail)
        value_ref[at, :] = (pre * below).astype(BF16)
        slope_ref[at, :] = below + pre * bell * (0.5 / math.pi) ** 0.5


def gelu_of_matmul(x, up, bias):
    rows, depth = x.shape
    columns = up.shape[1]
    step = 384 if columns % 384 == 0 else columns
    block = pl.BlockSpec((rows, step), lambda j: (0, j))
    return pl.pallas_call(
        partial(gelu_kernel, 640 if rows % 640 == 0 else rows),
        grid=(columns // step,),
        in_specs=[
            pl.BlockSpec((rows, depth), lambda j: (0, 0)),
            pl.BlockSpec((depth, step), lambda j: (0, j)),
            pl.BlockSpec((1, step), lambda j: (0, j)),
        ],
        out_specs=[block, block],
        out_shape=[
            jax.ShapeDtypeStruct((rows, columns), BF16),
            jax.ShapeDtypeStruct((rows, columns), F32),
        ],
        compiler_params=pltpu.CompilerParams(vmem_limit_bytes=40 * 2**20),
        cost_estimate=pl.CostEstimate(
            flops=2 * rows * depth * columns,
            bytes_accessed=2 * depth * (rows + columns) + 6 * rows * columns,
            transcendentals=rows * columns,
        ),
    )(x, up, bias.reshape(1, columns))


def feed_back_kernel(
    local, grad_ref, up_ref, down_ref, slope_ref, low_ref, sums_ref, own_ref, *back_refs
):
    pre_grad = times_transposed(grad_ref[...], down_ref[...]) * slope_ref[...]
    sums_ref[...] = jnp.sum(pre_grad, axis=0, keepdims=True)
    low = pre_grad.astype(BF16)
    low_ref[...] = low
    back = times_transposed(low, up_ref[...])
    own_ref[...] = back[:local]
    for k, back_ref in enumerate(back_refs):
        back_ref[...] = back[(k + 1) * local : (k + 2) * local].astype(BF16)


def feed_back(grad, up, down, slope, local):
    rows, depth = grad.shape
    columns = up.shape[1]
    return pl.pallas_call(
        partial(feed_back_kernel, local),
        out_shape=[
            jax.ShapeDtypeStruct((rows, columns), BF16),
            jax.ShapeDtypeStruct((1, columns), F32),
            jax.ShapeDtypeStruct((local, depth), F32),
        ]
        + [jax.ShapeDtypeStruct((local, depth), BF16)] * (rows // local - 1),
        compiler_params=pltpu.CompilerParams(vmem_limit_bytes=52 * 2**20),
        cost_estimate=pl.CostEstimate(
            flops=4 * rows * depth * columns,
            bytes_accessed=4 * depth * columns + 6 * rows * columns + 4 * rows * depth,
            transcendentals=0,
        ),
    )(grad, up, down, slope)


def on_device(
    nd, ns,
    inputs, skipped, item_lengths,
    skip_w, qkv_w, proj_w, fc1_w, fc2_w,
    skip_b, ln1_g, ln1_b, proj_b, ln2_g, ln2_b, fc1_b, fc2_b,
    cotangent,
):
    _, local, features = inputs.shape
    hidden_units = fc1_w.shape[1]
    n = nd * ns
    row_len = local * ns
    heads = HEADS // ns
    head_cols = heads * HEAD_DIM
    wide = 3 * head_cols
    small = features // n
    scale = HEAD_DIM ** (-0.5)
    hidden_part = hidden_units // nd
    joined_part = 2 * features // nd
    part = features // nd
    places = ns // 2
    dp_at = lax.axis_index("dp")
    seq_at = lax.axis_index("seq")
    core = seq_at % 2
    after = lax.optimization_barrier

    def swap(v, k):
        return lax.ppermute(v, "dp", [(i, i ^ k) for i in range(nd)])

    def other_core(v):
        return lax.ppermute(v, "seq", [(i, i ^ 1) for i in range(ns)])

    def index(v, at, axis=0):
        return lax.dynamic_index_in_dim(v, at, axis, keepdims=False)

    def gather_rows(v):
        return jnp.concatenate([v] + [swap(v, k) for k in range(1, nd)], axis=0)

    def add_blocks(own, low):
        for k in range(1, nd):
            own = own + swap(low[k], k).astype(F32)
        return own

    def low_rows(partial_sums):
        return partial_sums.astype(BF16).reshape(nd, local, features)

    def widen(v):
        v = v.reshape(v.shape[0], v.shape[1] // HEAD_DIM, HEAD_DIM)
        return jnp.pad(v, ((0, 0), (0, 0), (0, WIDE - HEAD_DIM))).reshape(v.shape[0], -1)

    def seq_exchange(v):
        return lax.all_to_all(v, "seq", 0, 0, tiled=True)

    def core_sums(terms):
        terms = terms.reshape((places, 2) + terms.shape[1:])
        given = index(terms, 1 - core, 1).astype(BF16)
        kept = index(terms, core, 1).astype(F32)
        return (kept + other_core(given).astype(F32)).astype(BF16)

    def chip_sums(sums):
        groups = [[i * 2 + c for i in range(places)] for c in range(2)]
        terms = lax.all_to_all(sums, "seq", 0, 0, axis_index_groups=groups, tiled=True)
        return jnp.sum(terms.reshape(sums.shape).astype(F32), axis=0)

    skip_part = lax.all_gather(skip_w, "seq", axis=0, tiled=True)

    own_vectors = (skip_b, ln1_g, ln1_b, proj_b, ln2_g, ln2_b, fc2_b, fc1_b)
    packed = jnp.concatenate(own_vectors)
    own_size = packed.shape[0]
    padded = -(-own_size // 1024) * 1024
    packed = jnp.pad(packed, (0, padded - own_size)).reshape(padded // 128, 128)
    packed = jnp.broadcast_to(packed[None], (n,) + packed.shape)
    vectors = lax.all_to_all(packed, ("dp", "seq"), 0, 0, tiled=True)
    vectors = vectors.reshape(n, padded).astype(F32)

    joined_slices = jnp.stack(
        [
            half[:, at * joined_part : (at + 1) * joined_part]
            for half in (inputs[0], skipped[0])
            for at in range(nd // 2)
        ]
    )
    joined_here = jnp.concatenate(
        [index(joined_slices, dp_at)]
        + [swap(index(joined_slices, dp_at ^ k), k) for k in range(1, nd)],
        axis=0,
    )
    at = lax.broadcasted_iota(jnp.int32, (features, features), 0)
    block, row = at // small, at % small
    row = ((block % nd) ^ dp_at) * part + (block // nd) * small + row
    order = (row == lax.broadcasted_iota(jnp.int32, (features, features), 1)).astype(BF16)
    qkv_out = qkv_w.reshape(small, 3, ns, head_cols).transpose(2, 0, 1, 3).reshape(ns, small, wide)
    segments = segment_of(item_lengths, jnp.arange(row_len, dtype=jnp.int32))
    qkv_out, skip_part, joined_here, vectors = after((qkv_out, skip_part, joined_here, vectors))
    def vector(at):
        return vectors[:, at * small : (at + 1) * small].reshape(features)

    b_skip, g_one, b_one, b_proj, g_two, b_two, b_down = (vector(i) for i in range(7))
    up_bias = lax.dynamic_slice_in_dim(vectors[:, 7 * small : own_size], dp_at * ns, ns, 0)
    up_bias = up_bias.reshape(hidden_part)

    first_terms = dot(joined_here, skip_part)
    first = add_blocks(first_terms[:local], low_rows(first_terms)) + b_skip
    qkv_mine = seq_exchange(qkv_out).reshape(part, wide)
    xhat_one, inverse_one = norm_pieces(first)
    normed_one = (xhat_one * g_one + b_one).astype(BF16)
    normed_one, qkv_mine, own_proj, own_up = after((normed_one, qkv_mine, proj_w, fc1_w))
    normed_one_row = lax.all_gather(normed_one, "seq", axis=0, tiled=True)

    up_slices = jnp.swapaxes(own_up.reshape(small, nd, hidden_part), 0, 1)
    up_slices = jnp.concatenate(
        [index(up_slices, dp_at)] + [swap(index(up_slices, dp_at ^ k), k) for k in range(1, nd)],
        axis=0,
    )
    qkv_mine, up_slices, order = after((qkv_mine, up_slices, order))
    qkv_mine = lax.all_gather(qkv_mine, "dp", axis=0, tiled=True)
    qkv_mine, own_proj = after((qkv_mine, own_proj))
    proj_rows = lax.all_gather(own_proj, "seq", axis=0, tiled=True)
    half = part // 2
    own_half = lax.dynamic_slice_in_dim(proj_rows, core * half, half, 0)
    proj_halves = [swap(own_half, k) for k in range(1, nd)]
    normed_one_row, qkv_mine, qkv_wide, segments, proj_rows = after(
        (normed_one_row, qkv_mine, widen(qkv_mine), segments, proj_rows)
    )
    up_part = lax.all_gather(up_slices, "seq", axis=0, tiled=True)
    triple = dot(normed_one_row, qkv_wide).astype(BF16)
    attended, attended_low, lse = attend(triple, segments, heads, scale)

    def heads_to_tokens(v):
        v = seq_exchange(v.reshape(ns, local, head_cols))
        return jnp.swapaxes(v, 0, 1).reshape(local, features)

    attended_low, grad_out, proj_halves, proj_rows = after(
        (attended_low, cotangent[0], proj_halves, proj_rows)
    )
    w_proj = lax.dynamic_update_slice_in_dim(
        jnp.zeros((features, features), BF16), proj_rows, dp_at * part, 0
    )
    for k in range(1, nd):
        place = (dp_at ^ k) * 2
        here = proj_halves[k - 1]
        there = other_core(here)
        w_proj = lax.dynamic_update_slice_in_dim(w_proj, here, (place + core) * half, 0)
        w_proj = lax.dynamic_update_slice_in_dim(w_proj, there, (place + 1 - core) * half, 0)
    grad_out_rows = gather_rows(grad_out)
    attended_low = heads_to_tokens(attended_low)
    attended_low, grad_out_rows, w_proj, order = after(
        (attended_low, grad_out_rows, w_proj, order)
    )
    own_down, attended_low, up_part = after((fc2_w, attended_low, up_part))
    down_part = lax.all_gather(own_down, "seq", axis=0, tiled=True)
    second = first + dot(attended_low, w_proj) + b_proj
    xhat_two, inverse_two = norm_pieces(second)
    normed_two = (xhat_two * g_two + b_two).astype(BF16)

    normed_two_rows = gather_rows(normed_two)
    up_part = inner(order, up_part).astype(BF16)
    normed_two_rows, up_part, order = after((normed_two_rows, up_part, order))
    hidden, slope = gelu_of_matmul(normed_two_rows, up_part, up_bias)

    fc2_terms = inner(hidden, grad_out_rows).astype(BF16)
    fc2_w_grad = lax.psum_scatter(fc2_terms, "seq", scatter_dimension=0, tiled=True)
    slope, fc2_terms = after((slope, fc2_terms))
    pre_low, up_sums, normed_two_grad, *up_blocks = feed_back(
        grad_out_rows, up_part, down_part, slope, local
    )
    up_blocks = [swap(block, k + 1) for k, block in enumerate(up_blocks)]
    fc1_terms = inner(times_transposed(normed_two_rows, order).astype(BF16), pre_low).astype(BF16)
    for block in up_blocks:
        normed_two_grad = normed_two_grad + block.astype(F32)
    normed_two_grad, fc1_terms = after((normed_two_grad, fc1_terms))
    through_two, ln2_g_grad, ln2_b_grad = norm_back(normed_two_grad, xhat_two, inverse_two, g_two)
    second_grad = grad_out.astype(F32) + through_two
    second_low = second_grad.astype(BF16)
    attended_grad = product_by_group(second_low, w_proj, ns)
    attended_grad, second_late, hidden_late, attended_low, fc1_terms = after(
        (attended_grad, second_low, hidden, attended_low, fc1_terms)
    )
    fc1_terms = lax.psum_scatter(fc1_terms, "seq", scatter_dimension=0, tiled=True)
    attended_grad = seq_exchange(attended_grad).reshape(row_len, head_cols)
    down_sums = dot(hidden_late, down_part)
    attended_slices = jnp.swapaxes(attended_low.reshape(local, nd, part), 0, 1)
    down_blocks = low_rows(down_sums)
    down_blocks = [swap(down_blocks[k], k) for k in range(1, nd)]
    attended_grad, down_blocks[0], second_late, attended_slices = after(
        (attended_grad, down_blocks[0], second_late, attended_slices)
    )
    triple_grad = jnp.concatenate(
        attend_back(triple, attended_grad, attended, lse, segments, heads, scale), axis=1
    )
    one_back = times_transposed(triple_grad, qkv_mine).astype(BF16)
    output = second + down_sums[:local] + b_down
    for block in down_blocks:
        output = output + block.astype(F32)
    output = output.astype(BF16)
    one_back, triple_late, output, second_late, fc1_terms, fc2_w_grad = after(
        (one_back, triple_grad, output, second_late, fc1_terms, fc2_w_grad)
    )
    normed_one_grad = lax.psum_scatter(one_back, "seq", scatter_dimension=0, tiled=True)
    second_rows = gather_rows(second_late)
    qkv_terms = inner(normed_one_row, triple_late).reshape(nd, part, wide)
    qkv_low, second_rows = after((qkv_terms.astype(BF16), second_rows))
    qkv_blocks = [swap(index(qkv_low, dp_at ^ k), k) for k in range(1, nd)]
    attended_rows = jnp.concatenate(
        [index(attended_slices, dp_at)]
        + [swap(index(attended_slices, dp_at ^ k), k) for k in range(1, nd)],
        axis=0,
    )
    proj_terms = inner(attended_rows, second_rows).reshape(ns, small, features)
    proj_sums = core_sums(proj_terms)
    qkv_sum = index(qkv_terms, dp_at)
    for block in qkv_blocks:
        qkv_sum = qkv_sum + block.astype(F32)
    qkv_sum = qkv_sum.astype(BF16).reshape(ns, small, wide)
    normed_one_grad = normed_one_grad.astype(F32)
    through_one, ln1_g_grad, ln1_b_grad = norm_back(normed_one_grad, xhat_one, inverse_one, g_one)
    first_grad = second_grad + through_one
    first_low = first_grad.astype(BF16)
    first_low_rows = gather_rows(first_low)
    proj_w_grad = chip_sums(proj_sums)
    qkv_w_grad = seq_exchange(qkv_sum)
    first_low_rows, first_grad, qkv_w_grad, proj_w_grad = after(
        (first_low_rows, first_grad, qkv_w_grad, proj_w_grad)
    )
    skip_terms = inner(joined_here, first_low_rows).astype(BF16)
    skip_w_grad = lax.psum_scatter(skip_terms, "seq", scatter_dimension=0, tiled=True).astype(F32)
    skip_terms, first_low_rows, first_grad, fc1_terms, qkv_w_grad = after(
        (skip_terms, first_low_rows, first_grad, fc1_terms, qkv_w_grad)
    )
    fc1_terms = fc1_terms.reshape(nd, small, hidden_part)
    fc1_blocks = jnp.stack([fc1_terms[0]] + [swap(fc1_terms[k], k) for k in range(1, nd)])
    vector_grads = jnp.stack(
        [
            jnp.sum(first_grad, axis=0),
            ln1_g_grad,
            ln1_b_grad,
            jnp.sum(second_grad, axis=0),
            ln2_g_grad,
            ln2_b_grad,
            jnp.sum(grad_out.astype(F32), axis=0),
        ]
    )
    vector_grads = jnp.swapaxes(vector_grads.reshape(7, n, small), 0, 1).reshape(n, 7 * small)
    up_grads = up_sums.reshape(ns, hidden_units // n)
    up_grads = lax.dynamic_update_slice_in_dim(
        jnp.zeros((n, hidden_units // n), F32), up_grads, dp_at * ns, 0
    )
    vector_grads = jnp.concatenate([vector_grads, up_grads], axis=1)
    vector_grads = jnp.pad(vector_grads, ((0, 0), (0, padded - own_size)))
    vector_grads = lax.all_to_all(
        vector_grads.reshape(n, padded // 128, 128), ("dp", "seq"), 0, 0, tiled=True
    )
    joined_grad_part = times_transposed(first_low_rows, skip_part).astype(BF16)
    joined_grad_part = joined_grad_part.reshape(nd, local, joined_part)
    away = [joined_grad_part[0]] + [swap(joined_grad_part[k], k) for k in range(1, nd)]
    away = jnp.stack(away)
    joined_grad = jnp.concatenate(
        [index(away, dp_at ^ k) for k in range(nd)], axis=1
    ).astype(F32)
    fc1_w_grad = jnp.concatenate([index(fc1_blocks, dp_at ^ k) for k in range(nd)], axis=1)
    qkv_w_grad = (
        qkv_w_grad.reshape(ns, small, 3, head_cols).transpose(1, 2, 0, 3)
        .reshape(small, 3 * features)
    )
    vector_grads = jnp.sum(vector_grads, axis=0).reshape(padded)
    skip_b_grad, ln1_g_grad, ln1_b_grad, proj_b_grad, ln2_g_grad, ln2_b_grad, fc2_b_grad = (
        vector_grads[i * small : (i + 1) * small] for i in range(7)
    )
    fc1_b_grad = vector_grads[7 * small : own_size]
    return (
        output[None], joined_grad[None, :, :features], joined_grad[None, :, features:],
        skip_w_grad, qkv_w_grad.astype(F32), proj_w_grad,
        fc1_w_grad.astype(F32), fc2_w_grad.astype(F32),
        skip_b_grad, ln1_g_grad, ln1_b_grad, proj_b_grad, ln2_g_grad, ln2_b_grad,
        fc1_b_grad, fc2_b_grad,
    )


def solution(mesh):
    tokens = P("dp", "seq", None)
    matrix = P(("dp", "seq"), None)
    flat = P(("dp", "seq"))
    in_specs = (tokens, tokens, P("dp", None)) + (matrix,) * 5 + (flat,) * 8 + (tokens,)
    out_specs = (tokens,) * 3 + (matrix,) * 5 + (flat,) * 8
    return jax.shard_map(
        partial(on_device, mesh.shape["dp"], mesh.shape["seq"]),
        mesh=mesh, in_specs=in_specs, out_specs=out_specs, check_vma=False,
    )
```

```python
import math
from functools import partial

import jax
import jax.numpy as jnp
from jax import lax
from jax.experimental import pallas as pl
from jax.experimental.pallas import tpu as pltpu
from jax.sharding import PartitionSpec as P

HEADS = 16
HEAD_DIM = 72
EPSILON = 1e-05
NEGATIVE = -1e30
WIDE = 128
F32 = jnp.float32
BF16 = jnp.bfloat16


def norm_pieces(hvals):
    centered = hvals - jnp.mean(hvals, axis=-1, keepdims=True)
    inverse = lax.rsqrt(jnp.mean(centered * centered, axis=-1, keepdims=True) + EPSILON)
    return centered * inverse, inverse


def norm_back(incoming, standardized, inverse, gain):
    scaled = incoming * gain
    passed = inverse * (
        scaled
        - jnp.mean(scaled, axis=-1, keepdims=True)
        - standardized * jnp.mean(scaled * standardized, axis=-1, keepdims=True)
    )
    return passed, jnp.sum(incoming * standardized, axis=0), jnp.sum(incoming, axis=0)


def segment_of(lengths, places):
    running = jnp.zeros((), jnp.int32)
    passed = jnp.zeros(places.shape, jnp.int32)
    for slot in range(lengths.shape[1]):
        running = running + lengths[0, slot]
        passed = passed + (running <= places).astype(jnp.int32)
    return passed


def dot(left, right):
    return jnp.dot(left, right, preferred_element_type=F32)


def inner(left, right):
    return lax.dot_general(left, right, (((0,), (0,)), ((), ())), preferred_element_type=F32)


def times_transposed(left, right):
    return lax.dot_general(left, right, (((1,), (1,)), ((), ())), preferred_element_type=F32)


def side_by_side(parts):
    return jnp.concatenate([part[:, :HEAD_DIM] for part in parts], axis=1)


def attend_kernel(heads, scale, q_ref, k_ref, v_ref, seg_q_ref, seg_k_ref, out_ref, low_ref, lse_ref):
    allowed = seg_q_ref[...] == seg_k_ref[...]
    lane = lax.broadcasted_iota(jnp.int32, (q_ref.shape[0], WIDE), 1)
    logs = jnp.zeros((q_ref.shape[0], WIDE), F32)
    outs = []
    for h in range(heads):
        at = slice(h * WIDE, (h + 1) * WIDE)
        logits = times_transposed(q_ref[:, at], k_ref[:, at]) * scale
        logits = jnp.where(allowed, logits, NEGATIVE)
        top = jnp.max(logits, axis=1, keepdims=True)
        weights = jnp.exp(logits - top)
        total = jnp.sum(weights, axis=1, keepdims=True)
        outs.append(dot(weights.astype(BF16), v_ref[:, at]) / total)
        out_ref[:, at] = outs[h]
        logs = jnp.where(lane == h, top + jnp.log(total), logs)
    lse_ref[...] = jnp.transpose(logs)[:8]
    low_ref[...] = side_by_side(outs).astype(BF16)


def attend(triple, segments, heads, scale):
    rows = triple.shape[0]
    wide = heads * WIDE
    step = 256 if rows % 256 == 0 else rows
    return pl.pallas_call(
        partial(attend_kernel, heads, scale),
        grid=(rows // step,),
        in_specs=[
            pl.BlockSpec((step, wide), lambda i: (i, 0)),
            pl.BlockSpec((rows, wide), lambda i: (0, 1)),
            pl.BlockSpec((rows, wide), lambda i: (0, 2)),
            pl.BlockSpec((step, 1), lambda i: (i, 0)),
            pl.BlockSpec((1, rows), lambda i: (0, 0)),
        ],
        out_specs=[
            pl.BlockSpec((step, wide), lambda i: (i, 0)),
            pl.BlockSpec((step, heads * HEAD_DIM), lambda i: (i, 0)),
            pl.BlockSpec((8, step), lambda i: (0, i)),
        ],
        out_shape=[
            jax.ShapeDtypeStruct((rows, wide), F32),
            jax.ShapeDtypeStruct((rows, heads * HEAD_DIM), BF16),
            jax.ShapeDtypeStruct((8, rows), F32),
        ],
        compiler_params=pltpu.CompilerParams(vmem_limit_bytes=48 * 2**20),
        cost_estimate=pl.CostEstimate(
            flops=8 * rows * rows * wide,
            bytes_accessed=10 * rows * wide,
            transcendentals=heads * rows * rows,
        ),
    )(triple, triple, triple, segments.reshape(rows, 1), segments.reshape(1, rows))


def attend_back_kernel(
    heads, scale, q_ref, k_ref, v_ref, out_grad_ref, out_ref, lse_ref, seg_q_ref, seg_k_ref,
    dq_ref, dkv_ref, sum_ref, grad_ref, delta_ref,
):
    step = pl.program_id(0)

    @pl.when(step == 0)
    def _():
        sum_ref[...] = jnp.zeros_like(sum_ref)
        ones = jnp.ones((8, WIDE), F32)
        for h in range(heads):
            grad = out_grad_ref[...]
            if h > 0:
                grad = pltpu.roll(grad.astype(F32), 2 * WIDE - HEAD_DIM, 1).astype(BF16)
            grad = grad[:, :WIDE]
            at = slice(h * WIDE, (h + 1) * WIDE)
            grad_ref[:, at] = grad
            delta = lax.dot_general(
                ones, grad.astype(F32) * out_ref[:, at], (((1,), (1,)), ((), ())),
                precision=lax.Precision.HIGHEST, preferred_element_type=F32,
            )
            delta_ref[h : h + 1, :] = delta[:1]

    allowed = seg_k_ref[...] == seg_q_ref[...]
    key_grads, value_grads = [], []
    for h in range(heads):
        at = slice(h * WIDE, (h + 1) * WIDE)
        queries, keys, out_grad = q_ref[:, at], k_ref[:, at], grad_ref[:, at]
        logits = times_transposed(keys, queries) * scale - lse_ref[h : h + 1, :]
        probs = jnp.where(allowed, jnp.exp(logits), 0.0)
        prob_grad = times_transposed(v_ref[:, at], out_grad)
        logit_grad = (probs * (prob_grad - delta_ref[h : h + 1, :]) * scale).astype(BF16)
        value_grads.append(dot(probs.astype(BF16), out_grad))
        key_grads.append(dot(logit_grad, queries))
        sum_ref[:, at] += inner(logit_grad, keys)
    dkv_ref[...] = side_by_side(key_grads + value_grads).astype(BF16)

    @pl.when(step == pl.num_programs(0) - 1)
    def _():
        dq_ref[...] = side_by_side(
            [sum_ref[:, h * WIDE : (h + 1) * WIDE] for h in range(heads)]
        ).astype(BF16)


def attend_back(triple, out_grad, out, lse, segments, heads, scale):
    rows = triple.shape[0]
    wide = heads * WIDE
    step = 256 if rows % 256 == 0 else rows
    whole = pl.BlockSpec((rows, wide), lambda i: (0, 0))
    out_grad = jnp.pad(out_grad, ((0, 0), (0, wide - out_grad.shape[1])))
    row = pl.BlockSpec((8, rows), lambda i: (0, 0))
    return pl.pallas_call(
        partial(attend_back_kernel, heads, scale),
        grid=(rows // step,),
        in_specs=[
            whole,
            pl.BlockSpec((step, wide), lambda i: (i, 1)),
            pl.BlockSpec((step, wide), lambda i: (i, 2)),
            whole,
            whole,
            row,
            pl.BlockSpec((1, rows), lambda i: (0, 0)),
            pl.BlockSpec((step, 1), lambda i: (i, 0)),
        ],
        out_specs=[
            pl.BlockSpec((rows, heads * HEAD_DIM), lambda i: (0, 0)),
            pl.BlockSpec((step, 2 * heads * HEAD_DIM), lambda i: (i, 0)),
        ],
        out_shape=[
            jax.ShapeDtypeStruct((rows, heads * HEAD_DIM), BF16),
            jax.ShapeDtypeStruct((rows, 2 * heads * HEAD_DIM), BF16),
        ],
        scratch_shapes=[
            pltpu.VMEM((rows, wide), F32),
            pltpu.VMEM((rows, wide), BF16),
            pltpu.VMEM((8, rows), F32),
        ],
        compiler_params=pltpu.CompilerParams(vmem_limit_bytes=48 * 2**20),
        cost_estimate=pl.CostEstimate(
            flops=20 * rows * rows * wide,
            bytes_accessed=14 * rows * wide,
            transcendentals=heads * rows * rows,
        ),
    )(
        triple, triple, triple, out_grad, out, lse,
        segments.reshape(1, rows), segments.reshape(rows, 1),
    )


def by_group_kernel(x_ref, w_ref, out_ref):
    groups, rows, columns = out_ref.shape
    product = times_transposed(x_ref[...], w_ref[...]).astype(BF16)
    for g in range(groups):
        out_ref[g] = product[:, g * columns : (g + 1) * columns]


def product_by_group(x, w, groups):
    rows, depth = x.shape
    columns = w.shape[0] // groups
    steps = 2
    return pl.pallas_call(
        by_group_kernel,
        grid=(steps,),
        in_specs=[
            pl.BlockSpec((rows, depth), lambda j: (0, 0)),
            pl.BlockSpec((w.shape[0] // steps, depth), lambda j: (j, 0)),
        ],
        out_specs=pl.BlockSpec((groups // steps, rows, columns), lambda j: (j, 0, 0)),
        out_shape=jax.ShapeDtypeStruct((groups, rows, columns), BF16),
        cost_estimate=pl.CostEstimate(
            flops=2 * rows * depth * w.shape[0],
            bytes_accessed=2 * depth * (rows + w.shape[0]) + 2 * rows * w.shape[0],
            transcendentals=0,
        ),
    )(x, w)


def gelu_kernel(rows_at_once, x_ref, up_ref, bias_ref, value_ref, slope_ref):
    for start in range(0, x_ref.shape[0], rows_at_once):
        at = pl.ds(start, rows_at_once)
        pre = dot(x_ref[at, :], up_ref[...]) + bias_ref[...]
        bell = jnp.exp(-0.5 * pre * pre)
        t = 1.0 / (1.0 + (0.3275911 * 0.5**0.5) * jnp.abs(pre))
        tail = 0.5 * 1.061405429
        for c in (-1.453152027, 1.421413741, -0.284496736, 0.254829592):
            tail = tail * t + 0.5 * c
        tail = tail * t * bell
        below = jnp.where(pre < 0.0, tail, 1.0 - tail)
        value_ref[at, :] = (pre * below).astype(BF16)
        slope_ref[at, :] = below + pre * bell * (0.5 / math.pi) ** 0.5


def gelu_of_matmul(x, up, bias):
    rows, depth = x.shape
    columns = up.shape[1]
    step = 384 if columns % 384 == 0 else columns
    block = pl.BlockSpec((rows, step), lambda j: (0, j))
    return pl.pallas_call(
        partial(gelu_kernel, 640 if rows % 640 == 0 else rows),
        grid=(columns // step,),
        in_specs=[
            pl.BlockSpec((rows, depth), lambda j: (0, 0)),
            pl.BlockSpec((depth, step), lambda j: (0, j)),
            pl.BlockSpec((1, step), lambda j: (0, j)),
        ],
        out_specs=[block, block],
        out_shape=[
            jax.ShapeDtypeStruct((rows, columns), BF16),
            jax.ShapeDtypeStruct((rows, columns), F32),
        ],
        compiler_params=pltpu.CompilerParams(vmem_limit_bytes=40 * 2**20),
        cost_estimate=pl.CostEstimate(
            flops=2 * rows * depth * columns,
            bytes_accessed=2 * depth * (rows + columns) + 6 * rows * columns,
            transcendentals=rows * columns,
        ),
    )(x, up, bias.reshape(1, columns))


def feed_back_kernel(
    local, grad_ref, up_ref, down_ref, slope_ref, low_ref, sums_ref, own_ref, *back_refs
):
    pre_grad = times_transposed(grad_ref[...], down_ref[...]) * slope_ref[...]
    sums_ref[...] = jnp.sum(pre_grad, axis=0, keepdims=True)
    low = pre_grad.astype(BF16)
    low_ref[...] = low
    back = times_transposed(low, up_ref[...])
    own_ref[...] = back[:local]
    for k, back_ref in enumerate(back_refs):
        back_ref[...] = back[(k + 1) * local : (k + 2) * local].astype(BF16)


def feed_back(grad, up, down, slope, local):
    rows, depth = grad.shape
    columns = up.shape[1]
    return pl.pallas_call(
        partial(feed_back_kernel, local),
        out_shape=[
            jax.ShapeDtypeStruct((rows, columns), BF16),
            jax.ShapeDtypeStruct((1, columns), F32),
            jax.ShapeDtypeStruct((local, depth), F32),
        ]
        + [jax.ShapeDtypeStruct((local, depth), BF16)] * (rows // local - 1),
        compiler_params=pltpu.CompilerParams(vmem_limit_bytes=52 * 2**20),
        cost_estimate=pl.CostEstimate(
            flops=4 * rows * depth * columns,
            bytes_accessed=4 * depth * columns + 6 * rows * columns + 4 * rows * depth,
            transcendentals=0,
        ),
    )(grad, up, down, slope)


def on_device(
    nd, ns,
    inputs, skipped, item_lengths,
    skip_w, qkv_w, proj_w, fc1_w, fc2_w,
    skip_b, ln1_g, ln1_b, proj_b, ln2_g, ln2_b, fc1_b, fc2_b,
    cotangent,
):
    _, local, features = inputs.shape
    hidden_units = fc1_w.shape[1]
    n = nd * ns
    row_len = local * ns
    heads = HEADS // ns
    head_cols = heads * HEAD_DIM
    wide = 3 * head_cols
    small = features // n
    scale = HEAD_DIM ** (-0.5)
    hidden_part = hidden_units // nd
    joined_part = 2 * features // nd
    part = features // nd
    places = ns // 2
    dp_at = lax.axis_index("dp")
    seq_at = lax.axis_index("seq")
    core = seq_at % 2
    after = lax.optimization_barrier

    def swap(v, k):
        return lax.ppermute(v, "dp", [(i, i ^ k) for i in range(nd)])

    def other_core(v):
        return lax.ppermute(v, "seq", [(i, i ^ 1) for i in range(ns)])

    def index(v, at, axis=0):
        return lax.dynamic_index_in_dim(v, at, axis, keepdims=False)

    def gather_rows(v):
        return jnp.concatenate([v] + [swap(v, k) for k in range(1, nd)], axis=0)

    def add_blocks(own, low):
        for k in range(1, nd):
            own = own + swap(low[k], k).astype(F32)
        return own

    def low_rows(partial_sums):
        return partial_sums.astype(BF16).reshape(nd, local, features)

    def widen(v):
        v = v.reshape(v.shape[0], v.shape[1] // HEAD_DIM, HEAD_DIM)
        return jnp.pad(v, ((0, 0), (0, 0), (0, WIDE - HEAD_DIM))).reshape(v.shape[0], -1)

    def seq_exchange(v):
        return lax.all_to_all(v, "seq", 0, 0, tiled=True)

    def core_sums(terms):
        terms = terms.reshape((places, 2) + terms.shape[1:])
        given = index(terms, 1 - core, 1).astype(BF16)
        kept = index(terms, core, 1).astype(F32)
        return (kept + other_core(given).astype(F32)).astype(BF16)

    def chip_sums(sums):
        groups = [[i * 2 + c for i in range(places)] for c in range(2)]
        terms = lax.all_to_all(sums, "seq", 0, 0, axis_index_groups=groups, tiled=True)
        return jnp.sum(terms.reshape(sums.shape).astype(F32), axis=0)

    skip_part = lax.all_gather(skip_w, "seq", axis=0, tiled=True)

    own_vectors = (skip_b, ln1_g, ln1_b, proj_b, ln2_g, ln2_b, fc2_b, fc1_b)
    packed = jnp.concatenate(own_vectors)
    own_size = packed.shape[0]
    padded = -(-own_size // 1024) * 1024
    packed = jnp.pad(packed, (0, padded - own_size)).reshape(padded // 128, 128)
    packed = jnp.broadcast_to(packed[None], (n,) + packed.shape)
    vectors = lax.all_to_all(packed, ("dp", "seq"), 0, 0, tiled=True)
    vectors = vectors.reshape(n, padded).astype(F32)

    joined_slices = jnp.stack(
        [
            half[:, at * joined_part : (at + 1) * joined_part]
            for half in (inputs[0], skipped[0])
            for at in range(nd // 2)
        ]
    )
    joined_here = jnp.concatenate(
        [index(joined_slices, dp_at)]
        + [swap(index(joined_slices, dp_at ^ k), k) for k in range(1, nd)],
        axis=0,
    )
    at = lax.broadcasted_iota(jnp.int32, (features, features), 0)
    block, row = at // small, at % small
    row = ((block % nd) ^ dp_at) * part + (block // nd) * small + row
    order = (row == lax.broadcasted_iota(jnp.int32, (features, features), 1)).astype(BF16)
    qkv_out = qkv_w.reshape(small, 3, ns, head_cols).transpose(2, 0, 1, 3).reshape(ns, small, wide)
    segments = segment_of(item_lengths, jnp.arange(row_len, dtype=jnp.int32))
    up_slices = jnp.swapaxes(fc1_w.reshape(small, nd, hidden_part), 0, 1)
    up_slices = jnp.concatenate(
        [index(up_slices, dp_at)] + [swap(index(up_slices, dp_at ^ k), k) for k in range(1, nd)],
        axis=0,
    )
    joined_here, grad_out = after((joined_here, cotangent[0]))
    grad_out_rows = gather_rows(grad_out)
    qkv_out, skip_part, joined_here, vectors, up_slices, grad_out_rows = after(
        (qkv_out, skip_part, joined_here, vectors, up_slices, grad_out_rows)
    )
    def vector(at):
        return vectors[:, at * small : (at + 1) * small].reshape(features)

    b_skip, g_one, b_one, b_proj, g_two, b_two, b_down = (vector(i) for i in range(7))
    up_bias = lax.dynamic_slice_in_dim(vectors[:, 7 * small : own_size], dp_at * ns, ns, 0)
    up_bias = up_bias.reshape(hidden_part)

    first_terms = dot(joined_here, skip_part)
    first = add_blocks(first_terms[:local], low_rows(first_terms)) + b_skip
    qkv_mine = seq_exchange(qkv_out).reshape(part, wide)
    xhat_one, inverse_one = norm_pieces(first)
    normed_one = (xhat_one * g_one + b_one).astype(BF16)
    normed_one, qkv_mine, own_proj = after((normed_one, qkv_mine, proj_w))
    normed_one_row = lax.all_gather(normed_one, "seq", axis=0, tiled=True)

    qkv_mine, order = after((qkv_mine, order))
    qkv_mine = lax.all_gather(qkv_mine, "dp", axis=0, tiled=True)
    qkv_mine, own_proj = after((qkv_mine, own_proj))
    proj_rows = lax.all_gather(own_proj, "seq", axis=0, tiled=True)
    half = part // 2
    own_half = lax.dynamic_slice_in_dim(proj_rows, core * half, half, 0)
    proj_halves = [swap(own_half, k) for k in range(1, nd)]
    normed_one_row, qkv_mine, qkv_wide, segments, proj_rows = after(
        (normed_one_row, qkv_mine, widen(qkv_mine), segments, proj_rows)
    )
    up_part = lax.all_gather(up_slices, "seq", axis=0, tiled=True)
    triple = dot(normed_one_row, qkv_wide).astype(BF16)
    attended, attended_low, lse = attend(triple, segments, heads, scale)

    def heads_to_tokens(v):
        v = seq_exchange(v.reshape(ns, local, head_cols))
        return jnp.swapaxes(v, 0, 1).reshape(local, features)

    attended_low, proj_halves, proj_rows = after((attended_low, proj_halves, proj_rows))
    w_proj = lax.dynamic_update_slice_in_dim(
        jnp.zeros((features, features), BF16), proj_rows, dp_at * part, 0
    )
    for k in range(1, nd):
        place = (dp_at ^ k) * 2
        here = proj_halves[k - 1]
        there = other_core(here)
        w_proj = lax.dynamic_update_slice_in_dim(w_proj, here, (place + core) * half, 0)
        w_proj = lax.dynamic_update_slice_in_dim(w_proj, there, (place + 1 - core) * half, 0)
    attended_low = heads_to_tokens(attended_low)
    attended_low, grad_out_rows, w_proj, order = after(
        (attended_low, grad_out_rows, w_proj, order)
    )
    own_down, attended_low, up_part = after((fc2_w, attended_low, up_part))
    down_part = lax.all_gather(own_down, "seq", axis=0, tiled=True)
    second = first + dot(attended_low, w_proj) + b_proj
    xhat_two, inverse_two = norm_pieces(second)
    normed_two = (xhat_two * g_two + b_two).astype(BF16)

    normed_two_rows = gather_rows(normed_two)
    up_part = inner(order, up_part).astype(BF16)
    normed_two_rows, up_part, order = after((normed_two_rows, up_part, order))
    hidden, slope = gelu_of_matmul(normed_two_rows, up_part, up_bias)

    fc2_terms = inner(hidden, grad_out_rows).astype(BF16)
    fc2_w_grad = lax.psum_scatter(fc2_terms, "seq", scatter_dimension=0, tiled=True)
    slope, fc2_terms = after((slope, fc2_terms))
    pre_low, up_sums, normed_two_grad, *up_blocks = feed_back(
        grad_out_rows, up_part, down_part, slope, local
    )
    up_blocks = [swap(block, k + 1) for k, block in enumerate(up_blocks)]
    fc1_terms = inner(times_transposed(normed_two_rows, order).astype(BF16), pre_low).astype(BF16)
    for block in up_blocks:
        normed_two_grad = normed_two_grad + block.astype(F32)
    normed_two_grad, fc1_terms = after((normed_two_grad, fc1_terms))
    through_two, ln2_g_grad, ln2_b_grad = norm_back(normed_two_grad, xhat_two, inverse_two, g_two)
    second_grad = grad_out.astype(F32) + through_two
    second_low = second_grad.astype(BF16)
    attended_grad = product_by_group(second_low, w_proj, ns)
    attended_grad, second_late, hidden_late, attended_low, fc1_terms = after(
        (attended_grad, second_low, hidden, attended_low, fc1_terms)
    )
    fc1_terms = lax.psum_scatter(fc1_terms, "seq", scatter_dimension=0, tiled=True)
    attended_grad = seq_exchange(attended_grad).reshape(row_len, head_cols)
    down_sums = dot(hidden_late, down_part)
    attended_slices = jnp.swapaxes(attended_low.reshape(local, nd, part), 0, 1)
    down_blocks = low_rows(down_sums)
    down_blocks = [swap(down_blocks[k], k) for k in range(1, nd)]
    attended_grad, down_blocks[0], second_late, attended_slices = after(
        (attended_grad, down_blocks[0], second_late, attended_slices)
    )
    triple_grad = jnp.concatenate(
        attend_back(triple, attended_grad, attended, lse, segments, heads, scale), axis=1
    )
    one_back = times_transposed(triple_grad, qkv_mine).astype(BF16)
    output = second + down_sums[:local] + b_down
    for block in down_blocks:
        output = output + block.astype(F32)
    output = output.astype(BF16)
    one_back, triple_late, output, second_late, fc1_terms, fc2_w_grad = after(
        (one_back, triple_grad, output, second_late, fc1_terms, fc2_w_grad)
    )
    normed_one_grad = lax.psum_scatter(one_back, "seq", scatter_dimension=0, tiled=True)
    second_rows = gather_rows(second_late)
    qkv_terms = inner(normed_one_row, triple_late).reshape(nd, part, wide)
    qkv_low, second_rows = after((qkv_terms.astype(BF16), second_rows))
    qkv_blocks = [swap(index(qkv_low, dp_at ^ k), k) for k in range(1, nd)]
    attended_rows = jnp.concatenate(
        [index(attended_slices, dp_at)]
        + [swap(index(attended_slices, dp_at ^ k), k) for k in range(1, nd)],
        axis=0,
    )
    proj_terms = inner(attended_rows, second_rows).reshape(ns, small, features)
    proj_sums = core_sums(proj_terms)
    qkv_sum = index(qkv_terms, dp_at)
    for block in qkv_blocks:
        qkv_sum = qkv_sum + block.astype(F32)
    qkv_sum = qkv_sum.astype(BF16).reshape(ns, small, wide)
    normed_one_grad = normed_one_grad.astype(F32)
    through_one, ln1_g_grad, ln1_b_grad = norm_back(normed_one_grad, xhat_one, inverse_one, g_one)
    first_grad = second_grad + through_one
    first_low = first_grad.astype(BF16)
    first_low_rows = gather_rows(first_low)
    proj_w_grad = chip_sums(proj_sums)
    qkv_w_grad = seq_exchange(qkv_sum)
    first_low_rows, first_grad, qkv_w_grad, proj_w_grad = after(
        (first_low_rows, first_grad, qkv_w_grad, proj_w_grad)
    )
    skip_terms = inner(joined_here, first_low_rows).astype(BF16)
    skip_w_grad = lax.psum_scatter(skip_terms, "seq", scatter_dimension=0, tiled=True).astype(F32)
    skip_terms, first_low_rows, first_grad, fc1_terms, qkv_w_grad = after(
        (skip_terms, first_low_rows, first_grad, fc1_terms, qkv_w_grad)
    )
    fc1_terms = fc1_terms.reshape(nd, small, hidden_part)
    fc1_blocks = jnp.stack([fc1_terms[0]] + [swap(fc1_terms[k], k) for k in range(1, nd)])
    vector_grads = jnp.stack(
        [
            jnp.sum(first_grad, axis=0),
            ln1_g_grad,
            ln1_b_grad,
            jnp.sum(second_grad, axis=0),
            ln2_g_grad,
            ln2_b_grad,
            jnp.sum(grad_out.astype(F32), axis=0),
        ]
    )
    vector_grads = jnp.swapaxes(vector_grads.reshape(7, n, small), 0, 1).reshape(n, 7 * small)
    up_grads = up_sums.reshape(ns, hidden_units // n)
    up_grads = lax.dynamic_update_slice_in_dim(
        jnp.zeros((n, hidden_units // n), F32), up_grads, dp_at * ns, 0
    )
    vector_grads = jnp.concatenate([vector_grads, up_grads], axis=1)
    vector_grads = jnp.pad(vector_grads, ((0, 0), (0, padded - own_size)))
    vector_grads = lax.all_to_all(
        vector_grads.reshape(n, padded // 128, 128), ("dp", "seq"), 0, 0, tiled=True
    )
    joined_grad_part = times_transposed(first_low_rows, skip_part).astype(BF16)
    joined_grad_part = joined_grad_part.reshape(nd, local, joined_part)
    away = [joined_grad_part[0]] + [swap(joined_grad_part[k], k) for k in range(1, nd)]
    away = jnp.stack(away)
    joined_grad = jnp.concatenate(
        [index(away, dp_at ^ k) for k in range(nd)], axis=1
    ).astype(F32)
    fc1_w_grad = jnp.concatenate([index(fc1_blocks, dp_at ^ k) for k in range(nd)], axis=1)
    qkv_w_grad = (
        qkv_w_grad.reshape(ns, small, 3, head_cols).transpose(1, 2, 0, 3)
        .reshape(small, 3 * features)
    )
    vector_grads = jnp.sum(vector_grads, axis=0).reshape(padded)
    skip_b_grad, ln1_g_grad, ln1_b_grad, proj_b_grad, ln2_g_grad, ln2_b_grad, fc2_b_grad = (
        vector_grads[i * small : (i + 1) * small] for i in range(7)
    )
    fc1_b_grad = vector_grads[7 * small : own_size]
    return (
        output[None], joined_grad[None, :, :features], joined_grad[None, :, features:],
        skip_w_grad, qkv_w_grad.astype(F32), proj_w_grad,
        fc1_w_grad.astype(F32), fc2_w_grad.astype(F32),
        skip_b_grad, ln1_g_grad, ln1_b_grad, proj_b_grad, ln2_g_grad, ln2_b_grad,
        fc1_b_grad, fc2_b_grad,
    )


def solution(mesh):
    tokens = P("dp", "seq", None)
    matrix = P(("dp", "seq"), None)
    flat = P(("dp", "seq"))
    in_specs = (tokens, tokens, P("dp", None)) + (matrix,) * 5 + (flat,) * 8 + (tokens,)
    out_specs = (tokens,) * 3 + (matrix,) * 5 + (flat,) * 8
    return jax.shard_map(
        partial(on_device, mesh.shape["dp"], mesh.shape["seq"]),
        mesh=mesh, in_specs=in_specs, out_specs=out_specs, check_vma=False,
    )
```

```python
import math
from functools import partial

import jax
import jax.numpy as jnp
from jax import lax
from jax.experimental import pallas as pl
from jax.experimental.pallas import tpu as pltpu
from jax.sharding import PartitionSpec as P

HEADS = 16
HEAD_DIM = 72
EPSILON = 1e-05
NEGATIVE = -1e30
WIDE = 128
F32 = jnp.float32
BF16 = jnp.bfloat16


def norm_pieces(hvals):
    centered = hvals - jnp.mean(hvals, axis=-1, keepdims=True)
    inverse = lax.rsqrt(jnp.mean(centered * centered, axis=-1, keepdims=True) + EPSILON)
    return centered * inverse, inverse


def norm_back(incoming, standardized, inverse, gain):
    scaled = incoming * gain
    passed = inverse * (
        scaled
        - jnp.mean(scaled, axis=-1, keepdims=True)
        - standardized * jnp.mean(scaled * standardized, axis=-1, keepdims=True)
    )
    return passed, jnp.sum(incoming * standardized, axis=0), jnp.sum(incoming, axis=0)


def segment_of(lengths, places):
    running = jnp.zeros((), jnp.int32)
    passed = jnp.zeros(places.shape, jnp.int32)
    for slot in range(lengths.shape[1]):
        running = running + lengths[0, slot]
        passed = passed + (running <= places).astype(jnp.int32)
    return passed


def dot(left, right):
    return jnp.dot(left, right, preferred_element_type=F32)


def inner(left, right):
    return lax.dot_general(left, right, (((0,), (0,)), ((), ())), preferred_element_type=F32)


def times_transposed(left, right):
    return lax.dot_general(left, right, (((1,), (1,)), ((), ())), preferred_element_type=F32)


def side_by_side(parts):
    return jnp.concatenate([part[:, :HEAD_DIM] for part in parts], axis=1)


def attend_kernel(heads, scale, q_ref, k_ref, v_ref, seg_q_ref, seg_k_ref, out_ref, low_ref, lse_ref):
    allowed = seg_q_ref[...] == seg_k_ref[...]
    lane = lax.broadcasted_iota(jnp.int32, (q_ref.shape[0], WIDE), 1)
    logs = jnp.zeros((q_ref.shape[0], WIDE), F32)
    outs = []
    for h in range(heads):
        at = slice(h * WIDE, (h + 1) * WIDE)
        logits = times_transposed(q_ref[:, at], k_ref[:, at]) * scale
        logits = jnp.where(allowed, logits, NEGATIVE)
        top = jnp.max(logits, axis=1, keepdims=True)
        weights = jnp.exp(logits - top)
        total = jnp.sum(weights, axis=1, keepdims=True)
        outs.append(dot(weights.astype(BF16), v_ref[:, at]) / total)
        out_ref[:, at] = outs[h]
        logs = jnp.where(lane == h, top + jnp.log(total), logs)
    lse_ref[...] = jnp.transpose(logs)[:8]
    low_ref[...] = side_by_side(outs).astype(BF16)


def attend(triple, segments, heads, scale):
    rows = triple.shape[0]
    wide = heads * WIDE
    step = 256 if rows % 256 == 0 else rows
    return pl.pallas_call(
        partial(attend_kernel, heads, scale),
        grid=(rows // step,),
        in_specs=[
            pl.BlockSpec((step, wide), lambda i: (i, 0)),
            pl.BlockSpec((rows, wide), lambda i: (0, 1)),
            pl.BlockSpec((rows, wide), lambda i: (0, 2)),
            pl.BlockSpec((step, 1), lambda i: (i, 0)),
            pl.BlockSpec((1, rows), lambda i: (0, 0)),
        ],
        out_specs=[
            pl.BlockSpec((step, wide), lambda i: (i, 0)),
            pl.BlockSpec((step, heads * HEAD_DIM), lambda i: (i, 0)),
            pl.BlockSpec((8, step), lambda i: (0, i)),
        ],
        out_shape=[
            jax.ShapeDtypeStruct((rows, wide), F32),
            jax.ShapeDtypeStruct((rows, heads * HEAD_DIM), BF16),
            jax.ShapeDtypeStruct((8, rows), F32),
        ],
        compiler_params=pltpu.CompilerParams(vmem_limit_bytes=48 * 2**20),
        cost_estimate=pl.CostEstimate(
            flops=8 * rows * rows * wide,
            bytes_accessed=10 * rows * wide,
            transcendentals=heads * rows * rows,
        ),
    )(triple, triple, triple, segments.reshape(rows, 1), segments.reshape(1, rows))


def attend_back_kernel(
    heads, scale, q_ref, k_ref, v_ref, out_grad_ref, out_ref, lse_ref, seg_q_ref, seg_k_ref,
    dq_ref, dkv_ref, sum_ref, grad_ref, delta_ref,
):
    step = pl.program_id(0)

    @pl.when(step == 0)
    def _():
        sum_ref[...] = jnp.zeros_like(sum_ref)
        ones = jnp.ones((8, WIDE), F32)
        for h in range(heads):
            grad = out_grad_ref[...]
            if h > 0:
                grad = pltpu.roll(grad.astype(F32), 2 * WIDE - HEAD_DIM, 1).astype(BF16)
            grad = grad[:, :WIDE]
            at = slice(h * WIDE, (h + 1) * WIDE)
            grad_ref[:, at] = grad
            delta = lax.dot_general(
                ones, grad.astype(F32) * out_ref[:, at], (((1,), (1,)), ((), ())),
                precision=lax.Precision.HIGHEST, preferred_element_type=F32,
            )
            delta_ref[h : h + 1, :] = delta[:1]

    allowed = seg_k_ref[...] == seg_q_ref[...]
    key_grads, value_grads = [], []
    for h in range(heads):
        at = slice(h * WIDE, (h + 1) * WIDE)
        queries, keys, out_grad = q_ref[:, at], k_ref[:, at], grad_ref[:, at]
        logits = times_transposed(keys, queries) * scale - lse_ref[h : h + 1, :]
        probs = jnp.where(allowed, jnp.exp(logits), 0.0)
        prob_grad = times_transposed(v_ref[:, at], out_grad)
        logit_grad = (probs * (prob_grad - delta_ref[h : h + 1, :]) * scale).astype(BF16)
        value_grads.append(dot(probs.astype(BF16), out_grad))
        key_grads.append(dot(logit_grad, queries))
        sum_ref[:, at] += inner(logit_grad, keys)
    dkv_ref[...] = side_by_side(key_grads + value_grads).astype(BF16)

    @pl.when(step == pl.num_programs(0) - 1)
    def _():
        dq_ref[...] = side_by_side(
            [sum_ref[:, h * WIDE : (h + 1) * WIDE] for h in range(heads)]
        ).astype(BF16)


def attend_back(triple, out_grad, out, lse, segments, heads, scale):
    rows = triple.shape[0]
    wide = heads * WIDE
    step = 256 if rows % 256 == 0 else rows
    whole = pl.BlockSpec((rows, wide), lambda i: (0, 0))
    out_grad = jnp.pad(out_grad, ((0, 0), (0, wide - out_grad.shape[1])))
    row = pl.BlockSpec((8, rows), lambda i: (0, 0))
    return pl.pallas_call(
        partial(attend_back_kernel, heads, scale),
        grid=(rows // step,),
        in_specs=[
            whole,
            pl.BlockSpec((step, wide), lambda i: (i, 1)),
            pl.BlockSpec((step, wide), lambda i: (i, 2)),
            whole,
            whole,
            row,
            pl.BlockSpec((1, rows), lambda i: (0, 0)),
            pl.BlockSpec((step, 1), lambda i: (i, 0)),
        ],
        out_specs=[
            pl.BlockSpec((rows, heads * HEAD_DIM), lambda i: (0, 0)),
            pl.BlockSpec((step, 2 * heads * HEAD_DIM), lambda i: (i, 0)),
        ],
        out_shape=[
            jax.ShapeDtypeStruct((rows, heads * HEAD_DIM), BF16),
            jax.ShapeDtypeStruct((rows, 2 * heads * HEAD_DIM), BF16),
        ],
        scratch_shapes=[
            pltpu.VMEM((rows, wide), F32),
            pltpu.VMEM((rows, wide), BF16),
            pltpu.VMEM((8, rows), F32),
        ],
        compiler_params=pltpu.CompilerParams(vmem_limit_bytes=48 * 2**20),
        cost_estimate=pl.CostEstimate(
            flops=20 * rows * rows * wide,
            bytes_accessed=14 * rows * wide,
            transcendentals=heads * rows * rows,
        ),
    )(
        triple, triple, triple, out_grad, out, lse,
        segments.reshape(1, rows), segments.reshape(rows, 1),
    )


def by_group_kernel(x_ref, w_ref, out_ref):
    groups, rows, columns = out_ref.shape
    product = times_transposed(x_ref[...], w_ref[...]).astype(BF16)
    for g in range(groups):
        out_ref[g] = product[:, g * columns : (g + 1) * columns]


def product_by_group(x, w, groups):
    rows, depth = x.shape
    columns = w.shape[0] // groups
    steps = 2
    return pl.pallas_call(
        by_group_kernel,
        grid=(steps,),
        in_specs=[
            pl.BlockSpec((rows, depth), lambda j: (0, 0)),
            pl.BlockSpec((w.shape[0] // steps, depth), lambda j: (j, 0)),
        ],
        out_specs=pl.BlockSpec((groups // steps, rows, columns), lambda j: (j, 0, 0)),
        out_shape=jax.ShapeDtypeStruct((groups, rows, columns), BF16),
        cost_estimate=pl.CostEstimate(
            flops=2 * rows * depth * w.shape[0],
            bytes_accessed=2 * depth * (rows + w.shape[0]) + 2 * rows * w.shape[0],
            transcendentals=0,
        ),
    )(x, w)


def gelu_kernel(rows_at_once, x_ref, up_ref, bias_ref, value_ref, slope_ref):
    for start in range(0, x_ref.shape[0], rows_at_once):
        at = pl.ds(start, rows_at_once)
        pre = dot(x_ref[at, :], up_ref[...]) + bias_ref[...]
        bell = jnp.exp(-0.5 * pre * pre)
        t = 1.0 / (1.0 + (0.3275911 * 0.5**0.5) * jnp.abs(pre))
        tail = 0.5 * 1.061405429
        for c in (-1.453152027, 1.421413741, -0.284496736, 0.254829592):
            tail = tail * t + 0.5 * c
        tail = tail * t * bell
        below = jnp.where(pre < 0.0, tail, 1.0 - tail)
        value_ref[at, :] = (pre * below).astype(BF16)
        slope_ref[at, :] = below + pre * bell * (0.5 / math.pi) ** 0.5


def gelu_of_matmul(x, up, bias):
    rows, depth = x.shape
    columns = up.shape[1]
    step = 384 if columns % 384 == 0 else columns
    block = pl.BlockSpec((rows, step), lambda j: (0, j))
    return pl.pallas_call(
        partial(gelu_kernel, 640 if rows % 640 == 0 else rows),
        grid=(columns // step,),
        in_specs=[
            pl.BlockSpec((rows, depth), lambda j: (0, 0)),
            pl.BlockSpec((depth, step), lambda j: (0, j)),
            pl.BlockSpec((1, step), lambda j: (0, j)),
        ],
        out_specs=[block, block],
        out_shape=[
            jax.ShapeDtypeStruct((rows, columns), BF16),
            jax.ShapeDtypeStruct((rows, columns), F32),
        ],
        compiler_params=pltpu.CompilerParams(vmem_limit_bytes=40 * 2**20),
        cost_estimate=pl.CostEstimate(
            flops=2 * rows * depth * columns,
            bytes_accessed=2 * depth * (rows + columns) + 6 * rows * columns,
            transcendentals=rows * columns,
        ),
    )(x, up, bias.reshape(1, columns))


def feed_back_kernel(
    local, grad_ref, up_ref, down_ref, slope_ref, low_ref, sums_ref, own_ref, *back_refs
):
    pre_grad = times_transposed(grad_ref[...], down_ref[...]) * slope_ref[...]
    sums_ref[...] = jnp.sum(pre_grad, axis=0, keepdims=True)
    low = pre_grad.astype(BF16)
    low_ref[...] = low
    back = times_transposed(low, up_ref[...])
    own_ref[...] = back[:local]
    for k, back_ref in enumerate(back_refs):
        back_ref[...] = back[(k + 1) * local : (k + 2) * local].astype(BF16)


def feed_back(grad, up, down, slope, local):
    rows, depth = grad.shape
    columns = up.shape[1]
    return pl.pallas_call(
        partial(feed_back_kernel, local),
        out_shape=[
            jax.ShapeDtypeStruct((rows, columns), BF16),
            jax.ShapeDtypeStruct((1, columns), F32),
            jax.ShapeDtypeStruct((local, depth), F32),
        ]
        + [jax.ShapeDtypeStruct((local, depth), BF16)] * (rows // local - 1),
        compiler_params=pltpu.CompilerParams(vmem_limit_bytes=52 * 2**20),
        cost_estimate=pl.CostEstimate(
            flops=4 * rows * depth * columns,
            bytes_accessed=4 * depth * columns + 6 * rows * columns + 4 * rows * depth,
            transcendentals=0,
        ),
    )(grad, up, down, slope)


def on_device(
    nd, ns,
    inputs, skipped, item_lengths,
    skip_w, qkv_w, proj_w, fc1_w, fc2_w,
    skip_b, ln1_g, ln1_b, proj_b, ln2_g, ln2_b, fc1_b, fc2_b,
    cotangent,
):
    _, local, features = inputs.shape
    hidden_units = fc1_w.shape[1]
    n = nd * ns
    row_len = local * ns
    heads = HEADS // ns
    head_cols = heads * HEAD_DIM
    wide = 3 * head_cols
    small = features // n
    scale = HEAD_DIM ** (-0.5)
    hidden_part = hidden_units // nd
    joined_part = 2 * features // nd
    part = features // nd
    places = ns // 2
    dp_at = lax.axis_index("dp")
    seq_at = lax.axis_index("seq")
    core = seq_at % 2
    after = lax.optimization_barrier

    def swap(v, k):
        return lax.ppermute(v, "dp", [(i, i ^ k) for i in range(nd)])

    def other_core(v):
        return lax.ppermute(v, "seq", [(i, i ^ 1) for i in range(ns)])

    def index(v, at, axis=0):
        return lax.dynamic_index_in_dim(v, at, axis, keepdims=False)

    def gather_rows(v):
        return jnp.concatenate([v] + [swap(v, k) for k in range(1, nd)], axis=0)

    def add_blocks(own, low):
        for k in range(1, nd):
            own = own + swap(low[k], k).astype(F32)
        return own

    def low_rows(partial_sums):
        return partial_sums.astype(BF16).reshape(nd, local, features)

    def widen(v):
        v = v.reshape(v.shape[0], v.shape[1] // HEAD_DIM, HEAD_DIM)
        return jnp.pad(v, ((0, 0), (0, 0), (0, WIDE - HEAD_DIM))).reshape(v.shape[0], -1)

    def seq_exchange(v):
        return lax.all_to_all(v, "seq", 0, 0, tiled=True)

    def core_sums(terms):
        terms = terms.reshape((places, 2) + terms.shape[1:])
        given = index(terms, 1 - core, 1).astype(BF16)
        kept = index(terms, core, 1).astype(F32)
        return (kept + other_core(given).astype(F32)).astype(BF16)

    def chip_sums(sums):
        groups = [[i * 2 + c for i in range(places)] for c in range(2)]
        terms = lax.all_to_all(sums, "seq", 0, 0, axis_index_groups=groups, tiled=True)
        return jnp.sum(terms.reshape(sums.shape).astype(F32), axis=0)

    skip_part = lax.all_gather(skip_w, "seq", axis=0, tiled=True)

    own_vectors = (skip_b, ln1_g, ln1_b, proj_b, ln2_g, ln2_b, fc2_b, fc1_b)
    packed = jnp.concatenate(own_vectors)
    own_size = packed.shape[0]
    padded = -(-own_size // 1024) * 1024
    packed = jnp.pad(packed, (0, padded - own_size)).reshape(padded // 128, 128)
    packed = jnp.broadcast_to(packed[None], (n,) + packed.shape)
    vectors = lax.all_to_all(packed, ("dp", "seq"), 0, 0, tiled=True)
    vectors = vectors.reshape(n, padded).astype(F32)

    joined_slices = jnp.stack(
        [
            half[:, at * joined_part : (at + 1) * joined_part]
            for half in (inputs[0], skipped[0])
            for at in range(nd // 2)
        ]
    )
    joined_here = jnp.concatenate(
        [index(joined_slices, dp_at)]
        + [swap(index(joined_slices, dp_at ^ k), k) for k in range(1, nd)],
        axis=0,
    )
    at = lax.broadcasted_iota(jnp.int32, (features, features), 0)
    block, row = at // small, at % small
    row = ((block % nd) ^ dp_at) * part + (block // nd) * small + row
    order = (row == lax.broadcasted_iota(jnp.int32, (features, features), 1)).astype(BF16)
    qkv_out = qkv_w.reshape(small, 3, ns, head_cols).transpose(2, 0, 1, 3).reshape(ns, small, wide)
    segments = segment_of(item_lengths, jnp.arange(row_len, dtype=jnp.int32))
    up_slices = jnp.swapaxes(fc1_w.reshape(small, nd, hidden_part), 0, 1)
    up_slices = jnp.concatenate(
        [index(up_slices, dp_at)] + [swap(index(up_slices, dp_at ^ k), k) for k in range(1, nd)],
        axis=0,
    )
    qkv_out, skip_part, joined_here, vectors, up_slices = after(
        (qkv_out, skip_part, joined_here, vectors, up_slices)
    )
    def vector(at):
        return vectors[:, at * small : (at + 1) * small].reshape(features)

    b_skip, g_one, b_one, b_proj, g_two, b_two, b_down = (vector(i) for i in range(7))
    up_bias = lax.dynamic_slice_in_dim(vectors[:, 7 * small : own_size], dp_at * ns, ns, 0)
    up_bias = up_bias.reshape(hidden_part)

    first_terms = dot(joined_here, skip_part)
    first = add_blocks(first_terms[:local], low_rows(first_terms)) + b_skip
    qkv_mine = seq_exchange(qkv_out).reshape(part, wide)
    xhat_one, inverse_one = norm_pieces(first)
    normed_one = (xhat_one * g_one + b_one).astype(BF16)
    normed_one, qkv_mine, own_proj = after((normed_one, qkv_mine, proj_w))
    normed_one_row = lax.all_gather(normed_one, "seq", axis=0, tiled=True)

    qkv_mine, order = after((qkv_mine, order))
    qkv_mine = lax.all_gather(qkv_mine, "dp", axis=0, tiled=True)
    qkv_mine, own_proj = after((qkv_mine, own_proj))
    proj_rows = lax.all_gather(own_proj, "seq", axis=0, tiled=True)
    half = part // 2
    own_half = lax.dynamic_slice_in_dim(proj_rows, core * half, half, 0)
    proj_halves = [swap(own_half, k) for k in range(1, nd)]
    normed_one_row, qkv_mine, qkv_wide, segments, proj_rows = after(
        (normed_one_row, qkv_mine, widen(qkv_mine), segments, proj_rows)
    )
    up_part = lax.all_gather(up_slices, "seq", axis=0, tiled=True)
    triple = dot(normed_one_row, qkv_wide).astype(BF16)
    attended, attended_low, lse = attend(triple, segments, heads, scale)

    def heads_to_tokens(v):
        v = seq_exchange(v.reshape(ns, local, head_cols))
        return jnp.swapaxes(v, 0, 1).reshape(local, features)

    attended_low, grad_out, proj_halves, proj_rows = after(
        (attended_low, cotangent[0], proj_halves, proj_rows)
    )
    w_proj = lax.dynamic_update_slice_in_dim(
        jnp.zeros((features, features), BF16), proj_rows, dp_at * part, 0
    )
    for k in range(1, nd):
        place = (dp_at ^ k) * 2
        here = proj_halves[k - 1]
        there = other_core(here)
        w_proj = lax.dynamic_update_slice_in_dim(w_proj, here, (place + core) * half, 0)
        w_proj = lax.dynamic_update_slice_in_dim(w_proj, there, (place + 1 - core) * half, 0)
    grad_out_rows = gather_rows(grad_out)
    attended_low = heads_to_tokens(attended_low)
    attended_low, grad_out_rows, w_proj, order = after(
        (attended_low, grad_out_rows, w_proj, order)
    )
    own_down, attended_low, up_part = after((fc2_w, attended_low, up_part))
    down_part = lax.all_gather(own_down, "seq", axis=0, tiled=True)
    second = first + dot(attended_low, w_proj) + b_proj
    xhat_two, inverse_two = norm_pieces(second)
    normed_two = (xhat_two * g_two + b_two).astype(BF16)

    normed_two_rows = gather_rows(normed_two)
    up_part = inner(order, up_part).astype(BF16)
    normed_two_rows, up_part, order = after((normed_two_rows, up_part, order))
    hidden, slope = gelu_of_matmul(normed_two_rows, up_part, up_bias)

    fc2_terms = inner(hidden, grad_out_rows).astype(BF16)
    fc2_w_grad = lax.psum_scatter(fc2_terms, "seq", scatter_dimension=0, tiled=True)
    slope, fc2_terms = after((slope, fc2_terms))
    pre_low, up_sums, normed_two_grad, *up_blocks = feed_back(
        grad_out_rows, up_part, down_part, slope, local
    )
    up_blocks = [swap(block, k + 1) for k, block in enumerate(up_blocks)]
    fc1_terms = inner(times_transposed(normed_two_rows, order).astype(BF16), pre_low).astype(BF16)
    for block in up_blocks:
        normed_two_grad = normed_two_grad + block.astype(F32)
    normed_two_grad, fc1_terms = after((normed_two_grad, fc1_terms))
    through_two, ln2_g_grad, ln2_b_grad = norm_back(normed_two_grad, xhat_two, inverse_two, g_two)
    second_grad = grad_out.astype(F32) + through_two
    second_low = second_grad.astype(BF16)
    attended_grad = product_by_group(second_low, w_proj, ns)
    attended_grad, second_late, hidden_late, attended_low, fc1_terms = after(
        (attended_grad, second_low, hidden, attended_low, fc1_terms)
    )
    fc1_terms = lax.psum_scatter(fc1_terms, "seq", scatter_dimension=0, tiled=True)
    attended_grad = seq_exchange(attended_grad).reshape(row_len, head_cols)
    down_sums = dot(hidden_late, down_part)
    attended_slices = jnp.swapaxes(attended_low.reshape(local, nd, part), 0, 1)
    down_blocks = low_rows(down_sums)
    down_blocks = [swap(down_blocks[k], k) for k in range(1, nd)]
    attended_grad, down_blocks[0], second_late, attended_slices = after(
        (attended_grad, down_blocks[0], second_late, attended_slices)
    )
    triple_grad = jnp.concatenate(
        attend_back(triple, attended_grad, attended, lse, segments, heads, scale), axis=1
    )
    one_back = times_transposed(triple_grad, qkv_mine).astype(BF16)
    output = second + down_sums[:local] + b_down
    for block in down_blocks:
        output = output + block.astype(F32)
    output = output.astype(BF16)
    one_back, triple_late, output, second_late, fc1_terms, fc2_w_grad = after(
        (one_back, triple_grad, output, second_late, fc1_terms, fc2_w_grad)
    )
    normed_one_grad = lax.psum_scatter(one_back, "seq", scatter_dimension=0, tiled=True)
    second_rows = gather_rows(second_late)
    qkv_terms = inner(normed_one_row, triple_late).reshape(nd, part, wide)
    qkv_low, second_rows = after((qkv_terms.astype(BF16), second_rows))
    qkv_blocks = [swap(index(qkv_low, dp_at ^ k), k) for k in range(1, nd)]
    attended_rows = jnp.concatenate(
        [index(attended_slices, dp_at)]
        + [swap(index(attended_slices, dp_at ^ k), k) for k in range(1, nd)],
        axis=0,
    )
    proj_terms = inner(attended_rows, second_rows).reshape(ns, small, features)
    proj_sums = core_sums(proj_terms)
    qkv_sum = index(qkv_terms, dp_at)
    for block in qkv_blocks:
        qkv_sum = qkv_sum + block.astype(F32)
    qkv_sum = qkv_sum.astype(BF16).reshape(ns, small, wide)
    normed_one_grad = normed_one_grad.astype(F32)
    through_one, ln1_g_grad, ln1_b_grad = norm_back(normed_one_grad, xhat_one, inverse_one, g_one)
    first_grad = second_grad + through_one
    first_low = first_grad.astype(BF16)
    first_low_rows = gather_rows(first_low)
    proj_w_grad = chip_sums(proj_sums)
    qkv_w_grad = seq_exchange(qkv_sum)
    first_low_rows, first_grad, qkv_w_grad, proj_w_grad = after(
        (first_low_rows, first_grad, qkv_w_grad, proj_w_grad)
    )
    skip_terms = inner(joined_here, first_low_rows).astype(BF16)
    skip_w_grad = lax.psum_scatter(skip_terms, "seq", scatter_dimension=0, tiled=True).astype(F32)
    skip_terms, first_low_rows, first_grad, fc1_terms, qkv_w_grad = after(
        (skip_terms, first_low_rows, first_grad, fc1_terms, qkv_w_grad)
    )
    fc1_terms = fc1_terms.reshape(nd, small, hidden_part)
    fc1_blocks = jnp.stack([fc1_terms[0]] + [swap(fc1_terms[k], k) for k in range(1, nd)])
    vector_grads = jnp.stack(
        [
            jnp.sum(first_grad, axis=0),
            ln1_g_grad,
            ln1_b_grad,
            jnp.sum(second_grad, axis=0),
            ln2_g_grad,
            ln2_b_grad,
            jnp.sum(grad_out.astype(F32), axis=0),
        ]
    )
    vector_grads = jnp.swapaxes(vector_grads.reshape(7, n, small), 0, 1).reshape(n, 7 * small)
    up_grads = up_sums.reshape(ns, hidden_units // n)
    up_grads = lax.dynamic_update_slice_in_dim(
        jnp.zeros((n, hidden_units // n), F32), up_grads, dp_at * ns, 0
    )
    vector_grads = jnp.concatenate([vector_grads, up_grads], axis=1)
    vector_grads = jnp.pad(vector_grads, ((0, 0), (0, padded - own_size)))
    vector_grads = lax.all_to_all(
        vector_grads.reshape(n, padded // 128, 128), ("dp", "seq"), 0, 0, tiled=True
    )
    joined_grad_part = times_transposed(first_low_rows, skip_part).astype(BF16)
    joined_grad_part = joined_grad_part.reshape(nd, local, joined_part)
    away = [joined_grad_part[0]] + [swap(joined_grad_part[k], k) for k in range(1, nd)]
    away = jnp.stack(away)
    joined_grad = jnp.concatenate(
        [index(away, dp_at ^ k) for k in range(nd)], axis=1
    ).astype(F32)
    fc1_w_grad = jnp.concatenate([index(fc1_blocks, dp_at ^ k) for k in range(nd)], axis=1)
    qkv_w_grad = (
        qkv_w_grad.reshape(ns, small, 3, head_cols).transpose(1, 2, 0, 3)
        .reshape(small, 3 * features)
    )
    vector_grads = jnp.sum(vector_grads, axis=0).reshape(padded)
    skip_b_grad, ln1_g_grad, ln1_b_grad, proj_b_grad, ln2_g_grad, ln2_b_grad, fc2_b_grad = (
        vector_grads[i * small : (i + 1) * small] for i in range(7)
    )
    fc1_b_grad = vector_grads[7 * small : own_size]
    return (
        output[None], joined_grad[None, :, :features], joined_grad[None, :, features:],
        skip_w_grad, qkv_w_grad.astype(F32), proj_w_grad,
        fc1_w_grad.astype(F32), fc2_w_grad.astype(F32),
        skip_b_grad, ln1_g_grad, ln1_b_grad, proj_b_grad, ln2_g_grad, ln2_b_grad,
        fc1_b_grad, fc2_b_grad,
    )


def solution(mesh):
    tokens = P("dp", "seq", None)
    matrix = P(("dp", "seq"), None)
    flat = P(("dp", "seq"))
    in_specs = (tokens, tokens, P("dp", None)) + (matrix,) * 5 + (flat,) * 8 + (tokens,)
    out_specs = (tokens,) * 3 + (matrix,) * 5 + (flat,) * 8
    return jax.shard_map(
        partial(on_device, mesh.shape["dp"], mesh.shape["seq"]),
        mesh=mesh, in_specs=in_specs, out_specs=out_specs, check_vma=False,
    )
```

```python
import math
from functools import partial

import jax
import jax.numpy as jnp
from jax import lax
from jax.experimental import pallas as pl
from jax.experimental.pallas import tpu as pltpu
from jax.sharding import PartitionSpec as P

HEADS = 16
HEAD_DIM = 72
EPSILON = 1e-05
NEGATIVE = -1e30
WIDE = 128
F32 = jnp.float32
BF16 = jnp.bfloat16


def norm_pieces(hvals):
    centered = hvals - jnp.mean(hvals, axis=-1, keepdims=True)
    inverse = lax.rsqrt(jnp.mean(centered * centered, axis=-1, keepdims=True) + EPSILON)
    return centered * inverse, inverse


def norm_back(incoming, standardized, inverse, gain):
    scaled = incoming * gain
    passed = inverse * (
        scaled
        - jnp.mean(scaled, axis=-1, keepdims=True)
        - standardized * jnp.mean(scaled * standardized, axis=-1, keepdims=True)
    )
    return passed, jnp.sum(incoming * standardized, axis=0), jnp.sum(incoming, axis=0)


def segment_of(lengths_ref, places):
    running = jnp.int32(0)
    passed = jnp.zeros(places.shape, jnp.int32)
    for slot in range(lengths_ref.shape[1]):
        running = running + lengths_ref[0, slot]
        passed = passed + (running <= places).astype(jnp.int32)
    return passed


def same_item(lengths_ref, rows, columns, first_row):
    of_rows = first_row + lax.broadcasted_iota(jnp.int32, (rows, 1), 0)
    of_columns = lax.broadcasted_iota(jnp.int32, (1, columns), 1)
    return segment_of(lengths_ref, of_rows) == segment_of(lengths_ref, of_columns)


def dot(left, right):
    return jnp.dot(left, right, preferred_element_type=F32)


def inner(left, right):
    return lax.dot_general(left, right, (((0,), (0,)), ((), ())), preferred_element_type=F32)


def times_transposed(left, right):
    return lax.dot_general(left, right, (((1,), (1,)), ((), ())), preferred_element_type=F32)


def side_by_side(parts):
    return jnp.concatenate([part[:, :HEAD_DIM] for part in parts], axis=1)


def attend_kernel(
    heads, scale, q_ref, k_ref, v_ref, lengths_ref, out_ref, low_ref, lse_ref
):
    step = q_ref.shape[0]
    allowed = same_item(lengths_ref, step, k_ref.shape[0], pl.program_id(0) * step)
    lane = lax.broadcasted_iota(jnp.int32, (q_ref.shape[0], WIDE), 1)
    logs = jnp.zeros((q_ref.shape[0], WIDE), F32)
    outs = []
    for h in range(heads):
        at = slice(h * WIDE, (h + 1) * WIDE)
        logits = times_transposed(q_ref[:, at], k_ref[:, at]) * scale
        logits = jnp.where(allowed, logits, NEGATIVE)
        top = jnp.max(logits, axis=1, keepdims=True)
        weights = jnp.exp(logits - top)
        total = jnp.sum(weights, axis=1, keepdims=True)
        outs.append(dot(weights.astype(BF16), v_ref[:, at]) / total)
        out_ref[:, at] = outs[h]
        logs = jnp.where(lane == h, top + jnp.log(total), logs)
    lse_ref[...] = jnp.transpose(logs)[:8]
    low_ref[...] = side_by_side(outs).astype(BF16)


def attend(triple, lengths, heads, scale):
    rows = triple.shape[0]
    wide = heads * WIDE
    step = 256 if rows % 256 == 0 else rows
    return pl.pallas_call(
        partial(attend_kernel, heads, scale),
        grid=(rows // step,),
        in_specs=[
            pl.BlockSpec((step, wide), lambda i: (i, 0)),
            pl.BlockSpec((rows, wide), lambda i: (0, 1)),
            pl.BlockSpec((rows, wide), lambda i: (0, 2)),
            pl.BlockSpec(memory_space=pltpu.SMEM),
        ],
        out_specs=[
            pl.BlockSpec((step, wide), lambda i: (i, 0)),
            pl.BlockSpec((step, heads * HEAD_DIM), lambda i: (i, 0)),
            pl.BlockSpec((8, step), lambda i: (0, i)),
        ],
        out_shape=[
            jax.ShapeDtypeStruct((rows, wide), F32),
            jax.ShapeDtypeStruct((rows, heads * HEAD_DIM), BF16),
            jax.ShapeDtypeStruct((8, rows), F32),
        ],
        compiler_params=pltpu.CompilerParams(vmem_limit_bytes=48 * 2**20),
        cost_estimate=pl.CostEstimate(
            flops=8 * rows * rows * wide,
            bytes_accessed=10 * rows * wide,
            transcendentals=heads * rows * rows,
        ),
    )(triple, triple, triple, lengths)


def attend_back_kernel(
    heads, scale, q_ref, k_ref, v_ref, out_grad_ref, out_ref, lse_ref, lengths_ref,
    dq_ref, dkv_ref, sum_ref, grad_ref, delta_ref,
):
    step = pl.program_id(0)

    @pl.when(step == 0)
    def _():
        sum_ref[...] = jnp.zeros_like(sum_ref)
        ones = jnp.ones((8, WIDE), F32)
        for h in range(heads):
            grad = out_grad_ref[...]
            if h > 0:
                grad = pltpu.roll(grad.astype(F32), 2 * WIDE - HEAD_DIM, 1).astype(BF16)
            grad = grad[:, :WIDE]
            at = slice(h * WIDE, (h + 1) * WIDE)
            grad_ref[:, at] = grad
            delta = lax.dot_general(
                ones, grad.astype(F32) * out_ref[:, at], (((1,), (1,)), ((), ())),
                precision=lax.Precision.HIGHEST, preferred_element_type=F32,
            )
            delta_ref[h : h + 1, :] = delta[:1]

    block, rows = k_ref.shape[0], q_ref.shape[0]
    allowed = same_item(lengths_ref, block, rows, step * block)
    key_grads, value_grads = [], []
    for h in range(heads):
        at = slice(h * WIDE, (h + 1) * WIDE)
        queries, keys, out_grad = q_ref[:, at], k_ref[:, at], grad_ref[:, at]
        logits = times_transposed(keys, queries) * scale - lse_ref[h : h + 1, :]
        probs = jnp.where(allowed, jnp.exp(logits), 0.0)
        prob_grad = times_transposed(v_ref[:, at], out_grad)
        logit_grad = (probs * (prob_grad - delta_ref[h : h + 1, :]) * scale).astype(BF16)
        value_grads.append(dot(probs.astype(BF16), out_grad))
        key_grads.append(dot(logit_grad, queries))
        sum_ref[:, at] += inner(logit_grad, keys)
    dkv_ref[...] = side_by_side(key_grads + value_grads).astype(BF16)

    @pl.when(step == pl.num_programs(0) - 1)
    def _():
        dq_ref[...] = side_by_side(
            [sum_ref[:, h * WIDE : (h + 1) * WIDE] for h in range(heads)]
        ).astype(BF16)


def attend_back(triple, out_grad, out, lse, lengths, heads, scale):
    rows = triple.shape[0]
    wide = heads * WIDE
    step = 256 if rows % 256 == 0 else rows
    whole = pl.BlockSpec((rows, wide), lambda i: (0, 0))
    out_grad = jnp.pad(out_grad, ((0, 0), (0, wide - out_grad.shape[1])))
    row = pl.BlockSpec((8, rows), lambda i: (0, 0))
    return pl.pallas_call(
        partial(attend_back_kernel, heads, scale),
        grid=(rows // step,),
        in_specs=[
            whole,
            pl.BlockSpec((step, wide), lambda i: (i, 1)),
            pl.BlockSpec((step, wide), lambda i: (i, 2)),
            whole,
            whole,
            row,
            pl.BlockSpec(memory_space=pltpu.SMEM),
        ],
        out_specs=[
            pl.BlockSpec((rows, heads * HEAD_DIM), lambda i: (0, 0)),
            pl.BlockSpec((step, 2 * heads * HEAD_DIM), lambda i: (i, 0)),
        ],
        out_shape=[
            jax.ShapeDtypeStruct((rows, heads * HEAD_DIM), BF16),
            jax.ShapeDtypeStruct((rows, 2 * heads * HEAD_DIM), BF16),
        ],
        scratch_shapes=[
            pltpu.VMEM((rows, wide), F32),
            pltpu.VMEM((rows, wide), BF16),
            pltpu.VMEM((8, rows), F32),
        ],
        compiler_params=pltpu.CompilerParams(vmem_limit_bytes=48 * 2**20),
        cost_estimate=pl.CostEstimate(
            flops=20 * rows * rows * wide,
            bytes_accessed=14 * rows * wide,
            transcendentals=heads * rows * rows,
        ),
    )(triple, triple, triple, out_grad, out, lse, lengths)


def by_group_kernel(x_ref, w_ref, out_ref):
    groups, rows, columns = out_ref.shape
    product = times_transposed(x_ref[...], w_ref[...]).astype(BF16)
    for g in range(groups):
        out_ref[g] = product[:, g * columns : (g + 1) * columns]


def product_by_group(x, w, groups):
    rows, depth = x.shape
    columns = w.shape[0] // groups
    steps = 2
    return pl.pallas_call(
        by_group_kernel,
        grid=(steps,),
        in_specs=[
            pl.BlockSpec((rows, depth), lambda j: (0, 0)),
            pl.BlockSpec((w.shape[0] // steps, depth), lambda j: (j, 0)),
        ],
        out_specs=pl.BlockSpec((groups // steps, rows, columns), lambda j: (j, 0, 0)),
        out_shape=jax.ShapeDtypeStruct((groups, rows, columns), BF16),
        cost_estimate=pl.CostEstimate(
            flops=2 * rows * depth * w.shape[0],
            bytes_accessed=2 * depth * (rows + w.shape[0]) + 2 * rows * w.shape[0],
            transcendentals=0,
        ),
    )(x, w)


def gelu_kernel(rows_at_once, x_ref, up_ref, bias_ref, value_ref, slope_ref):
    for start in range(0, x_ref.shape[0], rows_at_once):
        at = pl.ds(start, rows_at_once)
        pre = dot(x_ref[at, :], up_ref[...]) + bias_ref[...]
        bell = jnp.exp(-0.5 * pre * pre)
        t = 1.0 / (1.0 + (0.3275911 * 0.5**0.5) * jnp.abs(pre))
        tail = 0.5 * 1.061405429
        for c in (-1.453152027, 1.421413741, -0.284496736, 0.254829592):
            tail = tail * t + 0.5 * c
        tail = tail * t * bell
        below = jnp.where(pre < 0.0, tail, 1.0 - tail)
        value_ref[at, :] = (pre * below).astype(BF16)
        slope_ref[at, :] = below + pre * bell * (0.5 / math.pi) ** 0.5


def gelu_of_matmul(x, up, bias):
    rows, depth = x.shape
    columns = up.shape[1]
    step = 384 if columns % 384 == 0 else columns
    block = pl.BlockSpec((rows, step), lambda j: (0, j))
    return pl.pallas_call(
        partial(gelu_kernel, 640 if rows % 640 == 0 else rows),
        grid=(columns // step,),
        in_specs=[
            pl.BlockSpec((rows, depth), lambda j: (0, 0)),
            pl.BlockSpec((depth, step), lambda j: (0, j)),
            pl.BlockSpec((1, step), lambda j: (0, j)),
        ],
        out_specs=[block, block],
        out_shape=[
            jax.ShapeDtypeStruct((rows, columns), BF16),
            jax.ShapeDtypeStruct((rows, columns), F32),
        ],
        compiler_params=pltpu.CompilerParams(vmem_limit_bytes=40 * 2**20),
        cost_estimate=pl.CostEstimate(
            flops=2 * rows * depth * columns,
            bytes_accessed=2 * depth * (rows + columns) + 6 * rows * columns,
            transcendentals=rows * columns,
        ),
    )(x, up, bias.reshape(1, columns))


def feed_back_kernel(
    local, grad_ref, up_ref, down_ref, slope_ref, low_ref, sums_ref, own_ref, *back_refs
):
    pre_grad = times_transposed(grad_ref[...], down_ref[...]) * slope_ref[...]
    sums_ref[...] = jnp.sum(pre_grad, axis=0, keepdims=True)
    low = pre_grad.astype(BF16)
    low_ref[...] = low
    back = times_transposed(low, up_ref[...])
    own_ref[...] = back[:local]
    for k, back_ref in enumerate(back_refs):
        back_ref[...] = back[(k + 1) * local : (k + 2) * local].astype(BF16)


def feed_back(grad, up, down, slope, local):
    rows, depth = grad.shape
    columns = up.shape[1]
    return pl.pallas_call(
        partial(feed_back_kernel, local),
        out_shape=[
            jax.ShapeDtypeStruct((rows, columns), BF16),
            jax.ShapeDtypeStruct((1, columns), F32),
            jax.ShapeDtypeStruct((local, depth), F32),
        ]
        + [jax.ShapeDtypeStruct((local, depth), BF16)] * (rows // local - 1),
        compiler_params=pltpu.CompilerParams(vmem_limit_bytes=52 * 2**20),
        cost_estimate=pl.CostEstimate(
            flops=4 * rows * depth * columns,
            bytes_accessed=4 * depth * columns + 6 * rows * columns + 4 * rows * depth,
            transcendentals=0,
        ),
    )(grad, up, down, slope)


def on_device(
    nd, ns,
    inputs, skipped, item_lengths,
    skip_w, qkv_w, proj_w, fc1_w, fc2_w,
    skip_b, ln1_g, ln1_b, proj_b, ln2_g, ln2_b, fc1_b, fc2_b,
    cotangent,
):
    _, local, features = inputs.shape
    hidden_units = fc1_w.shape[1]
    n = nd * ns
    row_len = local * ns
    heads = HEADS // ns
    head_cols = heads * HEAD_DIM
    wide = 3 * head_cols
    small = features // n
    scale = HEAD_DIM ** (-0.5)
    hidden_part = hidden_units // nd
    joined_part = 2 * features // nd
    part = features // nd
    places = ns // 2
    dp_at = lax.axis_index("dp")
    seq_at = lax.axis_index("seq")
    core = seq_at % 2
    after = lax.optimization_barrier

    def swap(v, k):
        return lax.ppermute(v, "dp", [(i, i ^ k) for i in range(nd)])

    def other_core(v):
        return lax.ppermute(v, "seq", [(i, i ^ 1) for i in range(ns)])

    def index(v, at, axis=0):
        return lax.dynamic_index_in_dim(v, at, axis, keepdims=False)

    def gather_rows(v):
        return jnp.concatenate([v] + [swap(v, k) for k in range(1, nd)], axis=0)

    def add_blocks(own, low):
        for k in range(1, nd):
            own = own + swap(low[k], k).astype(F32)
        return own

    def low_rows(partial_sums):
        return partial_sums.astype(BF16).reshape(nd, local, features)

    def widen(v):
        v = v.reshape(v.shape[0], v.shape[1] // HEAD_DIM, HEAD_DIM)
        return jnp.pad(v, ((0, 0), (0, 0), (0, WIDE - HEAD_DIM))).reshape(v.shape[0], -1)

    def seq_exchange(v):
        return lax.all_to_all(v, "seq", 0, 0, tiled=True)

    def core_sums(terms):
        terms = terms.reshape((places, 2) + terms.shape[1:])
        given = index(terms, 1 - core, 1).astype(BF16)
        kept = index(terms, core, 1).astype(F32)
        return (kept + other_core(given).astype(F32)).astype(BF16)

    def chip_sums(sums):
        groups = [[i * 2 + c for i in range(places)] for c in range(2)]
        terms = lax.all_to_all(sums, "seq", 0, 0, axis_index_groups=groups, tiled=True)
        return jnp.sum(terms.reshape(sums.shape).astype(F32), axis=0)

    skip_part = lax.all_gather(skip_w, "seq", axis=0, tiled=True)

    own_vectors = (skip_b, ln1_g, ln1_b, proj_b, ln2_g, ln2_b, fc2_b, fc1_b)
    packed = jnp.concatenate(own_vectors)
    own_size = packed.shape[0]
    padded = -(-own_size // 1024) * 1024
    packed = jnp.pad(packed, (0, padded - own_size)).reshape(padded // 128, 128)
    packed = jnp.broadcast_to(packed[None], (n,) + packed.shape)
    vectors = lax.all_to_all(packed, ("dp", "seq"), 0, 0, tiled=True)
    vectors = vectors.reshape(n, padded).astype(F32)

    joined_slices = jnp.stack(
        [
            half[:, at * joined_part : (at + 1) * joined_part]
            for half in (inputs[0], skipped[0])
            for at in range(nd // 2)
        ]
    )
    joined_here = jnp.concatenate(
        [index(joined_slices, dp_at)]
        + [swap(index(joined_slices, dp_at ^ k), k) for k in range(1, nd)],
        axis=0,
    )
    at = lax.broadcasted_iota(jnp.int32, (features, features), 0)
    block, row = at // small, at % small
    row = ((block % nd) ^ dp_at) * part + (block // nd) * small + row
    order = (row == lax.broadcasted_iota(jnp.int32, (features, features), 1)).astype(BF16)
    qkv_out = qkv_w.reshape(small, 3, ns, head_cols).transpose(2, 0, 1, 3).reshape(ns, small, wide)
    up_slices = jnp.swapaxes(fc1_w.reshape(small, nd, hidden_part), 0, 1)
    up_slices = jnp.concatenate(
        [index(up_slices, dp_at)] + [swap(index(up_slices, dp_at ^ k), k) for k in range(1, nd)],
        axis=0,
    )
    qkv_out, skip_part, joined_here, vectors, up_slices = after(
        (qkv_out, skip_part, joined_here, vectors, up_slices)
    )
    def vector(at):
        return vectors[:, at * small : (at + 1) * small].reshape(features)

    b_skip, g_one, b_one, b_proj, g_two, b_two, b_down = (vector(i) for i in range(7))
    up_bias = lax.dynamic_slice_in_dim(vectors[:, 7 * small : own_size], dp_at * ns, ns, 0)
    up_bias = up_bias.reshape(hidden_part)

    first_terms = dot(joined_here, skip_part)
    first = add_blocks(first_terms[:local], low_rows(first_terms)) + b_skip
    qkv_mine = seq_exchange(qkv_out).reshape(part, wide)
    xhat_one, inverse_one = norm_pieces(first)
    normed_one = (xhat_one * g_one + b_one).astype(BF16)
    normed_one, qkv_mine, own_proj = after((normed_one, qkv_mine, proj_w))
    normed_one_row = lax.all_gather(normed_one, "seq", axis=0, tiled=True)

    qkv_mine = lax.all_gather(qkv_mine, "dp", axis=0, tiled=True)
    qkv_mine, own_proj = after((qkv_mine, own_proj))
    proj_rows = lax.all_gather(own_proj, "seq", axis=0, tiled=True)
    half = part // 2
    own_half = lax.dynamic_slice_in_dim(proj_rows, core * half, half, 0)
    proj_halves = [swap(own_half, k) for k in range(1, nd)]
    normed_one_row, qkv_mine, qkv_wide, proj_rows = after(
        (normed_one_row, qkv_mine, widen(qkv_mine), proj_rows)
    )
    up_part = lax.all_gather(up_slices, "seq", axis=0, tiled=True)
    triple = dot(normed_one_row, qkv_wide).astype(BF16)
    attended, attended_low, lse = attend(triple, item_lengths, heads, scale)

    def heads_to_tokens(v):
        v = seq_exchange(v.reshape(ns, local, head_cols))
        return jnp.swapaxes(v, 0, 1).reshape(local, features)

    attended_low, grad_out, proj_halves, proj_rows = after(
        (attended_low, cotangent[0], proj_halves, proj_rows)
    )
    w_proj = lax.dynamic_update_slice_in_dim(
        jnp.zeros((features, features), BF16), proj_rows, dp_at * part, 0
    )
    for k in range(1, nd):
        place = (dp_at ^ k) * 2
        here = proj_halves[k - 1]
        there = other_core(here)
        w_proj = lax.dynamic_update_slice_in_dim(w_proj, here, (place + core) * half, 0)
        w_proj = lax.dynamic_update_slice_in_dim(w_proj, there, (place + 1 - core) * half, 0)
    grad_out_rows = gather_rows(grad_out)
    attended_low = heads_to_tokens(attended_low)
    attended_low, grad_out_rows, w_proj = after((attended_low, grad_out_rows, w_proj))
    own_down, attended_low, up_part = after((fc2_w, attended_low, up_part))
    down_part = lax.all_gather(own_down, "seq", axis=0, tiled=True)
    second = first + dot(attended_low, w_proj) + b_proj
    xhat_two, inverse_two = norm_pieces(second)
    normed_two = (xhat_two * g_two + b_two).astype(BF16)

    normed_two_rows = gather_rows(normed_two)
    up_part = inner(order, up_part).astype(BF16)
    normed_two_rows, up_part = after((normed_two_rows, up_part))
    hidden, slope = gelu_of_matmul(normed_two_rows, up_part, up_bias)

    fc2_terms = inner(hidden, grad_out_rows).astype(BF16)
    fc2_w_grad = lax.psum_scatter(fc2_terms, "seq", scatter_dimension=0, tiled=True)
    slope, fc2_terms = after((slope, fc2_terms))
    pre_low, up_sums, normed_two_grad, *up_blocks = feed_back(
        grad_out_rows, up_part, down_part, slope, local
    )
    up_blocks = [swap(block, k + 1) for k, block in enumerate(up_blocks)]
    fc1_terms = inner(times_transposed(normed_two_rows, order).astype(BF16), pre_low).astype(BF16)
    for block in up_blocks:
        normed_two_grad = normed_two_grad + block.astype(F32)
    normed_two_grad, fc1_terms = after((normed_two_grad, fc1_terms))
    through_two, ln2_g_grad, ln2_b_grad = norm_back(normed_two_grad, xhat_two, inverse_two, g_two)
    second_grad = grad_out.astype(F32) + through_two
    second_low = second_grad.astype(BF16)
    attended_grad = product_by_group(second_low, w_proj, ns)
    attended_grad, second_late, hidden_late, attended_low, fc1_terms = after(
        (attended_grad, second_low, hidden, attended_low, fc1_terms)
    )
    fc1_terms = lax.psum_scatter(fc1_terms, "seq", scatter_dimension=0, tiled=True)
    attended_grad = seq_exchange(attended_grad).reshape(row_len, head_cols)
    down_sums = dot(hidden_late, down_part)
    attended_slices = jnp.swapaxes(attended_low.reshape(local, nd, part), 0, 1)
    down_blocks = low_rows(down_sums)
    down_blocks = [swap(down_blocks[k], k) for k in range(1, nd)]
    attended_grad, down_blocks[0], second_late, attended_slices = after(
        (attended_grad, down_blocks[0], second_late, attended_slices)
    )
    triple_grad = jnp.concatenate(
        attend_back(triple, attended_grad, attended, lse, item_lengths, heads, scale), axis=1
    )
    one_back = times_transposed(triple_grad, qkv_mine).astype(BF16)
    output = second + down_sums[:local] + b_down
    for block in down_blocks:
        output = output + block.astype(F32)
    output = output.astype(BF16)
    one_back, triple_late, output, second_late, fc1_terms, fc2_w_grad = after(
        (one_back, triple_grad, output, second_late, fc1_terms, fc2_w_grad)
    )
    normed_one_grad = lax.psum_scatter(one_back, "seq", scatter_dimension=0, tiled=True)
    second_rows = gather_rows(second_late)
    qkv_terms = inner(normed_one_row, triple_late).reshape(nd, part, wide)
    qkv_low, second_rows = after((qkv_terms.astype(BF16), second_rows))
    qkv_blocks = [swap(index(qkv_low, dp_at ^ k), k) for k in range(1, nd)]
    attended_rows = jnp.concatenate(
        [index(attended_slices, dp_at)]
        + [swap(index(attended_slices, dp_at ^ k), k) for k in range(1, nd)],
        axis=0,
    )
    proj_terms = inner(attended_rows, second_rows).reshape(ns, small, features)
    proj_sums = core_sums(proj_terms)
    qkv_sum = index(qkv_terms, dp_at)
    for block in qkv_blocks:
        qkv_sum = qkv_sum + block.astype(F32)
    qkv_sum = qkv_sum.astype(BF16).reshape(ns, small, wide)
    normed_one_grad = normed_one_grad.astype(F32)
    through_one, ln1_g_grad, ln1_b_grad = norm_back(normed_one_grad, xhat_one, inverse_one, g_one)
    first_grad = second_grad + through_one
    first_low = first_grad.astype(BF16)
    first_low_rows = gather_rows(first_low)
    proj_w_grad = chip_sums(proj_sums)
    qkv_w_grad = seq_exchange(qkv_sum)
    first_low_rows, first_grad, qkv_w_grad, proj_w_grad = after(
        (first_low_rows, first_grad, qkv_w_grad, proj_w_grad)
    )
    skip_terms = inner(joined_here, first_low_rows).astype(BF16)
    skip_w_grad = lax.psum_scatter(skip_terms, "seq", scatter_dimension=0, tiled=True).astype(F32)
    skip_terms, first_low_rows, first_grad, fc1_terms, qkv_w_grad = after(
        (skip_terms, first_low_rows, first_grad, fc1_terms, qkv_w_grad)
    )
    fc1_terms = fc1_terms.reshape(nd, small, hidden_part)
    fc1_blocks = jnp.stack([fc1_terms[0]] + [swap(fc1_terms[k], k) for k in range(1, nd)])
    vector_grads = jnp.stack(
        [
            jnp.sum(first_grad, axis=0),
            ln1_g_grad,
            ln1_b_grad,
            jnp.sum(second_grad, axis=0),
            ln2_g_grad,
            ln2_b_grad,
            jnp.sum(grad_out.astype(F32), axis=0),
        ]
    )
    vector_grads = jnp.swapaxes(vector_grads.reshape(7, n, small), 0, 1).reshape(n, 7 * small)
    up_grads = up_sums.reshape(ns, hidden_units // n)
    up_grads = lax.dynamic_update_slice_in_dim(
        jnp.zeros((n, hidden_units // n), F32), up_grads, dp_at * ns, 0
    )
    vector_grads = jnp.concatenate([vector_grads, up_grads], axis=1)
    vector_grads = jnp.pad(vector_grads, ((0, 0), (0, padded - own_size)))
    vector_grads = lax.all_to_all(
        vector_grads.reshape(n, padded // 128, 128), ("dp", "seq"), 0, 0, tiled=True
    )
    joined_grad_part = times_transposed(first_low_rows, skip_part).astype(BF16)
    joined_grad_part = joined_grad_part.reshape(nd, local, joined_part)
    away = [joined_grad_part[0]] + [swap(joined_grad_part[k], k) for k in range(1, nd)]
    away = jnp.stack(away)
    joined_grad = jnp.concatenate(
        [index(away, dp_at ^ k) for k in range(nd)], axis=1
    ).astype(F32)
    fc1_w_grad = jnp.concatenate([index(fc1_blocks, dp_at ^ k) for k in range(nd)], axis=1)
    qkv_w_grad = (
        qkv_w_grad.reshape(ns, small, 3, head_cols).transpose(1, 2, 0, 3)
        .reshape(small, 3 * features)
    )
    vector_grads = jnp.sum(vector_grads, axis=0).reshape(padded)
    skip_b_grad, ln1_g_grad, ln1_b_grad, proj_b_grad, ln2_g_grad, ln2_b_grad, fc2_b_grad = (
        vector_grads[i * small : (i + 1) * small] for i in range(7)
    )
    fc1_b_grad = vector_grads[7 * small : own_size]
    return (
        output[None], joined_grad[None, :, :features], joined_grad[None, :, features:],
        skip_w_grad, qkv_w_grad.astype(F32), proj_w_grad,
        fc1_w_grad.astype(F32), fc2_w_grad.astype(F32),
        skip_b_grad, ln1_g_grad, ln1_b_grad, proj_b_grad, ln2_g_grad, ln2_b_grad,
        fc1_b_grad, fc2_b_grad,
    )


def solution(mesh):
    tokens = P("dp", "seq", None)
    matrix = P(("dp", "seq"), None)
    flat = P(("dp", "seq"))
    in_specs = (tokens, tokens, P("dp", None)) + (matrix,) * 5 + (flat,) * 8 + (tokens,)
    out_specs = (tokens,) * 3 + (matrix,) * 5 + (flat,) * 8
    return jax.shard_map(
        partial(on_device, mesh.shape["dp"], mesh.shape["seq"]),
        mesh=mesh, in_specs=in_specs, out_specs=out_specs, check_vma=False,
    )
```

```python
import math
from functools import partial

import jax
import jax.numpy as jnp
from jax import lax
from jax.experimental import pallas as pl
from jax.experimental.pallas import tpu as pltpu
from jax.sharding import PartitionSpec as P

HEADS = 16
HEAD_DIM = 72
EPSILON = 1e-05
NEGATIVE = -1e30
WIDE = 128
F32 = jnp.float32
BF16 = jnp.bfloat16


def norm_pieces(hvals):
    centered = hvals - jnp.mean(hvals, axis=-1, keepdims=True)
    inverse = lax.rsqrt(jnp.mean(centered * centered, axis=-1, keepdims=True) + EPSILON)
    return centered * inverse, inverse


def norm_back(incoming, standardized, inverse, gain):
    scaled = incoming * gain
    passed = inverse * (
        scaled
        - jnp.mean(scaled, axis=-1, keepdims=True)
        - standardized * jnp.mean(scaled * standardized, axis=-1, keepdims=True)
    )
    return passed, jnp.sum(incoming * standardized, axis=0), jnp.sum(incoming, axis=0)


def segment_of(lengths_ref, places):
    running = jnp.int32(0)
    passed = jnp.zeros(places.shape, jnp.int32)
    for slot in range(lengths_ref.shape[1]):
        running = running + lengths_ref[0, slot]
        passed = passed + (running <= places).astype(jnp.int32)
    return passed


def same_item(lengths_ref, rows, columns, first_row):
    of_rows = first_row + lax.broadcasted_iota(jnp.int32, (rows, 1), 0)
    of_columns = lax.broadcasted_iota(jnp.int32, (1, columns), 1)
    return segment_of(lengths_ref, of_rows) == segment_of(lengths_ref, of_columns)


def dot(left, right):
    return jnp.dot(left, right, preferred_element_type=F32)


def inner(left, right):
    return lax.dot_general(left, right, (((0,), (0,)), ((), ())), preferred_element_type=F32)


def times_transposed(left, right):
    return lax.dot_general(left, right, (((1,), (1,)), ((), ())), preferred_element_type=F32)


def side_by_side(parts):
    return jnp.concatenate([part[:, :HEAD_DIM] for part in parts], axis=1)


def attend_kernel(
    heads, scale, q_ref, k_ref, v_ref, lengths_ref, out_ref, low_ref, lse_ref
):
    step = q_ref.shape[0]
    allowed = same_item(lengths_ref, step, k_ref.shape[0], pl.program_id(0) * step)
    lane = lax.broadcasted_iota(jnp.int32, (q_ref.shape[0], WIDE), 1)
    logs = jnp.zeros((q_ref.shape[0], WIDE), F32)
    outs = []
    for h in range(heads):
        at = slice(h * WIDE, (h + 1) * WIDE)
        logits = times_transposed(q_ref[:, at], k_ref[:, at]) * scale
        logits = jnp.where(allowed, logits, NEGATIVE)
        top = jnp.max(logits, axis=1, keepdims=True)
        weights = jnp.exp(logits - top)
        total = jnp.sum(weights, axis=1, keepdims=True)
        outs.append(dot(weights.astype(BF16), v_ref[:, at]) / total)
        out_ref[:, at] = outs[h]
        logs = jnp.where(lane == h, top + jnp.log(total), logs)
    lse_ref[...] = jnp.transpose(logs)[:8]
    low_ref[...] = side_by_side(outs).astype(BF16)


def attend(triple, lengths, heads, scale):
    rows = triple.shape[0]
    wide = heads * WIDE
    step = 256 if rows % 256 == 0 else rows
    return pl.pallas_call(
        partial(attend_kernel, heads, scale),
        grid=(rows // step,),
        in_specs=[
            pl.BlockSpec((step, wide), lambda i: (i, 0)),
            pl.BlockSpec((rows, wide), lambda i: (0, 1)),
            pl.BlockSpec((rows, wide), lambda i: (0, 2)),
            pl.BlockSpec(memory_space=pltpu.SMEM),
        ],
        out_specs=[
            pl.BlockSpec((step, wide), lambda i: (i, 0)),
            pl.BlockSpec((step, heads * HEAD_DIM), lambda i: (i, 0)),
            pl.BlockSpec((8, step), lambda i: (0, i)),
        ],
        out_shape=[
            jax.ShapeDtypeStruct((rows, wide), F32),
            jax.ShapeDtypeStruct((rows, heads * HEAD_DIM), BF16),
            jax.ShapeDtypeStruct((8, rows), F32),
        ],
        compiler_params=pltpu.CompilerParams(vmem_limit_bytes=48 * 2**20),
        cost_estimate=pl.CostEstimate(
            flops=8 * rows * rows * wide,
            bytes_accessed=10 * rows * wide,
            transcendentals=heads * rows * rows,
        ),
    )(triple, triple, triple, lengths)


def attend_back_kernel(
    heads, scale, q_ref, k_ref, v_ref, out_grad_ref, out_ref, lse_ref, lengths_ref,
    dq_ref, dkv_ref, sum_ref, grad_ref, delta_ref,
):
    step = pl.program_id(0)

    @pl.when(step == 0)
    def _():
        sum_ref[...] = jnp.zeros_like(sum_ref)
        ones = jnp.ones((8, WIDE), F32)
        for h in range(heads):
            grad = out_grad_ref[:, h * HEAD_DIM : (h + 1) * HEAD_DIM]
            gap = jnp.zeros((grad.shape[0], WIDE - HEAD_DIM), BF16)
            grad = jnp.concatenate([grad, gap], axis=1)
            at = slice(h * WIDE, (h + 1) * WIDE)
            grad_ref[:, at] = grad
            delta = lax.dot_general(
                ones, grad.astype(F32) * out_ref[:, at], (((1,), (1,)), ((), ())),
                precision=lax.Precision.HIGHEST, preferred_element_type=F32,
            )
            delta_ref[h : h + 1, :] = delta[:1]

    block, rows = k_ref.shape[0], q_ref.shape[0]
    allowed = same_item(lengths_ref, block, rows, step * block)
    key_grads, value_grads = [], []
    for h in range(heads):
        at = slice(h * WIDE, (h + 1) * WIDE)
        queries, keys, out_grad = q_ref[:, at], k_ref[:, at], grad_ref[:, at]
        logits = times_transposed(keys, queries) * scale - lse_ref[h : h + 1, :]
        probs = jnp.where(allowed, jnp.exp(logits), 0.0)
        prob_grad = times_transposed(v_ref[:, at], out_grad)
        logit_grad = (probs * (prob_grad - delta_ref[h : h + 1, :]) * scale).astype(BF16)
        value_grads.append(dot(probs.astype(BF16), out_grad))
        key_grads.append(dot(logit_grad, queries))
        sum_ref[:, at] += inner(logit_grad, keys)
    dkv_ref[...] = side_by_side(key_grads + value_grads).astype(BF16)

    @pl.when(step == pl.num_programs(0) - 1)
    def _():
        dq_ref[...] = side_by_side(
            [sum_ref[:, h * WIDE : (h + 1) * WIDE] for h in range(heads)]
        ).astype(BF16)


def attend_back(triple, out_grad, out, lse, lengths, heads, scale):
    rows = triple.shape[0]
    wide = heads * WIDE
    step = 256 if rows % 256 == 0 else rows
    whole = pl.BlockSpec((rows, wide), lambda i: (0, 0))
    row = pl.BlockSpec((8, rows), lambda i: (0, 0))
    return pl.pallas_call(
        partial(attend_back_kernel, heads, scale),
        grid=(rows // step,),
        in_specs=[
            whole,
            pl.BlockSpec((step, wide), lambda i: (i, 1)),
            pl.BlockSpec((step, wide), lambda i: (i, 2)),
            pl.BlockSpec((rows, heads * HEAD_DIM), lambda i: (0, 0)),
            whole,
            row,
            pl.BlockSpec(memory_space=pltpu.SMEM),
        ],
        out_specs=[
            pl.BlockSpec((rows, heads * HEAD_DIM), lambda i: (0, 0)),
            pl.BlockSpec((step, 2 * heads * HEAD_DIM), lambda i: (i, 0)),
        ],
        out_shape=[
            jax.ShapeDtypeStruct((rows, heads * HEAD_DIM), BF16),
            jax.ShapeDtypeStruct((rows, 2 * heads * HEAD_DIM), BF16),
        ],
        scratch_shapes=[
            pltpu.VMEM((rows, wide), F32),
            pltpu.VMEM((rows, wide), BF16),
            pltpu.VMEM((8, rows), F32),
        ],
        compiler_params=pltpu.CompilerParams(vmem_limit_bytes=48 * 2**20),
        cost_estimate=pl.CostEstimate(
            flops=20 * rows * rows * wide,
            bytes_accessed=14 * rows * wide,
            transcendentals=heads * rows * rows,
        ),
    )(triple, triple, triple, out_grad, out, lse, lengths)


def by_group_kernel(x_ref, w_ref, out_ref):
    groups, rows, columns = out_ref.shape
    product = times_transposed(x_ref[...], w_ref[...]).astype(BF16)
    for g in range(groups):
        out_ref[g] = product[:, g * columns : (g + 1) * columns]


def product_by_group(x, w, groups):
    rows, depth = x.shape
    columns = w.shape[0] // groups
    steps = 2
    return pl.pallas_call(
        by_group_kernel,
        grid=(steps,),
        in_specs=[
            pl.BlockSpec((rows, depth), lambda j: (0, 0)),
            pl.BlockSpec((w.shape[0] // steps, depth), lambda j: (j, 0)),
        ],
        out_specs=pl.BlockSpec((groups // steps, rows, columns), lambda j: (j, 0, 0)),
        out_shape=jax.ShapeDtypeStruct((groups, rows, columns), BF16),
        cost_estimate=pl.CostEstimate(
            flops=2 * rows * depth * w.shape[0],
            bytes_accessed=2 * depth * (rows + w.shape[0]) + 2 * rows * w.shape[0],
            transcendentals=0,
        ),
    )(x, w)


def gelu_kernel(rows_at_once, x_ref, up_ref, bias_ref, value_ref, slope_ref):
    for start in range(0, x_ref.shape[0], rows_at_once):
        at = pl.ds(start, rows_at_once)
        pre = dot(x_ref[at, :], up_ref[...]) + bias_ref[...]
        bell = jnp.exp(-0.5 * pre * pre)
        t = 1.0 / (1.0 + (0.3275911 * 0.5**0.5) * jnp.abs(pre))
        tail = 0.5 * 1.061405429
        for c in (-1.453152027, 1.421413741, -0.284496736, 0.254829592):
            tail = tail * t + 0.5 * c
        tail = tail * t * bell
        below = jnp.where(pre < 0.0, tail, 1.0 - tail)
        value_ref[at, :] = (pre * below).astype(BF16)
        slope_ref[at, :] = below + pre * bell * (0.5 / math.pi) ** 0.5


def gelu_of_matmul(x, up, bias):
    rows, depth = x.shape
    columns = up.shape[1]
    step = 384 if columns % 384 == 0 else columns
    block = pl.BlockSpec((rows, step), lambda j: (0, j))
    return pl.pallas_call(
        partial(gelu_kernel, 640 if rows % 640 == 0 else rows),
        grid=(columns // step,),
        in_specs=[
            pl.BlockSpec((rows, depth), lambda j: (0, 0)),
            pl.BlockSpec((depth, step), lambda j: (0, j)),
            pl.BlockSpec((1, step), lambda j: (0, j)),
        ],
        out_specs=[block, block],
        out_shape=[
            jax.ShapeDtypeStruct((rows, columns), BF16),
            jax.ShapeDtypeStruct((rows, columns), F32),
        ],
        compiler_params=pltpu.CompilerParams(vmem_limit_bytes=40 * 2**20),
        cost_estimate=pl.CostEstimate(
            flops=2 * rows * depth * columns,
            bytes_accessed=2 * depth * (rows + columns) + 6 * rows * columns,
            transcendentals=rows * columns,
        ),
    )(x, up, bias.reshape(1, columns))


def feed_back_kernel(
    local, grad_ref, up_ref, down_ref, slope_ref, low_ref, sums_ref, own_ref, *back_refs
):
    pre_grad = times_transposed(grad_ref[...], down_ref[...]) * slope_ref[...]
    sums_ref[...] = jnp.sum(pre_grad, axis=0, keepdims=True)
    low = pre_grad.astype(BF16)
    low_ref[...] = low
    back = times_transposed(low, up_ref[...])
    own_ref[...] = back[:local]
    for k, back_ref in enumerate(back_refs):
        back_ref[...] = back[(k + 1) * local : (k + 2) * local].astype(BF16)


def feed_back(grad, up, down, slope, local):
    rows, depth = grad.shape
    columns = up.shape[1]
    return pl.pallas_call(
        partial(feed_back_kernel, local),
        out_shape=[
            jax.ShapeDtypeStruct((rows, columns), BF16),
            jax.ShapeDtypeStruct((1, columns), F32),
            jax.ShapeDtypeStruct((local, depth), F32),
        ]
        + [jax.ShapeDtypeStruct((local, depth), BF16)] * (rows // local - 1),
        compiler_params=pltpu.CompilerParams(vmem_limit_bytes=52 * 2**20),
        cost_estimate=pl.CostEstimate(
            flops=4 * rows * depth * columns,
            bytes_accessed=4 * depth * columns + 6 * rows * columns + 4 * rows * depth,
            transcendentals=0,
        ),
    )(grad, up, down, slope)


def on_device(
    nd, ns,
    inputs, skipped, item_lengths,
    skip_w, qkv_w, proj_w, fc1_w, fc2_w,
    skip_b, ln1_g, ln1_b, proj_b, ln2_g, ln2_b, fc1_b, fc2_b,
    cotangent,
):
    _, local, features = inputs.shape
    hidden_units = fc1_w.shape[1]
    n = nd * ns
    row_len = local * ns
    heads = HEADS // ns
    head_cols = heads * HEAD_DIM
    wide = 3 * head_cols
    small = features // n
    scale = HEAD_DIM ** (-0.5)
    hidden_part = hidden_units // nd
    joined_part = 2 * features // nd
    part = features // nd
    places = ns // 2
    dp_at = lax.axis_index("dp")
    seq_at = lax.axis_index("seq")
    core = seq_at % 2
    after = lax.optimization_barrier

    def swap(v, k):
        return lax.ppermute(v, "dp", [(i, i ^ k) for i in range(nd)])

    def other_core(v):
        return lax.ppermute(v, "seq", [(i, i ^ 1) for i in range(ns)])

    def index(v, at, axis=0):
        return lax.dynamic_index_in_dim(v, at, axis, keepdims=False)

    def gather_rows(v):
        return jnp.concatenate([v] + [swap(v, k) for k in range(1, nd)], axis=0)

    def add_blocks(own, low):
        for k in range(1, nd):
            own = own + swap(low[k], k).astype(F32)
        return own

    def low_rows(partial_sums):
        return partial_sums.astype(BF16).reshape(nd, local, features)

    def widen(v):
        v = v.reshape(v.shape[0], v.shape[1] // HEAD_DIM, HEAD_DIM)
        return jnp.pad(v, ((0, 0), (0, 0), (0, WIDE - HEAD_DIM))).reshape(v.shape[0], -1)

    def seq_exchange(v):
        return lax.all_to_all(v, "seq", 0, 0, tiled=True)

    def core_sums(terms):
        terms = terms.reshape((places, 2) + terms.shape[1:])
        given = index(terms, 1 - core, 1).astype(BF16)
        kept = index(terms, core, 1).astype(F32)
        return (kept + other_core(given).astype(F32)).astype(BF16)

    def chip_sums(sums):
        groups = [[i * 2 + c for i in range(places)] for c in range(2)]
        terms = lax.all_to_all(sums, "seq", 0, 0, axis_index_groups=groups, tiled=True)
        return jnp.sum(terms.reshape(sums.shape).astype(F32), axis=0)

    skip_part = lax.all_gather(skip_w, "seq", axis=0, tiled=True)

    own_vectors = (skip_b, ln1_g, ln1_b, proj_b, ln2_g, ln2_b, fc2_b, fc1_b)
    packed = jnp.concatenate(own_vectors)
    own_size = packed.shape[0]
    padded = -(-own_size // 1024) * 1024
    packed = jnp.pad(packed, (0, padded - own_size)).reshape(padded // 128, 128)
    packed = jnp.broadcast_to(packed[None], (n,) + packed.shape)
    vectors = lax.all_to_all(packed, ("dp", "seq"), 0, 0, tiled=True)
    vectors = vectors.reshape(n, padded).astype(F32)

    joined_slices = jnp.stack(
        [
            half[:, at * joined_part : (at + 1) * joined_part]
            for half in (inputs[0], skipped[0])
            for at in range(nd // 2)
        ]
    )
    joined_here = jnp.concatenate(
        [index(joined_slices, dp_at)]
        + [swap(index(joined_slices, dp_at ^ k), k) for k in range(1, nd)],
        axis=0,
    )
    at = lax.broadcasted_iota(jnp.int32, (features, features), 0)
    block, row = at // small, at % small
    row = ((block % nd) ^ dp_at) * part + (block // nd) * small + row
    order = (row == lax.broadcasted_iota(jnp.int32, (features, features), 1)).astype(BF16)
    qkv_out = qkv_w.reshape(small, 3, ns, head_cols).transpose(2, 0, 1, 3).reshape(ns, small, wide)
    up_slices = jnp.swapaxes(fc1_w.reshape(small, nd, hidden_part), 0, 1)
    up_slices = jnp.concatenate(
        [index(up_slices, dp_at)] + [swap(index(up_slices, dp_at ^ k), k) for k in range(1, nd)],
        axis=0,
    )
    qkv_out, skip_part, joined_here, vectors, up_slices = after(
        (qkv_out, skip_part, joined_here, vectors, up_slices)
    )
    def vector(at):
        return vectors[:, at * small : (at + 1) * small].reshape(features)

    b_skip, g_one, b_one, b_proj, g_two, b_two, b_down = (vector(i) for i in range(7))
    up_bias = lax.dynamic_slice_in_dim(vectors[:, 7 * small : own_size], dp_at * ns, ns, 0)
    up_bias = up_bias.reshape(hidden_part)

    first_terms = dot(joined_here, skip_part)
    first = add_blocks(first_terms[:local], low_rows(first_terms)) + b_skip
    qkv_mine = seq_exchange(qkv_out).reshape(part, wide)
    xhat_one, inverse_one = norm_pieces(first)
    normed_one = (xhat_one * g_one + b_one).astype(BF16)
    normed_one, qkv_mine, own_proj = after((normed_one, qkv_mine, proj_w))
    normed_one_row = lax.all_gather(normed_one, "seq", axis=0, tiled=True)

    qkv_mine = lax.all_gather(qkv_mine, "dp", axis=0, tiled=True)
    qkv_mine, own_proj, grad_out = after((qkv_mine, own_proj, cotangent[0]))
    grad_out_rows = gather_rows(grad_out)
    proj_rows = lax.all_gather(own_proj, "seq", axis=0, tiled=True)
    half = part // 2
    own_half = lax.dynamic_slice_in_dim(proj_rows, core * half, half, 0)
    proj_halves = [swap(own_half, k) for k in range(1, nd)]
    normed_one_row, qkv_mine, qkv_wide, proj_rows, grad_out_rows = after(
        (normed_one_row, qkv_mine, widen(qkv_mine), proj_rows, grad_out_rows)
    )
    up_part = lax.all_gather(up_slices, "seq", axis=0, tiled=True)
    triple = dot(normed_one_row, qkv_wide).astype(BF16)
    attended, attended_low, lse = attend(triple, item_lengths, heads, scale)

    def heads_to_tokens(v):
        v = seq_exchange(v.reshape(ns, local, head_cols))
        return jnp.swapaxes(v, 0, 1).reshape(local, features)

    attended_low, proj_halves, proj_rows = after((attended_low, proj_halves, proj_rows))
    w_proj = lax.dynamic_update_slice_in_dim(
        jnp.zeros((features, features), BF16), proj_rows, dp_at * part, 0
    )
    for k in range(1, nd):
        place = (dp_at ^ k) * 2
        here = proj_halves[k - 1]
        there = other_core(here)
        w_proj = lax.dynamic_update_slice_in_dim(w_proj, here, (place + core) * half, 0)
        w_proj = lax.dynamic_update_slice_in_dim(w_proj, there, (place + 1 - core) * half, 0)
    attended_low = heads_to_tokens(attended_low)
    attended_low, grad_out_rows, w_proj = after((attended_low, grad_out_rows, w_proj))
    own_down, attended_low, up_part = after((fc2_w, attended_low, up_part))
    down_part = lax.all_gather(own_down, "seq", axis=0, tiled=True)
    second = first + dot(attended_low, w_proj) + b_proj
    xhat_two, inverse_two = norm_pieces(second)
    normed_two = (xhat_two * g_two + b_two).astype(BF16)

    normed_two_rows = gather_rows(normed_two)
    up_part = inner(order, up_part).astype(BF16)
    normed_two_rows, up_part = after((normed_two_rows, up_part))
    hidden, slope = gelu_of_matmul(normed_two_rows, up_part, up_bias)

    fc2_terms = inner(hidden, grad_out_rows).astype(BF16)
    fc2_w_grad = lax.psum_scatter(fc2_terms, "seq", scatter_dimension=0, tiled=True)
    slope, fc2_terms = after((slope, fc2_terms))
    pre_low, up_sums, normed_two_grad, *up_blocks = feed_back(
        grad_out_rows, up_part, down_part, slope, local
    )
    up_blocks = [swap(block, k + 1) for k, block in enumerate(up_blocks)]
    fc1_terms = inner(times_transposed(normed_two_rows, order).astype(BF16), pre_low).astype(BF16)
    for block in up_blocks:
        normed_two_grad = normed_two_grad + block.astype(F32)
    normed_two_grad, fc1_terms = after((normed_two_grad, fc1_terms))
    through_two, ln2_g_grad, ln2_b_grad = norm_back(normed_two_grad, xhat_two, inverse_two, g_two)
    second_grad = grad_out.astype(F32) + through_two
    second_low = second_grad.astype(BF16)
    attended_grad = product_by_group(second_low, w_proj, ns)
    attended_grad, second_late, hidden_late, attended_low, fc1_terms = after(
        (attended_grad, second_low, hidden, attended_low, fc1_terms)
    )
    fc1_terms = lax.psum_scatter(fc1_terms, "seq", scatter_dimension=0, tiled=True)
    attended_grad = seq_exchange(attended_grad).reshape(row_len, head_cols)
    down_sums = dot(hidden_late, down_part)
    attended_slices = jnp.swapaxes(attended_low.reshape(local, nd, part), 0, 1)
    down_blocks = low_rows(down_sums)
    down_blocks = [swap(down_blocks[k], k) for k in range(1, nd)]
    attended_grad, down_blocks[0], second_late, attended_slices = after(
        (attended_grad, down_blocks[0], second_late, attended_slices)
    )
    triple_grad = jnp.concatenate(
        attend_back(triple, attended_grad, attended, lse, item_lengths, heads, scale), axis=1
    )
    one_back = times_transposed(triple_grad, qkv_mine).astype(BF16)
    one_back, triple_late, down_blocks, second_late, fc1_terms, fc2_w_grad = after(
        (one_back, triple_grad, down_blocks, second_late, fc1_terms, fc2_w_grad)
    )
    output = second + down_sums[:local] + b_down
    for block in down_blocks:
        output = output + block.astype(F32)
    output = output.astype(BF16)
    normed_one_grad = lax.psum_scatter(one_back, "seq", scatter_dimension=0, tiled=True)
    second_rows = gather_rows(second_late)
    qkv_terms = inner(normed_one_row, triple_late).reshape(nd, part, wide)
    qkv_low, second_rows = after((qkv_terms.astype(BF16), second_rows))
    qkv_blocks = [swap(index(qkv_low, dp_at ^ k), k) for k in range(1, nd)]
    attended_rows = jnp.concatenate(
        [index(attended_slices, dp_at)]
        + [swap(index(attended_slices, dp_at ^ k), k) for k in range(1, nd)],
        axis=0,
    )
    proj_terms = inner(attended_rows, second_rows).reshape(ns, small, features)
    proj_sums = core_sums(proj_terms)
    qkv_sum = index(qkv_terms, dp_at)
    for block in qkv_blocks:
        qkv_sum = qkv_sum + block.astype(F32)
    qkv_sum = qkv_sum.astype(BF16).reshape(ns, small, wide)
    normed_one_grad = normed_one_grad.astype(F32)
    through_one, ln1_g_grad, ln1_b_grad = norm_back(normed_one_grad, xhat_one, inverse_one, g_one)
    first_grad = second_grad + through_one
    first_low = first_grad.astype(BF16)
    first_low_rows = gather_rows(first_low)
    proj_w_grad = chip_sums(proj_sums)
    qkv_w_grad = seq_exchange(qkv_sum)
    first_low_rows, first_grad, proj_w_grad = after((first_low_rows, first_grad, proj_w_grad))
    skip_terms = inner(joined_here, first_low_rows).astype(BF16)
    skip_w_grad = lax.psum_scatter(skip_terms, "seq", scatter_dimension=0, tiled=True).astype(F32)
    skip_terms, first_low_rows, first_grad, fc1_terms, qkv_w_grad = after(
        (skip_terms, first_low_rows, first_grad, fc1_terms, qkv_w_grad)
    )
    fc1_terms = fc1_terms.reshape(nd, small, hidden_part)
    fc1_blocks = jnp.stack([fc1_terms[0]] + [swap(fc1_terms[k], k) for k in range(1, nd)])
    vector_grads = jnp.stack(
        [
            jnp.sum(first_grad, axis=0),
            ln1_g_grad,
            ln1_b_grad,
            jnp.sum(second_grad, axis=0),
            ln2_g_grad,
            ln2_b_grad,
            jnp.sum(grad_out.astype(F32), axis=0),
        ]
    )
    vector_grads = jnp.swapaxes(vector_grads.reshape(7, n, small), 0, 1).reshape(n, 7 * small)
    up_grads = up_sums.reshape(ns, hidden_units // n)
    up_grads = lax.dynamic_update_slice_in_dim(
        jnp.zeros((n, hidden_units // n), F32), up_grads, dp_at * ns, 0
    )
    vector_grads = jnp.concatenate([vector_grads, up_grads], axis=1)
    vector_grads = jnp.pad(vector_grads, ((0, 0), (0, padded - own_size)))
    vector_grads = lax.all_to_all(
        vector_grads.reshape(n, padded // 128, 128), ("dp", "seq"), 0, 0, tiled=True
    )
    joined_grad_part = times_transposed(first_low_rows, skip_part).astype(BF16)
    joined_grad_part = joined_grad_part.reshape(nd, local, joined_part)
    away = [joined_grad_part[0]] + [swap(joined_grad_part[k], k) for k in range(1, nd)]
    away = jnp.stack(away)
    joined_grad = jnp.concatenate(
        [index(away, dp_at ^ k) for k in range(nd)], axis=1
    ).astype(F32)
    fc1_w_grad = jnp.concatenate([index(fc1_blocks, dp_at ^ k) for k in range(nd)], axis=1)
    qkv_w_grad = (
        qkv_w_grad.reshape(ns, small, 3, head_cols).transpose(1, 2, 0, 3)
        .reshape(small, 3 * features)
    )
    vector_grads = jnp.sum(vector_grads, axis=0).reshape(padded)
    skip_b_grad, ln1_g_grad, ln1_b_grad, proj_b_grad, ln2_g_grad, ln2_b_grad, fc2_b_grad = (
        vector_grads[i * small : (i + 1) * small] for i in range(7)
    )
    fc1_b_grad = vector_grads[7 * small : own_size]
    return (
        output[None], joined_grad[None, :, :features], joined_grad[None, :, features:],
        skip_w_grad, qkv_w_grad.astype(F32), proj_w_grad,
        fc1_w_grad.astype(F32), fc2_w_grad.astype(F32),
        skip_b_grad, ln1_g_grad, ln1_b_grad, proj_b_grad, ln2_g_grad, ln2_b_grad,
        fc1_b_grad, fc2_b_grad,
    )


def solution(mesh):
    tokens = P("dp", "seq", None)
    matrix = P(("dp", "seq"), None)
    flat = P(("dp", "seq"))
    in_specs = (tokens, tokens, P("dp", None)) + (matrix,) * 5 + (flat,) * 8 + (tokens,)
    out_specs = (tokens,) * 3 + (matrix,) * 5 + (flat,) * 8
    return jax.shard_map(
        partial(on_device, mesh.shape["dp"], mesh.shape["seq"]),
        mesh=mesh, in_specs=in_specs, out_specs=out_specs, check_vma=False,
    )
```

```python
import math
from functools import partial

import jax
import jax.numpy as jnp
from jax import lax
from jax.experimental import pallas as pl
from jax.experimental.pallas import tpu as pltpu
from jax.sharding import PartitionSpec as P

HEADS = 16
HEAD_DIM = 72
EPSILON = 1e-05
NEGATIVE = -1e30
WIDE = 128
F32 = jnp.float32
BF16 = jnp.bfloat16


def norm_pieces(hvals):
    centered = hvals - jnp.mean(hvals, axis=-1, keepdims=True)
    inverse = lax.rsqrt(jnp.mean(centered * centered, axis=-1, keepdims=True) + EPSILON)
    return centered * inverse, inverse


def norm_back(incoming, standardized, inverse, gain):
    scaled = incoming * gain
    passed = inverse * (
        scaled
        - jnp.mean(scaled, axis=-1, keepdims=True)
        - standardized * jnp.mean(scaled * standardized, axis=-1, keepdims=True)
    )
    return passed, jnp.sum(incoming * standardized, axis=0), jnp.sum(incoming, axis=0)


def segment_of(lengths_ref, places):
    running = jnp.int32(0)
    passed = jnp.zeros(places.shape, jnp.int32)
    for slot in range(lengths_ref.shape[1]):
        running = running + lengths_ref[0, slot]
        passed = passed + (running <= places).astype(jnp.int32)
    return passed


def same_item(lengths_ref, rows, columns, first_row):
    of_rows = first_row + lax.broadcasted_iota(jnp.int32, (rows, 1), 0)
    of_columns = lax.broadcasted_iota(jnp.int32, (1, columns), 1)
    return segment_of(lengths_ref, of_rows) == segment_of(lengths_ref, of_columns)


def dot(left, right):
    return jnp.dot(left, right, preferred_element_type=F32)


def inner(left, right):
    return lax.dot_general(left, right, (((0,), (0,)), ((), ())), preferred_element_type=F32)


def times_transposed(left, right):
    return lax.dot_general(left, right, (((1,), (1,)), ((), ())), preferred_element_type=F32)


def side_by_side(parts):
    return jnp.concatenate([part[:, :HEAD_DIM] for part in parts], axis=1)


def attend_kernel(
    heads, scale, q_ref, k_ref, v_ref, lengths_ref, out_ref, low_ref, lse_ref
):
    step = q_ref.shape[0]
    allowed = same_item(lengths_ref, step, k_ref.shape[0], pl.program_id(0) * step)
    lane = lax.broadcasted_iota(jnp.int32, (q_ref.shape[0], WIDE), 1)
    logs = jnp.zeros((q_ref.shape[0], WIDE), F32)
    outs = []
    for h in range(heads):
        at = slice(h * WIDE, (h + 1) * WIDE)
        logits = times_transposed(q_ref[:, at], k_ref[:, at]) * scale
        logits = jnp.where(allowed, logits, NEGATIVE)
        top = jnp.max(logits, axis=1, keepdims=True)
        weights = jnp.exp(logits - top)
        total = jnp.sum(weights, axis=1, keepdims=True)
        outs.append(dot(weights.astype(BF16), v_ref[:, at]) / total)
        out_ref[:, at] = outs[h]
        logs = jnp.where(lane == h, top + jnp.log(total), logs)
    lse_ref[...] = jnp.transpose(logs)[:8]
    low_ref[...] = side_by_side(outs).astype(BF16)


def attend(triple, lengths, heads, scale):
    rows = triple.shape[0]
    wide = heads * WIDE
    step = 256 if rows % 256 == 0 else rows
    return pl.pallas_call(
        partial(attend_kernel, heads, scale),
        grid=(rows // step,),
        in_specs=[
            pl.BlockSpec((step, wide), lambda i: (i, 0)),
            pl.BlockSpec((rows, wide), lambda i: (0, 1)),
            pl.BlockSpec((rows, wide), lambda i: (0, 2)),
            pl.BlockSpec(memory_space=pltpu.SMEM),
        ],
        out_specs=[
            pl.BlockSpec((step, wide), lambda i: (i, 0)),
            pl.BlockSpec((step, heads * HEAD_DIM), lambda i: (i, 0)),
            pl.BlockSpec((8, step), lambda i: (0, i)),
        ],
        out_shape=[
            jax.ShapeDtypeStruct((rows, wide), F32),
            jax.ShapeDtypeStruct((rows, heads * HEAD_DIM), BF16),
            jax.ShapeDtypeStruct((8, rows), F32),
        ],
        compiler_params=pltpu.CompilerParams(vmem_limit_bytes=48 * 2**20),
        cost_estimate=pl.CostEstimate(
            flops=8 * rows * rows * wide,
            bytes_accessed=10 * rows * wide,
            transcendentals=heads * rows * rows,
        ),
    )(triple, triple, triple, lengths)


def attend_back_kernel(
    heads, scale, q_ref, k_ref, v_ref, out_grad_ref, out_ref, lse_ref, lengths_ref,
    dq_ref, dkv_ref, sum_ref, grad_ref, delta_ref,
):
    step = pl.program_id(0)

    @pl.when(step == 0)
    def _():
        sum_ref[...] = jnp.zeros_like(sum_ref)
        ones = jnp.ones((8, WIDE), F32)
        for h in range(heads):
            grad = out_grad_ref[:, h * HEAD_DIM : (h + 1) * HEAD_DIM]
            gap = jnp.zeros((grad.shape[0], WIDE - HEAD_DIM), BF16)
            grad = jnp.concatenate([grad, gap], axis=1)
            at = slice(h * WIDE, (h + 1) * WIDE)
            grad_ref[:, at] = grad
            delta = lax.dot_general(
                ones, grad.astype(F32) * out_ref[:, at], (((1,), (1,)), ((), ())),
                precision=lax.Precision.HIGHEST, preferred_element_type=F32,
            )
            delta_ref[h : h + 1, :] = delta[:1]

    block, rows = k_ref.shape[0], q_ref.shape[0]
    allowed = same_item(lengths_ref, block, rows, step * block)
    key_grads, value_grads = [], []
    for h in range(heads):
        at = slice(h * WIDE, (h + 1) * WIDE)
        queries, keys, out_grad = q_ref[:, at], k_ref[:, at], grad_ref[:, at]
        logits = times_transposed(keys, queries) * scale - lse_ref[h : h + 1, :]
        probs = jnp.where(allowed, jnp.exp(logits), 0.0)
        prob_grad = times_transposed(v_ref[:, at], out_grad)
        logit_grad = (probs * (prob_grad - delta_ref[h : h + 1, :]) * scale).astype(BF16)
        value_grads.append(dot(probs.astype(BF16), out_grad))
        key_grads.append(dot(logit_grad, queries))
        sum_ref[:, at] += inner(logit_grad, keys)
    dkv_ref[...] = side_by_side(key_grads + value_grads).astype(BF16)

    @pl.when(step == pl.num_programs(0) - 1)
    def _():
        dq_ref[...] = side_by_side(
            [sum_ref[:, h * WIDE : (h + 1) * WIDE] for h in range(heads)]
        ).astype(BF16)


def attend_back(triple, out_grad, out, lse, lengths, heads, scale):
    rows = triple.shape[0]
    wide = heads * WIDE
    step = 256 if rows % 256 == 0 else rows
    whole = pl.BlockSpec((rows, wide), lambda i: (0, 0))
    row = pl.BlockSpec((8, rows), lambda i: (0, 0))
    return pl.pallas_call(
        partial(attend_back_kernel, heads, scale),
        grid=(rows // step,),
        in_specs=[
            whole,
            pl.BlockSpec((step, wide), lambda i: (i, 1)),
            pl.BlockSpec((step, wide), lambda i: (i, 2)),
            pl.BlockSpec((rows, heads * HEAD_DIM), lambda i: (0, 0)),
            whole,
            row,
            pl.BlockSpec(memory_space=pltpu.SMEM),
        ],
        out_specs=[
            pl.BlockSpec((rows, heads * HEAD_DIM), lambda i: (0, 0)),
            pl.BlockSpec((step, 2 * heads * HEAD_DIM), lambda i: (i, 0)),
        ],
        out_shape=[
            jax.ShapeDtypeStruct((rows, heads * HEAD_DIM), BF16),
            jax.ShapeDtypeStruct((rows, 2 * heads * HEAD_DIM), BF16),
        ],
        scratch_shapes=[
            pltpu.VMEM((rows, wide), F32),
            pltpu.VMEM((rows, wide), BF16),
            pltpu.VMEM((8, rows), F32),
        ],
        compiler_params=pltpu.CompilerParams(vmem_limit_bytes=48 * 2**20),
        cost_estimate=pl.CostEstimate(
            flops=20 * rows * rows * wide,
            bytes_accessed=14 * rows * wide,
            transcendentals=heads * rows * rows,
        ),
    )(triple, triple, triple, out_grad, out, lse, lengths)


def by_group_kernel(x_ref, w_ref, out_ref):
    groups, rows, columns = out_ref.shape
    product = times_transposed(x_ref[...], w_ref[...]).astype(BF16)
    for g in range(groups):
        out_ref[g] = product[:, g * columns : (g + 1) * columns]


def product_by_group(x, w, groups):
    rows, depth = x.shape
    columns = w.shape[0] // groups
    steps = 2
    return pl.pallas_call(
        by_group_kernel,
        grid=(steps,),
        in_specs=[
            pl.BlockSpec((rows, depth), lambda j: (0, 0)),
            pl.BlockSpec((w.shape[0] // steps, depth), lambda j: (j, 0)),
        ],
        out_specs=pl.BlockSpec((groups // steps, rows, columns), lambda j: (j, 0, 0)),
        out_shape=jax.ShapeDtypeStruct((groups, rows, columns), BF16),
        cost_estimate=pl.CostEstimate(
            flops=2 * rows * depth * w.shape[0],
            bytes_accessed=2 * depth * (rows + w.shape[0]) + 2 * rows * w.shape[0],
            transcendentals=0,
        ),
    )(x, w)


def gelu_kernel(rows_at_once, x_ref, up_ref, bias_ref, value_ref, slope_ref):
    for start in range(0, x_ref.shape[0], rows_at_once):
        at = pl.ds(start, rows_at_once)
        pre = dot(x_ref[at, :], up_ref[...]) + bias_ref[...]
        bell = jnp.exp(-0.5 * pre * pre)
        t = 1.0 / (1.0 + (0.3275911 * 0.5**0.5) * jnp.abs(pre))
        tail = 0.5 * 1.061405429
        for c in (-1.453152027, 1.421413741, -0.284496736, 0.254829592):
            tail = tail * t + 0.5 * c
        tail = tail * t * bell
        below = jnp.where(pre < 0.0, tail, 1.0 - tail)
        value_ref[at, :] = (pre * below).astype(BF16)
        slope_ref[at, :] = below + pre * bell * (0.5 / math.pi) ** 0.5


def gelu_of_matmul(x, up, bias):
    rows, depth = x.shape
    columns = up.shape[1]
    step = 384 if columns % 384 == 0 else columns
    block = pl.BlockSpec((rows, step), lambda j: (0, j))
    return pl.pallas_call(
        partial(gelu_kernel, 640 if rows % 640 == 0 else rows),
        grid=(columns // step,),
        in_specs=[
            pl.BlockSpec((rows, depth), lambda j: (0, 0)),
            pl.BlockSpec((depth, step), lambda j: (0, j)),
            pl.BlockSpec((1, step), lambda j: (0, j)),
        ],
        out_specs=[block, block],
        out_shape=[
            jax.ShapeDtypeStruct((rows, columns), BF16),
            jax.ShapeDtypeStruct((rows, columns), F32),
        ],
        compiler_params=pltpu.CompilerParams(vmem_limit_bytes=40 * 2**20),
        cost_estimate=pl.CostEstimate(
            flops=2 * rows * depth * columns,
            bytes_accessed=2 * depth * (rows + columns) + 6 * rows * columns,
            transcendentals=rows * columns,
        ),
    )(x, up, bias.reshape(1, columns))


def feed_back_kernel(
    local, grad_ref, up_ref, down_ref, slope_ref, low_ref, sums_ref, own_ref, *back_refs
):
    pre_grad = times_transposed(grad_ref[...], down_ref[...]) * slope_ref[...]
    sums_ref[...] = jnp.sum(pre_grad, axis=0, keepdims=True)
    low = pre_grad.astype(BF16)
    low_ref[...] = low
    back = times_transposed(low, up_ref[...])
    own_ref[...] = back[:local]
    for k, back_ref in enumerate(back_refs):
        back_ref[...] = back[(k + 1) * local : (k + 2) * local].astype(BF16)


def feed_back(grad, up, down, slope, local):
    rows, depth = grad.shape
    columns = up.shape[1]
    return pl.pallas_call(
        partial(feed_back_kernel, local),
        out_shape=[
            jax.ShapeDtypeStruct((rows, columns), BF16),
            jax.ShapeDtypeStruct((1, columns), F32),
            jax.ShapeDtypeStruct((local, depth), F32),
        ]
        + [jax.ShapeDtypeStruct((local, depth), BF16)] * (rows // local - 1),
        compiler_params=pltpu.CompilerParams(vmem_limit_bytes=52 * 2**20),
        cost_estimate=pl.CostEstimate(
            flops=4 * rows * depth * columns,
            bytes_accessed=4 * depth * columns + 6 * rows * columns + 4 * rows * depth,
            transcendentals=0,
        ),
    )(grad, up, down, slope)


def on_device(
    nd, ns,
    inputs, skipped, item_lengths,
    skip_w, qkv_w, proj_w, fc1_w, fc2_w,
    skip_b, ln1_g, ln1_b, proj_b, ln2_g, ln2_b, fc1_b, fc2_b,
    cotangent,
):
    _, local, features = inputs.shape
    hidden_units = fc1_w.shape[1]
    n = nd * ns
    row_len = local * ns
    heads = HEADS // ns
    head_cols = heads * HEAD_DIM
    wide = 3 * head_cols
    small = features // n
    scale = HEAD_DIM ** (-0.5)
    hidden_part = hidden_units // nd
    joined_part = 2 * features // nd
    part = features // nd
    places = ns // 2
    dp_at = lax.axis_index("dp")
    seq_at = lax.axis_index("seq")
    core = seq_at % 2
    after = lax.optimization_barrier

    def swap(v, k):
        return lax.ppermute(v, "dp", [(i, i ^ k) for i in range(nd)])

    def other_core(v):
        return lax.ppermute(v, "seq", [(i, i ^ 1) for i in range(ns)])

    def index(v, at, axis=0):
        return lax.dynamic_index_in_dim(v, at, axis, keepdims=False)

    def gather_rows(v):
        return jnp.concatenate([v] + [swap(v, k) for k in range(1, nd)], axis=0)

    def add_blocks(own, low):
        for k in range(1, nd):
            own = own + swap(low[k], k).astype(F32)
        return own

    def low_rows(partial_sums):
        return partial_sums.astype(BF16).reshape(nd, local, features)

    def widen(v):
        v = v.reshape(v.shape[0], v.shape[1] // HEAD_DIM, HEAD_DIM)
        return jnp.pad(v, ((0, 0), (0, 0), (0, WIDE - HEAD_DIM))).reshape(v.shape[0], -1)

    def seq_exchange(v):
        return lax.all_to_all(v, "seq", 0, 0, tiled=True)

    def core_sums(terms):
        terms = terms.reshape((places, 2) + terms.shape[1:])
        given = index(terms, 1 - core, 1).astype(BF16)
        kept = index(terms, core, 1).astype(F32)
        return (kept + other_core(given).astype(F32)).astype(BF16)

    def chip_sums(sums):
        groups = [[i * 2 + c for i in range(places)] for c in range(2)]
        terms = lax.all_to_all(sums, "seq", 0, 0, axis_index_groups=groups, tiled=True)
        return jnp.sum(terms.reshape(sums.shape).astype(F32), axis=0)

    skip_part = lax.all_gather(skip_w, "seq", axis=0, tiled=True)

    own_vectors = (skip_b, ln1_g, ln1_b, proj_b, ln2_g, ln2_b, fc2_b, fc1_b)
    packed = jnp.concatenate(own_vectors)
    own_size = packed.shape[0]
    padded = -(-own_size // 1024) * 1024
    packed = jnp.pad(packed, (0, padded - own_size)).reshape(padded // 128, 128)
    packed = jnp.broadcast_to(packed[None], (n,) + packed.shape)
    vectors = lax.all_to_all(packed, ("dp", "seq"), 0, 0, tiled=True)
    vectors = vectors.reshape(n, padded).astype(F32)

    joined_slices = jnp.stack(
        [
            half[:, at * joined_part : (at + 1) * joined_part]
            for half in (inputs[0], skipped[0])
            for at in range(nd // 2)
        ]
    )
    joined_here = jnp.concatenate(
        [index(joined_slices, dp_at)]
        + [swap(index(joined_slices, dp_at ^ k), k) for k in range(1, nd)],
        axis=0,
    )
    at = lax.broadcasted_iota(jnp.int32, (features, features), 0)
    block, row = at // small, at % small
    row = ((block % nd) ^ dp_at) * part + (block // nd) * small + row
    order = (row == lax.broadcasted_iota(jnp.int32, (features, features), 1)).astype(BF16)
    qkv_out = qkv_w.reshape(small, 3, ns, head_cols).transpose(2, 0, 1, 3).reshape(ns, small, wide)
    up_slices = jnp.swapaxes(fc1_w.reshape(small, nd, hidden_part), 0, 1)
    up_slices = jnp.concatenate(
        [index(up_slices, dp_at)] + [swap(index(up_slices, dp_at ^ k), k) for k in range(1, nd)],
        axis=0,
    )
    qkv_out, skip_part, joined_here, vectors, up_slices = after(
        (qkv_out, skip_part, joined_here, vectors, up_slices)
    )
    def vector(at):
        return vectors[:, at * small : (at + 1) * small].reshape(features)

    b_skip, g_one, b_one, b_proj, g_two, b_two, b_down = (vector(i) for i in range(7))
    up_bias = lax.dynamic_slice_in_dim(vectors[:, 7 * small : own_size], dp_at * ns, ns, 0)
    up_bias = up_bias.reshape(hidden_part)

    first_terms = dot(joined_here, skip_part)
    first = add_blocks(first_terms[:local], low_rows(first_terms)) + b_skip
    qkv_mine = seq_exchange(qkv_out).reshape(part, wide)
    xhat_one, inverse_one = norm_pieces(first)
    normed_one = (xhat_one * g_one + b_one).astype(BF16)
    normed_one, qkv_mine, own_proj = after((normed_one, qkv_mine, proj_w))
    normed_one_row = lax.all_gather(normed_one, "seq", axis=0, tiled=True)

    qkv_mine = lax.all_gather(qkv_mine, "dp", axis=0, tiled=True)
    qkv_mine, own_proj = after((qkv_mine, own_proj))
    proj_rows = lax.all_gather(own_proj, "seq", axis=0, tiled=True)
    half = part // 2
    own_half = lax.dynamic_slice_in_dim(proj_rows, core * half, half, 0)
    proj_halves = [swap(own_half, k) for k in range(1, nd)]
    normed_one_row, qkv_mine, qkv_wide, proj_rows = after(
        (normed_one_row, qkv_mine, widen(qkv_mine), proj_rows)
    )
    up_part = lax.all_gather(up_slices, "seq", axis=0, tiled=True)
    triple = dot(normed_one_row, qkv_wide).astype(BF16)
    attended, attended_low, lse = attend(triple, item_lengths, heads, scale)

    def heads_to_tokens(v):
        v = seq_exchange(v.reshape(ns, local, head_cols))
        return jnp.swapaxes(v, 0, 1).reshape(local, features)

    attended_low, grad_out, proj_halves, proj_rows = after(
        (attended_low, cotangent[0], proj_halves, proj_rows)
    )
    w_proj = lax.dynamic_update_slice_in_dim(
        jnp.zeros((features, features), BF16), proj_rows, dp_at * part, 0
    )
    for k in range(1, nd):
        place = (dp_at ^ k) * 2
        here = proj_halves[k - 1]
        there = other_core(here)
        w_proj = lax.dynamic_update_slice_in_dim(w_proj, here, (place + core) * half, 0)
        w_proj = lax.dynamic_update_slice_in_dim(w_proj, there, (place + 1 - core) * half, 0)
    grad_out_rows = gather_rows(grad_out)
    attended_low = heads_to_tokens(attended_low)
    attended_low, grad_out_rows, w_proj = after((attended_low, grad_out_rows, w_proj))
    own_down, attended_low, up_part = after((fc2_w, attended_low, up_part))
    down_part = lax.all_gather(own_down, "seq", axis=0, tiled=True)
    second = first + dot(attended_low, w_proj) + b_proj
    xhat_two, inverse_two = norm_pieces(second)
    normed_two = (xhat_two * g_two + b_two).astype(BF16)

    normed_two_rows = gather_rows(normed_two)
    up_part = inner(order, up_part).astype(BF16)
    normed_two_rows, up_part = after((normed_two_rows, up_part))
    hidden, slope = gelu_of_matmul(normed_two_rows, up_part, up_bias)

    fc2_terms = inner(hidden, grad_out_rows).astype(BF16)
    fc2_w_grad = lax.psum_scatter(fc2_terms, "seq", scatter_dimension=0, tiled=True)
    slope, fc2_terms = after((slope, fc2_terms))
    pre_low, up_sums, normed_two_grad, *up_blocks = feed_back(
        grad_out_rows, up_part, down_part, slope, local
    )
    up_blocks = [swap(block, k + 1) for k, block in enumerate(up_blocks)]
    fc1_terms = inner(times_transposed(normed_two_rows, order).astype(BF16), pre_low).astype(BF16)
    for block in up_blocks:
        normed_two_grad = normed_two_grad + block.astype(F32)
    normed_two_grad, fc1_terms = after((normed_two_grad, fc1_terms))
    through_two, ln2_g_grad, ln2_b_grad = norm_back(normed_two_grad, xhat_two, inverse_two, g_two)
    second_grad = grad_out.astype(F32) + through_two
    second_low = second_grad.astype(BF16)
    attended_grad = product_by_group(second_low, w_proj, ns)
    attended_grad, second_late, hidden_late, attended_low, fc1_terms = after(
        (attended_grad, second_low, hidden, attended_low, fc1_terms)
    )
    fc1_terms = lax.psum_scatter(fc1_terms, "seq", scatter_dimension=0, tiled=True)
    attended_grad = seq_exchange(attended_grad).reshape(row_len, head_cols)
    down_sums = dot(hidden_late, down_part)
    attended_slices = jnp.swapaxes(attended_low.reshape(local, nd, part), 0, 1)
    down_blocks = low_rows(down_sums)
    down_blocks = [swap(down_blocks[k], k) for k in range(1, nd)]
    attended_grad, down_blocks[0], second_late, attended_slices = after(
        (attended_grad, down_blocks[0], second_late, attended_slices)
    )
    triple_grad = jnp.concatenate(
        attend_back(triple, attended_grad, attended, lse, item_lengths, heads, scale), axis=1
    )
    one_back = times_transposed(triple_grad, qkv_mine).astype(BF16)
    one_back, triple_late, down_blocks, second_late, fc1_terms, fc2_w_grad = after(
        (one_back, triple_grad, down_blocks, second_late, fc1_terms, fc2_w_grad)
    )
    output = second + down_sums[:local] + b_down
    for block in down_blocks:
        output = output + block.astype(F32)
    output = output.astype(BF16)
    normed_one_grad = lax.psum_scatter(one_back, "seq", scatter_dimension=0, tiled=True)
    second_rows = gather_rows(second_late)
    qkv_terms = inner(normed_one_row, triple_late).reshape(nd, part, wide)
    qkv_low, second_rows = after((qkv_terms.astype(BF16), second_rows))
    qkv_blocks = [swap(index(qkv_low, dp_at ^ k), k) for k in range(1, nd)]
    attended_rows = jnp.concatenate(
        [index(attended_slices, dp_at)]
        + [swap(index(attended_slices, dp_at ^ k), k) for k in range(1, nd)],
        axis=0,
    )
    proj_terms = inner(attended_rows, second_rows).reshape(ns, small, features)
    proj_sums = core_sums(proj_terms)
    qkv_sum = index(qkv_terms, dp_at)
    for block in qkv_blocks:
        qkv_sum = qkv_sum + block.astype(F32)
    qkv_sum = qkv_sum.astype(BF16).reshape(ns, small, wide)
    normed_one_grad = normed_one_grad.astype(F32)
    through_one, ln1_g_grad, ln1_b_grad = norm_back(normed_one_grad, xhat_one, inverse_one, g_one)
    first_grad = second_grad + through_one
    first_low = first_grad.astype(BF16)
    first_low_rows = gather_rows(first_low)
    proj_w_grad = chip_sums(proj_sums)
    qkv_w_grad = seq_exchange(qkv_sum)
    first_low_rows, first_grad, proj_w_grad = after((first_low_rows, first_grad, proj_w_grad))
    skip_terms = inner(joined_here, first_low_rows).astype(BF16)
    skip_w_grad = lax.psum_scatter(skip_terms, "seq", scatter_dimension=0, tiled=True).astype(F32)
    skip_terms, first_low_rows, first_grad, fc1_terms, qkv_w_grad = after(
        (skip_terms, first_low_rows, first_grad, fc1_terms, qkv_w_grad)
    )
    fc1_terms = fc1_terms.reshape(nd, small, hidden_part)
    fc1_blocks = jnp.stack([fc1_terms[0]] + [swap(fc1_terms[k], k) for k in range(1, nd)])
    vector_grads = jnp.stack(
        [
            jnp.sum(first_grad, axis=0),
            ln1_g_grad,
            ln1_b_grad,
            jnp.sum(second_grad, axis=0),
            ln2_g_grad,
            ln2_b_grad,
            jnp.sum(grad_out.astype(F32), axis=0),
        ]
    )
    vector_grads = jnp.swapaxes(vector_grads.reshape(7, n, small), 0, 1).reshape(n, 7 * small)
    up_grads = up_sums.reshape(ns, hidden_units // n)
    up_grads = lax.dynamic_update_slice_in_dim(
        jnp.zeros((n, hidden_units // n), F32), up_grads, dp_at * ns, 0
    )
    vector_grads = jnp.concatenate([vector_grads, up_grads], axis=1)
    vector_grads = jnp.pad(vector_grads, ((0, 0), (0, padded - own_size)))
    vector_grads = lax.all_to_all(
        vector_grads.reshape(n, padded // 128, 128), ("dp", "seq"), 0, 0, tiled=True
    )
    joined_grad_part = times_transposed(first_low_rows, skip_part).astype(BF16)
    joined_grad_part = joined_grad_part.reshape(nd, local, joined_part)
    away = [joined_grad_part[0]] + [swap(joined_grad_part[k], k) for k in range(1, nd)]
    away = jnp.stack(away)
    joined_grad = jnp.concatenate(
        [index(away, dp_at ^ k) for k in range(nd)], axis=1
    ).astype(F32)
    fc1_w_grad = jnp.concatenate([index(fc1_blocks, dp_at ^ k) for k in range(nd)], axis=1)
    qkv_w_grad = (
        qkv_w_grad.reshape(ns, small, 3, head_cols).transpose(1, 2, 0, 3)
        .reshape(small, 3 * features)
    )
    vector_grads = jnp.sum(vector_grads, axis=0).reshape(padded)
    skip_b_grad, ln1_g_grad, ln1_b_grad, proj_b_grad, ln2_g_grad, ln2_b_grad, fc2_b_grad = (
        vector_grads[i * small : (i + 1) * small] for i in range(7)
    )
    fc1_b_grad = vector_grads[7 * small : own_size]
    return (
        output[None], joined_grad[None, :, :features], joined_grad[None, :, features:],
        skip_w_grad, qkv_w_grad.astype(F32), proj_w_grad,
        fc1_w_grad.astype(F32), fc2_w_grad.astype(F32),
        skip_b_grad, ln1_g_grad, ln1_b_grad, proj_b_grad, ln2_g_grad, ln2_b_grad,
        fc1_b_grad, fc2_b_grad,
    )


def solution(mesh):
    tokens = P("dp", "seq", None)
    matrix = P(("dp", "seq"), None)
    flat = P(("dp", "seq"))
    in_specs = (tokens, tokens, P("dp", None)) + (matrix,) * 5 + (flat,) * 8 + (tokens,)
    out_specs = (tokens,) * 3 + (matrix,) * 5 + (flat,) * 8
    return jax.shard_map(
        partial(on_device, mesh.shape["dp"], mesh.shape["seq"]),
        mesh=mesh, in_specs=in_specs, out_specs=out_specs, check_vma=False,
    )
```

```python
import math
from functools import partial

import jax
import jax.numpy as jnp
from jax import lax
from jax.experimental import pallas as pl
from jax.experimental.pallas import tpu as pltpu
from jax.sharding import PartitionSpec as P

HEADS = 16
HEAD_DIM = 72
EPSILON = 1e-05
NEGATIVE = -1e30
LOG2_E = math.log2(math.e)
WIDE = 128
F32 = jnp.float32
BF16 = jnp.bfloat16


def norm_pieces(hvals):
    centered = hvals - jnp.mean(hvals, axis=-1, keepdims=True)
    inverse = lax.rsqrt(jnp.mean(centered * centered, axis=-1, keepdims=True) + EPSILON)
    return centered * inverse, inverse


def norm_back(incoming, standardized, inverse, gain):
    scaled = incoming * gain
    passed = inverse * (
        scaled
        - jnp.mean(scaled, axis=-1, keepdims=True)
        - standardized * jnp.mean(scaled * standardized, axis=-1, keepdims=True)
    )
    return passed, jnp.sum(incoming * standardized, axis=0), jnp.sum(incoming, axis=0)


def segment_of(lengths_ref, places):
    running = jnp.int32(0)
    passed = jnp.zeros(places.shape, jnp.int32)
    for slot in range(lengths_ref.shape[1]):
        running = running + lengths_ref[0, slot]
        passed = passed + (running <= places).astype(jnp.int32)
    return passed


def same_item(lengths_ref, rows, columns, first_row):
    of_rows = first_row + lax.broadcasted_iota(jnp.int32, (rows, 1), 0)
    of_columns = lax.broadcasted_iota(jnp.int32, (1, columns), 1)
    return segment_of(lengths_ref, of_rows) == segment_of(lengths_ref, of_columns)


def dot(left, right):
    return jnp.dot(left, right, preferred_element_type=F32)


def inner(left, right):
    return lax.dot_general(left, right, (((0,), (0,)), ((), ())), preferred_element_type=F32)


def times_transposed(left, right):
    return lax.dot_general(left, right, (((1,), (1,)), ((), ())), preferred_element_type=F32)


def side_by_side(parts):
    return jnp.concatenate([part[:, :HEAD_DIM] for part in parts], axis=1)


def attend_kernel(
    heads, scale, q_ref, k_ref, v_ref, lengths_ref, out_ref, low_ref, lse_ref
):
    step = q_ref.shape[0]
    allowed = same_item(lengths_ref, step, k_ref.shape[0], pl.program_id(0) * step)
    lane = lax.broadcasted_iota(jnp.int32, (q_ref.shape[0], WIDE), 1)
    logs = jnp.zeros((q_ref.shape[0], WIDE), F32)
    outs = []
    for h in range(heads):
        at = slice(h * WIDE, (h + 1) * WIDE)
        logits = times_transposed(q_ref[:, at], k_ref[:, at]) * (scale * LOG2_E)
        logits = jnp.where(allowed, logits, NEGATIVE)
        top = jnp.max(logits, axis=1, keepdims=True)
        weights = jnp.exp2(logits - top)
        total = jnp.sum(weights, axis=1, keepdims=True)
        outs.append(dot(weights.astype(BF16), v_ref[:, at]) / total)
        out_ref[:, at] = outs[h]
        logs = jnp.where(lane == h, top + LOG2_E * jnp.log(total), logs)
    lse_ref[...] = jnp.transpose(logs)[:8]
    low_ref[...] = side_by_side(outs).astype(BF16)


def attend(triple, lengths, heads, scale):
    rows = triple.shape[0]
    wide = heads * WIDE
    step = 256 if rows % 256 == 0 else rows
    return pl.pallas_call(
        partial(attend_kernel, heads, scale),
        grid=(rows // step,),
        in_specs=[
            pl.BlockSpec((step, wide), lambda i: (i, 0)),
            pl.BlockSpec((rows, wide), lambda i: (0, 1)),
            pl.BlockSpec((rows, wide), lambda i: (0, 2)),
            pl.BlockSpec(memory_space=pltpu.SMEM),
        ],
        out_specs=[
            pl.BlockSpec((step, wide), lambda i: (i, 0)),
            pl.BlockSpec((step, heads * HEAD_DIM), lambda i: (i, 0)),
            pl.BlockSpec((8, step), lambda i: (0, i)),
        ],
        out_shape=[
            jax.ShapeDtypeStruct((rows, wide), F32),
            jax.ShapeDtypeStruct((rows, heads * HEAD_DIM), BF16),
            jax.ShapeDtypeStruct((8, rows), F32),
        ],
        compiler_params=pltpu.CompilerParams(vmem_limit_bytes=48 * 2**20),
        cost_estimate=pl.CostEstimate(
            flops=8 * rows * rows * wide,
            bytes_accessed=10 * rows * wide,
            transcendentals=heads * rows * rows,
        ),
    )(triple, triple, triple, lengths)


def attend_back_kernel(
    heads, scale, q_ref, k_ref, v_ref, out_grad_ref, out_ref, lse_ref, lengths_ref,
    dq_ref, dkv_ref, sum_ref, grad_ref, delta_ref,
):
    step = pl.program_id(0)

    @pl.when(step == 0)
    def _():
        sum_ref[...] = jnp.zeros_like(sum_ref)
        ones = jnp.ones((8, WIDE), F32)
        for h in range(heads):
            grad = out_grad_ref[:, h * HEAD_DIM : (h + 1) * HEAD_DIM]
            gap = jnp.zeros((grad.shape[0], WIDE - HEAD_DIM), BF16)
            grad = jnp.concatenate([grad, gap], axis=1)
            at = slice(h * WIDE, (h + 1) * WIDE)
            grad_ref[:, at] = grad
            delta = lax.dot_general(
                ones, grad.astype(F32) * out_ref[:, at], (((1,), (1,)), ((), ())),
                precision=lax.Precision.HIGHEST, preferred_element_type=F32,
            )
            delta_ref[h : h + 1, :] = delta[:1]

    block, rows = k_ref.shape[0], q_ref.shape[0]
    allowed = same_item(lengths_ref, block, rows, step * block)
    key_grads, value_grads = [], []
    for h in range(heads):
        at = slice(h * WIDE, (h + 1) * WIDE)
        queries, keys, out_grad = q_ref[:, at], k_ref[:, at], grad_ref[:, at]
        logits = times_transposed(keys, queries) * (scale * LOG2_E) - lse_ref[h : h + 1, :]
        probs = jnp.where(allowed, jnp.exp2(logits), 0.0)
        prob_grad = times_transposed(v_ref[:, at], out_grad)
        logit_grad = (probs * (prob_grad - delta_ref[h : h + 1, :])).astype(BF16)
        value_grads.append(dot(probs.astype(BF16), out_grad))
        key_grads.append(dot(logit_grad, queries) * scale)
        sum_ref[:, at] += inner(logit_grad, keys)
    dkv_ref[...] = side_by_side(key_grads + value_grads).astype(BF16)

    @pl.when(step == pl.num_programs(0) - 1)
    def _():
        dq_ref[...] = side_by_side(
            [sum_ref[:, h * WIDE : (h + 1) * WIDE] * scale for h in range(heads)]
        ).astype(BF16)


def attend_back(triple, out_grad, out, lse, lengths, heads, scale):
    rows = triple.shape[0]
    wide = heads * WIDE
    step = 256 if rows % 256 == 0 else rows
    whole = pl.BlockSpec((rows, wide), lambda i: (0, 0))
    row = pl.BlockSpec((8, rows), lambda i: (0, 0))
    return pl.pallas_call(
        partial(attend_back_kernel, heads, scale),
        grid=(rows // step,),
        in_specs=[
            whole,
            pl.BlockSpec((step, wide), lambda i: (i, 1)),
            pl.BlockSpec((step, wide), lambda i: (i, 2)),
            pl.BlockSpec((rows, heads * HEAD_DIM), lambda i: (0, 0)),
            whole,
            row,
            pl.BlockSpec(memory_space=pltpu.SMEM),
        ],
        out_specs=[
            pl.BlockSpec((rows, heads * HEAD_DIM), lambda i: (0, 0)),
            pl.BlockSpec((step, 2 * heads * HEAD_DIM), lambda i: (i, 0)),
        ],
        out_shape=[
            jax.ShapeDtypeStruct((rows, heads * HEAD_DIM), BF16),
            jax.ShapeDtypeStruct((rows, 2 * heads * HEAD_DIM), BF16),
        ],
        scratch_shapes=[
            pltpu.VMEM((rows, wide), F32),
            pltpu.VMEM((rows, wide), BF16),
            pltpu.VMEM((8, rows), F32),
        ],
        compiler_params=pltpu.CompilerParams(vmem_limit_bytes=48 * 2**20),
        cost_estimate=pl.CostEstimate(
            flops=20 * rows * rows * wide,
            bytes_accessed=14 * rows * wide,
            transcendentals=heads * rows * rows,
        ),
    )(triple, triple, triple, out_grad, out, lse, lengths)


def by_group_kernel(x_ref, w_ref, out_ref):
    groups, rows, columns = out_ref.shape
    product = times_transposed(x_ref[...], w_ref[...]).astype(BF16)
    for g in range(groups):
        out_ref[g] = product[:, g * columns : (g + 1) * columns]


def product_by_group(x, w, groups):
    rows, depth = x.shape
    columns = w.shape[0] // groups
    steps = 2
    return pl.pallas_call(
        by_group_kernel,
        grid=(steps,),
        in_specs=[
            pl.BlockSpec((rows, depth), lambda j: (0, 0)),
            pl.BlockSpec((w.shape[0] // steps, depth), lambda j: (j, 0)),
        ],
        out_specs=pl.BlockSpec((groups // steps, rows, columns), lambda j: (j, 0, 0)),
        out_shape=jax.ShapeDtypeStruct((groups, rows, columns), BF16),
        cost_estimate=pl.CostEstimate(
            flops=2 * rows * depth * w.shape[0],
            bytes_accessed=2 * depth * (rows + w.shape[0]) + 2 * rows * w.shape[0],
            transcendentals=0,
        ),
    )(x, w)


def gelu_kernel(rows_at_once, x_ref, up_ref, bias_ref, value_ref, slope_ref):
    for start in range(0, x_ref.shape[0], rows_at_once):
        at = pl.ds(start, rows_at_once)
        pre = dot(x_ref[at, :], up_ref[...]) + bias_ref[...]
        bell = jnp.exp(-0.5 * pre * pre)
        t = 1.0 / (1.0 + (0.3275911 * 0.5**0.5) * jnp.abs(pre))
        tail = 0.5 * 1.061405429
        for c in (-1.453152027, 1.421413741, -0.284496736, 0.254829592):
            tail = tail * t + 0.5 * c
        tail = tail * t * bell
        below = jnp.where(pre < 0.0, tail, 1.0 - tail)
        value_ref[at, :] = (pre * below).astype(BF16)
        slope_ref[at, :] = below + pre * bell * (0.5 / math.pi) ** 0.5


def gelu_of_matmul(x, up, bias):
    rows, depth = x.shape
    columns = up.shape[1]
    step = 384 if columns % 384 == 0 else columns
    block = pl.BlockSpec((rows, step), lambda j: (0, j))
    return pl.pallas_call(
        partial(gelu_kernel, 640 if rows % 640 == 0 else rows),
        grid=(columns // step,),
        in_specs=[
            pl.BlockSpec((rows, depth), lambda j: (0, 0)),
            pl.BlockSpec((depth, step), lambda j: (0, j)),
            pl.BlockSpec((1, step), lambda j: (0, j)),
        ],
        out_specs=[block, block],
        out_shape=[
            jax.ShapeDtypeStruct((rows, columns), BF16),
            jax.ShapeDtypeStruct((rows, columns), F32),
        ],
        compiler_params=pltpu.CompilerParams(vmem_limit_bytes=40 * 2**20),
        cost_estimate=pl.CostEstimate(
            flops=2 * rows * depth * columns,
            bytes_accessed=2 * depth * (rows + columns) + 6 * rows * columns,
            transcendentals=rows * columns,
        ),
    )(x, up, bias.reshape(1, columns))


def feed_back_kernel(
    local, grad_ref, up_ref, down_ref, slope_ref, low_ref, sums_ref, own_ref, *back_refs
):
    pre_grad = times_transposed(grad_ref[...], down_ref[...]) * slope_ref[...]
    sums_ref[...] = jnp.sum(pre_grad, axis=0, keepdims=True)
    low = pre_grad.astype(BF16)
    low_ref[...] = low
    back = times_transposed(low, up_ref[...])
    own_ref[...] = back[:local]
    for k, back_ref in enumerate(back_refs):
        back_ref[...] = back[(k + 1) * local : (k + 2) * local].astype(BF16)


def feed_back(grad, up, down, slope, local):
    rows, depth = grad.shape
    columns = up.shape[1]
    return pl.pallas_call(
        partial(feed_back_kernel, local),
        out_shape=[
            jax.ShapeDtypeStruct((rows, columns), BF16),
            jax.ShapeDtypeStruct((1, columns), F32),
            jax.ShapeDtypeStruct((local, depth), F32),
        ]
        + [jax.ShapeDtypeStruct((local, depth), BF16)] * (rows // local - 1),
        compiler_params=pltpu.CompilerParams(vmem_limit_bytes=52 * 2**20),
        cost_estimate=pl.CostEstimate(
            flops=4 * rows * depth * columns,
            bytes_accessed=4 * depth * columns + 6 * rows * columns + 4 * rows * depth,
            transcendentals=0,
        ),
    )(grad, up, down, slope)


def on_device(
    nd, ns,
    inputs, skipped, item_lengths,
    skip_w, qkv_w, proj_w, fc1_w, fc2_w,
    skip_b, ln1_g, ln1_b, proj_b, ln2_g, ln2_b, fc1_b, fc2_b,
    cotangent,
):
    _, local, features = inputs.shape
    hidden_units = fc1_w.shape[1]
    n = nd * ns
    row_len = local * ns
    heads = HEADS // ns
    head_cols = heads * HEAD_DIM
    wide = 3 * head_cols
    small = features // n
    scale = HEAD_DIM ** (-0.5)
    hidden_part = hidden_units // nd
    joined_part = 2 * features // nd
    part = features // nd
    places = ns // 2
    dp_at = lax.axis_index("dp")
    seq_at = lax.axis_index("seq")
    core = seq_at % 2
    after = lax.optimization_barrier

    def swap(v, k):
        return lax.ppermute(v, "dp", [(i, i ^ k) for i in range(nd)])

    def other_core(v):
        return lax.ppermute(v, "seq", [(i, i ^ 1) for i in range(ns)])

    def index(v, at, axis=0):
        return lax.dynamic_index_in_dim(v, at, axis, keepdims=False)

    def gather_rows(v):
        return jnp.concatenate([v] + [swap(v, k) for k in range(1, nd)], axis=0)

    def add_blocks(own, low):
        for k in range(1, nd):
            own = own + swap(low[k], k).astype(F32)
        return own

    def low_rows(partial_sums):
        return partial_sums.astype(BF16).reshape(nd, local, features)

    def widen(v):
        v = v.reshape(v.shape[0], v.shape[1] // HEAD_DIM, HEAD_DIM)
        return jnp.pad(v, ((0, 0), (0, 0), (0, WIDE - HEAD_DIM))).reshape(v.shape[0], -1)

    def seq_exchange(v):
        return lax.all_to_all(v, "seq", 0, 0, tiled=True)

    def core_sums(terms):
        terms = terms.reshape((places, 2) + terms.shape[1:])
        given = index(terms, 1 - core, 1).astype(BF16)
        kept = index(terms, core, 1).astype(F32)
        return (kept + other_core(given).astype(F32)).astype(BF16)

    def chip_sums(sums):
        groups = [[i * 2 + c for i in range(places)] for c in range(2)]
        terms = lax.all_to_all(sums, "seq", 0, 0, axis_index_groups=groups, tiled=True)
        return jnp.sum(terms.reshape(sums.shape).astype(F32), axis=0)

    skip_part = lax.all_gather(skip_w, "seq", axis=0, tiled=True)

    own_vectors = (skip_b, ln1_g, ln1_b, proj_b, ln2_g, ln2_b, fc2_b, fc1_b)
    packed = jnp.concatenate(own_vectors)
    own_size = packed.shape[0]
    padded = -(-own_size // 1024) * 1024
    packed = jnp.pad(packed, (0, padded - own_size)).reshape(padded // 128, 128)
    packed = jnp.broadcast_to(packed[None], (n,) + packed.shape)
    vectors = lax.all_to_all(packed, ("dp", "seq"), 0, 0, tiled=True)
    vectors = vectors.reshape(n, padded).astype(F32)

    joined_slices = jnp.stack(
        [
            half[:, at * joined_part : (at + 1) * joined_part]
            for half in (inputs[0], skipped[0])
            for at in range(nd // 2)
        ]
    )
    joined_here = jnp.concatenate(
        [index(joined_slices, dp_at)]
        + [swap(index(joined_slices, dp_at ^ k), k) for k in range(1, nd)],
        axis=0,
    )
    at = lax.broadcasted_iota(jnp.int32, (features, features), 0)
    block, row = at // small, at % small
    row = ((block % nd) ^ dp_at) * part + (block // nd) * small + row
    order = (row == lax.broadcasted_iota(jnp.int32, (features, features), 1)).astype(BF16)
    qkv_out = qkv_w.reshape(small, 3, ns, head_cols).transpose(2, 0, 1, 3).reshape(ns, small, wide)
    up_slices = jnp.swapaxes(fc1_w.reshape(small, nd, hidden_part), 0, 1)
    up_slices = jnp.concatenate(
        [index(up_slices, dp_at)] + [swap(index(up_slices, dp_at ^ k), k) for k in range(1, nd)],
        axis=0,
    )
    qkv_out, skip_part, joined_here, vectors, up_slices = after(
        (qkv_out, skip_part, joined_here, vectors, up_slices)
    )
    def vector(at):
        return vectors[:, at * small : (at + 1) * small].reshape(features)

    b_skip, g_one, b_one, b_proj, g_two, b_two, b_down = (vector(i) for i in range(7))
    up_bias = lax.dynamic_slice_in_dim(vectors[:, 7 * small : own_size], dp_at * ns, ns, 0)
    up_bias = up_bias.reshape(hidden_part)

    up_part = lax.all_gather(up_slices, "seq", axis=0, tiled=True)
    first_terms = dot(joined_here, skip_part)
    first = add_blocks(first_terms[:local], low_rows(first_terms)) + b_skip
    qkv_mine = seq_exchange(qkv_out).reshape(part, wide)
    xhat_one, inverse_one = norm_pieces(first)
    normed_one = (xhat_one * g_one + b_one).astype(BF16)
    normed_one, qkv_mine, own_proj = after((normed_one, qkv_mine, proj_w))
    normed_one_row = lax.all_gather(normed_one, "seq", axis=0, tiled=True)

    qkv_mine = lax.all_gather(qkv_mine, "dp", axis=0, tiled=True)
    qkv_mine, own_proj, grad_out = after((qkv_mine, own_proj, cotangent[0]))
    grad_out_rows = gather_rows(grad_out)
    proj_rows = lax.all_gather(own_proj, "seq", axis=0, tiled=True)
    half = part // 2
    own_half = lax.dynamic_slice_in_dim(proj_rows, core * half, half, 0)
    proj_halves = [swap(own_half, k) for k in range(1, nd)]
    normed_one_row, qkv_mine, qkv_wide, proj_rows, grad_out_rows, up_part = after(
        (normed_one_row, qkv_mine, widen(qkv_mine), proj_rows, grad_out_rows, up_part)
    )
    triple = dot(normed_one_row, qkv_wide).astype(BF16)
    attended, attended_low, lse = attend(triple, item_lengths, heads, scale)

    def heads_to_tokens(v):
        v = seq_exchange(v.reshape(ns, local, head_cols))
        return jnp.swapaxes(v, 0, 1).reshape(local, features)

    attended_low, proj_halves, proj_rows = after((attended_low, proj_halves, proj_rows))
    w_proj = lax.dynamic_update_slice_in_dim(
        jnp.zeros((features, features), BF16), proj_rows, dp_at * part, 0
    )
    for k in range(1, nd):
        place = (dp_at ^ k) * 2
        here = proj_halves[k - 1]
        there = other_core(here)
        w_proj = lax.dynamic_update_slice_in_dim(w_proj, here, (place + core) * half, 0)
        w_proj = lax.dynamic_update_slice_in_dim(w_proj, there, (place + 1 - core) * half, 0)
    attended_low = heads_to_tokens(attended_low)
    attended_low, grad_out_rows, w_proj = after((attended_low, grad_out_rows, w_proj))
    own_down, attended_low, up_part = after((fc2_w, attended_low, up_part))
    down_part = lax.all_gather(own_down, "seq", axis=0, tiled=True)
    second = first + dot(attended_low, w_proj) + b_proj
    xhat_two, inverse_two = norm_pieces(second)
    normed_two = (xhat_two * g_two + b_two).astype(BF16)

    normed_two_rows = gather_rows(normed_two)
    up_part = inner(order, up_part).astype(BF16)
    normed_two_rows, up_part = after((normed_two_rows, up_part))
    hidden, slope = gelu_of_matmul(normed_two_rows, up_part, up_bias)

    fc2_terms = inner(hidden, grad_out_rows).astype(BF16)
    fc2_w_grad = lax.psum_scatter(fc2_terms, "seq", scatter_dimension=0, tiled=True)
    slope, fc2_terms = after((slope, fc2_terms))
    pre_low, up_sums, normed_two_grad, *up_blocks = feed_back(
        grad_out_rows, up_part, down_part, slope, local
    )
    up_blocks = [swap(block, k + 1) for k, block in enumerate(up_blocks)]
    fc1_terms = inner(times_transposed(normed_two_rows, order).astype(BF16), pre_low).astype(BF16)
    for block in up_blocks:
        normed_two_grad = normed_two_grad + block.astype(F32)
    normed_two_grad, fc1_terms = after((normed_two_grad, fc1_terms))
    through_two, ln2_g_grad, ln2_b_grad = norm_back(normed_two_grad, xhat_two, inverse_two, g_two)
    second_grad = grad_out.astype(F32) + through_two
    second_low = second_grad.astype(BF16)
    attended_grad = product_by_group(second_low, w_proj, ns)
    attended_grad, second_late, hidden_late, attended_low, fc1_terms = after(
        (attended_grad, second_low, hidden, attended_low, fc1_terms)
    )
    fc1_terms = lax.psum_scatter(fc1_terms, "seq", scatter_dimension=0, tiled=True)
    attended_grad = seq_exchange(attended_grad).reshape(row_len, head_cols)
    down_sums = dot(hidden_late, down_part)
    attended_slices = jnp.swapaxes(attended_low.reshape(local, nd, part), 0, 1)
    down_blocks = low_rows(down_sums)
    down_blocks = [swap(down_blocks[k], k) for k in range(1, nd)]
    attended_grad, down_blocks[0], second_late, attended_slices = after(
        (attended_grad, down_blocks[0], second_late, attended_slices)
    )
    triple_grad = jnp.concatenate(
        attend_back(triple, attended_grad, attended, lse, item_lengths, heads, scale), axis=1
    )
    one_back = times_transposed(triple_grad, qkv_mine).astype(BF16)
    one_back, triple_late, down_blocks, second_late, fc1_terms, fc2_w_grad = after(
        (one_back, triple_grad, down_blocks, second_late, fc1_terms, fc2_w_grad)
    )
    output = second + down_sums[:local] + b_down
    for block in down_blocks:
        output = output + block.astype(F32)
    output = output.astype(BF16)
    normed_one_grad = lax.psum_scatter(one_back, "seq", scatter_dimension=0, tiled=True)
    second_rows = gather_rows(second_late)
    qkv_terms = inner(normed_one_row, triple_late).reshape(nd, part, wide)
    qkv_low, second_rows = after((qkv_terms.astype(BF16), second_rows))
    qkv_blocks = [swap(index(qkv_low, dp_at ^ k), k) for k in range(1, nd)]
    attended_rows = jnp.concatenate(
        [index(attended_slices, dp_at)]
        + [swap(index(attended_slices, dp_at ^ k), k) for k in range(1, nd)],
        axis=0,
    )
    proj_terms = inner(attended_rows, second_rows).reshape(ns, small, features)
    proj_sums = core_sums(proj_terms)
    qkv_sum = index(qkv_terms, dp_at)
    for block in qkv_blocks:
        qkv_sum = qkv_sum + block.astype(F32)
    qkv_sum = qkv_sum.astype(BF16).reshape(ns, small, wide)
    normed_one_grad = normed_one_grad.astype(F32)
    through_one, ln1_g_grad, ln1_b_grad = norm_back(normed_one_grad, xhat_one, inverse_one, g_one)
    first_grad = second_grad + through_one
    first_low = first_grad.astype(BF16)
    first_low_rows = gather_rows(first_low)
    proj_w_grad = chip_sums(proj_sums)
    qkv_w_grad = seq_exchange(qkv_sum)
    first_low_rows, first_grad, proj_w_grad = after((first_low_rows, first_grad, proj_w_grad))
    skip_terms = inner(joined_here, first_low_rows).astype(BF16)
    skip_w_grad = lax.psum_scatter(skip_terms, "seq", scatter_dimension=0, tiled=True).astype(F32)
    skip_terms, first_low_rows, first_grad, fc1_terms, qkv_w_grad = after(
        (skip_terms, first_low_rows, first_grad, fc1_terms, qkv_w_grad)
    )
    fc1_terms = fc1_terms.reshape(nd, small, hidden_part)
    fc1_blocks = jnp.stack([fc1_terms[0]] + [swap(fc1_terms[k], k) for k in range(1, nd)])
    vector_grads = jnp.stack(
        [
            jnp.sum(first_grad, axis=0),
            ln1_g_grad,
            ln1_b_grad,
            jnp.sum(second_grad, axis=0),
            ln2_g_grad,
            ln2_b_grad,
            jnp.sum(grad_out.astype(F32), axis=0),
        ]
    )
    vector_grads = jnp.swapaxes(vector_grads.reshape(7, n, small), 0, 1).reshape(n, 7 * small)
    up_grads = up_sums.reshape(ns, hidden_units // n)
    up_grads = lax.dynamic_update_slice_in_dim(
        jnp.zeros((n, hidden_units // n), F32), up_grads, dp_at * ns, 0
    )
    vector_grads = jnp.concatenate([vector_grads, up_grads], axis=1)
    vector_grads = jnp.pad(vector_grads, ((0, 0), (0, padded - own_size)))
    vector_grads = lax.all_to_all(
        vector_grads.reshape(n, padded // 128, 128), ("dp", "seq"), 0, 0, tiled=True
    )
    joined_grad_part = times_transposed(first_low_rows, skip_part).astype(BF16)
    joined_grad_part = joined_grad_part.reshape(nd, local, joined_part)
    away = [joined_grad_part[0]] + [swap(joined_grad_part[k], k) for k in range(1, nd)]
    away = jnp.stack(away)
    joined_grad = jnp.concatenate(
        [index(away, dp_at ^ k) for k in range(nd)], axis=1
    ).astype(F32)
    fc1_w_grad = jnp.concatenate([index(fc1_blocks, dp_at ^ k) for k in range(nd)], axis=1)
    qkv_w_grad = (
        qkv_w_grad.reshape(ns, small, 3, head_cols).transpose(1, 2, 0, 3)
        .reshape(small, 3 * features)
    )
    vector_grads = jnp.sum(vector_grads, axis=0).reshape(padded)
    skip_b_grad, ln1_g_grad, ln1_b_grad, proj_b_grad, ln2_g_grad, ln2_b_grad, fc2_b_grad = (
        vector_grads[i * small : (i + 1) * small] for i in range(7)
    )
    fc1_b_grad = vector_grads[7 * small : own_size]
    return (
        output[None], joined_grad[None, :, :features], joined_grad[None, :, features:],
        skip_w_grad, qkv_w_grad.astype(F32), proj_w_grad,
        fc1_w_grad.astype(F32), fc2_w_grad.astype(F32),
        skip_b_grad, ln1_g_grad, ln1_b_grad, proj_b_grad, ln2_g_grad, ln2_b_grad,
        fc1_b_grad, fc2_b_grad,
    )


def solution(mesh):
    tokens = P("dp", "seq", None)
    matrix = P(("dp", "seq"), None)
    flat = P(("dp", "seq"))
    in_specs = (tokens, tokens, P("dp", None)) + (matrix,) * 5 + (flat,) * 8 + (tokens,)
    out_specs = (tokens,) * 3 + (matrix,) * 5 + (flat,) * 8
    return jax.shard_map(
        partial(on_device, mesh.shape["dp"], mesh.shape["seq"]),
        mesh=mesh, in_specs=in_specs, out_specs=out_specs, check_vma=False,
    )
```

```python
import math
from functools import partial

import jax
import jax.numpy as jnp
from jax import lax
from jax.experimental import pallas as pl
from jax.experimental.pallas import tpu as pltpu
from jax.sharding import PartitionSpec as P

HEADS = 16
HEAD_DIM = 72
EPSILON = 1e-05
NEGATIVE = -1e30
LOG2_E = math.log2(math.e)
WIDE = 128
F32 = jnp.float32
BF16 = jnp.bfloat16


def norm_pieces(hvals):
    centered = hvals - jnp.mean(hvals, axis=-1, keepdims=True)
    inverse = lax.rsqrt(jnp.mean(centered * centered, axis=-1, keepdims=True) + EPSILON)
    return centered * inverse, inverse


def norm_back(incoming, standardized, inverse, gain):
    scaled = incoming * gain
    passed = inverse * (
        scaled
        - jnp.mean(scaled, axis=-1, keepdims=True)
        - standardized * jnp.mean(scaled * standardized, axis=-1, keepdims=True)
    )
    return passed, jnp.sum(incoming * standardized, axis=0), jnp.sum(incoming, axis=0)


def segment_of(lengths_ref, places):
    running = jnp.int32(0)
    passed = jnp.zeros(places.shape, jnp.int32)
    for slot in range(lengths_ref.shape[1]):
        running = running + lengths_ref[0, slot]
        passed = passed + (running <= places).astype(jnp.int32)
    return passed


def same_item(lengths_ref, rows, columns, first_row):
    of_rows = first_row + lax.broadcasted_iota(jnp.int32, (rows, 1), 0)
    of_columns = lax.broadcasted_iota(jnp.int32, (1, columns), 1)
    return segment_of(lengths_ref, of_rows) == segment_of(lengths_ref, of_columns)


def dot(left, right):
    return jnp.dot(left, right, preferred_element_type=F32)


def inner(left, right):
    return lax.dot_general(left, right, (((0,), (0,)), ((), ())), preferred_element_type=F32)


def times_transposed(left, right):
    return lax.dot_general(left, right, (((1,), (1,)), ((), ())), preferred_element_type=F32)


def side_by_side(parts):
    return jnp.concatenate([part[:, :HEAD_DIM] for part in parts], axis=1)


def attend_kernel(
    heads, scale, q_ref, k_ref, v_ref, lengths_ref, out_ref, low_ref, lse_ref
):
    step = q_ref.shape[0]
    allowed = same_item(lengths_ref, step, k_ref.shape[0], pl.program_id(0) * step)
    lane = lax.broadcasted_iota(jnp.int32, (q_ref.shape[0], WIDE), 1)
    logs = jnp.zeros((q_ref.shape[0], WIDE), F32)
    outs = []
    for h in range(heads):
        at = slice(h * WIDE, (h + 1) * WIDE)
        logits = times_transposed(q_ref[:, at], k_ref[:, at]) * (scale * LOG2_E)
        logits = jnp.where(allowed, logits, NEGATIVE)
        top = jnp.max(logits, axis=1, keepdims=True)
        weights = jnp.exp2(logits - top)
        total = jnp.sum(weights, axis=1, keepdims=True)
        outs.append(dot(weights.astype(BF16), v_ref[:, at]) / total)
        out_ref[:, at] = outs[h]
        logs = jnp.where(lane == h, top + LOG2_E * jnp.log(total), logs)
    lse_ref[...] = jnp.transpose(logs)[:8]
    low_ref[...] = side_by_side(outs).astype(BF16)


def attend(triple, lengths, heads, scale):
    rows = triple.shape[0]
    wide = heads * WIDE
    step = 256 if rows % 256 == 0 else rows
    return pl.pallas_call(
        partial(attend_kernel, heads, scale),
        grid=(rows // step,),
        in_specs=[
            pl.BlockSpec((step, wide), lambda i: (i, 0)),
            pl.BlockSpec((rows, wide), lambda i: (0, 1)),
            pl.BlockSpec((rows, wide), lambda i: (0, 2)),
            pl.BlockSpec(memory_space=pltpu.SMEM),
        ],
        out_specs=[
            pl.BlockSpec((step, wide), lambda i: (i, 0)),
            pl.BlockSpec((step, heads * HEAD_DIM), lambda i: (i, 0)),
            pl.BlockSpec((8, step), lambda i: (0, i)),
        ],
        out_shape=[
            jax.ShapeDtypeStruct((rows, wide), F32),
            jax.ShapeDtypeStruct((rows, heads * HEAD_DIM), BF16),
            jax.ShapeDtypeStruct((8, rows), F32),
        ],
        compiler_params=pltpu.CompilerParams(vmem_limit_bytes=48 * 2**20),
        cost_estimate=pl.CostEstimate(
            flops=8 * rows * rows * wide,
            bytes_accessed=10 * rows * wide,
            transcendentals=heads * rows * rows,
        ),
    )(triple, triple, triple, lengths)


def attend_back_kernel(
    heads, scale, q_ref, k_ref, v_ref, out_grad_ref, out_ref, lse_ref, lengths_ref,
    dq_ref, dkv_ref, sum_ref, grad_ref, delta_ref,
):
    step = pl.program_id(0)

    @pl.when(step == 0)
    def _():
        sum_ref[...] = jnp.zeros_like(sum_ref)
        ones = jnp.ones((8, WIDE), F32)
        for h in range(heads):
            grad = out_grad_ref[:, h * HEAD_DIM : (h + 1) * HEAD_DIM]
            gap = jnp.zeros((grad.shape[0], WIDE - HEAD_DIM), BF16)
            grad = jnp.concatenate([grad, gap], axis=1)
            at = slice(h * WIDE, (h + 1) * WIDE)
            grad_ref[:, at] = grad
            delta = lax.dot_general(
                ones, grad.astype(F32) * out_ref[:, at], (((1,), (1,)), ((), ())),
                precision=lax.Precision.HIGHEST, preferred_element_type=F32,
            )
            delta_ref[h : h + 1, :] = delta[:1]

    block, rows = k_ref.shape[0], q_ref.shape[0]
    allowed = same_item(lengths_ref, block, rows, step * block)
    key_grads, value_grads = [], []
    for h in range(heads):
        at = slice(h * WIDE, (h + 1) * WIDE)
        queries, keys, out_grad = q_ref[:, at], k_ref[:, at], grad_ref[:, at]
        logits = times_transposed(keys, queries) * (scale * LOG2_E) - lse_ref[h : h + 1, :]
        probs = jnp.where(allowed, jnp.exp2(logits), 0.0)
        prob_grad = times_transposed(v_ref[:, at], out_grad)
        logit_grad = (probs * (prob_grad - delta_ref[h : h + 1, :])).astype(BF16)
        value_grads.append(dot(probs.astype(BF16), out_grad))
        key_grads.append(dot(logit_grad, queries) * scale)
        sum_ref[:, at] += inner(logit_grad, keys)
    dkv_ref[...] = side_by_side(key_grads + value_grads).astype(BF16)

    @pl.when(step == pl.num_programs(0) - 1)
    def _():
        dq_ref[...] = side_by_side(
            [sum_ref[:, h * WIDE : (h + 1) * WIDE] * scale for h in range(heads)]
        ).astype(BF16)


def attend_back(triple, out_grad, out, lse, lengths, heads, scale):
    rows = triple.shape[0]
    wide = heads * WIDE
    step = 256 if rows % 256 == 0 else rows
    whole = pl.BlockSpec((rows, wide), lambda i: (0, 0))
    row = pl.BlockSpec((8, rows), lambda i: (0, 0))
    return pl.pallas_call(
        partial(attend_back_kernel, heads, scale),
        grid=(rows // step,),
        in_specs=[
            whole,
            pl.BlockSpec((step, wide), lambda i: (i, 1)),
            pl.BlockSpec((step, wide), lambda i: (i, 2)),
            pl.BlockSpec((rows, heads * HEAD_DIM), lambda i: (0, 0)),
            whole,
            row,
            pl.BlockSpec(memory_space=pltpu.SMEM),
        ],
        out_specs=[
            pl.BlockSpec((rows, heads * HEAD_DIM), lambda i: (0, 0)),
            pl.BlockSpec((step, 2 * heads * HEAD_DIM), lambda i: (i, 0)),
        ],
        out_shape=[
            jax.ShapeDtypeStruct((rows, heads * HEAD_DIM), BF16),
            jax.ShapeDtypeStruct((rows, 2 * heads * HEAD_DIM), BF16),
        ],
        scratch_shapes=[
            pltpu.VMEM((rows, wide), F32),
            pltpu.VMEM((rows, wide), BF16),
            pltpu.VMEM((8, rows), F32),
        ],
        compiler_params=pltpu.CompilerParams(vmem_limit_bytes=48 * 2**20),
        cost_estimate=pl.CostEstimate(
            flops=20 * rows * rows * wide,
            bytes_accessed=14 * rows * wide,
            transcendentals=heads * rows * rows,
        ),
    )(triple, triple, triple, out_grad, out, lse, lengths)


def by_group_kernel(x_ref, w_ref, out_ref):
    groups, rows, columns = out_ref.shape
    product = times_transposed(x_ref[...], w_ref[...]).astype(BF16)
    for g in range(groups):
        out_ref[g] = product[:, g * columns : (g + 1) * columns]


def product_by_group(x, w, groups):
    rows, depth = x.shape
    columns = w.shape[0] // groups
    steps = 2
    return pl.pallas_call(
        by_group_kernel,
        grid=(steps,),
        in_specs=[
            pl.BlockSpec((rows, depth), lambda j: (0, 0)),
            pl.BlockSpec((w.shape[0] // steps, depth), lambda j: (j, 0)),
        ],
        out_specs=pl.BlockSpec((groups // steps, rows, columns), lambda j: (j, 0, 0)),
        out_shape=jax.ShapeDtypeStruct((groups, rows, columns), BF16),
        cost_estimate=pl.CostEstimate(
            flops=2 * rows * depth * w.shape[0],
            bytes_accessed=2 * depth * (rows + w.shape[0]) + 2 * rows * w.shape[0],
            transcendentals=0,
        ),
    )(x, w)


def gelu_kernel(rows_at_once, x_ref, up_ref, bias_ref, value_ref, slope_ref):
    for start in range(0, x_ref.shape[0], rows_at_once):
        at = pl.ds(start, rows_at_once)
        pre = dot(x_ref[at, :], up_ref[...]) + bias_ref[...]
        bell = jnp.exp(-0.5 * pre * pre)
        t = 1.0 / (1.0 + (0.3275911 * 0.5**0.5) * jnp.abs(pre))
        tail = 0.5 * 1.061405429
        for c in (-1.453152027, 1.421413741, -0.284496736, 0.254829592):
            tail = tail * t + 0.5 * c
        tail = tail * t * bell
        below = jnp.where(pre < 0.0, tail, 1.0 - tail)
        value_ref[at, :] = (pre * below).astype(BF16)
        slope_ref[at, :] = below + pre * bell * (0.5 / math.pi) ** 0.5


def gelu_of_matmul(x, up, bias):
    rows, depth = x.shape
    columns = up.shape[1]
    step = 384 if columns % 384 == 0 else columns
    block = pl.BlockSpec((rows, step), lambda j: (0, j))
    return pl.pallas_call(
        partial(gelu_kernel, 640 if rows % 640 == 0 else rows),
        grid=(columns // step,),
        in_specs=[
            pl.BlockSpec((rows, depth), lambda j: (0, 0)),
            pl.BlockSpec((depth, step), lambda j: (0, j)),
            pl.BlockSpec((1, step), lambda j: (0, j)),
        ],
        out_specs=[block, block],
        out_shape=[
            jax.ShapeDtypeStruct((rows, columns), BF16),
            jax.ShapeDtypeStruct((rows, columns), F32),
        ],
        compiler_params=pltpu.CompilerParams(vmem_limit_bytes=40 * 2**20),
        cost_estimate=pl.CostEstimate(
            flops=2 * rows * depth * columns,
            bytes_accessed=2 * depth * (rows + columns) + 6 * rows * columns,
            transcendentals=rows * columns,
        ),
    )(x, up, bias.reshape(1, columns))


def feed_back_kernel(
    local, grad_ref, up_ref, down_ref, slope_ref, low_ref, sums_ref, own_ref, *back_refs
):
    pre_grad = times_transposed(grad_ref[...], down_ref[...]) * slope_ref[...]
    sums_ref[...] = jnp.sum(pre_grad, axis=0, keepdims=True)
    low = pre_grad.astype(BF16)
    low_ref[...] = low
    back = times_transposed(low, up_ref[...])
    own_ref[...] = back[:local]
    for k, back_ref in enumerate(back_refs):
        back_ref[...] = back[(k + 1) * local : (k + 2) * local].astype(BF16)


def feed_back(grad, up, down, slope, local):
    rows, depth = grad.shape
    columns = up.shape[1]
    return pl.pallas_call(
        partial(feed_back_kernel, local),
        out_shape=[
            jax.ShapeDtypeStruct((rows, columns), BF16),
            jax.ShapeDtypeStruct((1, columns), F32),
            jax.ShapeDtypeStruct((local, depth), F32),
        ]
        + [jax.ShapeDtypeStruct((local, depth), BF16)] * (rows // local - 1),
        compiler_params=pltpu.CompilerParams(vmem_limit_bytes=52 * 2**20),
        cost_estimate=pl.CostEstimate(
            flops=4 * rows * depth * columns,
            bytes_accessed=4 * depth * columns + 6 * rows * columns + 4 * rows * depth,
            transcendentals=0,
        ),
    )(grad, up, down, slope)


def on_device(
    nd, ns,
    inputs, skipped, item_lengths,
    skip_w, qkv_w, proj_w, fc1_w, fc2_w,
    skip_b, ln1_g, ln1_b, proj_b, ln2_g, ln2_b, fc1_b, fc2_b,
    cotangent,
):
    _, local, features = inputs.shape
    hidden_units = fc1_w.shape[1]
    n = nd * ns
    row_len = local * ns
    heads = HEADS // ns
    head_cols = heads * HEAD_DIM
    wide = 3 * head_cols
    small = features // n
    scale = HEAD_DIM ** (-0.5)
    hidden_part = hidden_units // nd
    joined_part = 2 * features // nd
    part = features // nd
    places = ns // 2
    dp_at = lax.axis_index("dp")
    seq_at = lax.axis_index("seq")
    core = seq_at % 2
    after = lax.optimization_barrier

    def swap(v, k):
        return lax.ppermute(v, "dp", [(i, i ^ k) for i in range(nd)])

    def other_core(v):
        return lax.ppermute(v, "seq", [(i, i ^ 1) for i in range(ns)])

    def index(v, at, axis=0):
        return lax.dynamic_index_in_dim(v, at, axis, keepdims=False)

    def gather_rows(v):
        return jnp.concatenate([v] + [swap(v, k) for k in range(1, nd)], axis=0)

    def add_blocks(own, low):
        for k in range(1, nd):
            own = own + swap(low[k], k).astype(F32)
        return own

    def low_rows(partial_sums):
        return partial_sums.astype(BF16).reshape(nd, local, features)

    def widen(v):
        v = v.reshape(v.shape[0], v.shape[1] // HEAD_DIM, HEAD_DIM)
        return jnp.pad(v, ((0, 0), (0, 0), (0, WIDE - HEAD_DIM))).reshape(v.shape[0], -1)

    def seq_exchange(v):
        return lax.all_to_all(v, "seq", 0, 0, tiled=True)

    def core_sums(terms):
        terms = terms.reshape((places, 2) + terms.shape[1:])
        given = index(terms, 1 - core, 1).astype(BF16)
        kept = index(terms, core, 1).astype(F32)
        return (kept + other_core(given).astype(F32)).astype(BF16)

    def chip_sums(sums):
        groups = [[i * 2 + c for i in range(places)] for c in range(2)]
        terms = lax.all_to_all(sums, "seq", 0, 0, axis_index_groups=groups, tiled=True)
        return jnp.sum(terms.reshape(sums.shape).astype(F32), axis=0)

    skip_part = lax.all_gather(skip_w, "seq", axis=0, tiled=True)

    own_vectors = (skip_b, ln1_g, ln1_b, proj_b, ln2_g, ln2_b, fc2_b, fc1_b)
    packed = jnp.concatenate(own_vectors)
    own_size = packed.shape[0]
    padded = -(-own_size // 1024) * 1024
    packed = jnp.pad(packed, (0, padded - own_size)).reshape(padded // 128, 128)
    packed = jnp.broadcast_to(packed[None], (n,) + packed.shape)
    vectors = lax.all_to_all(packed, ("dp", "seq"), 0, 0, tiled=True)
    vectors = vectors.reshape(n, padded).astype(F32)

    joined_slices = jnp.stack(
        [
            half[:, at * joined_part : (at + 1) * joined_part]
            for half in (inputs[0], skipped[0])
            for at in range(nd // 2)
        ]
    )
    joined_here = jnp.concatenate(
        [index(joined_slices, dp_at)]
        + [swap(index(joined_slices, dp_at ^ k), k) for k in range(1, nd)],
        axis=0,
    )
    at = lax.broadcasted_iota(jnp.int32, (features, features), 0)
    block, row = at // small, at % small
    row = ((block % nd) ^ dp_at) * part + (block // nd) * small + row
    order = (row == lax.broadcasted_iota(jnp.int32, (features, features), 1)).astype(BF16)
    qkv_out = qkv_w.reshape(small, 3, ns, head_cols).transpose(2, 0, 1, 3).reshape(ns, small, wide)
    up_slices = jnp.swapaxes(fc1_w.reshape(small, nd, hidden_part), 0, 1)
    up_slices = jnp.concatenate(
        [index(up_slices, dp_at)] + [swap(index(up_slices, dp_at ^ k), k) for k in range(1, nd)],
        axis=0,
    )
    qkv_out, skip_part, joined_here, vectors, up_slices = after(
        (qkv_out, skip_part, joined_here, vectors, up_slices)
    )
    def vector(at):
        return vectors[:, at * small : (at + 1) * small].reshape(features)

    b_skip, g_one, b_one, b_proj, g_two, b_two, b_down = (vector(i) for i in range(7))
    up_bias = lax.dynamic_slice_in_dim(vectors[:, 7 * small : own_size], dp_at * ns, ns, 0)
    up_bias = up_bias.reshape(hidden_part)

    first_terms = dot(joined_here, skip_part)
    first = add_blocks(first_terms[:local], low_rows(first_terms)) + b_skip
    qkv_mine = seq_exchange(qkv_out).reshape(part, wide)
    xhat_one, inverse_one = norm_pieces(first)
    normed_one = (xhat_one * g_one + b_one).astype(BF16)
    normed_one, qkv_mine, own_proj = after((normed_one, qkv_mine, proj_w))
    normed_one_row = lax.all_gather(normed_one, "seq", axis=0, tiled=True)

    qkv_mine = lax.all_gather(qkv_mine, "dp", axis=0, tiled=True)
    qkv_mine, own_proj, grad_out = after((qkv_mine, own_proj, cotangent[0]))
    grad_out_rows = gather_rows(grad_out)
    proj_rows = lax.all_gather(own_proj, "seq", axis=0, tiled=True)
    half = part // 2
    own_half = lax.dynamic_slice_in_dim(proj_rows, core * half, half, 0)
    proj_halves = [swap(own_half, k) for k in range(1, nd)]
    normed_one_row, qkv_mine, qkv_wide, proj_rows, grad_out_rows = after(
        (normed_one_row, qkv_mine, widen(qkv_mine), proj_rows, grad_out_rows)
    )
    up_part = lax.all_gather(up_slices, "seq", axis=0, tiled=True)
    triple = dot(normed_one_row, qkv_wide).astype(BF16)
    attended, attended_low, lse = attend(triple, item_lengths, heads, scale)

    def heads_to_tokens(v):
        v = seq_exchange(v.reshape(ns, local, head_cols))
        return jnp.swapaxes(v, 0, 1).reshape(local, features)

    attended_low, proj_halves, proj_rows = after((attended_low, proj_halves, proj_rows))
    w_proj = lax.dynamic_update_slice_in_dim(
        jnp.zeros((features, features), BF16), proj_rows, dp_at * part, 0
    )
    for k in range(1, nd):
        place = (dp_at ^ k) * 2
        here = proj_halves[k - 1]
        there = other_core(here)
        w_proj = lax.dynamic_update_slice_in_dim(w_proj, here, (place + core) * half, 0)
        w_proj = lax.dynamic_update_slice_in_dim(w_proj, there, (place + 1 - core) * half, 0)
    attended_low = heads_to_tokens(attended_low)
    attended_low, grad_out_rows, w_proj = after((attended_low, grad_out_rows, w_proj))
    own_down, attended_low, up_part = after((fc2_w, attended_low, up_part))
    down_part = lax.all_gather(own_down, "seq", axis=0, tiled=True)
    second = first + dot(attended_low, w_proj) + b_proj
    xhat_two, inverse_two = norm_pieces(second)
    normed_two = (xhat_two * g_two + b_two).astype(BF16)

    normed_two_rows = gather_rows(normed_two)
    up_part = inner(order, up_part).astype(BF16)
    normed_two_rows, up_part = after((normed_two_rows, up_part))
    hidden, slope = gelu_of_matmul(normed_two_rows, up_part, up_bias)

    fc2_terms = inner(hidden, grad_out_rows).astype(BF16)
    fc2_w_grad = lax.psum_scatter(fc2_terms, "seq", scatter_dimension=0, tiled=True)
    slope, fc2_terms = after((slope, fc2_terms))
    pre_low, up_sums, normed_two_grad, *up_blocks = feed_back(
        grad_out_rows, up_part, down_part, slope, local
    )
    up_blocks = [swap(block, k + 1) for k, block in enumerate(up_blocks)]
    fc1_terms = inner(times_transposed(normed_two_rows, order).astype(BF16), pre_low).astype(BF16)
    for block in up_blocks:
        normed_two_grad = normed_two_grad + block.astype(F32)
    normed_two_grad, fc1_terms = after((normed_two_grad, fc1_terms))
    through_two, ln2_g_grad, ln2_b_grad = norm_back(normed_two_grad, xhat_two, inverse_two, g_two)
    second_grad = grad_out.astype(F32) + through_two
    second_low = second_grad.astype(BF16)
    attended_grad = product_by_group(second_low, w_proj, ns)
    attended_grad, second_late, hidden_late, attended_low, fc1_terms = after(
        (attended_grad, second_low, hidden, attended_low, fc1_terms)
    )
    fc1_terms = lax.psum_scatter(fc1_terms, "seq", scatter_dimension=0, tiled=True)
    attended_grad = seq_exchange(attended_grad).reshape(row_len, head_cols)
    down_sums = dot(hidden_late, down_part)
    attended_slices = jnp.swapaxes(attended_low.reshape(local, nd, part), 0, 1)
    down_blocks = low_rows(down_sums)
    down_blocks = [swap(down_blocks[k], k) for k in range(1, nd)]
    attended_grad, down_blocks[0], second_late, attended_slices = after(
        (attended_grad, down_blocks[0], second_late, attended_slices)
    )
    triple_grad = jnp.concatenate(
        attend_back(triple, attended_grad, attended, lse, item_lengths, heads, scale), axis=1
    )
    one_back = times_transposed(triple_grad, qkv_mine).astype(BF16)
    one_back, triple_late, down_blocks, second_late, fc1_terms, fc2_w_grad = after(
        (one_back, triple_grad, down_blocks, second_late, fc1_terms, fc2_w_grad)
    )
    output = second + down_sums[:local] + b_down
    for block in down_blocks:
        output = output + block.astype(F32)
    output = output.astype(BF16)
    normed_one_grad = lax.psum_scatter(one_back, "seq", scatter_dimension=0, tiled=True)
    second_rows = gather_rows(second_late)
    qkv_terms = inner(normed_one_row, triple_late).reshape(nd, part, wide)
    qkv_low, second_rows = after((qkv_terms.astype(BF16), second_rows))
    qkv_blocks = [swap(index(qkv_low, dp_at ^ k), k) for k in range(1, nd)]
    attended_rows = jnp.concatenate(
        [index(attended_slices, dp_at)]
        + [swap(index(attended_slices, dp_at ^ k), k) for k in range(1, nd)],
        axis=0,
    )
    proj_terms = inner(attended_rows, second_rows).reshape(ns, small, features)
    proj_sums = core_sums(proj_terms)
    qkv_sum = index(qkv_terms, dp_at)
    for block in qkv_blocks:
        qkv_sum = qkv_sum + block.astype(F32)
    qkv_sum = qkv_sum.astype(BF16).reshape(ns, small, wide)
    normed_one_grad = normed_one_grad.astype(F32)
    through_one, ln1_g_grad, ln1_b_grad = norm_back(normed_one_grad, xhat_one, inverse_one, g_one)
    first_grad = second_grad + through_one
    first_low = first_grad.astype(BF16)
    first_low_rows = gather_rows(first_low)
    proj_w_grad = chip_sums(proj_sums)
    qkv_w_grad = seq_exchange(qkv_sum)
    first_low_rows, first_grad, proj_w_grad = after((first_low_rows, first_grad, proj_w_grad))
    skip_terms = inner(joined_here, first_low_rows).astype(BF16)
    skip_w_grad = lax.psum_scatter(skip_terms, "seq", scatter_dimension=0, tiled=True).astype(F32)
    skip_terms, first_low_rows, first_grad, fc1_terms, qkv_w_grad = after(
        (skip_terms, first_low_rows, first_grad, fc1_terms, qkv_w_grad)
    )
    fc1_terms = fc1_terms.reshape(nd, small, hidden_part)
    fc1_blocks = jnp.stack([fc1_terms[0]] + [swap(fc1_terms[k], k) for k in range(1, nd)])
    vector_grads = jnp.stack(
        [
            jnp.sum(first_grad, axis=0),
            ln1_g_grad,
            ln1_b_grad,
            jnp.sum(second_grad, axis=0),
            ln2_g_grad,
            ln2_b_grad,
            jnp.sum(grad_out.astype(F32), axis=0),
        ]
    )
    vector_grads = jnp.swapaxes(vector_grads.reshape(7, n, small), 0, 1).reshape(n, 7 * small)
    up_grads = up_sums.reshape(ns, hidden_units // n)
    up_grads = lax.dynamic_update_slice_in_dim(
        jnp.zeros((n, hidden_units // n), F32), up_grads, dp_at * ns, 0
    )
    vector_grads = jnp.concatenate([vector_grads, up_grads], axis=1)
    vector_grads = jnp.pad(vector_grads, ((0, 0), (0, padded - own_size)))
    vector_grads = lax.all_to_all(
        vector_grads.reshape(n, padded // 128, 128), ("dp", "seq"), 0, 0, tiled=True
    )
    joined_grad_part = times_transposed(first_low_rows, skip_part).astype(BF16)
    joined_grad_part = joined_grad_part.reshape(nd, local, joined_part)
    away = [joined_grad_part[0]] + [swap(joined_grad_part[k], k) for k in range(1, nd)]
    away = jnp.stack(away)
    joined_grad = jnp.concatenate(
        [index(away, dp_at ^ k) for k in range(nd)], axis=1
    ).astype(F32)
    fc1_w_grad = jnp.concatenate([index(fc1_blocks, dp_at ^ k) for k in range(nd)], axis=1)
    qkv_w_grad = (
        qkv_w_grad.reshape(ns, small, 3, head_cols).transpose(1, 2, 0, 3)
        .reshape(small, 3 * features)
    )
    vector_grads = jnp.sum(vector_grads, axis=0).reshape(padded)
    skip_b_grad, ln1_g_grad, ln1_b_grad, proj_b_grad, ln2_g_grad, ln2_b_grad, fc2_b_grad = (
        vector_grads[i * small : (i + 1) * small] for i in range(7)
    )
    fc1_b_grad = vector_grads[7 * small : own_size]
    return (
        output[None], joined_grad[None, :, :features], joined_grad[None, :, features:],
        skip_w_grad, qkv_w_grad.astype(F32), proj_w_grad,
        fc1_w_grad.astype(F32), fc2_w_grad.astype(F32),
        skip_b_grad, ln1_g_grad, ln1_b_grad, proj_b_grad, ln2_g_grad, ln2_b_grad,
        fc1_b_grad, fc2_b_grad,
    )


def solution(mesh):
    tokens = P("dp", "seq", None)
    matrix = P(("dp", "seq"), None)
    flat = P(("dp", "seq"))
    in_specs = (tokens, tokens, P("dp", None)) + (matrix,) * 5 + (flat,) * 8 + (tokens,)
    out_specs = (tokens,) * 3 + (matrix,) * 5 + (flat,) * 8
    return jax.shard_map(
        partial(on_device, mesh.shape["dp"], mesh.shape["seq"]),
        mesh=mesh, in_specs=in_specs, out_specs=out_specs, check_vma=False,
    )
```

```python
import math
from functools import partial

import jax
import jax.numpy as jnp
from jax import lax
from jax.experimental import pallas as pl
from jax.experimental.pallas import tpu as pltpu
from jax.sharding import PartitionSpec as P

HEADS = 16
HEAD_DIM = 72
EPSILON = 1e-05
NEGATIVE = -1e30
LOG2_E = math.log2(math.e)
WIDE = 128
F32 = jnp.float32
BF16 = jnp.bfloat16


def norm_pieces(hvals):
    centered = hvals - jnp.mean(hvals, axis=-1, keepdims=True)
    inverse = lax.rsqrt(jnp.mean(centered * centered, axis=-1, keepdims=True) + EPSILON)
    return centered * inverse, inverse


def norm_back(incoming, standardized, inverse, gain):
    scaled = incoming * gain
    passed = inverse * (
        scaled
        - jnp.mean(scaled, axis=-1, keepdims=True)
        - standardized * jnp.mean(scaled * standardized, axis=-1, keepdims=True)
    )
    return passed, jnp.sum(incoming * standardized, axis=0), jnp.sum(incoming, axis=0)


def segment_of(lengths_ref, places):
    running = jnp.int32(0)
    passed = jnp.zeros(places.shape, jnp.int32)
    for slot in range(lengths_ref.shape[1]):
        running = running + lengths_ref[0, slot]
        passed = passed + (running <= places).astype(jnp.int32)
    return passed


def same_item(lengths_ref, rows, columns, first_row):
    of_rows = first_row + lax.broadcasted_iota(jnp.int32, (rows, 1), 0)
    of_columns = lax.broadcasted_iota(jnp.int32, (1, columns), 1)
    return segment_of(lengths_ref, of_rows) == segment_of(lengths_ref, of_columns)


def dot(left, right):
    return jnp.dot(left, right, preferred_element_type=F32)


def inner(left, right):
    return lax.dot_general(left, right, (((0,), (0,)), ((), ())), preferred_element_type=F32)


def times_transposed(left, right):
    return lax.dot_general(left, right, (((1,), (1,)), ((), ())), preferred_element_type=F32)


def side_by_side(parts):
    return jnp.concatenate([part[:, :HEAD_DIM] for part in parts], axis=1)


def attend_kernel(
    heads, scale, q_ref, k_ref, v_ref, lengths_ref, out_ref, low_ref, lse_ref
):
    step = q_ref.shape[0]
    allowed = same_item(lengths_ref, step, k_ref.shape[0], pl.program_id(0) * step)
    lane = lax.broadcasted_iota(jnp.int32, (q_ref.shape[0], WIDE), 1)
    logs = jnp.zeros((q_ref.shape[0], WIDE), F32)
    outs = []
    for h in range(heads):
        at = slice(h * WIDE, (h + 1) * WIDE)
        logits = times_transposed(q_ref[:, at], k_ref[:, at]) * (scale * LOG2_E)
        logits = jnp.where(allowed, logits, NEGATIVE)
        top = jnp.max(logits, axis=1, keepdims=True)
        weights = jnp.exp2(logits - top)
        total = jnp.sum(weights, axis=1, keepdims=True)
        outs.append(dot(weights.astype(BF16), v_ref[:, at]) / total)
        out_ref[:, at] = outs[h]
        logs = jnp.where(lane == h, top + LOG2_E * jnp.log(total), logs)
    lse_ref[...] = jnp.transpose(logs)[:8]
    low_ref[...] = side_by_side(outs).astype(BF16)


def attend(triple, lengths, heads, scale):
    rows = triple.shape[0]
    wide = heads * WIDE
    step = 256 if rows % 256 == 0 else rows
    return pl.pallas_call(
        partial(attend_kernel, heads, scale),
        grid=(rows // step,),
        in_specs=[
            pl.BlockSpec((step, wide), lambda i: (i, 0)),
            pl.BlockSpec((rows, wide), lambda i: (0, 1)),
            pl.BlockSpec((rows, wide), lambda i: (0, 2)),
            pl.BlockSpec(memory_space=pltpu.SMEM),
        ],
        out_specs=[
            pl.BlockSpec((step, wide), lambda i: (i, 0)),
            pl.BlockSpec((step, heads * HEAD_DIM), lambda i: (i, 0)),
            pl.BlockSpec((8, step), lambda i: (0, i)),
        ],
        out_shape=[
            jax.ShapeDtypeStruct((rows, wide), F32),
            jax.ShapeDtypeStruct((rows, heads * HEAD_DIM), BF16),
            jax.ShapeDtypeStruct((8, rows), F32),
        ],
        compiler_params=pltpu.CompilerParams(vmem_limit_bytes=48 * 2**20),
        cost_estimate=pl.CostEstimate(
            flops=8 * rows * rows * wide,
            bytes_accessed=10 * rows * wide,
            transcendentals=heads * rows * rows,
        ),
    )(triple, triple, triple, lengths)


def attend_back_kernel(
    heads, scale, q_ref, k_ref, v_ref, out_grad_ref, out_ref, lse_ref, lengths_ref,
    dq_ref, dkv_ref, sum_ref, grad_ref, delta_ref,
):
    step = pl.program_id(0)

    @pl.when(step == 0)
    def _():
        sum_ref[...] = jnp.zeros_like(sum_ref)
        ones = jnp.ones((8, WIDE), F32)
        for h in range(heads):
            grad = out_grad_ref[:, h * HEAD_DIM : (h + 1) * HEAD_DIM]
            gap = jnp.zeros((grad.shape[0], WIDE - HEAD_DIM), BF16)
            grad = jnp.concatenate([grad, gap], axis=1)
            at = slice(h * WIDE, (h + 1) * WIDE)
            grad_ref[:, at] = grad
            delta = lax.dot_general(
                ones, grad.astype(F32) * out_ref[:, at], (((1,), (1,)), ((), ())),
                precision=lax.Precision.HIGHEST, preferred_element_type=F32,
            )
            delta_ref[h : h + 1, :] = delta[:1]

    block, rows = k_ref.shape[0], q_ref.shape[0]
    allowed = same_item(lengths_ref, block, rows, step * block)
    key_grads, value_grads = [], []
    for h in range(heads):
        at = slice(h * WIDE, (h + 1) * WIDE)
        queries, keys, out_grad = q_ref[:, at], k_ref[:, at], grad_ref[:, at]
        logits = times_transposed(keys, queries) * (scale * LOG2_E) - lse_ref[h : h + 1, :]
        probs = jnp.where(allowed, jnp.exp2(logits), 0.0)
        prob_grad = times_transposed(v_ref[:, at], out_grad)
        logit_grad = (probs * (prob_grad - delta_ref[h : h + 1, :])).astype(BF16)
        value_grads.append(dot(probs.astype(BF16), out_grad))
        key_grads.append(dot(logit_grad, queries) * scale)
        sum_ref[:, at] += inner(logit_grad, keys)
    dkv_ref[...] = side_by_side(key_grads + value_grads).astype(BF16)

    @pl.when(step == pl.num_programs(0) - 1)
    def _():
        dq_ref[...] = side_by_side(
            [sum_ref[:, h * WIDE : (h + 1) * WIDE] * scale for h in range(heads)]
        ).astype(BF16)


def attend_back(triple, out_grad, out, lse, lengths, heads, scale):
    rows = triple.shape[0]
    wide = heads * WIDE
    step = 256 if rows % 256 == 0 else rows
    whole = pl.BlockSpec((rows, wide), lambda i: (0, 0))
    row = pl.BlockSpec((8, rows), lambda i: (0, 0))
    return pl.pallas_call(
        partial(attend_back_kernel, heads, scale),
        grid=(rows // step,),
        in_specs=[
            whole,
            pl.BlockSpec((step, wide), lambda i: (i, 1)),
            pl.BlockSpec((step, wide), lambda i: (i, 2)),
            pl.BlockSpec((rows, heads * HEAD_DIM), lambda i: (0, 0)),
            whole,
            row,
            pl.BlockSpec(memory_space=pltpu.SMEM),
        ],
        out_specs=[
            pl.BlockSpec((rows, heads * HEAD_DIM), lambda i: (0, 0)),
            pl.BlockSpec((step, 2 * heads * HEAD_DIM), lambda i: (i, 0)),
        ],
        out_shape=[
            jax.ShapeDtypeStruct((rows, heads * HEAD_DIM), BF16),
            jax.ShapeDtypeStruct((rows, 2 * heads * HEAD_DIM), BF16),
        ],
        scratch_shapes=[
            pltpu.VMEM((rows, wide), F32),
            pltpu.VMEM((rows, wide), BF16),
            pltpu.VMEM((8, rows), F32),
        ],
        compiler_params=pltpu.CompilerParams(vmem_limit_bytes=48 * 2**20),
        cost_estimate=pl.CostEstimate(
            flops=20 * rows * rows * wide,
            bytes_accessed=14 * rows * wide,
            transcendentals=heads * rows * rows,
        ),
    )(triple, triple, triple, out_grad, out, lse, lengths)


def by_group_kernel(x_ref, w_ref, out_ref):
    groups, rows, columns = out_ref.shape
    product = times_transposed(x_ref[...], w_ref[...]).astype(BF16)
    for g in range(groups):
        out_ref[g] = product[:, g * columns : (g + 1) * columns]


def product_by_group(x, w, groups):
    rows, depth = x.shape
    columns = w.shape[0] // groups
    steps = 2
    return pl.pallas_call(
        by_group_kernel,
        grid=(steps,),
        in_specs=[
            pl.BlockSpec((rows, depth), lambda j: (0, 0)),
            pl.BlockSpec((w.shape[0] // steps, depth), lambda j: (j, 0)),
        ],
        out_specs=pl.BlockSpec((groups // steps, rows, columns), lambda j: (j, 0, 0)),
        out_shape=jax.ShapeDtypeStruct((groups, rows, columns), BF16),
        cost_estimate=pl.CostEstimate(
            flops=2 * rows * depth * w.shape[0],
            bytes_accessed=2 * depth * (rows + w.shape[0]) + 2 * rows * w.shape[0],
            transcendentals=0,
        ),
    )(x, w)


def gelu_kernel(rows_at_once, x_ref, up_ref, bias_ref, value_ref, slope_ref):
    for start in range(0, x_ref.shape[0], rows_at_once):
        at = pl.ds(start, rows_at_once)
        pre = dot(x_ref[at, :], up_ref[...]) + bias_ref[...]
        bell = jnp.exp(-0.5 * pre * pre)
        t = 1.0 / (1.0 + (0.3275911 * 0.5**0.5) * jnp.abs(pre))
        tail = 0.5 * 1.061405429
        for c in (-1.453152027, 1.421413741, -0.284496736, 0.254829592):
            tail = tail * t + 0.5 * c
        tail = tail * t * bell
        below = jnp.where(pre < 0.0, tail, 1.0 - tail)
        value_ref[at, :] = (pre * below).astype(BF16)
        slope_ref[at, :] = below + pre * bell * (0.5 / math.pi) ** 0.5


def gelu_of_matmul(x, up, bias):
    rows, depth = x.shape
    columns = up.shape[1]
    step = 384 if columns % 384 == 0 else columns
    block = pl.BlockSpec((rows, step), lambda j: (0, j))
    return pl.pallas_call(
        partial(gelu_kernel, 640 if rows % 640 == 0 else rows),
        grid=(columns // step,),
        in_specs=[
            pl.BlockSpec((rows, depth), lambda j: (0, 0)),
            pl.BlockSpec((depth, step), lambda j: (0, j)),
            pl.BlockSpec((1, step), lambda j: (0, j)),
        ],
        out_specs=[block, block],
        out_shape=[
            jax.ShapeDtypeStruct((rows, columns), BF16),
            jax.ShapeDtypeStruct((rows, columns), F32),
        ],
        compiler_params=pltpu.CompilerParams(vmem_limit_bytes=40 * 2**20),
        cost_estimate=pl.CostEstimate(
            flops=2 * rows * depth * columns,
            bytes_accessed=2 * depth * (rows + columns) + 6 * rows * columns,
            transcendentals=rows * columns,
        ),
    )(x, up, bias.reshape(1, columns))


def feed_back_kernel(
    local, grad_ref, up_ref, down_ref, slope_ref, low_ref, sums_ref, own_ref, *back_refs
):
    pre_grad = times_transposed(grad_ref[...], down_ref[...]) * slope_ref[...]
    sums_ref[...] = jnp.sum(pre_grad, axis=0, keepdims=True)
    low = pre_grad.astype(BF16)
    low_ref[...] = low
    back = times_transposed(low, up_ref[...])
    own_ref[...] = back[:local]
    for k, back_ref in enumerate(back_refs):
        back_ref[...] = back[(k + 1) * local : (k + 2) * local].astype(BF16)


def feed_back(grad, up, down, slope, local):
    rows, depth = grad.shape
    columns = up.shape[1]
    return pl.pallas_call(
        partial(feed_back_kernel, local),
        out_shape=[
            jax.ShapeDtypeStruct((rows, columns), BF16),
            jax.ShapeDtypeStruct((1, columns), F32),
            jax.ShapeDtypeStruct((local, depth), F32),
        ]
        + [jax.ShapeDtypeStruct((local, depth), BF16)] * (rows // local - 1),
        compiler_params=pltpu.CompilerParams(vmem_limit_bytes=52 * 2**20),
        cost_estimate=pl.CostEstimate(
            flops=4 * rows * depth * columns,
            bytes_accessed=4 * depth * columns + 6 * rows * columns + 4 * rows * depth,
            transcendentals=0,
        ),
    )(grad, up, down, slope)


def on_device(
    nd, ns,
    inputs, skipped, item_lengths,
    skip_w, qkv_w, proj_w, fc1_w, fc2_w,
    skip_b, ln1_g, ln1_b, proj_b, ln2_g, ln2_b, fc1_b, fc2_b,
    cotangent,
):
    _, local, features = inputs.shape
    hidden_units = fc1_w.shape[1]
    n = nd * ns
    row_len = local * ns
    heads = HEADS // ns
    head_cols = heads * HEAD_DIM
    wide = 3 * head_cols
    small = features // n
    scale = HEAD_DIM ** (-0.5)
    hidden_part = hidden_units // nd
    joined_part = 2 * features // nd
    part = features // nd
    places = ns // 2
    dp_at = lax.axis_index("dp")
    seq_at = lax.axis_index("seq")
    core = seq_at % 2
    after = lax.optimization_barrier

    def swap(v, k):
        return lax.ppermute(v, "dp", [(i, i ^ k) for i in range(nd)])

    def other_core(v):
        return lax.ppermute(v, "seq", [(i, i ^ 1) for i in range(ns)])

    def index(v, at, axis=0):
        return lax.dynamic_index_in_dim(v, at, axis, keepdims=False)

    def gather_rows(v):
        return jnp.concatenate([v] + [swap(v, k) for k in range(1, nd)], axis=0)

    def add_blocks(own, low):
        for k in range(1, nd):
            own = own + swap(low[k], k).astype(F32)
        return own

    def low_rows(partial_sums):
        return partial_sums.astype(BF16).reshape(nd, local, features)

    def widen(v):
        v = v.reshape(v.shape[0], v.shape[1] // HEAD_DIM, HEAD_DIM)
        return jnp.pad(v, ((0, 0), (0, 0), (0, WIDE - HEAD_DIM))).reshape(v.shape[0], -1)

    def seq_exchange(v):
        return lax.all_to_all(v, "seq", 0, 0, tiled=True)

    def core_sums(terms):
        terms = terms.reshape((places, 2) + terms.shape[1:])
        given = index(terms, 1 - core, 1).astype(BF16)
        kept = index(terms, core, 1).astype(F32)
        return (kept + other_core(given).astype(F32)).astype(BF16)

    def chip_sums(sums):
        groups = [[i * 2 + c for i in range(places)] for c in range(2)]
        terms = lax.all_to_all(sums, "seq", 0, 0, axis_index_groups=groups, tiled=True)
        return jnp.sum(terms.reshape(sums.shape).astype(F32), axis=0)

    skip_part = lax.all_gather(skip_w, "seq", axis=0, tiled=True)

    own_vectors = (skip_b, ln1_g, ln1_b, proj_b, ln2_g, ln2_b, fc2_b, fc1_b)
    packed = jnp.concatenate(own_vectors)
    own_size = packed.shape[0]
    padded = -(-own_size // 1024) * 1024
    packed = jnp.pad(packed, (0, padded - own_size)).reshape(padded // 128, 128)
    packed = jnp.broadcast_to(packed[None], (n,) + packed.shape)
    vectors = lax.all_to_all(packed, ("dp", "seq"), 0, 0, tiled=True)
    vectors = vectors.reshape(n, padded).astype(F32)

    joined_slices = jnp.stack(
        [
            half[:, at * joined_part : (at + 1) * joined_part]
            for half in (inputs[0], skipped[0])
            for at in range(nd // 2)
        ]
    )
    joined_here = jnp.concatenate(
        [index(joined_slices, dp_at)]
        + [swap(index(joined_slices, dp_at ^ k), k) for k in range(1, nd)],
        axis=0,
    )
    at = lax.broadcasted_iota(jnp.int32, (features, features), 0)
    block, row = at // small, at % small
    row = ((block % nd) ^ dp_at) * part + (block // nd) * small + row
    order = (row == lax.broadcasted_iota(jnp.int32, (features, features), 1)).astype(BF16)
    qkv_out = qkv_w.reshape(small, 3, ns, head_cols).transpose(2, 0, 1, 3).reshape(ns, small, wide)
    up_slices = jnp.swapaxes(fc1_w.reshape(small, nd, hidden_part), 0, 1)
    up_slices = jnp.concatenate(
        [index(up_slices, dp_at)] + [swap(index(up_slices, dp_at ^ k), k) for k in range(1, nd)],
        axis=0,
    )
    qkv_out, skip_part, joined_here, vectors, up_slices = after(
        (qkv_out, skip_part, joined_here, vectors, up_slices)
    )
    def vector(at):
        return vectors[:, at * small : (at + 1) * small].reshape(features)

    b_skip, g_one, b_one, b_proj, g_two, b_two, b_down = (vector(i) for i in range(7))
    up_bias = lax.dynamic_slice_in_dim(vectors[:, 7 * small : own_size], dp_at * ns, ns, 0)
    up_bias = up_bias.reshape(hidden_part)

    first_terms = dot(joined_here, skip_part)
    first = add_blocks(first_terms[:local], low_rows(first_terms)) + b_skip
    qkv_mine = seq_exchange(qkv_out).reshape(part, wide)
    xhat_one, inverse_one = norm_pieces(first)
    normed_one = (xhat_one * g_one + b_one).astype(BF16)
    normed_one, qkv_mine, own_proj = after((normed_one, qkv_mine, proj_w))
    normed_one_row = lax.all_gather(normed_one, "seq", axis=0, tiled=True)

    qkv_mine = lax.all_gather(qkv_mine, "dp", axis=0, tiled=True)
    qkv_mine, own_proj, grad_out = after((qkv_mine, own_proj, cotangent[0]))
    grad_blocks = [grad_out] + [swap(grad_out, k) for k in range(1, nd)]
    proj_rows = lax.all_gather(own_proj, "seq", axis=0, tiled=True)
    half = part // 2
    own_half = lax.dynamic_slice_in_dim(proj_rows, core * half, half, 0)
    proj_halves = [swap(own_half, k) for k in range(1, nd)]
    normed_one_row, qkv_mine, qkv_wide, proj_rows, grad_blocks = after(
        (normed_one_row, qkv_mine, widen(qkv_mine), proj_rows, grad_blocks)
    )
    up_part = lax.all_gather(up_slices, "seq", axis=0, tiled=True)
    triple = dot(normed_one_row, qkv_wide).astype(BF16)
    attended, attended_low, lse = attend(triple, item_lengths, heads, scale)

    def heads_to_tokens(v):
        v = seq_exchange(v.reshape(ns, local, head_cols))
        return jnp.swapaxes(v, 0, 1).reshape(local, features)

    attended_low, proj_halves, proj_rows, grad_blocks = after(
        (attended_low, proj_halves, proj_rows, grad_blocks)
    )
    grad_out_rows = jnp.concatenate(grad_blocks, axis=0)
    w_proj = lax.dynamic_update_slice_in_dim(
        jnp.zeros((features, features), BF16), proj_rows, dp_at * part, 0
    )
    for k in range(1, nd):
        place = (dp_at ^ k) * 2
        here = proj_halves[k - 1]
        there = other_core(here)
        w_proj = lax.dynamic_update_slice_in_dim(w_proj, here, (place + core) * half, 0)
        w_proj = lax.dynamic_update_slice_in_dim(w_proj, there, (place + 1 - core) * half, 0)
    attended_low = heads_to_tokens(attended_low)
    attended_low, grad_out_rows, w_proj = after((attended_low, grad_out_rows, w_proj))
    own_down, attended_low, up_part = after((fc2_w, attended_low, up_part))
    down_part = lax.all_gather(own_down, "seq", axis=0, tiled=True)
    second = first + dot(attended_low, w_proj) + b_proj
    xhat_two, inverse_two = norm_pieces(second)
    normed_two = (xhat_two * g_two + b_two).astype(BF16)

    normed_two_rows = gather_rows(normed_two)
    up_part = inner(order, up_part).astype(BF16)
    normed_two_rows, up_part = after((normed_two_rows, up_part))
    hidden, slope = gelu_of_matmul(normed_two_rows, up_part, up_bias)

    fc2_terms = inner(hidden, grad_out_rows).astype(BF16)
    fc2_w_grad = lax.psum_scatter(fc2_terms, "seq", scatter_dimension=0, tiled=True)
    slope, fc2_terms = after((slope, fc2_terms))
    pre_low, up_sums, normed_two_grad, *up_blocks = feed_back(
        grad_out_rows, up_part, down_part, slope, local
    )
    up_blocks = [swap(block, k + 1) for k, block in enumerate(up_blocks)]
    fc1_terms = inner(times_transposed(normed_two_rows, order).astype(BF16), pre_low).astype(BF16)
    for block in up_blocks:
        normed_two_grad = normed_two_grad + block.astype(F32)
    normed_two_grad, fc1_terms = after((normed_two_grad, fc1_terms))
    through_two, ln2_g_grad, ln2_b_grad = norm_back(normed_two_grad, xhat_two, inverse_two, g_two)
    second_grad = grad_out.astype(F32) + through_two
    second_low = second_grad.astype(BF16)
    attended_grad = product_by_group(second_low, w_proj, ns)
    attended_grad, second_late, hidden_late, attended_low, fc1_terms = after(
        (attended_grad, second_low, hidden, attended_low, fc1_terms)
    )
    fc1_terms = lax.psum_scatter(fc1_terms, "seq", scatter_dimension=0, tiled=True)
    attended_grad = seq_exchange(attended_grad).reshape(row_len, head_cols)
    down_sums = dot(hidden_late, down_part)
    attended_slices = jnp.swapaxes(attended_low.reshape(local, nd, part), 0, 1)
    down_blocks = low_rows(down_sums)
    down_blocks = [swap(down_blocks[k], k) for k in range(1, nd)]
    attended_grad, down_blocks[0], second_late, attended_slices = after(
        (attended_grad, down_blocks[0], second_late, attended_slices)
    )
    triple_grad = jnp.concatenate(
        attend_back(triple, attended_grad, attended, lse, item_lengths, heads, scale), axis=1
    )
    one_back = times_transposed(triple_grad, qkv_mine).astype(BF16)
    one_back, triple_late, down_blocks, second_late, fc1_terms, fc2_w_grad = after(
        (one_back, triple_grad, down_blocks, second_late, fc1_terms, fc2_w_grad)
    )
    output = second + down_sums[:local] + b_down
    for block in down_blocks:
        output = output + block.astype(F32)
    output = output.astype(BF16)
    normed_one_grad = lax.psum_scatter(one_back, "seq", scatter_dimension=0, tiled=True)
    second_rows = gather_rows(second_late)
    qkv_terms = inner(normed_one_row, triple_late).reshape(nd, part, wide)
    qkv_low, second_rows = after((qkv_terms.astype(BF16), second_rows))
    qkv_blocks = [swap(index(qkv_low, dp_at ^ k), k) for k in range(1, nd)]
    attended_rows = jnp.concatenate(
        [index(attended_slices, dp_at)]
        + [swap(index(attended_slices, dp_at ^ k), k) for k in range(1, nd)],
        axis=0,
    )
    proj_terms = inner(attended_rows, second_rows).reshape(ns, small, features)
    proj_sums = core_sums(proj_terms)
    qkv_sum = index(qkv_terms, dp_at)
    for block in qkv_blocks:
        qkv_sum = qkv_sum + block.astype(F32)
    qkv_sum = qkv_sum.astype(BF16).reshape(ns, small, wide)
    normed_one_grad = normed_one_grad.astype(F32)
    through_one, ln1_g_grad, ln1_b_grad = norm_back(normed_one_grad, xhat_one, inverse_one, g_one)
    first_grad = second_grad + through_one
    first_low = first_grad.astype(BF16)
    first_low_rows = gather_rows(first_low)
    proj_w_grad = chip_sums(proj_sums)
    qkv_w_grad = seq_exchange(qkv_sum)
    first_low_rows, first_grad, proj_w_grad = after((first_low_rows, first_grad, proj_w_grad))
    skip_terms = inner(joined_here, first_low_rows).astype(BF16)
    skip_w_grad = lax.psum_scatter(skip_terms, "seq", scatter_dimension=0, tiled=True).astype(F32)
    skip_terms, first_low_rows, first_grad, fc1_terms, qkv_w_grad = after(
        (skip_terms, first_low_rows, first_grad, fc1_terms, qkv_w_grad)
    )
    fc1_terms = fc1_terms.reshape(nd, small, hidden_part)
    fc1_blocks = jnp.stack([fc1_terms[0]] + [swap(fc1_terms[k], k) for k in range(1, nd)])
    vector_grads = jnp.stack(
        [
            jnp.sum(first_grad, axis=0),
            ln1_g_grad,
            ln1_b_grad,
            jnp.sum(second_grad, axis=0),
            ln2_g_grad,
            ln2_b_grad,
            jnp.sum(grad_out.astype(F32), axis=0),
        ]
    )
    vector_grads = jnp.swapaxes(vector_grads.reshape(7, n, small), 0, 1).reshape(n, 7 * small)
    up_grads = up_sums.reshape(ns, hidden_units // n)
    up_grads = lax.dynamic_update_slice_in_dim(
        jnp.zeros((n, hidden_units // n), F32), up_grads, dp_at * ns, 0
    )
    vector_grads = jnp.concatenate([vector_grads, up_grads], axis=1)
    vector_grads = jnp.pad(vector_grads, ((0, 0), (0, padded - own_size)))
    vector_grads = lax.all_to_all(
        vector_grads.reshape(n, padded // 128, 128), ("dp", "seq"), 0, 0, tiled=True
    )
    joined_grad_part = times_transposed(first_low_rows, skip_part).astype(BF16)
    joined_grad_part = joined_grad_part.reshape(nd, local, joined_part)
    away = [joined_grad_part[0]] + [swap(joined_grad_part[k], k) for k in range(1, nd)]
    away = jnp.stack(away)
    joined_grad = jnp.concatenate(
        [index(away, dp_at ^ k) for k in range(nd)], axis=1
    ).astype(F32)
    fc1_w_grad = jnp.concatenate([index(fc1_blocks, dp_at ^ k) for k in range(nd)], axis=1)
    qkv_w_grad = (
        qkv_w_grad.reshape(ns, small, 3, head_cols).transpose(1, 2, 0, 3)
        .reshape(small, 3 * features)
    )
    vector_grads = jnp.sum(vector_grads, axis=0).reshape(padded)
    skip_b_grad, ln1_g_grad, ln1_b_grad, proj_b_grad, ln2_g_grad, ln2_b_grad, fc2_b_grad = (
        vector_grads[i * small : (i + 1) * small] for i in range(7)
    )
    fc1_b_grad = vector_grads[7 * small : own_size]
    return (
        output[None], joined_grad[None, :, :features], joined_grad[None, :, features:],
        skip_w_grad, qkv_w_grad.astype(F32), proj_w_grad,
        fc1_w_grad.astype(F32), fc2_w_grad.astype(F32),
        skip_b_grad, ln1_g_grad, ln1_b_grad, proj_b_grad, ln2_g_grad, ln2_b_grad,
        fc1_b_grad, fc2_b_grad,
    )


def solution(mesh):
    tokens = P("dp", "seq", None)
    matrix = P(("dp", "seq"), None)
    flat = P(("dp", "seq"))
    in_specs = (tokens, tokens, P("dp", None)) + (matrix,) * 5 + (flat,) * 8 + (tokens,)
    out_specs = (tokens,) * 3 + (matrix,) * 5 + (flat,) * 8
    return jax.shard_map(
        partial(on_device, mesh.shape["dp"], mesh.shape["seq"]),
        mesh=mesh, in_specs=in_specs, out_specs=out_specs, check_vma=False,
    )
```
